32 devices in a mesh: groups: 2 (over x), dp: 8 (over z, y), tensor: 2 (over core).
Axes of the slice: x: 2, y: 2, z: 4, core: 2. Of those that a mesh axis runs over, the one named last changes fastest.
Arguments:
- activations: bfloat16 [4096, 28672], P(('groups', 'dp'), 'tensor'), parts along dimension 0, may hold values from -6 to 6
- out_grads: bfloat16 [4096, 8192], P(('groups', 'dp'), 'tensor'), parts along dimension 0, may hold values from -6 to 6
- proj_in: bfloat16 [28672, 64], P('tensor'), may hold values from -0.03125 to 0.03125
- proj_out: bfloat16 [8192, 64], P('tensor'), may hold values from -0.0625 to 0.0625
- stored: bfloat16 [16384, 4096], P(('groups', 'dp')), parts along dimension 0, may hold values from -0.375 to 0.375
- counts: int32 [256], P(('groups', 'dp')), parts along dimension 0, may hold values from 1 to 16
- query_ids: int32 [512], P('groups'), parts along dimension 0, may hold values from 0 to 127
Outputs:
- gram: float32 [8192, 4096], P(('groups', 'dp'), 'tensor'), parts along dimension 0
- scores: float32 [512, 128], P('groups', 'dp'), parts along dimension 0
The draws below stay inside these ranges and needn't reach their ends.
There are 2 independent parts, one for each index of `groups`. The reference program is written for one: setup_inputs(seed, part) draws one part's arguments, and reference() takes and returns one part's arrays. A program takes and returns all parts, laid end to end along the dimension named above; an argument that names none is the same for every part. Nothing has to cross between parts.
All inputs are finite; a program needn't handle non-finite values.
Results may differ from the reference program's by a relative error of at most 0.015.
Values may be sent and summed in bfloat16 or wider, within the bound.
No kernel may reach another device: no remote copies, remote signals or barrier semaphores. Data moves between devices by JAX's collectives and lax.ppermute only.
A program may use at most 192 MiB of HBM per device.

```python
import jax
import jax.numpy as jnp
from jax import lax

D = 8192
FF = 28672
R = 64
K = 4096
SEQ = 16
QUERIES = 256
EXAMPLES = 128
TOK_ROWS = 2048
CACHE_ROWS = 8192
N_DP = 8


def place_ends(values, own_key, low, top_value):
    extent = values.shape
    place = [jax.random.randint(jax.random.fold_in(own_key, axis), (), 0, extent[axis]) for axis in range(len(extent))]
    values = values.at[tuple(place)].set(low)
    longest = extent.index(max(extent))
    place[longest] = (place[longest] + 1) % extent[longest]
    return values.at[tuple(place)].set(top_value)


def steps_of(own_key, dims, split, least, largest):
    level = 1.0
    for dim, shards_of in split:
        steps = jax.random.uniform(jax.random.fold_in(jax.random.fold_in(own_key, 6), dim), (shards_of,), jnp.float32, least / len(split), largest / len(split))
        level = level * jnp.repeat(jnp.exp(steps), dims[dim] // shards_of).reshape((-1,) + (1,) * (len(dims) - 1 - dim))
    return level


def bell_draw(rng, dims, scale, most, cuts=(), kind=jnp.bfloat16):
    values = scale * jax.random.normal(rng, dims, jnp.float32)
    if cuts:
        values = values * steps_of(rng, dims, cuts, -0.22, 0.18)
    return jnp.clip(values, -most, most).astype(kind)


def setup_inputs(seed: int = 0, part: int = 0) -> dict:
    splits = jax.random.split(jax.random.key(seed), 8)
    part_splits = jax.random.split(jax.random.fold_in(splits[7], part), 8)
    activations = bell_draw(part_splits[0], (TOK_ROWS, FF), 1.0, 6.0, ((0, 8), (1, 2)))
    out_grads = bell_draw(part_splits[1], (TOK_ROWS, D), 1.0, 6.0, ((0, 8), (1, 2)))
    proj_in = bell_draw(splits[2], (FF, R), FF ** -0.5, 0.03125, ((0, 2),))
    proj_out = bell_draw(splits[3], (D, R), D ** -0.5, 0.0625, ((0, 2),))
    stored = bell_draw(part_splits[4], (CACHE_ROWS, K), (CACHE_ROWS // 32) ** -0.5, 0.375, ((0, 8),))
    counts = place_ends(jax.random.randint(part_splits[5], (EXAMPLES,), 1, SEQ + 1), jax.random.fold_in(part_splits[5], 1), 1, SEQ).astype(jnp.int32)
    query_ids = place_ends(jax.random.randint(part_splits[6], (QUERIES,), 0, EXAMPLES), jax.random.fold_in(part_splits[6], 1), 0, EXAMPLES - 1).astype(jnp.int32)
    return {"activations": activations, "out_grads": out_grads, "proj_in": proj_in, "proj_out": proj_out, "stored": stored, "counts": counts, "query_ids": query_ids}


damping = 1.0

def example_vectors(act_proj, grad_proj, counts, seq_len):
    examples = counts.shape[0]
    rank = act_proj.shape[1]
    position = jnp.arange(seq_len, dtype=jnp.int32)[None, :]
    count_f = counts.astype(jnp.float32)[:, None]
    weights = jnp.where(position < counts[:, None], 1.0 / count_f, jnp.float32(0.0))
    outer = jnp.einsum('es,esi,esj->eij', weights, act_proj.reshape(examples, seq_len, rank), grad_proj.reshape(examples, seq_len, rank))
    return outer.reshape(examples, rank * rank).astype(jnp.bfloat16)

def reference(activations, out_grads, proj_in, proj_out, stored, counts, query_ids):
    highest = lax.Precision.HIGHEST
    act_proj = jnp.dot(activations.astype(jnp.float32), proj_in.astype(jnp.float32), preferred_element_type=jnp.float32)
    grad_proj = jnp.dot(out_grads.astype(jnp.float32), proj_out.astype(jnp.float32), preferred_element_type=jnp.float32)
    vectors = example_vectors(act_proj, grad_proj, counts, SEQ)
    gram = jnp.dot(stored.T.astype(jnp.float32), stored.astype(jnp.float32), preferred_element_type=jnp.float32)
    gram = gram + jnp.dot(vectors.T.astype(jnp.float32), vectors.astype(jnp.float32), preferred_element_type=jnp.float32)
    gram = gram + damping * jnp.eye(K, dtype=jnp.float32)
    width = K // N_DP
    corner = jnp.linalg.cholesky(gram[:width, :width])
    whiten = lax.linalg.triangular_solve(corner, gram[:width, :], left_side=True, lower=True)
    columns = vectors.astype(jnp.float32).T
    queries = columns[:, query_ids]
    u_train = lax.linalg.triangular_solve(corner, columns[:width, :], left_side=True, lower=True)
    r_train = columns - jnp.dot(whiten.T, u_train, precision=highest)
    u_query = lax.linalg.triangular_solve(corner, queries[:width, :], left_side=True, lower=True)
    r_query = queries - jnp.dot(whiten.T, u_query, precision=highest)
    scores = jnp.dot(u_query.T, u_train, precision=highest) + jnp.dot(r_query.T, r_train, precision=highest)
    return (gram, scores / R)
```

```python
import jax
import jax.numpy as jnp
from jax import lax
from jax.experimental import pallas as pl
from jax.experimental.pallas import tpu as pltpu
from jax.sharding import PartitionSpec as P

R = 64
SEQ = 16
damping = 1.0
EXACT = lax.Precision.HIGHEST
SWAP = [(0, 1), (1, 0)]
VMEM_BYTES = 40 * 1024 * 1024


def ring_order(mesh):
    count = mesh.shape["dp"]
    coords = [getattr(device, "coords", None) for device in mesh.devices[0, :, 0]]
    if None in coords:
        return list(range(count))
    moving = [axis for axis in range(3) if len({place[axis] for place in coords}) > 1]
    fast = [axis for axis in moving if coords[0][axis] != coords[1][axis]]
    if len(moving) == 2 and len(fast) == 1 and len({place[fast[0]] for place in coords}) == 2:
        return list(range(0, count, 2)) + list(range(1, count, 2))[::-1]
    return list(range(count))


def lead_dot(left, right, precision=None):
    return lax.dot_general(
        left, right, (((0,), (0,)), ((), ())), precision=precision, preferred_element_type=jnp.float32
    )


def exact_dot(left, right):
    return jnp.dot(left, right, precision=EXACT, preferred_element_type=jnp.float32)


def panel_kernel(place_ref, left_ref, right_ref, out_ref):
    out_ref[0] = jnp.dot(left_ref[...].T, right_ref[...], preferred_element_type=jnp.float32)


def panel_parts(stored, tensor_index, owners, group, width):
    rows = stored.shape[0]
    return pl.pallas_call(
        panel_kernel,
        grid_spec=pltpu.PrefetchScalarGridSpec(
            num_scalar_prefetch=1,
            grid=(owners,),
            in_specs=[
                pl.BlockSpec((rows, group), lambda o, place: (0, 2 * o + place[0])),
                pl.BlockSpec((rows, width), lambda o, place: (0, 0)),
            ],
            out_specs=pl.BlockSpec((1, group, width), lambda o, place: (o, 0, 0)),
        ),
        out_shape=jax.ShapeDtypeStruct((owners, group, width), jnp.float32),
        compiler_params=pltpu.CompilerParams(vmem_limit_bytes=VMEM_BYTES),
        cost_estimate=pl.CostEstimate(
            flops=2 * rows * owners * group * width,
            bytes_accessed=2 * rows * group * owners + 4 * owners * group * width,
            transcendentals=0,
        ),
        name="panel_parts",
    )(jnp.reshape(tensor_index, (1,)).astype(jnp.int32), stored, stored)


def window_part(stored, owner, first, count, arrived, last=False):
    rows, full = stored.shape
    groups = full // owner[1]
    group = owner[1]

    def kernel(place_ref, left_ref, right_ref, *refs):
        turned = refs[-1]

        @pl.when(pl.program_id(0) == 0)
        def _():
            turned[...] = left_ref[...].T

        total = jnp.dot(turned[...], right_ref[...], preferred_element_type=jnp.float32)
        for ref in refs[: len(arrived)]:
            total = total + ref[...].astype(jnp.float32)
        if last:
            refs[-3][...] = total
            refs[-2][0] = total.T.astype(jnp.bfloat16)
        else:
            refs[-2][...] = total.astype(jnp.bfloat16)

    block = pl.BlockSpec((group, group), lambda k, place: (0, k))
    if last:
        out_specs = [block, pl.BlockSpec((1, group, group), lambda k, place: (k, 0, 0))]
        out_shape = [
            jax.ShapeDtypeStruct((group, count * group), jnp.float32),
            jax.ShapeDtypeStruct((count, group, group), jnp.bfloat16),
        ]
    else:
        out_specs = block
        out_shape = jax.ShapeDtypeStruct((group, count * group), jnp.bfloat16)
    return pl.pallas_call(
        kernel,
        grid_spec=pltpu.PrefetchScalarGridSpec(
            num_scalar_prefetch=1,
            grid=(count,),
            in_specs=[
                pl.BlockSpec((rows, group), lambda k, place: (0, place[0])),
                pl.BlockSpec((rows, group), lambda k, place: (0, lax.rem(place[0] + first + k, groups))),
            ]
            + [block] * len(arrived),
            out_specs=out_specs,
            scratch_shapes=[pltpu.VMEM((group, rows), jnp.bfloat16)],
        ),
        out_shape=out_shape,
        compiler_params=pltpu.CompilerParams(vmem_limit_bytes=VMEM_BYTES),
        cost_estimate=pl.CostEstimate(
            flops=2 * rows * count * group * group,
            bytes_accessed=2 * rows * group * (count + 1) + 4 * count * group * group,
            transcendentals=0,
        ),
        name="window_part",
    )(jnp.reshape(owner[0], (1,)).astype(jnp.int32), stored, stored, *arrived)


def solve_kernel(matrix_ref, right_ref, out_ref, work, inverse, residual):
    size = matrix_ref.shape[0]
    block = inverse.shape[0]
    work[...] = matrix_ref[...]
    out_ref[...] = right_ref[...]
    row_ids = lax.broadcasted_iota(jnp.int32, (block, block), 0)
    col_ids = lax.broadcasted_iota(jnp.int32, (block, block), 1)
    eye = (row_ids == col_ids).astype(jnp.float32)
    for start in range(0, size, block):
        here = slice(start, start + block)
        rest = slice(start + block, size)
        corner = work[here, here]
        norm = jnp.max(jnp.sum(jnp.abs(corner), axis=0))
        inverse[...] = eye / norm
        residual[...] = eye - corner / norm

        def unfinished(state):
            step, worst = state
            return jnp.logical_and(step < 40, worst > 1e-5)

        def improve(state):
            step, _ = state
            better = inverse[...] + exact_dot(inverse[...], residual[...])
            left_over = eye - exact_dot(work[here, here], better)
            inverse[...] = better
            residual[...] = left_over
            return step + 1, jnp.max(jnp.abs(left_over))

        lax.while_loop(unfinished, improve, (jnp.int32(0), jnp.float32(1.0)))
        found = inverse[...] + exact_dot(inverse[...], residual[...])
        solved = exact_dot(found, out_ref[here, :])
        out_ref[here, :] = solved
        if start + block < size:
            across = exact_dot(found, work[here, rest])
            down = work[rest, here]
            work[rest, rest] = work[rest, rest] - exact_dot(down, across)
            out_ref[rest, :] = out_ref[rest, :] - exact_dot(down, solved)
            work[here, rest] = across
    for start in range(size - 2 * block, -1, -block):
        here = slice(start, start + block)
        rest = slice(start + block, size)
        out_ref[here, :] = out_ref[here, :] - exact_dot(work[here, rest], out_ref[rest, :])


def solve(matrix, right):
    size, columns = right.shape
    block = 128
    return pl.pallas_call(
        solve_kernel,
        out_shape=jax.ShapeDtypeStruct((size, columns), jnp.float32),
        scratch_shapes=[
            pltpu.VMEM((size, size), jnp.float32),
            pltpu.VMEM((block, block), jnp.float32),
            pltpu.VMEM((block, block), jnp.float32),
        ],
        compiler_params=pltpu.CompilerParams(vmem_limit_bytes=VMEM_BYTES),
        cost_estimate=pl.CostEstimate(flops=12 * size**3, bytes_accessed=4 * size * (size + 2 * columns), transcendentals=0),
        name="solve",
    )(matrix, right)


def full_rows(place, near, far, turned, group):
    near_count = near.shape[1] // group
    far_count = far.shape[1] // group
    turned_count = turned.shape[0]
    half = near_count + far_count - 1
    groups = 2 * half

    def offset(c, place, mine):
        side = place[1] if mine else 1 - place[1]
        return lax.rem(side * half + c - place[0] + groups, groups)

    def near_map(mine):
        return lambda c, place: (0, jnp.minimum(offset(c, place, mine), near_count - 1))

    def far_map(mine):
        return lambda c, place: (0, jnp.clip(offset(c, place, mine) - near_count, 0, far_count - 1))

    def turned_map(mine):
        return lambda c, place: (jnp.clip(groups - 1 - offset(c, place, mine), 0, turned_count - 1), 0, 0)

    def kernel(place_ref, near_a, far_a, turned_a, near_b, far_b, turned_b, mine_ref, send_ref):
        c = pl.program_id(0)

        def pick(which, near_ref, far_ref, turned_ref, out_ref):
            step = offset(c, place_ref, which)

            @pl.when(step < near_count)
            def _():
                out_ref[...] = near_ref[...].astype(out_ref.dtype)

            @pl.when(jnp.logical_and(step >= near_count, step <= half))
            def _():
                out_ref[...] = far_ref[...].astype(out_ref.dtype)

            @pl.when(step > half)
            def _():
                out_ref[...] = turned_ref[0].astype(out_ref.dtype)

        pick(True, near_a, far_a, turned_a, mine_ref)
        pick(False, near_b, far_b, turned_b, send_ref)

    def sources(mine):
        return [
            pl.BlockSpec((group, group), near_map(mine)),
            pl.BlockSpec((group, group), far_map(mine)),
            pl.BlockSpec((1, group, group), turned_map(mine)),
        ]

    block = pl.BlockSpec((group, group), lambda c, place: (0, c))
    return pl.pallas_call(
        kernel,
        grid_spec=pltpu.PrefetchScalarGridSpec(
            num_scalar_prefetch=1,
            grid=(half,),
            in_specs=sources(True) + sources(False),
            out_specs=[block, block],
        ),
        out_shape=[
            jax.ShapeDtypeStruct((group, half * group), jnp.float32),
            jax.ShapeDtypeStruct((group, half * group), jnp.bfloat16),
        ],
        compiler_params=pltpu.CompilerParams(vmem_limit_bytes=VMEM_BYTES),
        name="full_rows",
    )(place, near, far, turned, near, far, turned)


def finish(place, mine, other, vectors, group):
    examples = vectors.shape[0]
    half_cols = mine.shape[1]
    wide = half_cols // 2

    def kernel(place_ref, mine_ref, other_ref, rows_ref, cols_ref, out_ref):
        r, c = pl.program_id(0), pl.program_id(1)
        added = jnp.dot(rows_ref[...].T, cols_ref[...], preferred_element_type=jnp.float32)
        row_ids = (place_ref[0] - place_ref[1] + r) * group + lax.broadcasted_iota(jnp.int32, (group, wide), 0)
        col_ids = place_ref[1] * half_cols + c * wide + lax.broadcasted_iota(jnp.int32, (group, wide), 1)
        added = added + jnp.where(row_ids == col_ids, jnp.float32(damping), jnp.float32(0.0))

        @pl.when(r == place_ref[1])
        def _():
            out_ref[...] = added + mine_ref[...]

        @pl.when(r != place_ref[1])
        def _():
            out_ref[...] = added + other_ref[...].astype(jnp.float32)

    return pl.pallas_call(
        kernel,
        grid_spec=pltpu.PrefetchScalarGridSpec(
            num_scalar_prefetch=1,
            grid=(2, 2),
            in_specs=[
                pl.BlockSpec((group, wide), lambda r, c, place: (0, c)),
                pl.BlockSpec((group, wide), lambda r, c, place: (0, c)),
                pl.BlockSpec((examples, group), lambda r, c, place: (0, place[0] - place[1] + r)),
                pl.BlockSpec((examples, wide), lambda r, c, place: (0, 2 * place[1] + c)),
            ],
            out_specs=pl.BlockSpec((group, wide), lambda r, c, place: (r, c)),
        ),
        out_shape=jax.ShapeDtypeStruct((2 * group, half_cols), jnp.float32),
        compiler_params=pltpu.CompilerParams(vmem_limit_bytes=VMEM_BYTES),
        name="finish",
    )(place, mine, other, vectors, vectors)


def in_order(tensor_index, mine, other, axis):
    return jnp.where(
        tensor_index == 0,
        jnp.concatenate([mine, other], axis=axis),
        jnp.concatenate([other, mine], axis=axis),
    )


def local(ring, activations, out_grads, proj_in, proj_out, stored, counts, query_ids):
    owners = len(ring)
    full = stored.shape[1]
    width = full // owners
    group = width // 2
    groups = 2 * owners
    half = owners // 2
    t = lax.axis_index("tensor")
    d = lax.axis_index("dp")
    g = 2 * d + t
    place = jnp.stack([g, t]).astype(jnp.int32)
    around = jnp.array(ring + ring + ring, jnp.int32)
    spot = jnp.array([ring.index(index) for index in range(owners)], jnp.int32)[d]
    ahead = [(ring[p], ring[(p + 1) % owners]) for p in range(owners)]
    back = [(ring[(p + 1) % owners], ring[p]) for p in range(owners)]

    def owner_at(step):
        return around[spot + owners + step]

    sides = jnp.concatenate(
        [
            jnp.dot(activations, proj_in, preferred_element_type=jnp.float32),
            jnp.dot(out_grads, proj_out, preferred_element_type=jnp.float32),
        ],
        axis=1,
    )
    sides = sides + lax.ppermute(sides, "tensor", SWAP)

    panels = panel_parts(stored, t, owners, group, width)
    corner_rows = lax.psum(panels[0], "dp")

    def panel_at(step):
        return lax.dynamic_index_in_dim(panels, owner_at(step), 0, keepdims=False)

    examples = counts.shape[0]
    rank = proj_in.shape[1]
    position = jnp.arange(SEQ, dtype=jnp.int32)[None, :]
    weights = jnp.where(
        position < counts[:, None], 1.0 / counts.astype(jnp.float32)[:, None], jnp.float32(0.0)
    )
    act_half = lax.dynamic_slice_in_dim(sides, t * (rank // 2), rank // 2, 1)
    outer = jnp.einsum(
        "es,esi,esj->eij",
        weights,
        act_half.reshape(examples, SEQ, rank // 2),
        sides[:, rank:].reshape(examples, SEQ, rank),
        precision=EXACT,
    )
    vectors_half = outer.reshape(examples, full // 2).astype(jnp.bfloat16)
    gathered_half = lax.all_gather(vectors_half, "dp", axis=0, tiled=True)
    vectors = in_order(t, gathered_half, lax.ppermute(gathered_half, "tensor", SWAP), 1)

    near_count = groups // 4 + 1
    far_count = groups // 2 + 1 - near_count

    def window(step, first, count, arrived):
        return window_part(stored, (2 * owner_at(step) + t, group), first, count, arrived)

    far_ahead, far_back, near_ahead, near_back = [], [], [], []
    panel_ahead = panel_back = None
    for step in range(half, 0, -1):
        whole_step = step < half
        part_ahead, part_back = panel_at(step), panel_at(-step)
        if not whole_step:
            part_ahead, part_back = part_ahead[:, :group], part_back[:, group:]
        elif step == half - 1:
            blank = jnp.zeros_like(panel_ahead)
            part_ahead = part_ahead + jnp.concatenate([panel_ahead, blank], axis=1)
            part_back = part_back + jnp.concatenate([blank, panel_back], axis=1)
        else:
            part_ahead, part_back = part_ahead + panel_ahead, part_back + panel_back
        panel_ahead = lax.ppermute(part_ahead, "dp", ahead)
        panel_back = lax.ppermute(part_back, "dp", back)
        far_ahead = [lax.ppermute(window(step, near_count, far_count, far_ahead), "dp", ahead)]
        if whole_step:
            far_back = [lax.ppermute(window(-step, near_count, far_count, far_back), "dp", back)]
    for step in range(half, 0, -1):
        near_back = [lax.ppermute(window(-step, 0, near_count, near_back), "dp", back)]
        if step < half:
            near_ahead = [lax.ppermute(window(step, 0, near_count, near_ahead), "dp", ahead)]

    corner = in_order(t, corner_rows, lax.ppermute(corner_rows, "tensor", SWAP), 0)
    first_cols = vectors[:, :width]
    eye = jnp.eye(width, dtype=jnp.float32)
    corner = corner + lead_dot(first_cols, first_cols) + damping * eye
    scale = lax.rsqrt(jnp.sum(corner * eye, axis=1))
    first_rows = first_cols.astype(jnp.float32).T
    solved = solve(corner * scale[:, None] * scale[None, :], first_rows * scale[:, None]) * scale[:, None]
    own_cols = lax.dynamic_slice_in_dim(vectors, g * group, group, 1)
    row_ids = g * group + jnp.arange(group, dtype=jnp.int32)[:, None]
    damped = jnp.where(row_ids == jnp.arange(width, dtype=jnp.int32)[None, :], jnp.float32(damping), 0.0)
    panel = panel_at(0) + panel_ahead + panel_back + lead_dot(own_cols, first_cols) + damped
    rest = own_cols.astype(jnp.float32).T - exact_dot(panel, solved)
    pairs = lead_dot(rest, rest, EXACT)
    pairs = pairs + jnp.where(g == 0, lead_dot(first_rows, solved, EXACT), 0.0)
    pairs = lax.psum(pairs, ("dp", "tensor"))
    own_pairs = lax.dynamic_slice_in_dim(pairs, d * examples, examples, 1)
    chosen = (query_ids[:, None] == jnp.arange(pairs.shape[0], dtype=jnp.int32)[None, :]).astype(jnp.float32)
    scores = exact_dot(chosen, own_pairs) / R

    far, far_turned = window_part(
        stored, (g, group), near_count, far_count, far_ahead + far_back, last=True
    )
    near, near_turned = window_part(stored, (g, group), 0, near_count, near_ahead + near_back, last=True)
    turned = []
    for shift in range(1, groups // 2):
        block = near_turned[shift] if shift < near_count else far_turned[shift - near_count]
        turned.append(
            lax.ppermute(block, ("dp", "tensor"), [(h, (h + shift) % groups) for h in range(groups)])
        )
    mine, send = full_rows(place, near, far, jnp.stack(turned), group)
    other = lax.ppermute(send, "tensor", SWAP)
    return finish(place, mine, other, vectors, group), scores


def solution(mesh):
    placed = (
        P(("groups", "dp"), "tensor"),
        P(("groups", "dp"), "tensor"),
        P("tensor", None),
        P("tensor", None),
        P(("groups", "dp"), None),
        P(("groups", "dp")),
        P("groups"),
    )
    ring = ring_order(mesh)

    def program(*args):
        return local(ring, *args)

    return jax.shard_map(
        program,
        mesh=mesh,
        in_specs=placed,
        out_specs=(P(("groups", "dp"), "tensor"), P("groups", "dp")),
        check_vma=False,
    )
```

```python
import jax
import jax.numpy as jnp
from jax import lax
from jax.experimental import pallas as pl
from jax.experimental.pallas import tpu as pltpu
from jax.sharding import PartitionSpec as P

R = 64
SEQ = 16
damping = 1.0
EXACT = lax.Precision.HIGHEST
SWAP = [(0, 1), (1, 0)]
VMEM_BYTES = 56 * 1024 * 1024


class Ring:
    def __init__(self, mesh):
        self.count = mesh.shape["dp"]
        self.half = self.count // 2
        coords = [getattr(device, "coords", None) for device in mesh.devices[0, :, 0]]
        self.folded = False
        if None not in coords:
            moving = [axis for axis in range(3) if len({place[axis] for place in coords}) > 1]
            fast = [axis for axis in moving if coords[0][axis] != coords[1][axis]]
            self.folded = len(moving) == 2 and len(fast) == 1 and len({place[fast[0]] for place in coords}) == 2
        reach = [0, 0]
        self.offsets = []
        for distance in range(self.half - 1, 0, -1):
            side = 0 if reach[0] <= reach[1] else 1
            reach[side] += distance
            self.offsets.append(distance if side == 0 else -distance)

    def index_at(self, position):
        if isinstance(position, int):
            position = position % self.count
            if not self.folded:
                return position
            return 2 * position if position < self.half else 2 * (self.count - 1 - position) + 1
        position = lax.rem(position + 2 * self.count, self.count)
        if not self.folded:
            return position
        return jnp.where(position < self.half, 2 * position, 2 * (self.count - 1 - position) + 1)

    def position_of(self, index):
        if not self.folded:
            return index
        return jnp.where(lax.rem(index, 2) == 0, index // 2, self.count - 1 - index // 2)

    def shift(self, step):
        return [(self.index_at(p), self.index_at(p + step)) for p in range(self.count)]


def lead_dot(left, right, precision=None):
    return lax.dot_general(
        left, right, (((0,), (0,)), ((), ())), precision=precision, preferred_element_type=jnp.float32
    )


def exact_dot(left, right):
    return jnp.dot(left, right, precision=EXACT, preferred_element_type=jnp.float32)


def trail_dot(left, right):
    return lax.dot_general(
        left, right, (((1,), (1,)), ((), ())), precision=EXACT, preferred_element_type=jnp.float32
    )


def window_part(ring, place, stored, group, step, slots, arrived, last=False):
    rows = stored.shape[0]
    count = len(slots)

    def position(ref):
        return lax.rem(ring.position_of(ref[0]) + step + 2 * ring.count, ring.count)

    def left_map(ref):
        return 2 * ring.index_at(position(ref)) + ref[1]

    def right_map(slot, ref):
        offset, core = slot
        owner = position(ref)
        if core is None:
            core = jnp.where(owner < ring.half, ref[1], 1 - ref[1])
        return 2 * ring.index_at(owner + offset) + core

    def kernel(place_ref, left_ref, *refs):
        rights, refs = refs[:count], refs[count:]
        sums, outs = refs[: len(arrived)], refs[len(arrived) :]
        turned = left_ref[...].T
        for k in range(count):
            cols = slice(k * group, (k + 1) * group)
            total = jnp.dot(turned, rights[k][...], preferred_element_type=jnp.float32)
            for ref in sums:
                total = total + ref[:, cols].astype(jnp.float32)
            total = total.astype(jnp.bfloat16)
            if last:
                outs[0][k] = total
                outs[1][k] = total.T
            else:
                outs[0][:, cols] = total

    flat = pl.BlockSpec((group, count * group), lambda i, ref: (0, 0))
    if last:
        out_specs = [pl.BlockSpec((count, group, group), lambda i, ref: (0, 0, 0))] * 2
        out_shape = [jax.ShapeDtypeStruct((count, group, group), jnp.bfloat16)] * 2
    else:
        out_specs = flat
        out_shape = jax.ShapeDtypeStruct((group, count * group), jnp.bfloat16)
    in_specs = [pl.BlockSpec((rows, group), lambda i, ref: (0, left_map(ref)))]
    for slot in slots:
        in_specs.append(pl.BlockSpec((rows, group), lambda i, ref, slot=slot: (0, right_map(slot, ref))))
    return pl.pallas_call(
        kernel,
        grid_spec=pltpu.PrefetchScalarGridSpec(
            num_scalar_prefetch=1,
            grid=(1,),
            in_specs=in_specs + [flat] * len(arrived),
            out_specs=out_specs,
        ),
        out_shape=out_shape,
        compiler_params=pltpu.CompilerParams(vmem_limit_bytes=VMEM_BYTES),
        cost_estimate=pl.CostEstimate(
            flops=2 * rows * count * group * group,
            bytes_accessed=2 * rows * group * (count + 1) + 4 * count * group * group,
            transcendentals=0,
        ),
        name="window_part",
    )(place, *([stored] * (count + 1)), *arrived)


def solve_kernel(matrix_ref, right_ref, out_ref, work, inverse, residual):
    size = matrix_ref.shape[0]
    block = inverse.shape[0]
    work[...] = matrix_ref[...]
    out_ref[...] = right_ref[...]
    row_ids = lax.broadcasted_iota(jnp.int32, (block, block), 0)
    col_ids = lax.broadcasted_iota(jnp.int32, (block, block), 1)
    eye = (row_ids == col_ids).astype(jnp.float32)
    for start in range(0, size, block):
        here = slice(start, start + block)
        rest = slice(start + block, size)
        corner = work[here, here]
        norm = jnp.max(jnp.sum(jnp.abs(corner), axis=0))
        inverse[...] = eye / norm
        residual[...] = eye - corner / norm

        def unfinished(state):
            step, worst = state
            return jnp.logical_and(step < 40, worst > 1e-5)

        def improve(state):
            step, _ = state
            better = inverse[...] + exact_dot(inverse[...], residual[...])
            left_over = eye - exact_dot(work[here, here], better)
            inverse[...] = better
            residual[...] = left_over
            return step + 1, jnp.max(jnp.abs(left_over))

        lax.while_loop(unfinished, improve, (jnp.int32(0), jnp.float32(1.0)))
        found = inverse[...] + exact_dot(inverse[...], residual[...])
        solved = exact_dot(found, out_ref[here, :])
        out_ref[here, :] = solved
        if start + block < size:
            across = exact_dot(found, work[here, rest])
            down = work[rest, here]
            work[rest, rest] = work[rest, rest] - exact_dot(down, across)
            out_ref[rest, :] = out_ref[rest, :] - exact_dot(down, solved)
            work[here, rest] = across
    for start in range(size - 2 * block, -1, -block):
        here = slice(start, start + block)
        rest = slice(start + block, size)
        out_ref[here, :] = out_ref[here, :] - exact_dot(work[here, rest], out_ref[rest, :])


def solve(matrix, right):
    size, columns = right.shape
    block = 128
    return pl.pallas_call(
        solve_kernel,
        out_shape=jax.ShapeDtypeStruct((size, columns), jnp.float32),
        scratch_shapes=[
            pltpu.VMEM((size, size), jnp.float32),
            pltpu.VMEM((block, block), jnp.float32),
            pltpu.VMEM((block, block), jnp.float32),
        ],
        compiler_params=pltpu.CompilerParams(vmem_limit_bytes=VMEM_BYTES),
        cost_estimate=pl.CostEstimate(flops=12 * size**3, bytes_accessed=4 * size * (size + 2 * columns), transcendentals=0),
        name="solve",
    )(matrix, right)


def split_terms(value):
    high = value.astype(jnp.bfloat16)
    value = value - high.astype(jnp.float32)
    middle = value.astype(jnp.bfloat16)
    value = value - middle.astype(jnp.float32)
    return high, middle, value.astype(jnp.bfloat16)


def spread_back(place, stored, solved, owners, group):
    rows = stored.shape[0]
    width, examples = solved.shape

    def kernel(place_ref, first_ref, solved_ref, cols_ref, out_ref, terms):
        @pl.when(pl.program_id(0) == 0)
        def _():
            total = jnp.zeros((rows, examples), jnp.float32)
            for term in split_terms(solved_ref[...]):
                total = total + jnp.dot(first_ref[...], term, preferred_element_type=jnp.float32)
            for index, term in enumerate(split_terms(total.T)):
                terms[index * examples : (index + 1) * examples, :] = term

        product = jnp.dot(terms[...], cols_ref[...], preferred_element_type=jnp.float32)
        out_ref[0] = product[:examples] + product[examples : 2 * examples] + product[2 * examples :]

    return pl.pallas_call(
        kernel,
        grid_spec=pltpu.PrefetchScalarGridSpec(
            num_scalar_prefetch=1,
            grid=(owners,),
            in_specs=[
                pl.BlockSpec((rows, width), lambda o, ref: (0, 0)),
                pl.BlockSpec((width, examples), lambda o, ref: (0, 0)),
                pl.BlockSpec((rows, group), lambda o, ref: (0, 2 * o + ref[1])),
            ],
            out_specs=pl.BlockSpec((1, examples, group), lambda o, ref: (o, 0, 0)),
            scratch_shapes=[pltpu.VMEM((3 * examples, rows), jnp.bfloat16)],
        ),
        out_shape=jax.ShapeDtypeStruct((owners, examples, group), jnp.float32),
        compiler_params=pltpu.CompilerParams(vmem_limit_bytes=VMEM_BYTES),
        cost_estimate=pl.CostEstimate(
            flops=6 * rows * examples * (width + owners * group),
            bytes_accessed=2 * rows * (width + owners * group) + 4 * owners * examples * group,
            transcendentals=0,
        ),
        name="spread_back",
    )(place, stored, solved, stored)


def source_table(ring, slots):
    table = [0] * ring.count
    held = [0] * ring.count
    for index, (offset, core) in enumerate(slots):
        if core is None:
            table[ring.half] = index
            held[ring.half] = -1
        elif core == 0:
            table[offset % ring.count] = index
    place = len(slots)
    for offset in ring.offsets:
        table[-offset % ring.count] = place
        held[-offset % ring.count] = 1
        place += 2
    return table, held, place


def for_sibling(ring, place, table, held, arrived_quarter, blocks, group):
    fetch = block_fetch(ring, table, arrived_quarter)

    def chip(c, ref):
        return (1 - ref[1]) * ring.half + c

    def kernel(place_ref, first_ref, second_ref, out_ref):
        out_ref[0] = first_ref[0]
        out_ref[1] = second_ref[0]

    return pl.pallas_call(
        kernel,
        grid_spec=pltpu.PrefetchScalarGridSpec(
            num_scalar_prefetch=1,
            grid=(ring.half,),
            in_specs=[
                pl.BlockSpec((1, group, group), lambda c, ref, j=j: (fetch(chip(c, ref), j, ref), 0, 0)) for j in (0, 1)
            ],
            out_specs=pl.BlockSpec((2, group, group), lambda c, ref: (c, 0, 0)),
        ),
        out_shape=jax.ShapeDtypeStruct((2 * ring.half, group, group), jnp.bfloat16),
        compiler_params=pltpu.CompilerParams(vmem_limit_bytes=VMEM_BYTES),
        name="for_sibling",
    )(place, blocks, blocks)


def block_fetch(ring, table, arrived_quarter):
    def fetch(chip, j, ref):
        here = ring.position_of(ref[0])
        offset = lax.rem(ring.position_of(chip) - here + 2 * ring.count, ring.count)
        found = jnp.int32(0)
        for index, start in enumerate(table):
            found = jnp.where(offset == index, start, found)
        own = (j == ref[1]) == (here < ring.half)
        quarter = jnp.where(own, table[ring.half], arrived_quarter)
        return jnp.where(offset == ring.half, quarter, found + j)

    return fetch


def finish(ring, place, table, held, arrived_quarter, blocks, other, vectors, group):
    examples = vectors.shape[0]
    fetch = block_fetch(ring, table, arrived_quarter)

    def chip(c, ref):
        return ref[1] * ring.half + c

    def by_columns(c, ref):
        here = ring.position_of(ref[0])
        offset = lax.rem(ring.position_of(chip(c, ref)) - here + 2 * ring.count, ring.count)
        found = jnp.int32(0)
        for index, kind in enumerate(held):
            if kind == 1:
                found = jnp.where(offset == index, 1, found)
        return jnp.where(offset == ring.half, (here < ring.half).astype(jnp.int32), found) == 1

    def local_map(c, r, u, ref):
        return fetch(chip(c, ref), jnp.where(by_columns(c, ref), r, u), ref), 0, 0

    def other_map(c, r, u, ref):
        return 2 * c + jnp.where(by_columns(c, ref), r, u), 0, 0

    def kernel(place_ref, local_a, local_b, other_a, other_b, rows_ref, cols_ref, out_ref):
        c, r = pl.program_id(0), pl.program_id(1)
        added = jnp.dot(rows_ref[...].T, cols_ref[...], preferred_element_type=jnp.float32)
        row_ids = (2 * place_ref[0] + r) * group + lax.broadcasted_iota(jnp.int32, added.shape, 0)
        col_ids = 2 * chip(c, place_ref) * group + lax.broadcasted_iota(jnp.int32, added.shape, 1)
        added = added + jnp.where(row_ids == col_ids, jnp.float32(damping), jnp.float32(0.0))
        columns = by_columns(c, place_ref)
        for u, local_ref, other_ref in ((0, local_a, other_a), (1, local_b, other_b)):
            cols = slice(u * group, (u + 1) * group)
            mine = jnp.where(columns, u, r) == place_ref[1]

            @pl.when(mine)
            def _():
                out_ref[:, cols] = added[:, cols] + local_ref[0].astype(jnp.float32)

            @pl.when(jnp.logical_not(mine))
            def _():
                out_ref[:, cols] = added[:, cols] + other_ref[0].astype(jnp.float32)

    one = (1, group, group)
    return pl.pallas_call(
        kernel,
        grid_spec=pltpu.PrefetchScalarGridSpec(
            num_scalar_prefetch=1,
            grid=(ring.half, 2),
            in_specs=[pl.BlockSpec(one, lambda c, r, ref, u=u: local_map(c, r, u, ref)) for u in (0, 1)]
            + [pl.BlockSpec(one, lambda c, r, ref, u=u: other_map(c, r, u, ref)) for u in (0, 1)]
            + [
                pl.BlockSpec((examples, group), lambda c, r, ref: (0, 2 * ref[0] + r)),
                pl.BlockSpec((examples, 2 * group), lambda c, r, ref: (0, chip(c, ref))),
            ],
            out_specs=pl.BlockSpec((group, 2 * group), lambda c, r, ref: (r, c)),
        ),
        out_shape=jax.ShapeDtypeStruct((2 * group, 2 * ring.half * group), jnp.float32),
        compiler_params=pltpu.CompilerParams(vmem_limit_bytes=VMEM_BYTES),
        name="finish",
    )(place, blocks, blocks, other, other, vectors, vectors)


def in_order(index, mine, other, axis):
    return jnp.where(
        index == 0,
        jnp.concatenate([mine, other], axis=axis),
        jnp.concatenate([other, mine], axis=axis),
    )


def pair_swap(value, count):
    return lax.ppermute(value, "dp", [(index, index ^ 1) for index in range(count)])


def far_shift(value, step, count):
    return lax.ppermute(value, "dp", [(index, (index + 2 * step) % count) for index in range(count)])


def scatter_pairs(value, pair, count):
    pairs = count // 2
    size = value.shape[0] // pairs

    def slice_of(index):
        return lax.dynamic_slice_in_dim(value, index * size, size, 0)

    total = slice_of(pair)
    for step in range(1, pairs):
        total = total + far_shift(slice_of(lax.rem(pair + step, pairs)), step, count)
    return total


def gather_pairs(value, pair, count):
    pairs = count // 2
    size = value.shape[0]
    whole = jnp.zeros((pairs * size,) + value.shape[1:], value.dtype)
    whole = lax.dynamic_update_slice_in_dim(whole, value, pair * size, 0)
    for step in range(1, pairs):
        came = far_shift(value, step, count)
        whole = lax.dynamic_update_slice_in_dim(whole, came, lax.rem(pair - step + pairs, pairs) * size, 0)
    return whole


def local(ring, activations, out_grads, proj_in, proj_out, stored, counts, query_ids):
    owners = ring.count
    full = stored.shape[1]
    width = full // owners
    group = width // 2
    half = ring.half
    t = lax.axis_index("tensor")
    d = lax.axis_index("dp")
    pair, side = d // 2, lax.rem(d, 2)
    g = 2 * d + t
    place = jnp.stack([d, t]).astype(jnp.int32)

    first_stored = stored[:, :width]
    corner_rows = lead_dot(lax.dynamic_slice_in_dim(first_stored, t * group, group, 1), first_stored)
    corner_rows = scatter_pairs(corner_rows, pair, owners)
    corner_rows = gather_pairs(corner_rows + pair_swap(corner_rows, owners), pair, owners)
    corner = in_order(t, corner_rows, lax.ppermute(corner_rows, "tensor", SWAP), 0)

    sides = jnp.concatenate(
        [
            jnp.dot(activations, proj_in, preferred_element_type=jnp.float32),
            jnp.dot(out_grads, proj_out, preferred_element_type=jnp.float32),
        ],
        axis=1,
    )
    sides = sides + lax.ppermute(sides, "tensor", SWAP)

    examples = counts.shape[0]
    rank = proj_in.shape[1]
    position = jnp.arange(SEQ, dtype=jnp.int32)[None, :]
    weights = jnp.where(
        position < counts[:, None], 1.0 / counts.astype(jnp.float32)[:, None], jnp.float32(0.0)
    )
    act_half = lax.dynamic_slice_in_dim(sides, t * (rank // 2), rank // 2, 1)
    outer = jnp.einsum(
        "es,esi,esj->eij",
        weights,
        act_half.reshape(examples, SEQ, rank // 2),
        sides[:, rank:].reshape(examples, SEQ, rank),
        precision=EXACT,
    )
    own_half = outer.reshape(examples, full // 2).astype(jnp.bfloat16)
    pair_half = in_order(side, own_half, pair_swap(own_half, owners), 0)
    gathered_half = gather_pairs(pair_half, pair, owners)
    vectors = in_order(t, gathered_half, lax.ppermute(gathered_half, "tensor", SWAP), 1)

    split = (len(ring.offsets) + 1) // 2
    far_slots = [(half, None)]
    for offset in ring.offsets[:split]:
        far_slots += [(offset, 0), (offset, 1)]
    near_slots = []
    for offset in ring.offsets[split:] + [0]:
        near_slots += [(offset, 0), (offset, 1)]

    def part(step, slots, arrived, last=False):
        return window_part(ring, place, stored, group, step, slots, arrived, last)

    ahead, back = ring.shift(1), ring.shift(-1)
    far_ahead, far_back, near_ahead, near_back = [], [], [], []
    for step in range(half, 0, -1):
        far_ahead = [lax.ppermute(part(step, far_slots, far_ahead), "dp", ahead)]
        if step < half:
            far_back = [lax.ppermute(part(-step, far_slots, far_back), "dp", back)]
    for step in range(half, 0, -1):
        near_back = [lax.ppermute(part(-step, near_slots, near_back), "dp", back)]
        if step < half:
            near_ahead = [lax.ppermute(part(step, near_slots, near_ahead), "dp", ahead)]

    all_examples = vectors.shape[0]
    first_cols = vectors[:, :width]
    eye = jnp.eye(width, dtype=jnp.float32)
    corner = corner + lead_dot(first_cols, first_cols) + damping * eye
    scale = lax.rsqrt(jnp.sum(corner * eye, axis=1))
    first_cols = first_cols.astype(jnp.float32)
    solved = solve(corner * scale[:, None] * scale[None, :], first_cols.T * scale[:, None]) * scale[:, None]
    first_pairs = exact_dot(first_cols, solved)
    terms = spread_back(place, stored, solved, owners, group)
    terms = scatter_pairs(terms, pair, owners)
    away = lax.dynamic_index_in_dim(terms, 1 - side, 0, keepdims=False)
    terms = lax.dynamic_index_in_dim(terms, side, 0, keepdims=False) + pair_swap(away, owners)
    own_cols = lax.dynamic_slice_in_dim(vectors, g * group, group, 1).astype(jnp.float32)
    damped = lax.dynamic_slice_in_dim(solved.T, lax.rem(g, 2) * group, group, 1)
    damped = jnp.where(g < 2, damping * damped, 0.0)
    rest = own_cols - lead_dot(first_pairs, own_cols, EXACT) - terms - damped
    pairs = trail_dot(rest, rest) + jnp.where(g == 0, first_pairs, 0.0)
    pairs = scatter_pairs(pairs, pair, owners)
    away = lax.dynamic_slice_in_dim(pairs, (1 - side) * examples, examples, 0)
    pairs = lax.dynamic_slice_in_dim(pairs, side * examples, examples, 0) + pair_swap(away, owners)
    pairs = pairs + lax.ppermute(pairs, "tensor", SWAP)
    chosen = (query_ids[:, None] == jnp.arange(all_examples, dtype=jnp.int32)[None, :]).astype(jnp.float32)
    scores = trail_dot(chosen, pairs) / R

    far, far_turned = part(0, far_slots, far_ahead + far_back, last=True)
    near, near_turned = part(0, near_slots, near_ahead + near_back, last=True)
    slots = far_slots + near_slots
    came = []
    for offset in ring.offsets + [half]:
        if offset == half:
            block = far_turned[:1]
        elif (offset, 0) in far_slots:
            block = far_turned[far_slots.index((offset, 0)) :][:2]
        else:
            block = near_turned[near_slots.index((offset, 0)) :][:2]
        came.append(lax.ppermute(block, "dp", ring.shift(offset)))
    blocks = jnp.concatenate([far, near] + came, axis=0)
    table, held, arrived_quarter = source_table(ring, slots)
    send = for_sibling(ring, place, table, held, arrived_quarter, blocks, group)
    other = lax.ppermute(send, "tensor", SWAP)
    return finish(ring, place, table, held, arrived_quarter, blocks, other, vectors, group), scores


def solution(mesh):
    placed = (
        P(("groups", "dp"), "tensor"),
        P(("groups", "dp"), "tensor"),
        P("tensor", None),
        P("tensor", None),
        P(("groups", "dp"), None),
        P(("groups", "dp")),
        P("groups"),
    )
    ring = Ring(mesh)

    def program(*args):
        return local(ring, *args)

    return jax.shard_map(
        program,
        mesh=mesh,
        in_specs=placed,
        out_specs=(P(("groups", "dp"), "tensor"), P("groups", "dp")),
        check_vma=False,
    )
```

```python
import jax
import jax.numpy as jnp
from jax import lax
from jax.experimental import pallas as pl
from jax.experimental.pallas import tpu as pltpu
from jax.sharding import PartitionSpec as P

R = 64
SEQ = 16
damping = 1.0
EXACT = lax.Precision.HIGHEST
SWAP = [(0, 1), (1, 0)]
VMEM_BYTES = 56 * 1024 * 1024


class Ring:
    def __init__(self, mesh):
        self.count = mesh.shape["dp"]
        self.half = self.count // 2
        coords = [getattr(device, "coords", None) for device in mesh.devices[0, :, 0]]
        self.folded = False
        if None not in coords:
            moving = [axis for axis in range(3) if len({place[axis] for place in coords}) > 1]
            fast = [axis for axis in moving if coords[0][axis] != coords[1][axis]]
            self.folded = len(moving) == 2 and len(fast) == 1 and len({place[fast[0]] for place in coords}) == 2
        reach = [0, 0]
        self.offsets = []
        for distance in range(self.half - 1, 0, -1):
            side = 0 if reach[0] <= reach[1] else 1
            reach[side] += distance
            self.offsets.append(distance if side == 0 else -distance)

    def index_at(self, position):
        if isinstance(position, int):
            position = position % self.count
            if not self.folded:
                return position
            return 2 * position if position < self.half else 2 * (self.count - 1 - position) + 1
        position = lax.rem(position + 2 * self.count, self.count)
        if not self.folded:
            return position
        return jnp.where(position < self.half, 2 * position, 2 * (self.count - 1 - position) + 1)

    def position_of(self, index):
        if not self.folded:
            return index
        return jnp.where(lax.rem(index, 2) == 0, index // 2, self.count - 1 - index // 2)

    def shift(self, step):
        return [(self.index_at(p), self.index_at(p + step)) for p in range(self.count)]


def lead_dot(left, right, precision=None):
    return lax.dot_general(
        left, right, (((0,), (0,)), ((), ())), precision=precision, preferred_element_type=jnp.float32
    )


def exact_dot(left, right):
    return jnp.dot(left, right, precision=EXACT, preferred_element_type=jnp.float32)


def pairs_of(slots):
    found = []
    for index, (offset, core) in enumerate(slots):
        if core is None:
            found.append((offset, 1, index))
        elif core == 0:
            found.append((offset, 2, index))
    return found


def window_terms(ring, place, stored, vectors, group, steps, far_slots, near_slots):
    rows, full = stored.shape
    new_rows = vectors.shape[0]
    taps = jnp.array(steps, jnp.int32)

    def kernel(place_ref, step_ref, stored_ref, vectors_ref, far_ref, near_ref):
        owner = ring.position_of(place_ref[0]) + step_ref[pl.program_id(0)] + ring.count
        owner = lax.rem(owner, ring.count)
        core = place_ref[1]
        left = pl.ds(pl.multiple_of((2 * ring.index_at(owner) + core) * group, group), group)
        turned = stored_ref[:, left].T
        turned_new = vectors_ref[:, left].T
        for slots, out_ref in ((far_slots, far_ref), (near_slots, near_ref)):
            for offset, blocks, first in pairs_of(slots):
                column = 2 * ring.index_at(owner + offset)
                if blocks == 1:
                    column = column + jnp.where(owner < ring.half, core, 1 - core)
                right = pl.ds(pl.multiple_of(column * group, blocks * group), blocks * group)
                total = jnp.dot(turned, stored_ref[:, right], preferred_element_type=jnp.float32)
                total = total + jnp.dot(turned_new, vectors_ref[:, right], preferred_element_type=jnp.float32)
                out_ref[0, :, first * group : (first + blocks) * group] = total.astype(jnp.bfloat16)

    def out(slots):
        return pl.BlockSpec((1, group, len(slots) * group), lambda i, a, b: (i, 0, 0))

    def shape(slots):
        return jax.ShapeDtypeStruct((len(steps), group, len(slots) * group), jnp.bfloat16)

    blocks = len(far_slots) + len(near_slots)
    return pl.pallas_call(
        kernel,
        grid_spec=pltpu.PrefetchScalarGridSpec(
            num_scalar_prefetch=2,
            grid=(len(steps),),
            in_specs=[
                pl.BlockSpec((rows, full), lambda i, a, b: (0, 0), pipeline_mode=pl.Buffered(1)),
                pl.BlockSpec((new_rows, full), lambda i, a, b: (0, 0), pipeline_mode=pl.Buffered(1)),
            ],
            out_specs=[out(far_slots), out(near_slots)],
        ),
        out_shape=[shape(far_slots), shape(near_slots)],
        compiler_params=pltpu.CompilerParams(vmem_limit_bytes=VMEM_BYTES),
        cost_estimate=pl.CostEstimate(
            flops=4 * rows * len(steps) * blocks * group * group,
            bytes_accessed=2 * rows * full + 2 * len(steps) * blocks * group * group,
            transcendentals=0,
        ),
        name="window_terms",
    )(place, taps, stored, vectors)


def close_window(own, ahead, back, slots, group):
    count = len(slots)
    chips = [chip for chip in pairs_of(slots) if chip[0] != 0]

    def kernel(own_ref, ahead_ref, back_ref, blocks_ref, *turned_refs):
        for k in range(count):
            cols = slice(k * group, (k + 1) * group)
            total = own_ref[0, :, cols].astype(jnp.float32)
            total = total + ahead_ref[:, cols].astype(jnp.float32) + back_ref[:, cols].astype(jnp.float32)
            total = total.astype(jnp.bfloat16)
            blocks_ref[k] = total
            for (_, blocks, first), turned_ref in zip(chips, turned_refs):
                if first <= k < first + blocks:
                    turned_ref[k - first] = total.T

    index = own.shape[0] - 1
    flat = pl.BlockSpec((group, count * group), lambda i: (0, 0))
    sizes = [count] + [blocks for _, blocks, _ in chips]
    return pl.pallas_call(
        kernel,
        grid=(1,),
        in_specs=[pl.BlockSpec((1, group, count * group), lambda i: (index, 0, 0)), flat, flat],
        out_specs=[pl.BlockSpec((size, group, group), lambda i: (0, 0, 0)) for size in sizes],
        out_shape=[jax.ShapeDtypeStruct((size, group, group), jnp.bfloat16) for size in sizes],
        compiler_params=pltpu.CompilerParams(vmem_limit_bytes=VMEM_BYTES),
        cost_estimate=pl.CostEstimate(flops=4 * count * group**2, bytes_accessed=10 * count * group**2, transcendentals=0),
        name="close_window",
    )(own, ahead, back)


def rough_dot(left, right):
    return jnp.dot(left.astype(jnp.bfloat16), right.astype(jnp.bfloat16), preferred_element_type=jnp.float32)


def solve_kernel(matrix_ref, right_ref, out_ref, work, inverse, residual):
    size = matrix_ref.shape[0]
    block = inverse.shape[0]
    work[...] = matrix_ref[...]
    out_ref[...] = right_ref[...]
    row_ids = lax.broadcasted_iota(jnp.int32, (block, block), 0)
    col_ids = lax.broadcasted_iota(jnp.int32, (block, block), 1)
    eye = (row_ids == col_ids).astype(jnp.float32)
    for start in range(0, size, block):
        here = slice(start, start + block)
        rest = slice(start + block, size)
        corner = work[here, here]
        norm = jnp.max(jnp.sum(jnp.abs(corner), axis=0))
        inverse[...] = eye / norm
        residual[...] = eye - corner / norm

        def improve(dot):
            def step_of(state):
                step, _ = state
                better = inverse[...] + dot(inverse[...], residual[...])
                left_over = eye - dot(work[here, here], better)
                inverse[...] = better
                residual[...] = left_over
                return step + 1, jnp.max(jnp.abs(left_over))

            return step_of

        def until(steps, bound):
            return lambda state: jnp.logical_and(state[0] < steps, state[1] > bound)

        begin = (jnp.int32(0), jnp.float32(1.0))
        lax.while_loop(until(10, 0.02), improve(rough_dot), begin)
        left_over = eye - exact_dot(work[here, here], inverse[...])
        good = jnp.max(jnp.sum(jnp.abs(left_over), axis=0)) < 0.7
        inverse[...] = jnp.where(good, inverse[...], eye / norm)
        residual[...] = jnp.where(good, left_over, eye - work[here, here] / norm)
        lax.while_loop(until(40, 5e-5), improve(exact_dot), begin)
        found = inverse[...] + exact_dot(inverse[...], residual[...])
        solved = exact_dot(found, out_ref[here, :])
        out_ref[here, :] = solved
        if start + block < size:
            across = exact_dot(found, work[here, rest])
            down = work[rest, here]
            work[rest, rest] = work[rest, rest] - exact_dot(down, across)
            out_ref[rest, :] = out_ref[rest, :] - exact_dot(down, solved)
            work[here, rest] = across
    for start in range(size - 2 * block, -1, -block):
        here = slice(start, start + block)
        rest = slice(start + block, size)
        out_ref[here, :] = out_ref[here, :] - exact_dot(work[here, rest], out_ref[rest, :])


def solve(matrix, right):
    size, columns = right.shape
    block = 128
    return pl.pallas_call(
        solve_kernel,
        out_shape=jax.ShapeDtypeStruct((size, columns), jnp.float32),
        scratch_shapes=[
            pltpu.VMEM((size, size), jnp.float32),
            pltpu.VMEM((block, block), jnp.float32),
            pltpu.VMEM((block, block), jnp.float32),
        ],
        compiler_params=pltpu.CompilerParams(vmem_limit_bytes=VMEM_BYTES),
        cost_estimate=pl.CostEstimate(flops=12 * size**3, bytes_accessed=4 * size * (size + 2 * columns), transcendentals=0),
        name="solve",
    )(matrix, right)


def split_terms(value):
    high = value.astype(jnp.bfloat16)
    value = value - high.astype(jnp.float32)
    middle = value.astype(jnp.bfloat16)
    value = value - middle.astype(jnp.float32)
    return high, middle, value.astype(jnp.bfloat16)


def spread_back(place, stored, solved, owners, group):
    rows = stored.shape[0]
    width, examples = solved.shape

    def kernel(place_ref, first_ref, solved_ref, cols_ref, out_ref, terms):
        @pl.when(pl.program_id(0) == 0)
        def _():
            total = jnp.zeros((rows, examples), jnp.float32)
            for term in split_terms(solved_ref[...]):
                total = total + jnp.dot(first_ref[...], term, preferred_element_type=jnp.float32)
            for index, term in enumerate(split_terms(total.T)[:2]):
                terms[index * examples : (index + 1) * examples, :] = term

        product = jnp.dot(terms[...], cols_ref[...], preferred_element_type=jnp.float32)
        out_ref[0] = (product[:examples] + product[examples:]).astype(jnp.bfloat16)

    return pl.pallas_call(
        kernel,
        grid_spec=pltpu.PrefetchScalarGridSpec(
            num_scalar_prefetch=1,
            grid=(owners,),
            in_specs=[
                pl.BlockSpec((rows, width), lambda o, ref: (0, 0)),
                pl.BlockSpec((width, examples), lambda o, ref: (0, 0)),
                pl.BlockSpec((rows, group), lambda o, ref: (0, 2 * o + ref[1])),
            ],
            out_specs=pl.BlockSpec((1, examples, group), lambda o, ref: (o, 0, 0)),
            scratch_shapes=[pltpu.VMEM((2 * examples, rows), jnp.bfloat16)],
        ),
        out_shape=jax.ShapeDtypeStruct((owners, examples, group), jnp.bfloat16),
        compiler_params=pltpu.CompilerParams(vmem_limit_bytes=VMEM_BYTES),
        cost_estimate=pl.CostEstimate(
            flops=6 * rows * examples * (width + owners * group),
            bytes_accessed=2 * rows * (width + owners * group) + 2 * owners * examples * group,
            transcendentals=0,
        ),
        name="spread_back",
    )(place, stored, solved, stored)


def assembly_tables(ring, slots, d, t):
    start = [0] * ring.count
    arrived = [0] * ring.count
    for offset, _, first in pairs_of(slots):
        start[offset % ring.count] = first
    place = len(slots)
    for offset in ring.offsets:
        start[-offset % ring.count] = place
        arrived[-offset % ring.count] = 1
        place += 2
    here = ring.position_of(d)
    early = here < ring.half

    def look_up(values, offset):
        found = jnp.zeros_like(offset)
        for index, value in enumerate(values):
            if value:
                found = jnp.where(offset == index, value, found)
        return found

    def offsets_of(chips):
        return lax.rem(ring.position_of(chips) - here + 2 * ring.count, ring.count)

    def fetch(offset, j):
        own = (j == t) == early
        quarter = jnp.where(own, start[ring.half], place)
        return jnp.where(offset == ring.half, quarter, look_up(start, offset) + j)

    chips = jnp.arange(ring.half, dtype=jnp.int32)
    j = jnp.arange(2, dtype=jnp.int32)[None, :]
    send = fetch(offsets_of((1 - t) * ring.half + chips)[:, None], j)
    offset = offsets_of(t * ring.half + chips)[:, None, None]
    r = jnp.arange(2, dtype=jnp.int32)[None, :, None]
    u = jnp.arange(2, dtype=jnp.int32)[None, None, :]
    by_columns = jnp.where(offset == ring.half, early.astype(jnp.int32), look_up(arrived, offset)) == 1
    j = jnp.where(by_columns, r, u)
    local = fetch(offset, j)
    other = 2 * chips[:, None, None] + j
    mine = (jnp.where(by_columns, u, r) == t).astype(jnp.int32)
    final = jnp.stack([local, other, mine]).reshape(-1)
    return send.reshape(-1).astype(jnp.int32), final.astype(jnp.int32)


def for_sibling(table, blocks, group):
    total = table.shape[0]
    wide = min(4, total)

    def kernel(table_ref, *refs):
        for k in range(wide):
            refs[-1][k] = refs[k][0]

    return pl.pallas_call(
        kernel,
        grid_spec=pltpu.PrefetchScalarGridSpec(
            num_scalar_prefetch=1,
            grid=(total // wide,),
            in_specs=[
                pl.BlockSpec((1, group, group), lambda c, ref, k=k: (ref[wide * c + k], 0, 0)) for k in range(wide)
            ],
            out_specs=pl.BlockSpec((wide, group, group), lambda c, ref: (c, 0, 0)),
        ),
        out_shape=jax.ShapeDtypeStruct((total, group, group), jnp.bfloat16),
        compiler_params=pltpu.CompilerParams(vmem_limit_bytes=VMEM_BYTES),
        name="for_sibling",
    )(table, *([blocks] * wide))


def finish(place, table, blocks, other, half, group):
    wide = half // 2
    total = 4 * half

    def at(kind, r, c, k, u, ref):
        return ref[kind * total + 4 * (wide * c + k) + 2 * r + u]

    def spec(kind, k, u):
        return pl.BlockSpec((1, group, group), lambda r, c, ref, place: (at(kind, r, c, k, u, ref), 0, 0))

    order = [(k, u) for k in range(wide) for u in (0, 1)]

    def kernel(table_ref, place_ref, *refs):
        r, c = pl.program_id(0), pl.program_id(1)
        out_ref = refs[-1]
        shape = (group, group)
        gap = lax.broadcasted_iota(jnp.int32, shape, 1) - lax.broadcasted_iota(jnp.int32, shape, 0)
        for index, (k, u) in enumerate(order):
            cols = slice(index * group, (index + 1) * group)
            chip = place_ref[1] * half + wide * c + k
            apart = (2 * place_ref[0] + r - 2 * chip - u) * group
            added = jnp.where(gap == apart, jnp.float32(damping), jnp.float32(0.0))
            mine = at(2, r, c, k, u, table_ref) == 1

            @pl.when(mine)
            def _():
                out_ref[:, cols] = added + refs[index][0].astype(jnp.float32)

            @pl.when(jnp.logical_not(mine))
            def _():
                out_ref[:, cols] = added + refs[len(order) + index][0].astype(jnp.float32)

    return pl.pallas_call(
        kernel,
        grid_spec=pltpu.PrefetchScalarGridSpec(
            num_scalar_prefetch=2,
            grid=(2, 2),
            in_specs=[spec(0, k, u) for k, u in order] + [spec(1, k, u) for k, u in order],
            out_specs=pl.BlockSpec((group, 2 * wide * group), lambda r, c, ref, place: (r, c)),
        ),
        out_shape=jax.ShapeDtypeStruct((2 * group, 2 * half * group), jnp.float32),
        compiler_params=pltpu.CompilerParams(vmem_limit_bytes=VMEM_BYTES),
        name="finish",
    )(table, place, *([blocks] * len(order)), *([other] * len(order)))


def in_order(index, mine, other, axis):
    return jnp.where(
        index == 0,
        jnp.concatenate([mine, other], axis=axis),
        jnp.concatenate([other, mine], axis=axis),
    )


def pair_swap(value, count):
    return lax.ppermute(value, "dp", [(index, index ^ 1) for index in range(count)])


def far_shift(value, step, count):
    return lax.ppermute(value, "dp", [(index, (index + 2 * step) % count) for index in range(count)])


def exchange_pairs(slice_of, pair, count):
    pairs = count // 2
    came = [slice_of(pair)]
    for step in range(1, pairs):
        came.append(far_shift(slice_of(lax.rem(pair + step, pairs)), step, count))
    return came


def natural(came, pair):
    pairs = len(came)
    pieces = []
    for index in range(pairs):
        behind = lax.rem(pair - index + pairs, pairs)
        piece = came[0]
        for step in range(1, pairs):
            piece = jnp.where(behind == step, came[step], piece)
        pieces.append(piece)
    return pieces


def scatter_pairs(value, pair, count):
    size = value.shape[0] // (count // 2)

    def slice_of(index):
        return lax.dynamic_slice_in_dim(value, index * size, size, 0)

    return sum(piece.astype(jnp.float32) for piece in exchange_pairs(slice_of, pair, count))


def local(ring, activations, out_grads, proj_in, proj_out, stored, counts, query_ids):
    owners = ring.count
    full = stored.shape[1]
    width = full // owners
    group = width // 2
    half = ring.half
    t = lax.axis_index("tensor")
    d = lax.axis_index("dp")
    pair, side = d // 2, lax.rem(d, 2)
    g = 2 * d + t
    place = jnp.stack([d, t]).astype(jnp.int32)

    first_stored = stored[:, :width]
    corner_rows = lead_dot(lax.dynamic_slice_in_dim(first_stored, t * group, group, 1), first_stored)
    corner_rows = scatter_pairs(corner_rows, pair, owners)
    corner_rows = corner_rows + pair_swap(corner_rows, owners)
    corner_rows = exchange_pairs(lambda index: corner_rows, pair, owners)
    corner_rows = jnp.concatenate(natural(corner_rows, pair), axis=0)
    corner = in_order(t, corner_rows, lax.ppermute(corner_rows, "tensor", SWAP), 0)

    sides = jnp.concatenate(
        [
            jnp.dot(activations, proj_in, preferred_element_type=jnp.float32),
            jnp.dot(out_grads, proj_out, preferred_element_type=jnp.float32),
        ],
        axis=1,
    )
    sides = sides + lax.ppermute(sides, "tensor", SWAP)

    examples = counts.shape[0]
    all_examples = examples * owners
    rank = proj_in.shape[1]
    position = jnp.arange(SEQ, dtype=jnp.int32)[None, :]
    weights = jnp.where(
        position < counts[:, None], 1.0 / counts.astype(jnp.float32)[:, None], jnp.float32(0.0)
    )
    outer = jnp.einsum(
        "es,esi,esj->eij",
        weights,
        sides[:, :rank].reshape(examples, SEQ, rank),
        sides[:, rank:].reshape(examples, SEQ, rank),
        precision=EXACT,
    )
    vectors = outer.reshape(examples, full).astype(jnp.bfloat16)

    def columns_for(index):
        groups = [lax.dynamic_slice_in_dim(vectors, (4 * index + 2 * s + t) * group, group, 1) for s in (0, 1)]
        return jnp.concatenate([vectors[:, :width]] + groups, axis=1)

    came = natural(exchange_pairs(columns_for, pair, owners), pair)
    came = jnp.concatenate(came, axis=0)
    kept = jnp.where(side == 0, came[:, : width + group], jnp.concatenate([came[:, :width], came[:, width + group :]], axis=1))
    away = jnp.where(side == 0, jnp.concatenate([came[:, :width], came[:, width + group :]], axis=1), came[:, : width + group])
    shape = (owners // 2, 1, examples, width + group)
    known = in_order(side, kept.reshape(shape), pair_swap(away, owners).reshape(shape), 1)
    known = known.reshape(all_examples, width + group)
    first_cols, own_cols = known[:, :width], known[:, width:].astype(jnp.float32)

    split = (len(ring.offsets) + 1) // 2
    far_slots = [(half, None)]
    for offset in ring.offsets[:split]:
        far_slots += [(offset, 0), (offset, 1)]
    near_slots = []
    for offset in ring.offsets[split:] + [0]:
        near_slots += [(offset, 0), (offset, 1)]

    def terms_of(steps):
        return window_terms(ring, place, stored, vectors, group, steps, far_slots, near_slots)

    outermost = terms_of([half])
    second = terms_of([half - 1, 1 - half])
    later_steps = [s for step in range(half - 2, 0, -1) for s in (step, -step)] + [0]
    later = terms_of(later_steps)

    def term(kind, step):
        if abs(step) == half:
            return outermost[kind][0]
        if abs(step) == half - 1:
            return second[kind][0 if step > 0 else 1]
        return later[kind][later_steps.index(step)]

    ahead, back = ring.shift(1), ring.shift(-1)

    def passed_on(kind, step, arrived):
        value = term(kind, step)
        if arrived is not None:
            value = (value.astype(jnp.float32) + arrived.astype(jnp.float32)).astype(jnp.bfloat16)
        return lax.ppermute(value, "dp", ahead if step > 0 else back)

    far_ahead = far_back = near_ahead = near_back = None
    for step in range(half, 0, -1):
        far_ahead = passed_on(0, step, far_ahead)
        near_back = passed_on(1, -step, near_back)
        if step < half:
            far_back = passed_on(0, -step, far_back)
            near_ahead = passed_on(1, step, near_ahead)

    eye = jnp.eye(width, dtype=jnp.float32)
    corner = corner + lead_dot(first_cols, first_cols) + damping * eye
    scale = lax.rsqrt(jnp.sum(corner * eye, axis=1))
    first_cols = first_cols.astype(jnp.float32)
    solved = solve(corner * scale[:, None] * scale[None, :], first_cols.T * scale[:, None]) * scale[:, None]
    first_pairs = exact_dot(first_cols, solved)
    terms = spread_back(place, stored, solved, owners, group)
    terms = scatter_pairs(terms, pair, owners)
    away = jnp.where(side == 0, terms[1], terms[0]).astype(jnp.bfloat16)
    terms = jnp.where(side == 0, terms[0], terms[1]) + pair_swap(away, owners).astype(jnp.float32)
    damped = lax.dynamic_slice_in_dim(solved.T, lax.rem(g, 2) * group, group, 1)
    damped = jnp.where(g < 2, damping * damped, 0.0)
    rest = own_cols - lead_dot(first_pairs, own_cols, EXACT) - terms - damped
    pairs = lax.dot_general(rest, rest, (((1,), (1,)), ((), ())), precision=EXACT, preferred_element_type=jnp.float32)
    pairs = pairs + jnp.where(g == 0, first_pairs, 0.0)
    pairs = scatter_pairs(pairs, pair, owners)
    away = lax.dynamic_slice_in_dim(pairs, (1 - side) * examples, examples, 0)
    pairs = lax.dynamic_slice_in_dim(pairs, side * examples, examples, 0) + pair_swap(away, owners)
    pairs = pairs + lax.ppermute(pairs, "tensor", SWAP)
    chosen = (query_ids[:, None] == jnp.arange(all_examples, dtype=jnp.int32)[None, :]).astype(jnp.float32)
    scores = lax.dot_general(chosen, pairs, (((1,), (1,)), ((), ())), precision=EXACT, preferred_element_type=jnp.float32) / R

    far = close_window(later[0], far_ahead, far_back, far_slots, group)
    near = close_window(later[1], near_ahead, near_back, near_slots, group)
    turned = {}
    for (found, slots) in ((far, far_slots), (near, near_slots)):
        chips = [chip for chip in pairs_of(slots) if chip[0] != 0]
        for (offset, _, _), block in zip(chips, found[1:]):
            turned[offset] = block
    came = [lax.ppermute(turned[offset], "dp", ring.shift(offset)) for offset in ring.offsets + [half]]
    blocks = jnp.concatenate([far[0], near[0]] + came, axis=0)
    send_table, final_table = assembly_tables(ring, far_slots + near_slots, d, t)
    other = lax.ppermute(for_sibling(send_table, blocks, group), "tensor", SWAP)
    return finish(place, final_table, blocks, other, half, group), scores


def solution(mesh):
    placed = (
        P(("groups", "dp"), "tensor"),
        P(("groups", "dp"), "tensor"),
        P("tensor", None),
        P("tensor", None),
        P(("groups", "dp"), None),
        P(("groups", "dp")),
        P("groups"),
    )
    ring = Ring(mesh)

    def program(*args):
        return local(ring, *args)

    return jax.shard_map(
        program,
        mesh=mesh,
        in_specs=placed,
        out_specs=(P(("groups", "dp"), "tensor"), P("groups", "dp")),
        check_vma=False,
    )
```

```python
import jax
import jax.numpy as jnp
from jax import lax
from jax.experimental import pallas as pl
from jax.experimental.pallas import tpu as pltpu
from jax.sharding import PartitionSpec as P

R = 64
SEQ = 16
damping = 1.0
EXACT = lax.Precision.HIGHEST
SWAP = [(0, 1), (1, 0)]
VMEM_BYTES = 56 * 1024 * 1024
LIGHT = pl.CostEstimate(flops=10**6, bytes_accessed=10**5, transcendentals=0)
ANYWHERE = pl.BlockSpec(memory_space=pl.ANY)


class Ring:
    def __init__(self, mesh):
        self.count = mesh.shape["dp"]
        self.half = self.count // 2
        coords = [getattr(device, "coords", None) for device in mesh.devices[0, :, 0]]
        self.folded = False
        if None not in coords:
            moving = [axis for axis in range(3) if len({place[axis] for place in coords}) > 1]
            fast = [axis for axis in moving if coords[0][axis] != coords[1][axis]]
            self.folded = len(moving) == 2 and len(fast) == 1 and len({place[fast[0]] for place in coords}) == 2
        reach = [0, 0]
        self.offsets = []
        for distance in range(self.half - 1, 0, -1):
            side = 0 if reach[0] <= reach[1] else 1
            reach[side] += distance
            self.offsets.append(distance if side == 0 else -distance)

    def index_at(self, position):
        if isinstance(position, int):
            position = position % self.count
            if not self.folded:
                return position
            return 2 * position if position < self.half else 2 * (self.count - 1 - position) + 1
        position = lax.rem(position + 2 * self.count, self.count)
        if not self.folded:
            return position
        return jnp.where(position < self.half, 2 * position, 2 * (self.count - 1 - position) + 1)

    def position_of(self, index):
        if not self.folded:
            return index
        return jnp.where(lax.rem(index, 2) == 0, index // 2, self.count - 1 - index // 2)

    def shift(self, step):
        return [(self.index_at(p), self.index_at(p + step)) for p in range(self.count)]


def lead_dot(left, right, precision=None):
    return lax.dot_general(
        left, right, (((0,), (0,)), ((), ())), precision=precision, preferred_element_type=jnp.float32
    )


def exact_dot(left, right):
    return jnp.dot(left, right, precision=EXACT, preferred_element_type=jnp.float32)


def pairs_of(slots):
    found = []
    for index, (offset, core) in enumerate(slots):
        if core is None:
            found.append((offset, 1, index))
        elif core == 0:
            found.append((offset, 2, index))
    return found


def window_terms(ring, place, stored, vectors, group, steps, parts, after=()):
    rows, full = stored.shape
    new_rows = vectors.shape[0]
    taps = jnp.array(steps, jnp.int32)

    def kernel(place_ref, step_ref, stored_ref, vectors_ref, *refs):
        owner = ring.position_of(place_ref[0]) + step_ref[pl.program_id(0)] + ring.count
        owner = lax.rem(owner, ring.count)
        core = place_ref[1]
        left = pl.ds(pl.multiple_of((2 * ring.index_at(owner) + core) * group, group), group)
        turned = stored_ref[:, left].T
        turned_new = vectors_ref[:, left].T
        for slots, out_ref in zip(parts, refs[len(after) :]):
            for offset, blocks, first in pairs_of(slots):
                column = 2 * ring.index_at(owner + offset)
                if blocks == 1:
                    column = column + jnp.where(owner < ring.half, core, 1 - core)
                right = pl.ds(pl.multiple_of(column * group, blocks * group), blocks * group)
                total = jnp.dot(turned, stored_ref[:, right], preferred_element_type=jnp.float32)
                total = total + jnp.dot(turned_new, vectors_ref[:, right], preferred_element_type=jnp.float32)
                out_ref[0, :, first * group : (first + blocks) * group] = total.astype(jnp.bfloat16)

    def out(slots):
        return pl.BlockSpec((1, group, len(slots) * group), lambda i, a, b: (i, 0, 0))

    def shape(slots):
        return jax.ShapeDtypeStruct((len(steps), group, len(slots) * group), jnp.bfloat16)

    return pl.pallas_call(
        kernel,
        grid_spec=pltpu.PrefetchScalarGridSpec(
            num_scalar_prefetch=2,
            grid=(len(steps),),
            in_specs=[
                pl.BlockSpec((rows, full), lambda i, a, b: (0, 0), pipeline_mode=pl.Buffered(1)),
                pl.BlockSpec((new_rows, full), lambda i, a, b: (0, 0), pipeline_mode=pl.Buffered(1)),
            ]
            + [ANYWHERE] * len(after),
            out_specs=[out(slots) for slots in parts],
        ),
        out_shape=[shape(slots) for slots in parts],
        compiler_params=pltpu.CompilerParams(vmem_limit_bytes=VMEM_BYTES),
        cost_estimate=LIGHT,
        name="window_terms",
    )(place, taps, stored, vectors, *after)


def add_terms(terms, index, arrived, sizes, group, after=()):
    count = terms.shape[2] // group

    def kernel(terms_ref, *refs):
        outs = refs[len(arrived) + len(after) :]
        for k in range(count):
            total = terms_ref[0, :, k * group : (k + 1) * group].astype(jnp.float32)
            for ref, (array, first) in zip(refs, arrived):
                if first <= k < first + array.shape[1] // group:
                    total = total + ref[:, (k - first) * group : (k - first + 1) * group].astype(jnp.float32)
            place, start = 0, 0
            while k - start >= sizes[place]:
                start += sizes[place]
                place += 1
            outs[place][:, (k - start) * group : (k - start + 1) * group] = total.astype(jnp.bfloat16)

    def flat(columns):
        return pl.BlockSpec((group, columns), lambda i: (0, 0))

    return pl.pallas_call(
        kernel,
        grid=(1,),
        in_specs=[pl.BlockSpec((1, group, count * group), lambda i: (index, 0, 0))]
        + [flat(array.shape[1]) for array, _ in arrived]
        + [ANYWHERE] * len(after),
        out_specs=[flat(size * group) for size in sizes],
        out_shape=[jax.ShapeDtypeStruct((group, size * group), jnp.bfloat16) for size in sizes],
        compiler_params=pltpu.CompilerParams(vmem_limit_bytes=VMEM_BYTES),
        cost_estimate=LIGHT,
        name="add_terms",
    )(terms, *[array for array, _ in arrived], *after)


def close_window(terms, base, ahead, back, slots, group):
    count = len(slots)
    chips = [chip for chip in pairs_of(slots) if chip[0] != 0]

    def kernel(own_ref, ahead_ref, back_ref, blocks_ref, *turned_refs):
        for k in range(count):
            cols = slice(k * group, (k + 1) * group)
            total = own_ref[0, :, (base + k) * group : (base + k + 1) * group].astype(jnp.float32)
            total = total + ahead_ref[:, cols].astype(jnp.float32) + back_ref[:, cols].astype(jnp.float32)
            total = total.astype(jnp.bfloat16)
            blocks_ref[k] = total
            for (_, blocks, first), turned_ref in zip(chips, turned_refs):
                if first <= k < first + blocks:
                    turned_ref[k - first] = total.T

    index = terms.shape[0] - 1
    flat = pl.BlockSpec((group, count * group), lambda i: (0, 0))
    sizes = [count] + [blocks for _, blocks, _ in chips]
    return pl.pallas_call(
        kernel,
        grid=(1,),
        in_specs=[pl.BlockSpec((1,) + terms.shape[1:], lambda i: (index, 0, 0)), flat, flat],
        out_specs=[pl.BlockSpec((size, group, group), lambda i: (0, 0, 0)) for size in sizes],
        out_shape=[jax.ShapeDtypeStruct((size, group, group), jnp.bfloat16) for size in sizes],
        compiler_params=pltpu.CompilerParams(vmem_limit_bytes=VMEM_BYTES),
        cost_estimate=LIGHT,
        name="close_window",
    )(terms, ahead, back)


def rough_dot(left, right):
    return jnp.dot(left.astype(jnp.bfloat16), right.astype(jnp.bfloat16), preferred_element_type=jnp.float32)


def split_terms(value):
    high = value.astype(jnp.bfloat16)
    value = value - high.astype(jnp.float32)
    middle = value.astype(jnp.bfloat16)
    value = value - middle.astype(jnp.float32)
    return high, middle, value.astype(jnp.bfloat16)


def identity(size):
    rows = lax.broadcasted_iota(jnp.int32, (size, size), 0)
    cols = lax.broadcasted_iota(jnp.int32, (size, size), 1)
    return (rows == cols).astype(jnp.float32)


def eliminate(matrix_ref, right_ref, out_ref, work, block):
    size = matrix_ref.shape[0]
    work[...] = matrix_ref[...]
    out_ref[...] = right_ref[...]
    eye = identity(block)
    for start in range(0, size, block):
        here = slice(start, start + block)
        rest = slice(start + block, size)
        corner = work[here, here]
        norm = jnp.max(jnp.sum(jnp.abs(corner), axis=0))

        def unfinished(state):
            return jnp.logical_and(state[0] < 40, state[1] > 5e-5)

        def improve(state):
            step, _, inverse = state
            better = inverse + exact_dot(inverse, eye - exact_dot(work[here, here], inverse))
            left_over = eye - exact_dot(work[here, here], better)
            return step + 1, jnp.max(jnp.abs(left_over)), better

        found = lax.while_loop(unfinished, improve, (jnp.int32(0), jnp.float32(1.0), eye / norm))[2]
        found = found + exact_dot(found, eye - exact_dot(work[here, here], found))
        solved = exact_dot(found, out_ref[here, :])
        out_ref[here, :] = solved
        if start + block < size:
            across = exact_dot(found, work[here, rest])
            down = work[rest, here]
            work[rest, rest] = work[rest, rest] - exact_dot(down, across)
            out_ref[rest, :] = out_ref[rest, :] - exact_dot(down, solved)
            work[here, rest] = across
    for start in range(size - 2 * block, -1, -block):
        here = slice(start, start + block)
        rest = slice(start + block, size)
        out_ref[here, :] = out_ref[here, :] - exact_dot(work[here, rest], out_ref[rest, :])


def solve(place, mine, other, first_cols, after=()):
    group, width = mine.shape
    examples = first_cols.shape[0]

    def kernel(place_ref, mine_ref, other_ref, first_ref, *refs):
        out_ref, pairs_ref, matrix, right, power, inverse = refs[len(after) :]
        eye = identity(width)
        t = place_ref[1]
        matrix[pl.ds(pl.multiple_of(t * group, group), group), :] = mine_ref[...]
        matrix[pl.ds(pl.multiple_of((1 - t) * group, group), group), :] = other_ref[...]
        turned = first_ref[...].T
        full = matrix[...] + jnp.dot(turned, first_ref[...], preferred_element_type=jnp.float32) + damping * eye
        diagonal = full * eye
        rows_scale = lax.rsqrt(jnp.sum(diagonal, axis=1, keepdims=True))
        cols_scale = lax.rsqrt(jnp.sum(diagonal, axis=0, keepdims=True))
        full = full * rows_scale * cols_scale
        matrix[...] = full
        right[...] = turned.astype(jnp.float32) * rows_scale

        sums = jnp.max(jnp.sum(jnp.abs(full), axis=0))
        squared = rough_dot(full, full)
        norm = jnp.sqrt(jnp.max(jnp.sum(jnp.abs(squared), axis=0)) + sums * sums / 128)
        start = eye - full / norm
        inverse[...] = eye + start
        power[...] = start.astype(jnp.bfloat16)
        for _ in range(7):
            raised = jnp.dot(power[...], power[...], preferred_element_type=jnp.float32).astype(jnp.bfloat16)
            power[...] = raised
            held = inverse[...]
            inverse[...] = held + jnp.dot(held.astype(jnp.bfloat16), raised, preferred_element_type=jnp.float32)
        power[...] = (inverse[...] / norm).astype(jnp.bfloat16)

        largest = jnp.max(jnp.abs(right[...]))
        out_ref[...] = jnp.dot(power[...], right[...].astype(jnp.bfloat16), preferred_element_type=jnp.float32)

        def unfinished(state):
            return jnp.logical_and(state[0] < 12, jnp.logical_not(state[1] <= 5e-5 * largest))

        def refine(state):
            left_over = right[...] - exact_dot(matrix[...], out_ref[...])
            change = jnp.dot(power[...], left_over.astype(jnp.bfloat16), preferred_element_type=jnp.float32)
            out_ref[...] = out_ref[...] + change
            return state[0] + 1, jnp.max(jnp.abs(left_over))

        worst = lax.while_loop(unfinished, refine, (jnp.int32(0), 1.0 + largest))[1]

        @pl.when(jnp.logical_not(worst <= 5e-5 * largest))
        def _():
            eliminate(matrix, right, out_ref, inverse, 128)

        solved = out_ref[...] * rows_scale
        out_ref[...] = solved
        pairs = jnp.zeros((examples, examples), jnp.float32)
        for term in split_terms(solved):
            pairs = pairs + jnp.dot(first_ref[...], term, preferred_element_type=jnp.float32)
        pairs_ref[...] = pairs

    whole = pl.BlockSpec(memory_space=pltpu.VMEM)
    return pl.pallas_call(
        kernel,
        in_specs=[pl.BlockSpec(memory_space=pltpu.SMEM)] + [whole] * 3 + [ANYWHERE] * len(after),
        out_shape=[
            jax.ShapeDtypeStruct((width, examples), jnp.float32),
            jax.ShapeDtypeStruct((examples, examples), jnp.float32),
        ],
        scratch_shapes=[
            pltpu.VMEM((width, width), jnp.float32),
            pltpu.VMEM((width, examples), jnp.float32),
            pltpu.VMEM((width, width), jnp.bfloat16),
            pltpu.VMEM((width, width), jnp.float32),
        ],
        compiler_params=pltpu.CompilerParams(vmem_limit_bytes=VMEM_BYTES),
        cost_estimate=LIGHT,
        name="solve",
    )(place, mine, other, first_cols, *after)


def spread_back(place, stored, solved, owners, group, after=()):
    rows = stored.shape[0]
    width, examples = solved.shape
    pairs = owners // 2

    def kernel(place_ref, first_ref, solved_ref, *refs):
        cols, outs = refs[:owners], refs[owners + len(after) :]
        total = jnp.zeros((rows, examples), jnp.float32)
        for term in split_terms(solved_ref[...]):
            total = total + jnp.dot(first_ref[...], term, preferred_element_type=jnp.float32)
        terms = jnp.concatenate(split_terms(total.T)[:2], axis=0)
        for index in range(owners):
            product = jnp.dot(terms, cols[index][...], preferred_element_type=jnp.float32)
            outs[index // 2][index % 2] = (product[:examples] + product[examples:]).astype(jnp.bfloat16)

    def owner(index, ref):
        return 2 * lax.rem(ref[0] // 2 + index // 2, pairs) + index % 2

    return pl.pallas_call(
        kernel,
        grid_spec=pltpu.PrefetchScalarGridSpec(
            num_scalar_prefetch=1,
            grid=(1,),
            in_specs=[
                pl.BlockSpec((rows, width), lambda i, ref: (0, 0)),
                pl.BlockSpec((width, examples), lambda i, ref: (0, 0)),
            ]
            + [
                pl.BlockSpec((rows, group), lambda i, ref, index=index: (0, 2 * owner(index, ref) + ref[1]))
                for index in range(owners)
            ]
            + [ANYWHERE] * len(after),
            out_specs=[pl.BlockSpec((2, examples, group), lambda i, ref: (0, 0, 0))] * pairs,
        ),
        out_shape=[jax.ShapeDtypeStruct((2, examples, group), jnp.bfloat16)] * pairs,
        compiler_params=pltpu.CompilerParams(vmem_limit_bytes=VMEM_BYTES),
        cost_estimate=LIGHT,
        name="spread_back",
    )(place, stored, solved, *([stored] * owners), *after)


def assembly_tables(ring, slots, d, t):
    start = [0] * ring.count
    arrived = [0] * ring.count
    for offset, _, first in pairs_of(slots):
        start[offset % ring.count] = first
    place = len(slots)
    for offset in ring.offsets:
        start[-offset % ring.count] = place
        arrived[-offset % ring.count] = 1
        place += 2
    here = ring.position_of(d)
    early = here < ring.half

    def look_up(values, offset):
        found = jnp.zeros_like(offset)
        for index, value in enumerate(values):
            if value:
                found = jnp.where(offset == index, value, found)
        return found

    def offsets_of(chips):
        return lax.rem(ring.position_of(chips) - here + 2 * ring.count, ring.count)

    def fetch(offset, j):
        own = (j == t) == early
        quarter = jnp.where(own, start[ring.half], place)
        return jnp.where(offset == ring.half, quarter, look_up(start, offset) + j)

    chips = jnp.arange(ring.half, dtype=jnp.int32)
    j = jnp.arange(2, dtype=jnp.int32)[None, :]
    send = fetch(offsets_of((1 - t) * ring.half + chips)[:, None], j)
    offset = offsets_of(t * ring.half + chips)[:, None, None]
    r = jnp.arange(2, dtype=jnp.int32)[None, :, None]
    u = jnp.arange(2, dtype=jnp.int32)[None, None, :]
    by_columns = jnp.where(offset == ring.half, early.astype(jnp.int32), look_up(arrived, offset)) == 1
    j = jnp.where(by_columns, r, u)
    local = fetch(offset, j)
    other = 2 * chips[:, None, None] + j
    mine = (jnp.where(by_columns, u, r) == t).astype(jnp.int32)
    final = jnp.stack([local, other, mine]).reshape(-1)
    return send.reshape(-1).astype(jnp.int32), final.astype(jnp.int32)


def for_sibling(table, blocks, group):
    total = table.shape[0]
    wide = min(4, total)

    def kernel(table_ref, *refs):
        for k in range(wide):
            refs[-1][k] = refs[k][0]

    return pl.pallas_call(
        kernel,
        grid_spec=pltpu.PrefetchScalarGridSpec(
            num_scalar_prefetch=1,
            grid=(total // wide,),
            in_specs=[
                pl.BlockSpec((1, group, group), lambda c, ref, k=k: (ref[wide * c + k], 0, 0)) for k in range(wide)
            ],
            out_specs=pl.BlockSpec((wide, group, group), lambda c, ref: (c, 0, 0)),
        ),
        out_shape=jax.ShapeDtypeStruct((total, group, group), jnp.bfloat16),
        compiler_params=pltpu.CompilerParams(vmem_limit_bytes=VMEM_BYTES),
        cost_estimate=LIGHT,
        name="for_sibling",
    )(table, *([blocks] * wide))


def finish(place, table, blocks, other, half, group):
    wide = half // 2
    total = 4 * half

    def at(kind, r, c, k, u, ref):
        return ref[kind * total + 4 * (wide * c + k) + 2 * r + u]

    def spec(kind, k, u):
        return pl.BlockSpec((1, group, group), lambda r, c, ref, place: (at(kind, r, c, k, u, ref), 0, 0))

    order = [(k, u) for k in range(wide) for u in (0, 1)]

    def kernel(table_ref, place_ref, *refs):
        r, c = pl.program_id(0), pl.program_id(1)
        out_ref = refs[-1]
        shape = (group, group)
        gap = lax.broadcasted_iota(jnp.int32, shape, 1) - lax.broadcasted_iota(jnp.int32, shape, 0)
        for index, (k, u) in enumerate(order):
            cols = slice(index * group, (index + 1) * group)
            chip = place_ref[1] * half + wide * c + k
            apart = (2 * place_ref[0] + r - 2 * chip - u) * group
            added = jnp.where(gap == apart, jnp.float32(damping), jnp.float32(0.0))
            mine = at(2, r, c, k, u, table_ref) == 1

            @pl.when(mine)
            def _():
                out_ref[:, cols] = added + refs[index][0].astype(jnp.float32)

            @pl.when(jnp.logical_not(mine))
            def _():
                out_ref[:, cols] = added + refs[len(order) + index][0].astype(jnp.float32)

    return pl.pallas_call(
        kernel,
        grid_spec=pltpu.PrefetchScalarGridSpec(
            num_scalar_prefetch=2,
            grid=(2, 2),
            in_specs=[spec(0, k, u) for k, u in order] + [spec(1, k, u) for k, u in order],
            out_specs=pl.BlockSpec((group, 2 * wide * group), lambda r, c, ref, place: (r, c)),
        ),
        out_shape=jax.ShapeDtypeStruct((2 * group, 2 * half * group), jnp.float32),
        compiler_params=pltpu.CompilerParams(vmem_limit_bytes=VMEM_BYTES),
        cost_estimate=LIGHT,
        name="finish",
    )(table, place, *([blocks] * len(order)), *([other] * len(order)))


def in_order(index, mine, other, axis):
    return jnp.where(
        index == 0,
        jnp.concatenate([mine, other], axis=axis),
        jnp.concatenate([other, mine], axis=axis),
    )


def pair_swap(value, count):
    return lax.ppermute(value, "dp", [(index, index ^ 1) for index in range(count)])


def far_shift(value, step, count):
    return lax.ppermute(value, "dp", [(index, (index + 2 * step) % count) for index in range(count)])


def exchange_pairs(slice_of, pair, count):
    pairs = count // 2
    came = [slice_of(pair)]
    for step in range(1, pairs):
        came.append(far_shift(slice_of(lax.rem(pair + step, pairs)), step, count))
    return came


def natural(came, pair):
    pairs = len(came)
    pieces = []
    for index in range(pairs):
        behind = lax.rem(pair - index + pairs, pairs)
        piece = came[0]
        for step in range(1, pairs):
            piece = jnp.where(behind == step, came[step], piece)
        pieces.append(piece)
    return pieces


def scatter_pairs(value, pair, count):
    size = value.shape[0] // (count // 2)

    def slice_of(index):
        return lax.dynamic_slice_in_dim(value, index * size, size, 0)

    return sum(piece.astype(jnp.float32) for piece in exchange_pairs(slice_of, pair, count))


def local(ring, activations, out_grads, proj_in, proj_out, stored, counts, query_ids):
    owners = ring.count
    full = stored.shape[1]
    width = full // owners
    group = width // 2
    half = ring.half
    t = lax.axis_index("tensor")
    d = lax.axis_index("dp")
    pair, side = d // 2, lax.rem(d, 2)
    g = 2 * d + t
    place = jnp.stack([d, t]).astype(jnp.int32)

    first_stored = stored[:, :width]
    corner_rows = lead_dot(lax.dynamic_slice_in_dim(first_stored, t * group, group, 1), first_stored)
    corner_rows = scatter_pairs(corner_rows, pair, owners)
    corner_rows = corner_rows + pair_swap(corner_rows, owners)
    corner_rows = exchange_pairs(lambda index: corner_rows, pair, owners)
    corner_rows = jnp.concatenate(natural(corner_rows, pair), axis=0)
    corner_other = lax.ppermute(corner_rows, "tensor", SWAP)

    sides = jnp.concatenate(
        [
            jnp.dot(activations, proj_in, preferred_element_type=jnp.float32),
            jnp.dot(out_grads, proj_out, preferred_element_type=jnp.float32),
        ],
        axis=1,
    )
    sides = sides + lax.ppermute(sides, "tensor", SWAP)

    examples = counts.shape[0]
    all_examples = examples * owners
    rank = proj_in.shape[1]
    position = jnp.arange(SEQ, dtype=jnp.int32)[None, :]
    weights = jnp.where(
        position < counts[:, None], 1.0 / counts.astype(jnp.float32)[:, None], jnp.float32(0.0)
    )
    outer = jnp.einsum(
        "es,esi,esj->eij",
        weights,
        sides[:, :rank].reshape(examples, SEQ, rank),
        sides[:, rank:].reshape(examples, SEQ, rank),
        precision=EXACT,
    )
    vectors = outer.reshape(examples, full).astype(jnp.bfloat16)

    def columns_for(index):
        groups = [lax.dynamic_slice_in_dim(vectors, (4 * index + 2 * s + t) * group, group, 1) for s in (0, 1)]
        return jnp.concatenate([vectors[:, :width]] + groups, axis=1)

    came = natural(exchange_pairs(columns_for, pair, owners), pair)
    came = jnp.concatenate(came, axis=0)
    kept = jnp.where(side == 0, came[:, : width + group], jnp.concatenate([came[:, :width], came[:, width + group :]], axis=1))
    away = jnp.where(side == 0, jnp.concatenate([came[:, :width], came[:, width + group :]], axis=1), came[:, : width + group])
    shape = (owners // 2, 1, examples, width + group)
    known = in_order(side, kept.reshape(shape), pair_swap(away, owners).reshape(shape), 1)
    known = known.reshape(all_examples, width + group)
    first_cols, own_cols = known[:, :width], known[:, width:].astype(jnp.float32)

    split = (len(ring.offsets) + 1) // 2
    far_slots = [(half, None)]
    for offset in ring.offsets[:split]:
        far_slots += [(offset, 0), (offset, 1)]
    near_slots = []
    for offset in ring.offsets[split:] + [0]:
        near_slots += [(offset, 0), (offset, 1)]

    slots = far_slots + near_slots
    far_count, near_count = len(far_slots), len(near_slots)
    ahead, back = ring.shift(1), ring.shift(-1)

    def terms_of(steps, parts, after=()):
        return window_terms(ring, place, stored, vectors, group, steps, parts, after)

    far, near = terms_of([half], [far_slots, near_slots])
    far, near = far[0], near[0]
    second = terms_of([half - 1, 1 - half], [slots], [far])[0]
    far_ahead = lax.ppermute(far, "dp", ahead)
    near_back = lax.ppermute(near, "dp", back)
    last = [far_count, near_count] if half == 2 else [far_count + near_count]
    going = add_terms(second, 0, [(far_ahead, 0)], last, group)
    coming = add_terms(second, 1, [(near_back, far_count)], last, group)

    later_steps = [s for step in range(half - 2, 0, -1) for s in (step, -step)] + [0]
    later = terms_of(later_steps, [slots], [going[0], coming[0]])[0]
    solved, first_pairs = solve(place, corner_rows, corner_other, first_cols, [later])
    token = solved
    for step in range(half - 2, 0, -1):
        last = [far_count, near_count] if step == 1 else [far_count + near_count]
        going = [lax.ppermute(value, "dp", ahead) for value in going]
        coming = [lax.ppermute(value, "dp", back) for value in coming]
        index = later_steps.index(step)
        going = add_terms(later, index, [(going[0], 0)], last, group, [token])
        coming = add_terms(later, index + 1, [(coming[0], 0)], last, group, [token])
        if step == half - 2:
            pieces = spread_back(place, stored, solved, owners, group, [going[0], coming[0]])
            token = pieces[0]
    going = [lax.ppermute(value, "dp", ahead) for value in going]
    coming = [lax.ppermute(value, "dp", back) for value in coming]

    terms = pieces[0].astype(jnp.float32)
    for step in range(1, owners // 2):
        terms = terms + far_shift(pieces[step], step, owners).astype(jnp.float32)
    away = jnp.where(side == 0, terms[1], terms[0]).astype(jnp.bfloat16)
    terms = jnp.where(side == 0, terms[0], terms[1]) + pair_swap(away, owners).astype(jnp.float32)
    damped = lax.dynamic_slice_in_dim(solved.T, lax.rem(g, 2) * group, group, 1)
    damped = jnp.where(g < 2, damping * damped, 0.0)
    rest = own_cols - lead_dot(first_pairs, own_cols, EXACT) - terms - damped
    pairs = lax.dot_general(rest, rest, (((1,), (1,)), ((), ())), precision=EXACT, preferred_element_type=jnp.float32)
    pairs = pairs + jnp.where(g == 0, first_pairs, 0.0)
    pairs = scatter_pairs(pairs, pair, owners)
    away = lax.dynamic_slice_in_dim(pairs, (1 - side) * examples, examples, 0)
    pairs = lax.dynamic_slice_in_dim(pairs, side * examples, examples, 0) + pair_swap(away, owners)
    pairs = pairs + lax.ppermute(pairs, "tensor", SWAP)
    chosen = (query_ids[:, None] == jnp.arange(all_examples, dtype=jnp.int32)[None, :]).astype(jnp.float32)
    scores = lax.dot_general(chosen, pairs, (((1,), (1,)), ((), ())), precision=EXACT, preferred_element_type=jnp.float32) / R

    far = close_window(later, 0, going[0], coming[0], far_slots, group)
    near = close_window(later, far_count, going[1], coming[1], near_slots, group)
    turned = {}
    for (found, slots) in ((far, far_slots), (near, near_slots)):
        chips = [chip for chip in pairs_of(slots) if chip[0] != 0]
        for (offset, _, _), block in zip(chips, found[1:]):
            turned[offset] = block
    came = [lax.ppermute(turned[offset], "dp", ring.shift(offset)) for offset in ring.offsets + [half]]
    blocks = jnp.concatenate([far[0], near[0]] + came, axis=0)
    send_table, final_table = assembly_tables(ring, far_slots + near_slots, d, t)
    other = lax.ppermute(for_sibling(send_table, blocks, group), "tensor", SWAP)
    return finish(place, final_table, blocks, other, half, group), scores


def solution(mesh):
    placed = (
        P(("groups", "dp"), "tensor"),
        P(("groups", "dp"), "tensor"),
        P("tensor", None),
        P("tensor", None),
        P(("groups", "dp"), None),
        P(("groups", "dp")),
        P("groups"),
    )
    ring = Ring(mesh)

    def program(*args):
        return local(ring, *args)

    return jax.shard_map(
        program,
        mesh=mesh,
        in_specs=placed,
        out_specs=(P(("groups", "dp"), "tensor"), P("groups", "dp")),
        check_vma=False,
    )
```

```python
import jax
import jax.numpy as jnp
from jax import lax
from jax.experimental import pallas as pl
from jax.experimental.pallas import tpu as pltpu
from jax.sharding import PartitionSpec as P

R = 64
SEQ = 16
damping = 1.0
EXACT = lax.Precision.HIGHEST
SWAP = [(0, 1), (1, 0)]
VMEM_BYTES = 56 * 1024 * 1024
LIGHT = pl.CostEstimate(flops=10**6, bytes_accessed=10**5, transcendentals=0)
ANYWHERE = pl.BlockSpec(memory_space=pl.ANY)


class Ring:
    def __init__(self, mesh):
        self.count = mesh.shape["dp"]
        self.half = self.count // 2
        coords = [getattr(device, "coords", None) for device in mesh.devices[0, :, 0]]
        self.folded = False
        if None not in coords:
            moving = [axis for axis in range(3) if len({place[axis] for place in coords}) > 1]
            fast = [axis for axis in moving if coords[0][axis] != coords[1][axis]]
            self.folded = len(moving) == 2 and len(fast) == 1 and len({place[fast[0]] for place in coords}) == 2
        reach = [0, 0]
        self.offsets = []
        for distance in range(self.half - 1, 0, -1):
            side = 0 if reach[0] <= reach[1] else 1
            reach[side] += distance
            self.offsets.append(distance if side == 0 else -distance)

    def index_at(self, position):
        if isinstance(position, int):
            position = position % self.count
            if not self.folded:
                return position
            return 2 * position if position < self.half else 2 * (self.count - 1 - position) + 1
        position = lax.rem(position + 2 * self.count, self.count)
        if not self.folded:
            return position
        return jnp.where(position < self.half, 2 * position, 2 * (self.count - 1 - position) + 1)

    def position_of(self, index):
        if not self.folded:
            return index
        return jnp.where(lax.rem(index, 2) == 0, index // 2, self.count - 1 - index // 2)

    def shift(self, step):
        return [(self.index_at(p), self.index_at(p + step)) for p in range(self.count)]


def lead_dot(left, right, precision=None):
    return lax.dot_general(
        left, right, (((0,), (0,)), ((), ())), precision=precision, preferred_element_type=jnp.float32
    )


def exact_dot(left, right):
    return jnp.dot(left, right, precision=EXACT, preferred_element_type=jnp.float32)


def pairs_of(slots):
    found = []
    for index, (offset, core) in enumerate(slots):
        if core is None:
            found.append((offset, 1, index))
        elif core == 0:
            found.append((offset, 2, index))
    return found


def project(activations, proj_in, out_grads, proj_out, after=()):
    tokens, inner = activations.shape
    shorter = out_grads.shape[1]
    rank = proj_in.shape[1]
    chunk = 2048 if inner % 2048 == 0 and shorter % 2048 == 0 else shorter
    steps, early = inner // chunk, shorter // chunk

    def kernel(act_ref, in_ref, grad_ref, out_ref, *refs):
        sides_ref = refs[-1]
        i = pl.program_id(0)

        @pl.when(i == 0)
        def _():
            sides_ref[...] = jnp.zeros_like(sides_ref)

        sides_ref[:, :rank] += jnp.dot(act_ref[...], in_ref[...], preferred_element_type=jnp.float32)

        @pl.when(i < early)
        def _():
            sides_ref[:, rank:] += jnp.dot(grad_ref[...], out_ref[...], preferred_element_type=jnp.float32)

    return pl.pallas_call(
        kernel,
        grid=(steps,),
        in_specs=[
            pl.BlockSpec((tokens, chunk), lambda i: (0, i)),
            pl.BlockSpec((chunk, rank), lambda i: (i, 0)),
            pl.BlockSpec((tokens, chunk), lambda i: (0, jnp.minimum(i, early - 1))),
            pl.BlockSpec((chunk, rank), lambda i: (jnp.minimum(i, early - 1), 0)),
        ]
        + [ANYWHERE] * len(after),
        out_specs=pl.BlockSpec((tokens, 2 * rank), lambda i: (0, 0)),
        out_shape=jax.ShapeDtypeStruct((tokens, 2 * rank), jnp.float32),
        compiler_params=pltpu.CompilerParams(vmem_limit_bytes=VMEM_BYTES),
        cost_estimate=LIGHT,
        name="project",
    )(activations, proj_in, out_grads, proj_out, *after)


def corner_terms(place, stored, width, pairs):
    rows = stored.shape[0]
    group = width // 2
    size = group // pairs

    def kernel(place_ref, left_ref, right_ref, *refs):
        whole = refs[-1]
        whole[...] = jnp.dot(left_ref[...].T, right_ref[...], preferred_element_type=jnp.float32)
        for index in range(pairs):
            first = lax.rem(place_ref[0] // 2 + index, pairs) * size
            refs[index][...] = whole[pl.ds(pl.multiple_of(first, size), size), :]

    return pl.pallas_call(
        kernel,
        grid_spec=pltpu.PrefetchScalarGridSpec(
            num_scalar_prefetch=1,
            grid=(1,),
            in_specs=[
                pl.BlockSpec((rows, group), lambda i, ref: (0, ref[1])),
                pl.BlockSpec((rows, width), lambda i, ref: (0, 0)),
            ],
            out_specs=[pl.BlockSpec((size, width), lambda i, ref: (0, 0))] * pairs,
            scratch_shapes=[pltpu.VMEM((group, width), jnp.float32)],
        ),
        out_shape=[jax.ShapeDtypeStruct((size, width), jnp.float32)] * pairs,
        compiler_params=pltpu.CompilerParams(vmem_limit_bytes=VMEM_BYTES),
        cost_estimate=LIGHT,
        name="corner_terms",
    )(place, stored, stored)


def window_terms(ring, place, stored, vectors, group, steps, parts, after=()):
    rows = stored.shape[0]
    new_rows, full = vectors.shape
    count = ring.count
    taps = jnp.array(steps, jnp.int32)
    chips = [chip for slots in parts for chip in pairs_of(slots)]
    wanted = []
    for step in steps:
        for offset in [0] + [chip[0] for chip in chips]:
            apart = (step - steps[0] + offset) % count
            if apart not in wanted:
                wanted.append(apart)
    at_first = [offset % count for offset in [0] + [chip[0] for chip in chips]]

    def kernel(place_ref, step_ref, stored_ref, vectors_ref, *refs):
        outs, held, arrived = refs[len(after) : -2], refs[-2], refs[-1]
        i = pl.program_id(0)
        begin = ring.position_of(place_ref[0]) + step_ref[0] + count
        owner = lax.rem(ring.position_of(place_ref[0]) + step_ref[i] + count, count)
        moved = lax.rem(step_ref[i] - step_ref[0] + 2 * count, count)
        core = place_ref[1]

        def load(apart):
            source = pl.multiple_of(2 * ring.index_at(begin + apart) * group, 2 * group)
            return pltpu.make_async_copy(stored_ref.at[:, pl.ds(source, 2 * group)], held.at[apart], arrived.at[apart])

        @pl.when(i == 0)
        def _():
            for apart in wanted:
                load(apart).start()

        rest = [apart for apart in wanted if apart not in at_first]
        if rest:

            @pl.when(i == 1)
            def _():
                for apart in rest:
                    load(apart).wait()

        waited = set()

        def ready(offset):
            apart = offset % count
            if apart not in waited:
                waited.add(apart)

                @pl.when(i == 0)
                def _():
                    load(apart).wait()

            return lax.rem(moved + apart, count)

        own = pl.ds(pl.multiple_of(core * group, group), group)
        turned = held[ready(0), :, own].T
        turned_new = vectors_ref[:, pl.ds(pl.multiple_of((2 * ring.index_at(owner) + core) * group, group), group)].T
        for slots, out_ref in zip(parts, outs):
            for offset, blocks, first in pairs_of(slots):
                slot = ready(offset)
                column = 2 * ring.index_at(owner + offset)
                if blocks == 1:
                    side = jnp.where(owner < ring.half, core, 1 - core)
                    right = held[slot, :, pl.ds(pl.multiple_of(side * group, group), group)]
                    column = column + side
                else:
                    right = held[slot]
                total = jnp.dot(turned, right, preferred_element_type=jnp.float32)
                right = vectors_ref[:, pl.ds(pl.multiple_of(column * group, blocks * group), blocks * group)]
                total = total + jnp.dot(turned_new, right, preferred_element_type=jnp.float32)
                out_ref[0, :, first * group : (first + blocks) * group] = total.astype(jnp.bfloat16)

    def out(slots):
        return pl.BlockSpec((1, group, len(slots) * group), lambda i, a, b: (i, 0, 0))

    def shape(slots):
        return jax.ShapeDtypeStruct((len(steps), group, len(slots) * group), jnp.bfloat16)

    return pl.pallas_call(
        kernel,
        grid_spec=pltpu.PrefetchScalarGridSpec(
            num_scalar_prefetch=2,
            grid=(len(steps),),
            in_specs=[ANYWHERE, pl.BlockSpec((new_rows, full), lambda i, a, b: (0, 0), pipeline_mode=pl.Buffered(1))]
            + [ANYWHERE] * len(after),
            out_specs=[out(slots) for slots in parts],
            scratch_shapes=[
                pltpu.VMEM((count, rows, 2 * group), jnp.bfloat16),
                pltpu.SemaphoreType.DMA((count,)),
            ],
        ),
        out_shape=[shape(slots) for slots in parts],
        compiler_params=pltpu.CompilerParams(vmem_limit_bytes=VMEM_BYTES),
        cost_estimate=LIGHT,
        name="window_terms",
    )(place, taps, stored, vectors, *after)


def add_terms(terms, index, arrived, sizes, group, after=()):
    count = terms.shape[2] // group

    def kernel(terms_ref, *refs):
        outs = refs[len(arrived) + len(after) :]
        for k in range(count):
            total = terms_ref[0, :, k * group : (k + 1) * group].astype(jnp.float32)
            for ref, (array, first) in zip(refs, arrived):
                if first <= k < first + array.shape[1] // group:
                    total = total + ref[:, (k - first) * group : (k - first + 1) * group].astype(jnp.float32)
            place, start = 0, 0
            while k - start >= sizes[place]:
                start += sizes[place]
                place += 1
            outs[place][:, (k - start) * group : (k - start + 1) * group] = total.astype(jnp.bfloat16)

    cuts = 4 if group >= 256 else 2

    def flat(columns):
        return pl.BlockSpec((group // cuts, columns), lambda i: (i, 0))

    return pl.pallas_call(
        kernel,
        grid=(cuts,),
        in_specs=[pl.BlockSpec((1, group // cuts, count * group), lambda i: (index, i, 0))]
        + [flat(array.shape[1]) for array, _ in arrived]
        + [ANYWHERE] * len(after),
        out_specs=[flat(size * group) for size in sizes],
        out_shape=[jax.ShapeDtypeStruct((group, size * group), jnp.bfloat16) for size in sizes],
        compiler_params=pltpu.CompilerParams(vmem_limit_bytes=VMEM_BYTES),
        cost_estimate=LIGHT,
        name="add_terms",
    )(terms, *[array for array, _ in arrived], *after)


def close_window(terms, base, ahead, back, slots, group):
    count = len(slots)
    chips = [chip for chip in pairs_of(slots) if chip[0] != 0]

    def kernel(own_ref, ahead_ref, back_ref, blocks_ref, *turned_refs):
        for k in range(count):
            cols = slice(k * group, (k + 1) * group)
            total = own_ref[0, :, (base + k) * group : (base + k + 1) * group].astype(jnp.float32)
            total = total + ahead_ref[:, cols].astype(jnp.float32) + back_ref[:, cols].astype(jnp.float32)
            total = total.astype(jnp.bfloat16)
            blocks_ref[k] = total
            for (_, blocks, first), turned_ref in zip(chips, turned_refs):
                if first <= k < first + blocks:
                    turned_ref[k - first] = total.T

    index = terms.shape[0] - 1
    flat = pl.BlockSpec((group, count * group), lambda i: (0, 0))
    sizes = [count] + [blocks for _, blocks, _ in chips]
    return pl.pallas_call(
        kernel,
        grid=(1,),
        in_specs=[pl.BlockSpec((1,) + terms.shape[1:], lambda i: (index, 0, 0)), flat, flat],
        out_specs=[pl.BlockSpec((size, group, group), lambda i: (0, 0, 0)) for size in sizes],
        out_shape=[jax.ShapeDtypeStruct((size, group, group), jnp.bfloat16) for size in sizes],
        compiler_params=pltpu.CompilerParams(vmem_limit_bytes=VMEM_BYTES),
        cost_estimate=LIGHT,
        name="close_window",
    )(terms, ahead, back)


def rough_dot(left, right):
    return jnp.dot(left.astype(jnp.bfloat16), right.astype(jnp.bfloat16), preferred_element_type=jnp.float32)


def split_terms(value):
    high = value.astype(jnp.bfloat16)
    value = value - high.astype(jnp.float32)
    middle = value.astype(jnp.bfloat16)
    value = value - middle.astype(jnp.float32)
    return high, middle, value.astype(jnp.bfloat16)


def identity(size):
    rows = lax.broadcasted_iota(jnp.int32, (size, size), 0)
    cols = lax.broadcasted_iota(jnp.int32, (size, size), 1)
    return (rows == cols).astype(jnp.float32)


def eliminate(matrix_ref, right_ref, out_ref, work, block):
    size = matrix_ref.shape[0]
    work[...] = matrix_ref[...]
    out_ref[...] = right_ref[...]
    eye = identity(block)
    for start in range(0, size, block):
        here = slice(start, start + block)
        rest = slice(start + block, size)
        corner = work[here, here]
        norm = jnp.max(jnp.sum(jnp.abs(corner), axis=0))

        def unfinished(state):
            return jnp.logical_and(state[0] < 40, state[1] > 5e-5)

        def improve(state):
            step, _, inverse = state
            better = inverse + exact_dot(inverse, eye - exact_dot(work[here, here], inverse))
            left_over = eye - exact_dot(work[here, here], better)
            return step + 1, jnp.max(jnp.abs(left_over)), better

        found = lax.while_loop(unfinished, improve, (jnp.int32(0), jnp.float32(1.0), eye / norm))[2]
        found = found + exact_dot(found, eye - exact_dot(work[here, here], found))
        solved = exact_dot(found, out_ref[here, :])
        out_ref[here, :] = solved
        if start + block < size:
            across = exact_dot(found, work[here, rest])
            down = work[rest, here]
            work[rest, rest] = work[rest, rest] - exact_dot(down, across)
            out_ref[rest, :] = out_ref[rest, :] - exact_dot(down, solved)
            work[here, rest] = across
    for start in range(size - 2 * block, -1, -block):
        here = slice(start, start + block)
        rest = slice(start + block, size)
        out_ref[here, :] = out_ref[here, :] - exact_dot(work[here, rest], out_ref[rest, :])


def solve(place, pairs_count, mine, other, kept, came, after=()):
    group, width = mine.shape
    examples = 2 * kept.shape[0]
    size = kept.shape[0] // pairs_count

    def kernel(place_ref, mine_ref, other_ref, kept_ref, came_ref, *refs):
        out_ref, pairs_ref, matrix, right, power, inverse, first_ref = refs[len(after) :]
        for start in range(0, kept_ref.shape[0], size):
            near, far = kept_ref[start : start + size, :width], came_ref[start : start + size, :width]
            even = lax.rem(place_ref[0], 2) == 0
            first_ref[2 * start : 2 * start + size, :] = jnp.where(even, near, far)
            first_ref[2 * start + size : 2 * start + 2 * size, :] = jnp.where(even, far, near)
        eye = identity(width)
        t = place_ref[1]
        matrix[pl.ds(pl.multiple_of(t * group, group), group), :] = mine_ref[...]
        matrix[pl.ds(pl.multiple_of((1 - t) * group, group), group), :] = other_ref[...]
        turned = first_ref[...].T
        full = matrix[...] + jnp.dot(turned, first_ref[...], preferred_element_type=jnp.float32) + damping * eye
        diagonal = full * eye
        rows_scale = lax.rsqrt(jnp.sum(diagonal, axis=1, keepdims=True))
        cols_scale = lax.rsqrt(jnp.sum(diagonal, axis=0, keepdims=True))
        full = full * rows_scale * cols_scale
        matrix[...] = full
        right[...] = turned.astype(jnp.float32) * rows_scale

        sums = jnp.max(jnp.sum(jnp.abs(full), axis=0))
        squared = rough_dot(full, full)
        norm = jnp.sqrt(jnp.max(jnp.sum(jnp.abs(squared), axis=0)) + sums * sums / 128)
        start = eye - full / norm
        inverse[...] = eye + start
        power[...] = start.astype(jnp.bfloat16)
        for _ in range(7):
            raised = jnp.dot(power[...], power[...], preferred_element_type=jnp.float32).astype(jnp.bfloat16)
            power[...] = raised
            held = inverse[...]
            inverse[...] = held + jnp.dot(held.astype(jnp.bfloat16), raised, preferred_element_type=jnp.float32)
        power[...] = (inverse[...] / norm).astype(jnp.bfloat16)

        largest = jnp.max(jnp.abs(right[...]))
        out_ref[...] = jnp.dot(power[...], right[...].astype(jnp.bfloat16), preferred_element_type=jnp.float32)

        def unfinished(state):
            return jnp.logical_and(state[0] < 12, jnp.logical_not(state[1] <= 5e-5 * largest))

        def refine(state):
            left_over = right[...] - exact_dot(matrix[...], out_ref[...])
            change = jnp.dot(power[...], left_over.astype(jnp.bfloat16), preferred_element_type=jnp.float32)
            out_ref[...] = out_ref[...] + change
            return state[0] + 1, jnp.max(jnp.abs(left_over))

        worst = lax.while_loop(unfinished, refine, (jnp.int32(0), 1.0 + largest))[1]

        @pl.when(jnp.logical_not(worst <= 5e-5 * largest))
        def _():
            eliminate(matrix, right, out_ref, inverse, 128)

        solved = out_ref[...] * rows_scale
        out_ref[...] = solved
        pairs = jnp.zeros((examples, examples), jnp.float32)
        for term in split_terms(solved):
            pairs = pairs + jnp.dot(first_ref[...], term, preferred_element_type=jnp.float32)
        pairs_ref[...] = pairs

    whole = pl.BlockSpec(memory_space=pltpu.VMEM)
    return pl.pallas_call(
        kernel,
        in_specs=[pl.BlockSpec(memory_space=pltpu.SMEM)] + [whole] * 4 + [ANYWHERE] * len(after),
        out_shape=[
            jax.ShapeDtypeStruct((width, examples), jnp.float32),
            jax.ShapeDtypeStruct((examples, examples), jnp.float32),
        ],
        scratch_shapes=[
            pltpu.VMEM((width, width), jnp.float32),
            pltpu.VMEM((width, examples), jnp.float32),
            pltpu.VMEM((width, width), jnp.bfloat16),
            pltpu.VMEM((width, width), jnp.float32),
            pltpu.VMEM((examples, width), jnp.bfloat16),
        ],
        compiler_params=pltpu.CompilerParams(vmem_limit_bytes=VMEM_BYTES),
        cost_estimate=LIGHT,
        name="solve",
    )(place, mine, other, kept, came, *after)


def spread_back(place, stored, solved, owners, group, after=()):
    rows = stored.shape[0]
    width, examples = solved.shape
    pairs = owners // 2

    def kernel(place_ref, first_ref, solved_ref, *refs):
        cols, outs = refs[:owners], refs[owners + len(after) :]
        total = jnp.zeros((rows, examples), jnp.float32)
        for term in split_terms(solved_ref[...]):
            total = total + jnp.dot(first_ref[...], term, preferred_element_type=jnp.float32)
        terms = jnp.concatenate(split_terms(total.T)[:2], axis=0)
        for index in range(owners):
            product = jnp.dot(terms, cols[index][...], preferred_element_type=jnp.float32)
            outs[index // 2][index % 2] = (product[:examples] + product[examples:]).astype(jnp.bfloat16)

    def owner(index, ref):
        return 2 * lax.rem(ref[0] // 2 + index // 2, pairs) + index % 2

    return pl.pallas_call(
        kernel,
        grid_spec=pltpu.PrefetchScalarGridSpec(
            num_scalar_prefetch=1,
            grid=(1,),
            in_specs=[
                pl.BlockSpec((rows, width), lambda i, ref: (0, 0)),
                pl.BlockSpec((width, examples), lambda i, ref: (0, 0)),
            ]
            + [
                pl.BlockSpec((rows, group), lambda i, ref, index=index: (0, 2 * owner(index, ref) + ref[1]))
                for index in range(owners)
            ]
            + [ANYWHERE] * len(after),
            out_specs=[pl.BlockSpec((2, examples, group), lambda i, ref: (0, 0, 0))] * pairs,
        ),
        out_shape=[jax.ShapeDtypeStruct((2, examples, group), jnp.bfloat16)] * pairs,
        compiler_params=pltpu.CompilerParams(vmem_limit_bytes=VMEM_BYTES),
        cost_estimate=LIGHT,
        name="spread_back",
    )(place, stored, solved, *([stored] * owners), *after)


def assembly_tables(ring, slots, d, t):
    start = [0] * ring.count
    arrived = [0] * ring.count
    for offset, _, first in pairs_of(slots):
        start[offset % ring.count] = first
    place = len(slots)
    for offset in ring.offsets:
        start[-offset % ring.count] = place
        arrived[-offset % ring.count] = 1
        place += 2
    here = ring.position_of(d)
    early = here < ring.half

    def look_up(values, offset):
        found = jnp.zeros_like(offset)
        for index, value in enumerate(values):
            if value:
                found = jnp.where(offset == index, value, found)
        return found

    def offsets_of(chips):
        return lax.rem(ring.position_of(chips) - here + 2 * ring.count, ring.count)

    def fetch(offset, j):
        own = (j == t) == early
        quarter = jnp.where(own, start[ring.half], place)
        return jnp.where(offset == ring.half, quarter, look_up(start, offset) + j)

    chips = jnp.arange(ring.half, dtype=jnp.int32)
    j = jnp.arange(2, dtype=jnp.int32)[None, :]
    send = fetch(offsets_of((1 - t) * ring.half + chips)[:, None], j)
    offset = offsets_of(t * ring.half + chips)[:, None, None]
    r = jnp.arange(2, dtype=jnp.int32)[None, :, None]
    u = jnp.arange(2, dtype=jnp.int32)[None, None, :]
    by_columns = jnp.where(offset == ring.half, early.astype(jnp.int32), look_up(arrived, offset)) == 1
    j = jnp.where(by_columns, r, u)
    local = fetch(offset, j)
    other = 2 * chips[:, None, None] + j
    mine = (jnp.where(by_columns, u, r) == t).astype(jnp.int32)
    final = jnp.stack([local, other, mine]).reshape(-1)
    return send.reshape(-1).astype(jnp.int32), final.astype(jnp.int32)


def for_sibling(table, blocks, group):
    total = table.shape[0]
    wide = min(4, total)

    def kernel(table_ref, *refs):
        for k in range(wide):
            refs[-1][k] = refs[k][0]

    return pl.pallas_call(
        kernel,
        grid_spec=pltpu.PrefetchScalarGridSpec(
            num_scalar_prefetch=1,
            grid=(total // wide,),
            in_specs=[
                pl.BlockSpec((1, group, group), lambda c, ref, k=k: (ref[wide * c + k], 0, 0)) for k in range(wide)
            ],
            out_specs=pl.BlockSpec((wide, group, group), lambda c, ref: (c, 0, 0)),
        ),
        out_shape=jax.ShapeDtypeStruct((total, group, group), jnp.bfloat16),
        compiler_params=pltpu.CompilerParams(vmem_limit_bytes=VMEM_BYTES),
        cost_estimate=LIGHT,
        name="for_sibling",
    )(table, *([blocks] * wide))


def finish(place, table, blocks, other, half, group):
    wide = half // 2
    total = 4 * half

    def at(kind, r, c, k, u, ref):
        return ref[kind * total + 4 * (wide * c + k) + 2 * r + u]

    def spec(kind, k, u):
        return pl.BlockSpec((1, group, group), lambda r, c, ref, place: (at(kind, r, c, k, u, ref), 0, 0))

    order = [(k, u) for k in range(wide) for u in (0, 1)]

    def kernel(table_ref, place_ref, *refs):
        r, c = pl.program_id(0), pl.program_id(1)
        out_ref = refs[-1]
        shape = (group, group)
        gap = lax.broadcasted_iota(jnp.int32, shape, 1) - lax.broadcasted_iota(jnp.int32, shape, 0)
        for index, (k, u) in enumerate(order):
            cols = slice(index * group, (index + 1) * group)
            chip = place_ref[1] * half + wide * c + k
            apart = (2 * place_ref[0] + r - 2 * chip - u) * group
            added = jnp.where(gap == apart, jnp.float32(damping), jnp.float32(0.0))
            mine = at(2, r, c, k, u, table_ref) == 1

            @pl.when(mine)
            def _():
                out_ref[:, cols] = added + refs[index][0].astype(jnp.float32)

            @pl.when(jnp.logical_not(mine))
            def _():
                out_ref[:, cols] = added + refs[len(order) + index][0].astype(jnp.float32)

    return pl.pallas_call(
        kernel,
        grid_spec=pltpu.PrefetchScalarGridSpec(
            num_scalar_prefetch=2,
            grid=(2, 2),
            in_specs=[spec(0, k, u) for k, u in order] + [spec(1, k, u) for k, u in order],
            out_specs=pl.BlockSpec((group, 2 * wide * group), lambda r, c, ref, place: (r, c)),
        ),
        out_shape=jax.ShapeDtypeStruct((2 * group, 2 * half * group), jnp.float32),
        compiler_params=pltpu.CompilerParams(vmem_limit_bytes=VMEM_BYTES),
        cost_estimate=LIGHT,
        name="finish",
    )(table, place, *([blocks] * len(order)), *([other] * len(order)))


def in_order(index, mine, other, axis):
    return jnp.where(
        index == 0,
        jnp.concatenate([mine, other], axis=axis),
        jnp.concatenate([other, mine], axis=axis),
    )


def pair_swap(value, count):
    return lax.ppermute(value, "dp", [(index, index ^ 1) for index in range(count)])


def far_shift(value, step, count):
    return lax.ppermute(value, "dp", [(index, (index + 2 * step) % count) for index in range(count)])


def exchange_pairs(slice_of, pair, count):
    pairs = count // 2
    came = [slice_of(pair)]
    for step in range(1, pairs):
        came.append(far_shift(slice_of(lax.rem(pair + step, pairs)), step, count))
    return came


def natural(came, pair):
    pairs = len(came)
    pieces = []
    for index in range(pairs):
        behind = lax.rem(pair - index + pairs, pairs)
        piece = came[0]
        for step in range(1, pairs):
            piece = jnp.where(behind == step, came[step], piece)
        pieces.append(piece)
    return pieces


def scatter_pairs(value, pair, count):
    size = value.shape[0] // (count // 2)

    def slice_of(index):
        return lax.dynamic_slice_in_dim(value, index * size, size, 0)

    return sum(piece.astype(jnp.float32) for piece in exchange_pairs(slice_of, pair, count))


def local(ring, activations, out_grads, proj_in, proj_out, stored, counts, query_ids):
    owners = ring.count
    full = stored.shape[1]
    width = full // owners
    group = width // 2
    half = ring.half
    t = lax.axis_index("tensor")
    d = lax.axis_index("dp")
    pair, side = d // 2, lax.rem(d, 2)
    g = 2 * d + t
    place = jnp.stack([d, t]).astype(jnp.int32)

    pairs_count = owners // 2
    corner_pieces = corner_terms(place, stored, width, pairs_count)
    corner_rows = corner_pieces[0]
    for step in range(1, pairs_count):
        corner_rows = corner_rows + far_shift(corner_pieces[step], step, owners)
    corner_payload = corner_rows

    sides = project(activations, proj_in, out_grads, proj_out, [corner_pieces[0]])
    sides = sides + lax.ppermute(sides, "tensor", SWAP)

    examples = counts.shape[0]
    all_examples = examples * owners
    rank = proj_in.shape[1]
    position = jnp.arange(SEQ, dtype=jnp.int32)[None, :]
    weights = jnp.where(
        position < counts[:, None], 1.0 / counts.astype(jnp.float32)[:, None], jnp.float32(0.0)
    )
    outer = jnp.einsum(
        "es,esi,esj->eij",
        weights,
        sides[:, :rank].reshape(examples, SEQ, rank),
        sides[:, rank:].reshape(examples, SEQ, rank),
        precision=EXACT,
    )
    vectors = outer.reshape(examples, full).astype(jnp.bfloat16)

    def columns_for(index):
        groups = [lax.dynamic_slice_in_dim(vectors, (4 * index + 2 * s + t) * group, group, 1) for s in (0, 1)]
        return jnp.concatenate([vectors[:, :width]] + groups, axis=1)

    payloads = [columns_for(lax.rem(pair + step, pairs_count)) for step in range(pairs_count)]

    split = (len(ring.offsets) + 1) // 2
    far_slots = [(half, None)]
    for offset in ring.offsets[:split]:
        far_slots += [(offset, 0), (offset, 1)]
    near_slots = []
    for offset in ring.offsets[split:] + [0]:
        near_slots += [(offset, 0), (offset, 1)]

    slots = far_slots + near_slots
    far_count, near_count = len(far_slots), len(near_slots)
    ahead, back = ring.shift(1), ring.shift(-1)

    def terms_of(steps, parts, after=()):
        return window_terms(ring, place, stored, vectors, group, steps, parts, after)

    far, near = terms_of([half], [far_slots, near_slots], payloads + [corner_payload])
    far, near = far[0], near[0]

    came = [payloads[0]] + [far_shift(payloads[step], step, owners) for step in range(1, pairs_count)]
    came = jnp.concatenate(natural(came, pair), axis=0)
    second_group = jnp.concatenate([came[:, :width], came[:, width + group :]], axis=1)
    first_group = came[:, : width + group]
    kept = jnp.where(side == 0, first_group, second_group)
    away = jnp.where(side == 0, second_group, first_group)
    corner_rows = corner_payload + pair_swap(corner_payload, owners)
    second = terms_of([half - 1, 1 - half], [slots], [far, away, corner_rows])[0]
    came = pair_swap(away, owners)
    corner_rows = [corner_rows] + [far_shift(corner_rows, step, owners) for step in range(1, pairs_count)]
    corner_rows = jnp.concatenate(natural(corner_rows, pair), axis=0)
    corner_other = lax.ppermute(corner_rows, "tensor", SWAP)
    shape = (pairs_count, 1, examples, group)
    own_cols = in_order(side, kept[:, width:].reshape(shape), came[:, width:].reshape(shape), 1)
    own_cols = own_cols.reshape(all_examples, group).astype(jnp.float32)
    far_ahead = lax.ppermute(far, "dp", ahead)
    near_back = lax.ppermute(near, "dp", back)
    last = [far_count, near_count] if half == 2 else [far_count + near_count]
    going = add_terms(second, 0, [(far_ahead, 0)], last, group)
    coming = add_terms(second, 1, [(near_back, far_count)], last, group)

    later_steps = [s for step in range(half - 2, 0, -1) for s in (step, -step)] + [0]
    later = terms_of(later_steps, [slots], [going[0], coming[0]])[0]
    solved, first_pairs = solve(place, pairs_count, corner_rows, corner_other, kept, came, [later])
    token = solved
    for step in range(half - 2, 0, -1):
        last = [far_count, near_count] if step == 1 else [far_count + near_count]
        going = [lax.ppermute(value, "dp", ahead) for value in going]
        coming = [lax.ppermute(value, "dp", back) for value in coming]
        index = later_steps.index(step)
        going = add_terms(later, index, [(going[0], 0)], last, group, [token])
        coming = add_terms(later, index + 1, [(coming[0], 0)], last, group, [token])
        if step == half - 2:
            pieces = spread_back(place, stored, solved, owners, group, [going[0], coming[0]])
            token = pieces[0]
    going = [lax.ppermute(value, "dp", ahead) for value in going]
    coming = [lax.ppermute(value, "dp", back) for value in coming]

    terms = pieces[0].astype(jnp.float32)
    for step in range(1, owners // 2):
        terms = terms + far_shift(pieces[step], step, owners).astype(jnp.float32)
    away = jnp.where(side == 0, terms[1], terms[0]).astype(jnp.bfloat16)
    terms = jnp.where(side == 0, terms[0], terms[1]) + pair_swap(away, owners).astype(jnp.float32)
    damped = lax.dynamic_slice_in_dim(solved.T, lax.rem(g, 2) * group, group, 1)
    damped = jnp.where(g < 2, damping * damped, 0.0)
    rest = own_cols - lead_dot(first_pairs, own_cols, EXACT) - terms - damped
    pairs = lax.dot_general(rest, rest, (((1,), (1,)), ((), ())), precision=EXACT, preferred_element_type=jnp.float32)
    pairs = pairs + jnp.where(g == 0, first_pairs, 0.0)
    pairs = scatter_pairs(pairs, pair, owners)
    away = lax.dynamic_slice_in_dim(pairs, (1 - side) * examples, examples, 0)
    pairs = lax.dynamic_slice_in_dim(pairs, side * examples, examples, 0) + pair_swap(away, owners)
    pairs = pairs + lax.ppermute(pairs, "tensor", SWAP)
    chosen = (query_ids[:, None] == jnp.arange(all_examples, dtype=jnp.int32)[None, :]).astype(jnp.float32)
    scores = lax.dot_general(chosen, pairs, (((1,), (1,)), ((), ())), precision=EXACT, preferred_element_type=jnp.float32) / R

    far = close_window(later, 0, going[0], coming[0], far_slots, group)
    near = close_window(later, far_count, going[1], coming[1], near_slots, group)
    turned = {}
    for (found, slots) in ((far, far_slots), (near, near_slots)):
        chips = [chip for chip in pairs_of(slots) if chip[0] != 0]
        for (offset, _, _), block in zip(chips, found[1:]):
            turned[offset] = block
    came = [lax.ppermute(turned[offset], "dp", ring.shift(offset)) for offset in ring.offsets + [half]]
    blocks = jnp.concatenate([far[0], near[0]] + came, axis=0)
    send_table, final_table = assembly_tables(ring, far_slots + near_slots, d, t)
    other = lax.ppermute(for_sibling(send_table, blocks, group), "tensor", SWAP)
    return finish(place, final_table, blocks, other, half, group), scores


def solution(mesh):
    placed = (
        P(("groups", "dp"), "tensor"),
        P(("groups", "dp"), "tensor"),
        P("tensor", None),
        P("tensor", None),
        P(("groups", "dp"), None),
        P(("groups", "dp")),
        P("groups"),
    )
    ring = Ring(mesh)

    def program(*args):
        return local(ring, *args)

    return jax.shard_map(
        program,
        mesh=mesh,
        in_specs=placed,
        out_specs=(P(("groups", "dp"), "tensor"), P("groups", "dp")),
        check_vma=False,
    )
```

```python
import jax
import jax.numpy as jnp
from jax import lax
from jax.experimental import pallas as pl
from jax.experimental.pallas import tpu as pltpu
from jax.sharding import PartitionSpec as P

R = 64
SEQ = 16
damping = 1.0
EXACT = lax.Precision.HIGHEST
SWAP = [(0, 1), (1, 0)]
VMEM_BYTES = 56 * 1024 * 1024
SMALL_BYTES = 12 * 1024 * 1024
LIGHT = pl.CostEstimate(flops=10**6, bytes_accessed=10**5, transcendentals=0)
ANYWHERE = pl.BlockSpec(memory_space=pl.ANY)


class Ring:
    def __init__(self, mesh):
        self.count = mesh.shape["dp"]
        self.half = self.count // 2
        coords = [getattr(device, "coords", None) for device in mesh.devices[0, :, 0]]
        self.folded = False
        if None not in coords:
            moving = [axis for axis in range(3) if len({place[axis] for place in coords}) > 1]
            fast = [axis for axis in moving if coords[0][axis] != coords[1][axis]]
            self.folded = len(moving) == 2 and len(fast) == 1 and len({place[fast[0]] for place in coords}) == 2
        reach = [0, 0]
        self.offsets = []
        for distance in range(self.half - 1, 0, -1):
            side = 0 if reach[0] <= reach[1] else 1
            reach[side] += distance
            self.offsets.append(distance if side == 0 else -distance)

    def index_at(self, position):
        if isinstance(position, int):
            position = position % self.count
            if not self.folded:
                return position
            return 2 * position if position < self.half else 2 * (self.count - 1 - position) + 1
        position = lax.rem(position + 2 * self.count, self.count)
        if not self.folded:
            return position
        return jnp.where(position < self.half, 2 * position, 2 * (self.count - 1 - position) + 1)

    def position_of(self, index):
        if not self.folded:
            return index
        return jnp.where(lax.rem(index, 2) == 0, index // 2, self.count - 1 - index // 2)

    def shift(self, step):
        return [(self.index_at(p), self.index_at(p + step)) for p in range(self.count)]


def lead_dot(left, right, precision=None):
    return lax.dot_general(
        left, right, (((0,), (0,)), ((), ())), precision=precision, preferred_element_type=jnp.float32
    )


def exact_dot(left, right):
    return jnp.dot(left, right, precision=EXACT, preferred_element_type=jnp.float32)


def pairs_of(slots):
    found = []
    for index, (offset, core) in enumerate(slots):
        if core is None:
            found.append((offset, 1, index))
        elif core == 0:
            found.append((offset, 2, index))
    return found


def window_terms(ring, place, stored, vectors, group, steps, parts, after=()):
    rows, full = stored.shape
    new_rows = vectors.shape[0]
    chips = [(part,) + chip for part, slots in enumerate(parts) for chip in pairs_of(slots)]
    taps = jnp.array(list(steps) + [offset for _, offset, _, _ in chips], jnp.int32)

    def owner_of(i, place_ref, taps_ref):
        return lax.rem(ring.position_of(place_ref[0]) + taps_ref[i] + ring.count, ring.count)

    def chip_of(i, k, place_ref, taps_ref):
        return ring.index_at(owner_of(i, place_ref, taps_ref) + taps_ref[len(steps) + k])

    def kernel(place_ref, taps_ref, left_ref, right_ref, left_new_ref, right_new_ref, *refs):
        outs, turned, turned_new = refs[len(after) : -2], refs[-2], refs[-1]
        i, k = pl.program_id(0), pl.program_id(1)
        owner = owner_of(i, place_ref, taps_ref)

        @pl.when(k == 0)
        def _():
            turned[...] = left_ref[...].T
            turned_new[...] = left_new_ref[...].T

        for index, (part, _, blocks, first) in enumerate(chips):

            @pl.when(k == index)
            def _():
                columns = slice(0, 2 * group)
                if blocks == 1:
                    side = jnp.where(owner < ring.half, place_ref[1], 1 - place_ref[1])
                    columns = pl.ds(pl.multiple_of(side * group, group), group)
                total = jnp.dot(turned[...], right_ref[:, columns], preferred_element_type=jnp.float32)
                total = total + jnp.dot(turned_new[...], right_new_ref[:, columns], preferred_element_type=jnp.float32)
                outs[part][0, :, first * group : (first + blocks) * group] = total.astype(jnp.bfloat16)

    def left_map(i, k, place_ref, taps_ref):
        return 0, 2 * ring.index_at(owner_of(i, place_ref, taps_ref)) + place_ref[1]

    def right_map(i, k, place_ref, taps_ref):
        return 0, chip_of(i, k, place_ref, taps_ref)

    def out(slots):
        return pl.BlockSpec((1, group, len(slots) * group), lambda i, k, a, b: (i, 0, 0))

    def shape(slots):
        return jax.ShapeDtypeStruct((len(steps), group, len(slots) * group), jnp.bfloat16)

    return pl.pallas_call(
        kernel,
        grid_spec=pltpu.PrefetchScalarGridSpec(
            num_scalar_prefetch=2,
            grid=(len(steps), len(chips)),
            in_specs=[
                pl.BlockSpec((rows, group), left_map),
                pl.BlockSpec((rows, 2 * group), right_map),
                pl.BlockSpec((new_rows, group), left_map),
                pl.BlockSpec((new_rows, 2 * group), right_map),
            ]
            + [ANYWHERE] * len(after),
            out_specs=[out(slots) for slots in parts],
            scratch_shapes=[pltpu.VMEM((group, rows), jnp.bfloat16), pltpu.VMEM((group, new_rows), jnp.bfloat16)],
        ),
        out_shape=[shape(slots) for slots in parts],
        compiler_params=pltpu.CompilerParams(vmem_limit_bytes=VMEM_BYTES),
        cost_estimate=LIGHT,
        name="window_terms",
    )(place, taps, stored, stored, vectors, vectors, *after)


def add_terms(terms, index, arrived, sizes, group, after=()):
    count = terms.shape[2] // group

    def kernel(terms_ref, *refs):
        outs = refs[len(arrived) + len(after) :]
        for k in range(count):
            total = terms_ref[0, :, k * group : (k + 1) * group].astype(jnp.float32)
            for ref, (array, first) in zip(refs, arrived):
                if first <= k < first + array.shape[1] // group:
                    total = total + ref[:, (k - first) * group : (k - first + 1) * group].astype(jnp.float32)
            place, start = 0, 0
            while k - start >= sizes[place]:
                start += sizes[place]
                place += 1
            outs[place][:, (k - start) * group : (k - start + 1) * group] = total.astype(jnp.bfloat16)

    def flat(columns):
        return pl.BlockSpec((group, columns), lambda i: (0, 0))

    return pl.pallas_call(
        kernel,
        grid=(1,),
        in_specs=[pl.BlockSpec((1, group, count * group), lambda i: (index, 0, 0))]
        + [flat(array.shape[1]) for array, _ in arrived]
        + [ANYWHERE] * len(after),
        out_specs=[flat(size * group) for size in sizes],
        out_shape=[jax.ShapeDtypeStruct((group, size * group), jnp.bfloat16) for size in sizes],
        compiler_params=pltpu.CompilerParams(vmem_limit_bytes=SMALL_BYTES),
        cost_estimate=LIGHT,
        name="add_terms",
    )(terms, *[array for array, _ in arrived], *after)


def close_window(terms, base, ahead, back, slots, group):
    count = len(slots)
    chips = [chip for chip in pairs_of(slots) if chip[0] != 0]

    def kernel(own_ref, ahead_ref, back_ref, blocks_ref, *turned_refs):
        for k in range(count):
            cols = slice(k * group, (k + 1) * group)
            total = own_ref[0, :, (base + k) * group : (base + k + 1) * group].astype(jnp.float32)
            total = total + ahead_ref[:, cols].astype(jnp.float32) + back_ref[:, cols].astype(jnp.float32)
            total = total.astype(jnp.bfloat16)
            blocks_ref[k] = total
            for (_, blocks, first), turned_ref in zip(chips, turned_refs):
                if first <= k < first + blocks:
                    turned_ref[k - first] = total.T

    index = terms.shape[0] - 1
    flat = pl.BlockSpec((group, count * group), lambda i: (0, 0))
    sizes = [count] + [blocks for _, blocks, _ in chips]
    return pl.pallas_call(
        kernel,
        grid=(1,),
        in_specs=[pl.BlockSpec((1,) + terms.shape[1:], lambda i: (index, 0, 0)), flat, flat],
        out_specs=[pl.BlockSpec((size, group, group), lambda i: (0, 0, 0)) for size in sizes],
        out_shape=[jax.ShapeDtypeStruct((size, group, group), jnp.bfloat16) for size in sizes],
        compiler_params=pltpu.CompilerParams(vmem_limit_bytes=SMALL_BYTES),
        cost_estimate=LIGHT,
        name="close_window",
    )(terms, ahead, back)


def rough_dot(left, right):
    return jnp.dot(left.astype(jnp.bfloat16), right.astype(jnp.bfloat16), preferred_element_type=jnp.float32)


def split_terms(value):
    high = value.astype(jnp.bfloat16)
    value = value - high.astype(jnp.float32)
    middle = value.astype(jnp.bfloat16)
    value = value - middle.astype(jnp.float32)
    return high, middle, value.astype(jnp.bfloat16)


def identity(size):
    rows = lax.broadcasted_iota(jnp.int32, (size, size), 0)
    cols = lax.broadcasted_iota(jnp.int32, (size, size), 1)
    return (rows == cols).astype(jnp.float32)


def eliminate(matrix_ref, right_ref, out_ref, work, block):
    size = matrix_ref.shape[0]
    work[...] = matrix_ref[...]
    out_ref[...] = right_ref[...]
    eye = identity(block)
    for start in range(0, size, block):
        here = slice(start, start + block)
        rest = slice(start + block, size)
        corner = work[here, here]
        norm = jnp.max(jnp.sum(jnp.abs(corner), axis=0))

        def unfinished(state):
            return jnp.logical_and(state[0] < 40, state[1] > 5e-5)

        def improve(state):
            step, _, inverse = state
            better = inverse + exact_dot(inverse, eye - exact_dot(work[here, here], inverse))
            left_over = eye - exact_dot(work[here, here], better)
            return step + 1, jnp.max(jnp.abs(left_over)), better

        found = lax.while_loop(unfinished, improve, (jnp.int32(0), jnp.float32(1.0), eye / norm))[2]
        found = found + exact_dot(found, eye - exact_dot(work[here, here], found))
        solved = exact_dot(found, out_ref[here, :])
        out_ref[here, :] = solved
        if start + block < size:
            across = exact_dot(found, work[here, rest])
            down = work[rest, here]
            work[rest, rest] = work[rest, rest] - exact_dot(down, across)
            out_ref[rest, :] = out_ref[rest, :] - exact_dot(down, solved)
            work[here, rest] = across
    for start in range(size - 2 * block, -1, -block):
        here = slice(start, start + block)
        rest = slice(start + block, size)
        out_ref[here, :] = out_ref[here, :] - exact_dot(work[here, rest], out_ref[rest, :])


def solve(place, pairs_count, mine, other, kept, came, after=()):
    group, width = mine.shape
    examples = 2 * kept.shape[0]
    size = kept.shape[0] // pairs_count

    def kernel(place_ref, mine_ref, other_ref, kept_ref, came_ref, *refs):
        out_ref, pairs_ref, matrix, right, power, inverse, first_ref = refs[len(after) :]
        for start in range(0, kept_ref.shape[0], size):
            near, far = kept_ref[start : start + size, :width], came_ref[start : start + size, :width]
            even = lax.rem(place_ref[0], 2) == 0
            first_ref[2 * start : 2 * start + size, :] = jnp.where(even, near, far)
            first_ref[2 * start + size : 2 * start + 2 * size, :] = jnp.where(even, far, near)
        eye = identity(width)
        t = place_ref[1]
        matrix[pl.ds(pl.multiple_of(t * group, group), group), :] = mine_ref[...]
        matrix[pl.ds(pl.multiple_of((1 - t) * group, group), group), :] = other_ref[...]
        turned = first_ref[...].T
        full = matrix[...] + jnp.dot(turned, first_ref[...], preferred_element_type=jnp.float32) + damping * eye
        diagonal = full * eye
        rows_scale = lax.rsqrt(jnp.sum(diagonal, axis=1, keepdims=True))
        cols_scale = lax.rsqrt(jnp.sum(diagonal, axis=0, keepdims=True))
        full = full * rows_scale * cols_scale
        matrix[...] = full
        right[...] = turned.astype(jnp.float32) * rows_scale

        sums = jnp.max(jnp.sum(jnp.abs(full), axis=0))
        squared = rough_dot(full, full)
        norm = jnp.sqrt(jnp.max(jnp.sum(jnp.abs(squared), axis=0)) + sums * sums / 128)
        start = eye - full / norm
        inverse[...] = eye + start
        power[...] = start.astype(jnp.bfloat16)
        for _ in range(7):
            raised = jnp.dot(power[...], power[...], preferred_element_type=jnp.float32).astype(jnp.bfloat16)
            power[...] = raised
            held = inverse[...]
            inverse[...] = held + jnp.dot(held.astype(jnp.bfloat16), raised, preferred_element_type=jnp.float32)
        power[...] = (inverse[...] / norm).astype(jnp.bfloat16)

        largest = jnp.max(jnp.abs(right[...]))
        out_ref[...] = jnp.dot(power[...], right[...].astype(jnp.bfloat16), preferred_element_type=jnp.float32)

        def unfinished(state):
            return jnp.logical_and(state[0] < 12, jnp.logical_not(state[1] <= 5e-5 * largest))

        def refine(state):
            left_over = right[...] - exact_dot(matrix[...], out_ref[...])
            change = jnp.dot(power[...], left_over.astype(jnp.bfloat16), preferred_element_type=jnp.float32)
            out_ref[...] = out_ref[...] + change
            return state[0] + 1, jnp.max(jnp.abs(left_over))

        worst = lax.while_loop(unfinished, refine, (jnp.int32(0), 1.0 + largest))[1]

        @pl.when(jnp.logical_not(worst <= 5e-5 * largest))
        def _():
            eliminate(matrix, right, out_ref, inverse, 128)

        solved = out_ref[...] * rows_scale
        out_ref[...] = solved
        pairs = jnp.zeros((examples, examples), jnp.float32)
        for term in split_terms(solved):
            pairs = pairs + jnp.dot(first_ref[...], term, preferred_element_type=jnp.float32)
        pairs_ref[...] = pairs

    whole = pl.BlockSpec(memory_space=pltpu.VMEM)
    return pl.pallas_call(
        kernel,
        in_specs=[pl.BlockSpec(memory_space=pltpu.SMEM)] + [whole] * 4 + [ANYWHERE] * len(after),
        out_shape=[
            jax.ShapeDtypeStruct((width, examples), jnp.float32),
            jax.ShapeDtypeStruct((examples, examples), jnp.float32),
        ],
        scratch_shapes=[
            pltpu.VMEM((width, width), jnp.float32),
            pltpu.VMEM((width, examples), jnp.float32),
            pltpu.VMEM((width, width), jnp.bfloat16),
            pltpu.VMEM((width, width), jnp.float32),
            pltpu.VMEM((examples, width), jnp.bfloat16),
        ],
        compiler_params=pltpu.CompilerParams(vmem_limit_bytes=VMEM_BYTES),
        cost_estimate=LIGHT,
        name="solve",
    )(place, mine, other, kept, came, *after)


def spread_back(place, stored, solved, owners, group, after=()):
    rows = stored.shape[0]
    width, examples = solved.shape
    pairs = owners // 2

    def kernel(place_ref, first_ref, solved_ref, *refs):
        cols, outs = refs[:owners], refs[owners + len(after) :]
        total = jnp.zeros((rows, examples), jnp.float32)
        for term in split_terms(solved_ref[...]):
            total = total + jnp.dot(first_ref[...], term, preferred_element_type=jnp.float32)
        terms = jnp.concatenate(split_terms(total.T)[:2], axis=0)
        for index in range(owners):
            product = jnp.dot(terms, cols[index][...], preferred_element_type=jnp.float32)
            outs[index // 2][index % 2] = (product[:examples] + product[examples:]).astype(jnp.bfloat16)

    def owner(index, ref):
        return 2 * lax.rem(ref[0] // 2 + index // 2, pairs) + index % 2

    return pl.pallas_call(
        kernel,
        grid_spec=pltpu.PrefetchScalarGridSpec(
            num_scalar_prefetch=1,
            grid=(1,),
            in_specs=[
                pl.BlockSpec((rows, width), lambda i, ref: (0, 0)),
                pl.BlockSpec((width, examples), lambda i, ref: (0, 0)),
            ]
            + [
                pl.BlockSpec((rows, group), lambda i, ref, index=index: (0, 2 * owner(index, ref) + ref[1]))
                for index in range(owners)
            ]
            + [ANYWHERE] * len(after),
            out_specs=[pl.BlockSpec((2, examples, group), lambda i, ref: (0, 0, 0))] * pairs,
        ),
        out_shape=[jax.ShapeDtypeStruct((2, examples, group), jnp.bfloat16)] * pairs,
        compiler_params=pltpu.CompilerParams(vmem_limit_bytes=VMEM_BYTES),
        cost_estimate=LIGHT,
        name="spread_back",
    )(place, stored, solved, *([stored] * owners), *after)


def pair_products(place, pairs, own_cols, first_pairs, mine, other, solved, after=()):
    examples, group = own_cols.shape
    size = examples // pairs

    def kernel(place_ref, own_ref, first_ref, mine_ref, other_ref, solved_ref, *refs):
        outs, whole = refs[len(after) : -1], refs[-1]
        g = 2 * place_ref[0] + place_ref[1]
        own = own_ref[...]
        damped = solved_ref[pl.ds(pl.multiple_of(place_ref[1] * group, group), group), :].T
        rest = own - lax.dot_general(
            first_ref[...], own, (((0,), (0,)), ((), ())), precision=EXACT, preferred_element_type=jnp.float32
        )
        rest = rest - mine_ref[...] - other_ref[...].astype(jnp.float32) - jnp.where(g < 2, damping * damped, 0.0)
        products = lax.dot_general(
            rest, rest, (((1,), (1,)), ((), ())), precision=EXACT, preferred_element_type=jnp.float32
        )
        whole[...] = products + jnp.where(g == 0, first_ref[...], 0.0)
        for index in range(pairs):
            start = lax.rem(place_ref[0] // 2 + index, pairs) * size
            outs[index][...] = whole[pl.ds(pl.multiple_of(start, size), size), :]

    vmem = pl.BlockSpec(memory_space=pltpu.VMEM)
    return pl.pallas_call(
        kernel,
        in_specs=[pl.BlockSpec(memory_space=pltpu.SMEM)] + [vmem] * 5 + [ANYWHERE] * len(after),
        out_specs=[vmem] * pairs,
        out_shape=[jax.ShapeDtypeStruct((size, examples), jnp.float32)] * pairs,
        scratch_shapes=[pltpu.VMEM((examples, examples), jnp.float32)],
        compiler_params=pltpu.CompilerParams(vmem_limit_bytes=SMALL_BYTES),
        cost_estimate=LIGHT,
        name="pair_products",
    )(place, own_cols, first_pairs, mine, other, solved, *after)


def assembly_tables(ring, slots, d, t):
    start = [0] * ring.count
    arrived = [0] * ring.count
    for offset, _, first in pairs_of(slots):
        start[offset % ring.count] = first
    place = len(slots)
    for offset in ring.offsets:
        start[-offset % ring.count] = place
        arrived[-offset % ring.count] = 1
        place += 2
    here = ring.position_of(d)
    early = here < ring.half

    def look_up(values, offset):
        found = jnp.zeros_like(offset)
        for index, value in enumerate(values):
            if value:
                found = jnp.where(offset == index, value, found)
        return found

    def offsets_of(chips):
        return lax.rem(ring.position_of(chips) - here + 2 * ring.count, ring.count)

    def fetch(offset, j):
        own = (j == t) == early
        quarter = jnp.where(own, start[ring.half], place)
        return jnp.where(offset == ring.half, quarter, look_up(start, offset) + j)

    chips = jnp.arange(ring.half, dtype=jnp.int32)
    j = jnp.arange(2, dtype=jnp.int32)[None, :]
    send = fetch(offsets_of((1 - t) * ring.half + chips)[:, None], j)
    offset = offsets_of(t * ring.half + chips)[:, None, None]
    r = jnp.arange(2, dtype=jnp.int32)[None, :, None]
    u = jnp.arange(2, dtype=jnp.int32)[None, None, :]
    by_columns = jnp.where(offset == ring.half, early.astype(jnp.int32), look_up(arrived, offset)) == 1
    j = jnp.where(by_columns, r, u)
    local = fetch(offset, j)
    other = 2 * chips[:, None, None] + j
    mine = (jnp.where(by_columns, u, r) == t).astype(jnp.int32)
    final = jnp.stack([local, other, mine]).reshape(-1)
    return send.reshape(-1).astype(jnp.int32), final.astype(jnp.int32)


def for_sibling(table, blocks, group):
    total = table.shape[0]
    wide = min(4, total)

    def kernel(table_ref, *refs):
        for k in range(wide):
            refs[-1][k] = refs[k][0]

    return pl.pallas_call(
        kernel,
        grid_spec=pltpu.PrefetchScalarGridSpec(
            num_scalar_prefetch=1,
            grid=(total // wide,),
            in_specs=[
                pl.BlockSpec((1, group, group), lambda c, ref, k=k: (ref[wide * c + k], 0, 0)) for k in range(wide)
            ],
            out_specs=pl.BlockSpec((wide, group, group), lambda c, ref: (c, 0, 0)),
        ),
        out_shape=jax.ShapeDtypeStruct((total, group, group), jnp.bfloat16),
        compiler_params=pltpu.CompilerParams(vmem_limit_bytes=SMALL_BYTES),
        cost_estimate=LIGHT,
        name="for_sibling",
    )(table, *([blocks] * wide))


def finish(place, table, blocks, other, half, group):
    wide = half // 2
    total = 4 * half

    def at(kind, r, c, k, u, ref):
        return ref[kind * total + 4 * (wide * c + k) + 2 * r + u]

    def spec(kind, k, u):
        return pl.BlockSpec((1, group, group), lambda r, c, ref, place: (at(kind, r, c, k, u, ref), 0, 0))

    order = [(k, u) for k in range(wide) for u in (0, 1)]

    def kernel(table_ref, place_ref, *refs):
        r, c = pl.program_id(0), pl.program_id(1)
        out_ref = refs[-1]
        shape = (group, group)
        gap = lax.broadcasted_iota(jnp.int32, shape, 1) - lax.broadcasted_iota(jnp.int32, shape, 0)
        for index, (k, u) in enumerate(order):
            cols = slice(index * group, (index + 1) * group)
            chip = place_ref[1] * half + wide * c + k
            apart = (2 * place_ref[0] + r - 2 * chip - u) * group
            added = jnp.where(gap == apart, jnp.float32(damping), jnp.float32(0.0))
            mine = at(2, r, c, k, u, table_ref) == 1

            @pl.when(mine)
            def _():
                out_ref[:, cols] = added + refs[index][0].astype(jnp.float32)

            @pl.when(jnp.logical_not(mine))
            def _():
                out_ref[:, cols] = added + refs[len(order) + index][0].astype(jnp.float32)

    return pl.pallas_call(
        kernel,
        grid_spec=pltpu.PrefetchScalarGridSpec(
            num_scalar_prefetch=2,
            grid=(2, 2),
            in_specs=[spec(0, k, u) for k, u in order] + [spec(1, k, u) for k, u in order],
            out_specs=pl.BlockSpec((group, 2 * wide * group), lambda r, c, ref, place: (r, c)),
        ),
        out_shape=jax.ShapeDtypeStruct((2 * group, 2 * half * group), jnp.float32),
        compiler_params=pltpu.CompilerParams(vmem_limit_bytes=SMALL_BYTES),
        cost_estimate=LIGHT,
        name="finish",
    )(table, place, *([blocks] * len(order)), *([other] * len(order)))


def in_order(index, mine, other, axis):
    return jnp.where(
        index == 0,
        jnp.concatenate([mine, other], axis=axis),
        jnp.concatenate([other, mine], axis=axis),
    )


def pair_swap(value, count):
    return lax.ppermute(value, "dp", [(index, index ^ 1) for index in range(count)])


def far_shift(value, step, count):
    return lax.ppermute(value, "dp", [(index, (index + 2 * step) % count) for index in range(count)])


def exchange_pairs(slice_of, pair, count):
    pairs = count // 2
    came = [slice_of(pair)]
    for step in range(1, pairs):
        came.append(far_shift(slice_of(lax.rem(pair + step, pairs)), step, count))
    return came


def natural(came, pair):
    pairs = len(came)
    pieces = []
    for index in range(pairs):
        behind = lax.rem(pair - index + pairs, pairs)
        piece = came[0]
        for step in range(1, pairs):
            piece = jnp.where(behind == step, came[step], piece)
        pieces.append(piece)
    return pieces


def scatter_pairs(value, pair, count):
    size = value.shape[0] // (count // 2)

    def slice_of(index):
        return lax.dynamic_slice_in_dim(value, index * size, size, 0)

    return sum(piece.astype(jnp.float32) for piece in exchange_pairs(slice_of, pair, count))


def local(ring, activations, out_grads, proj_in, proj_out, stored, counts, query_ids):
    owners = ring.count
    full = stored.shape[1]
    width = full // owners
    group = width // 2
    half = ring.half
    t = lax.axis_index("tensor")
    d = lax.axis_index("dp")
    pair, side = d // 2, lax.rem(d, 2)
    g = 2 * d + t
    place = jnp.stack([d, t]).astype(jnp.int32)

    pairs_count = owners // 2
    first_stored = stored[:, :width]
    corner_rows = lead_dot(lax.dynamic_slice_in_dim(first_stored, t * group, group, 1), first_stored)
    corner_payload = scatter_pairs(corner_rows, pair, owners)

    sides = jnp.concatenate(
        [
            jnp.dot(activations, proj_in, preferred_element_type=jnp.float32),
            jnp.dot(out_grads, proj_out, preferred_element_type=jnp.float32),
        ],
        axis=1,
    )
    sides = sides + lax.ppermute(sides, "tensor", SWAP)

    examples = counts.shape[0]
    all_examples = examples * owners
    rank = proj_in.shape[1]
    position = jnp.arange(SEQ, dtype=jnp.int32)[None, :]
    weights = jnp.where(
        position < counts[:, None], 1.0 / counts.astype(jnp.float32)[:, None], jnp.float32(0.0)
    )
    outer = jnp.einsum(
        "es,esi,esj->eij",
        weights,
        sides[:, :rank].reshape(examples, SEQ, rank),
        sides[:, rank:].reshape(examples, SEQ, rank),
        precision=EXACT,
    )
    vectors = outer.reshape(examples, full).astype(jnp.bfloat16)

    def columns_for(index):
        groups = [lax.dynamic_slice_in_dim(vectors, (4 * index + 2 * s + t) * group, group, 1) for s in (0, 1)]
        return jnp.concatenate([vectors[:, :width]] + groups, axis=1)

    payloads = [columns_for(lax.rem(pair + step, pairs_count)) for step in range(pairs_count)]

    split = (len(ring.offsets) + 1) // 2
    far_slots = [(half, None)]
    for offset in ring.offsets[:split]:
        far_slots += [(offset, 0), (offset, 1)]
    near_slots = []
    for offset in ring.offsets[split:] + [0]:
        near_slots += [(offset, 0), (offset, 1)]

    slots = far_slots + near_slots
    far_count, near_count = len(far_slots), len(near_slots)
    ahead, back = ring.shift(1), ring.shift(-1)

    def terms_of(steps, parts, after=()):
        return window_terms(ring, place, stored, vectors, group, steps, parts, after)

    came = [payloads[0]] + [far_shift(payloads[step], step, owners) for step in range(1, pairs_count)]
    came = jnp.concatenate(natural(came, pair), axis=0)
    second_group = jnp.concatenate([came[:, :width], came[:, width + group :]], axis=1)
    first_group = came[:, : width + group]
    kept = jnp.where(side == 0, first_group, second_group)
    away = jnp.where(side == 0, second_group, first_group)
    received = pair_swap(away, owners)
    far, near = terms_of([half], [far_slots, near_slots], [away, corner_payload])
    far, near = far[0], near[0]

    corner_rows = corner_payload + pair_swap(corner_payload, owners)
    second = terms_of([half - 1, 1 - half], [slots], [far])[0]
    corner_rows = [corner_rows] + [far_shift(corner_rows, step, owners) for step in range(1, pairs_count)]
    corner_rows = jnp.concatenate(natural(corner_rows, pair), axis=0)
    corner_other = lax.ppermute(corner_rows, "tensor", SWAP)
    shape = (pairs_count, 1, examples, group)
    own_cols = in_order(side, kept[:, width:].reshape(shape), received[:, width:].reshape(shape), 1)
    own_cols = own_cols.reshape(all_examples, group).astype(jnp.float32)
    far_ahead = lax.ppermute(far, "dp", ahead)
    near_back = lax.ppermute(near, "dp", back)
    last = [far_count, near_count] if half == 2 else [far_count + near_count]
    going = add_terms(second, 0, [(far_ahead, 0)], last, group, [corner_rows, received])
    coming = add_terms(second, 1, [(near_back, far_count)], last, group, [corner_rows, received])

    later_steps = [s for step in range(half - 2, 0, -1) for s in (step, -step)] + [0]
    later = terms_of(later_steps, [slots], [going[0], coming[0]])[0]
    solved, first_pairs = solve(place, pairs_count, corner_rows, corner_other, kept, received, [later])
    token = solved
    for step in range(half - 2, 0, -1):
        last = [far_count, near_count] if step == 1 else [far_count + near_count]
        going = [lax.ppermute(value, "dp", ahead) for value in going]
        coming = [lax.ppermute(value, "dp", back) for value in coming]
        index = later_steps.index(step)
        going = add_terms(later, index, [(going[0], 0)], last, group, [token])
        coming = add_terms(later, index + 1, [(coming[0], 0)], last, group, [token])
        if step == half - 2:
            pieces = spread_back(place, stored, solved, owners, group, [going[0], coming[0]])
            token = pieces[0]
    going = [lax.ppermute(value, "dp", ahead) for value in going]
    coming = [lax.ppermute(value, "dp", back) for value in coming]

    terms = pieces[0].astype(jnp.float32)
    for step in range(1, owners // 2):
        terms = terms + far_shift(pieces[step], step, owners).astype(jnp.float32)
    away = jnp.where(side == 0, terms[1], terms[0]).astype(jnp.bfloat16)
    terms = jnp.where(side == 0, terms[0], terms[1])
    terms_other = pair_swap(away, owners)

    far = close_window(later, 0, going[0], coming[0], far_slots, group)
    near = close_window(later, far_count, going[1], coming[1], near_slots, group)
    turned = {}
    for (found, slots) in ((far, far_slots), (near, near_slots)):
        chips = [chip for chip in pairs_of(slots) if chip[0] != 0]
        for (offset, _, _), block in zip(chips, found[1:]):
            turned[offset] = block
    shifted = {
        offset: lax.ppermute(turned[offset], "dp", ring.shift(offset))
        for offset in [half] + ring.offsets
    }
    came = [shifted[offset] for offset in ring.offsets + [half]]
    early = [shifted[offset] for offset in [half] + ring.offsets[:split]]
    pairs = pair_products(place, pairs_count, own_cols, first_pairs, terms, terms_other, solved, early)
    pairs = pairs[0] + sum(far_shift(pairs[step], step, owners) for step in range(1, pairs_count))
    away = lax.dynamic_slice_in_dim(pairs, (1 - side) * examples, examples, 0)
    pairs = lax.dynamic_slice_in_dim(pairs, side * examples, examples, 0) + pair_swap(away, owners)
    pairs = pairs + lax.ppermute(pairs, "tensor", SWAP)
    chosen = (query_ids[:, None] == jnp.arange(all_examples, dtype=jnp.int32)[None, :]).astype(jnp.float32)
    scores = lax.dot_general(chosen, pairs, (((1,), (1,)), ((), ())), precision=EXACT, preferred_element_type=jnp.float32) / R
    blocks = jnp.concatenate([far[0], near[0]] + came, axis=0)
    send_table, final_table = assembly_tables(ring, far_slots + near_slots, d, t)
    other = lax.ppermute(for_sibling(send_table, blocks, group), "tensor", SWAP)
    return finish(place, final_table, blocks, other, half, group), scores


def solution(mesh):
    placed = (
        P(("groups", "dp"), "tensor"),
        P(("groups", "dp"), "tensor"),
        P("tensor", None),
        P("tensor", None),
        P(("groups", "dp"), None),
        P(("groups", "dp")),
        P("groups"),
    )
    ring = Ring(mesh)

    def program(*args):
        return local(ring, *args)

    return jax.shard_map(
        program,
        mesh=mesh,
        in_specs=placed,
        out_specs=(P(("groups", "dp"), "tensor"), P("groups", "dp")),
        check_vma=False,
    )
```

```python
import jax
import jax.numpy as jnp
from jax import lax
from jax.experimental import pallas as pl
from jax.experimental.pallas import tpu as pltpu
from jax.sharding import PartitionSpec as P

R = 64
SEQ = 16
damping = 1.0
EXACT = lax.Precision.HIGHEST
SWAP = [(0, 1), (1, 0)]
VMEM_BYTES = 56 * 1024 * 1024
SMALL_BYTES = 12 * 1024 * 1024
LIGHT = pl.CostEstimate(flops=10**6, bytes_accessed=10**5, transcendentals=0)
ANYWHERE = pl.BlockSpec(memory_space=pl.ANY)
MAIN = pl.BlockSpec(memory_space=pltpu.HBM)
FAST = pl.BlockSpec(memory_space=pltpu.VMEM)


class Ring:
    def __init__(self, mesh):
        self.count = mesh.shape["dp"]
        self.half = self.count // 2
        coords = [getattr(device, "coords", None) for device in mesh.devices[0, :, 0]]
        self.folded = False
        if None not in coords:
            moving = [axis for axis in range(3) if len({place[axis] for place in coords}) > 1]
            fast = [axis for axis in moving if coords[0][axis] != coords[1][axis]]
            self.folded = len(moving) == 2 and len(fast) == 1 and len({place[fast[0]] for place in coords}) == 2
        reach = [0, 0]
        self.offsets = []
        for distance in range(self.half - 1, 0, -1):
            side = 0 if reach[0] <= reach[1] else 1
            reach[side] += distance
            self.offsets.append(distance if side == 0 else -distance)

    def index_at(self, position):
        if isinstance(position, int):
            position = position % self.count
            if not self.folded:
                return position
            return 2 * position if position < self.half else 2 * (self.count - 1 - position) + 1
        position = lax.rem(position + 2 * self.count, self.count)
        if not self.folded:
            return position
        return jnp.where(position < self.half, 2 * position, 2 * (self.count - 1 - position) + 1)

    def position_of(self, index):
        if not self.folded:
            return index
        return jnp.where(lax.rem(index, 2) == 0, index // 2, self.count - 1 - index // 2)

    def shift(self, step):
        return [(self.index_at(p), self.index_at(p + step)) for p in range(self.count)]


def lead_dot(left, right, precision=None):
    return lax.dot_general(
        left, right, (((0,), (0,)), ((), ())), precision=precision, preferred_element_type=jnp.float32
    )


def exact_dot(left, right):
    return jnp.dot(left, right, precision=EXACT, preferred_element_type=jnp.float32)


def pairs_of(slots):
    found = []
    for index, (offset, core) in enumerate(slots):
        if core is None:
            found.append((offset, 1, index))
        elif core == 0:
            found.append((offset, 2, index))
    return found


def window_terms(ring, place, stored, vectors, group, steps, parts, after=()):
    rows, full = stored.shape
    new_rows = vectors.shape[0]
    taps = jnp.array(steps, jnp.int32)
    blocks_in_all = sum(len(slots) for slots in parts)
    chunk = rows // 4

    def kernel(place_ref, step_ref, stored_ref, vectors_ref, *refs):
        outs, (held, total, arrived) = refs[len(after) : -3], refs[-3:]
        i = pl.program_id(0)
        owner = lax.rem(ring.position_of(place_ref[0]) + step_ref[i] + ring.count, ring.count)
        core = place_ref[1]

        def load(index):
            rows_of = pl.ds(index * chunk, chunk)
            return pltpu.make_async_copy(stored_ref.at[rows_of], held.at[rows_of], arrived.at[index])

        @pl.when(i == 0)
        def _():
            for index in range(4):
                load(index).start()

        left = pl.ds(pl.multiple_of((2 * ring.index_at(owner) + core) * group, group), group)
        chips, base = [], 0
        for part, slots in enumerate(parts):
            for offset, blocks, first in pairs_of(slots):
                column = 2 * ring.index_at(owner + offset)
                if blocks == 1:
                    column = column + jnp.where(owner < ring.half, core, 1 - core)
                right = pl.ds(pl.multiple_of(column * group, blocks * group), blocks * group)
                here = slice((base + first) * group, (base + first + blocks) * group)
                chips.append((part, right, here, slice(first * group, (first + blocks) * group)))
            base += len(slots)
        turned_new = vectors_ref[:, left].T

        @pl.when(i == 0)
        def _():
            for _, right, here, _ in chips:
                total[:, here] = jnp.dot(turned_new, vectors_ref[:, right], preferred_element_type=jnp.float32)
            for index in range(4):
                load(index).wait()
                rows_of = slice(index * chunk, (index + 1) * chunk)
                turned = held[rows_of, left].T
                for part, right, here, there in chips:
                    added = total[:, here] + jnp.dot(turned, held[rows_of, right], preferred_element_type=jnp.float32)
                    if index < 3:
                        total[:, here] = added
                    else:
                        outs[part][0, :, there] = added.astype(jnp.bfloat16)

        if len(steps) > 1:

            @pl.when(i > 0)
            def _():
                turned = held[:, left].T
                for part, right, _, there in chips:
                    added = jnp.dot(turned, held[:, right], preferred_element_type=jnp.float32)
                    added = added + jnp.dot(turned_new, vectors_ref[:, right], preferred_element_type=jnp.float32)
                    outs[part][0, :, there] = added.astype(jnp.bfloat16)

    def out(slots):
        return pl.BlockSpec((1, group, len(slots) * group), lambda i, a, b: (i, 0, 0))

    def shape(slots):
        return jax.ShapeDtypeStruct((len(steps), group, len(slots) * group), jnp.bfloat16)

    return pl.pallas_call(
        kernel,
        grid_spec=pltpu.PrefetchScalarGridSpec(
            num_scalar_prefetch=2,
            grid=(len(steps),),
            in_specs=[MAIN, pl.BlockSpec((new_rows, full), lambda i, a, b: (0, 0))] + [ANYWHERE] * len(after),
            out_specs=[out(slots) for slots in parts],
            scratch_shapes=[
                pltpu.VMEM((rows, full), jnp.bfloat16),
                pltpu.VMEM((group, blocks_in_all * group), jnp.float32),
                pltpu.SemaphoreType.DMA((4,)),
            ],
        ),
        out_shape=[shape(slots) for slots in parts],
        compiler_params=pltpu.CompilerParams(vmem_limit_bytes=VMEM_BYTES),
        cost_estimate=LIGHT,
        name="window_terms",
    )(place, taps, stored, vectors, *after)


def add_terms(terms, index, arrived, sizes, group, after=()):
    count = terms.shape[2] // group

    def kernel(terms_ref, *refs):
        outs, own, done = refs[len(arrived) + len(after) : -2], refs[-2], refs[-1]
        fetch = pltpu.make_async_copy(terms_ref.at[index], own, done)
        fetch.start()
        fetch.wait()
        for k in range(count):
            total = own[:, k * group : (k + 1) * group].astype(jnp.float32)
            for ref, (array, first) in zip(refs, arrived):
                if first <= k < first + array.shape[1] // group:
                    total = total + ref[:, (k - first) * group : (k - first + 1) * group].astype(jnp.float32)
            place, start = 0, 0
            while k - start >= sizes[place]:
                start += sizes[place]
                place += 1
            outs[place][:, (k - start) * group : (k - start + 1) * group] = total.astype(jnp.bfloat16)

    return pl.pallas_call(
        kernel,
        in_specs=[MAIN] + [FAST] * len(arrived) + [ANYWHERE] * len(after),
        out_specs=[FAST] * len(sizes),
        out_shape=[jax.ShapeDtypeStruct((group, size * group), jnp.bfloat16) for size in sizes],
        scratch_shapes=[pltpu.VMEM(terms.shape[1:], jnp.bfloat16), pltpu.SemaphoreType.DMA],
        compiler_params=pltpu.CompilerParams(vmem_limit_bytes=SMALL_BYTES),
        cost_estimate=LIGHT,
        name="add_terms",
    )(terms, *[array for array, _ in arrived], *after)


def close_window(terms, base, ahead, back, slots, group, after=()):
    count = len(slots)
    chips = [chip for chip in pairs_of(slots) if chip[0] != 0]
    index = terms.shape[0] - 1

    def kernel(terms_ref, ahead_ref, back_ref, *refs):
        blocks_ref, turned_refs, (own, done) = refs[len(after)], refs[len(after) + 1 : -2], refs[-2:]
        fetch = pltpu.make_async_copy(terms_ref.at[index], own, done)
        fetch.start()
        fetch.wait()
        for k in range(count):
            cols = slice(k * group, (k + 1) * group)
            total = own[:, (base + k) * group : (base + k + 1) * group].astype(jnp.float32)
            total = total + ahead_ref[:, cols].astype(jnp.float32) + back_ref[:, cols].astype(jnp.float32)
            total = total.astype(jnp.bfloat16)
            blocks_ref[k] = total
            for (_, blocks, first), turned_ref in zip(chips, turned_refs):
                if first <= k < first + blocks:
                    turned_ref[k - first] = total.T

    sizes = [count] + [blocks for _, blocks, _ in chips]
    return pl.pallas_call(
        kernel,
        in_specs=[MAIN, FAST, FAST] + [ANYWHERE] * len(after),
        out_specs=[FAST] * len(sizes),
        out_shape=[jax.ShapeDtypeStruct((size, group, group), jnp.bfloat16) for size in sizes],
        scratch_shapes=[pltpu.VMEM(terms.shape[1:], jnp.bfloat16), pltpu.SemaphoreType.DMA],
        compiler_params=pltpu.CompilerParams(vmem_limit_bytes=SMALL_BYTES),
        cost_estimate=LIGHT,
        name="close_window",
    )(terms, ahead, back, *after)


def rough_dot(left, right):
    return jnp.dot(left.astype(jnp.bfloat16), right.astype(jnp.bfloat16), preferred_element_type=jnp.float32)


def split_terms(value):
    high = value.astype(jnp.bfloat16)
    value = value - high.astype(jnp.float32)
    middle = value.astype(jnp.bfloat16)
    value = value - middle.astype(jnp.float32)
    return high, middle, value.astype(jnp.bfloat16)


def identity(size):
    rows = lax.broadcasted_iota(jnp.int32, (size, size), 0)
    cols = lax.broadcasted_iota(jnp.int32, (size, size), 1)
    return (rows == cols).astype(jnp.float32)


def eliminate(matrix_ref, right_ref, out_ref, work, block):
    size = matrix_ref.shape[0]
    work[...] = matrix_ref[...]
    out_ref[...] = right_ref[...]
    eye = identity(block)
    for start in range(0, size, block):
        here = slice(start, start + block)
        rest = slice(start + block, size)
        corner = work[here, here]
        norm = jnp.max(jnp.sum(jnp.abs(corner), axis=0))

        def unfinished(state):
            return jnp.logical_and(state[0] < 40, state[1] > 5e-5)

        def improve(state):
            step, _, inverse = state
            better = inverse + exact_dot(inverse, eye - exact_dot(work[here, here], inverse))
            left_over = eye - exact_dot(work[here, here], better)
            return step + 1, jnp.max(jnp.abs(left_over)), better

        found = lax.while_loop(unfinished, improve, (jnp.int32(0), jnp.float32(1.0), eye / norm))[2]
        found = found + exact_dot(found, eye - exact_dot(work[here, here], found))
        solved = exact_dot(found, out_ref[here, :])
        out_ref[here, :] = solved
        if start + block < size:
            across = exact_dot(found, work[here, rest])
            down = work[rest, here]
            work[rest, rest] = work[rest, rest] - exact_dot(down, across)
            out_ref[rest, :] = out_ref[rest, :] - exact_dot(down, solved)
            work[here, rest] = across
    for start in range(size - 2 * block, -1, -block):
        here = slice(start, start + block)
        rest = slice(start + block, size)
        out_ref[here, :] = out_ref[here, :] - exact_dot(work[here, rest], out_ref[rest, :])


def solve(place, pairs_count, mine, other, kept, came, after=()):
    group, width = mine.shape
    examples = 2 * kept.shape[0]
    size = kept.shape[0] // pairs_count

    def kernel(place_ref, mine_ref, other_ref, kept_ref, came_ref, *refs):
        out_ref, pairs_ref, matrix, right, power, inverse, first_ref = refs[len(after) :]
        for start in range(0, kept_ref.shape[0], size):
            near, far = kept_ref[start : start + size, :width], came_ref[start : start + size, :width]
            even = lax.rem(place_ref[0], 2) == 0
            first_ref[2 * start : 2 * start + size, :] = jnp.where(even, near, far)
            first_ref[2 * start + size : 2 * start + 2 * size, :] = jnp.where(even, far, near)
        eye = identity(width)
        t = place_ref[1]
        matrix[pl.ds(pl.multiple_of(t * group, group), group), :] = mine_ref[...]
        matrix[pl.ds(pl.multiple_of((1 - t) * group, group), group), :] = other_ref[...]
        turned = first_ref[...].T
        full = matrix[...] + jnp.dot(turned, first_ref[...], preferred_element_type=jnp.float32) + damping * eye
        diagonal = full * eye
        rows_scale = lax.rsqrt(jnp.sum(diagonal, axis=1, keepdims=True))
        cols_scale = lax.rsqrt(jnp.sum(diagonal, axis=0, keepdims=True))
        full = full * rows_scale * cols_scale
        matrix[...] = full
        right[...] = turned.astype(jnp.float32) * rows_scale

        sums = jnp.max(jnp.sum(jnp.abs(full), axis=0))
        squared = rough_dot(full, full)
        norm = jnp.sqrt(jnp.max(jnp.sum(jnp.abs(squared), axis=0)) + sums * sums / 128)
        start = eye - full / norm
        inverse[...] = eye + start
        power[...] = start.astype(jnp.bfloat16)
        for _ in range(7):
            raised = jnp.dot(power[...], power[...], preferred_element_type=jnp.float32).astype(jnp.bfloat16)
            power[...] = raised
            held = inverse[...]
            inverse[...] = held + jnp.dot(held.astype(jnp.bfloat16), raised, preferred_element_type=jnp.float32)
        power[...] = (inverse[...] / norm).astype(jnp.bfloat16)

        largest = jnp.max(jnp.abs(right[...]))
        out_ref[...] = jnp.dot(power[...], right[...].astype(jnp.bfloat16), preferred_element_type=jnp.float32)

        def unfinished(state):
            return jnp.logical_and(state[0] < 12, jnp.logical_not(state[1] <= 5e-5 * largest))

        def refine(state):
            left_over = right[...] - exact_dot(matrix[...], out_ref[...])
            change = jnp.dot(power[...], left_over.astype(jnp.bfloat16), preferred_element_type=jnp.float32)
            out_ref[...] = out_ref[...] + change
            return state[0] + 1, jnp.max(jnp.abs(left_over))

        worst = lax.while_loop(unfinished, refine, (jnp.int32(0), 1.0 + largest))[1]

        @pl.when(jnp.logical_not(worst <= 5e-5 * largest))
        def _():
            eliminate(matrix, right, out_ref, inverse, 128)

        solved = out_ref[...] * rows_scale
        out_ref[...] = solved
        pairs = jnp.zeros((examples, examples), jnp.float32)
        for term in split_terms(solved):
            pairs = pairs + jnp.dot(first_ref[...], term, preferred_element_type=jnp.float32)
        pairs_ref[...] = pairs

    whole = pl.BlockSpec(memory_space=pltpu.VMEM)
    return pl.pallas_call(
        kernel,
        in_specs=[pl.BlockSpec(memory_space=pltpu.SMEM)] + [whole] * 4 + [ANYWHERE] * len(after),
        out_shape=[
            jax.ShapeDtypeStruct((width, examples), jnp.float32),
            jax.ShapeDtypeStruct((examples, examples), jnp.float32),
        ],
        scratch_shapes=[
            pltpu.VMEM((width, width), jnp.float32),
            pltpu.VMEM((width, examples), jnp.float32),
            pltpu.VMEM((width, width), jnp.bfloat16),
            pltpu.VMEM((width, width), jnp.float32),
            pltpu.VMEM((examples, width), jnp.bfloat16),
        ],
        compiler_params=pltpu.CompilerParams(vmem_limit_bytes=VMEM_BYTES),
        cost_estimate=LIGHT,
        name="solve",
    )(place, mine, other, kept, came, *after)


def spread_back(place, stored, solved, owners, group, after=()):
    rows = stored.shape[0]
    width, examples = solved.shape
    pairs = owners // 2

    def kernel(place_ref, first_ref, solved_ref, *refs):
        cols, outs = refs[:owners], refs[owners + len(after) :]
        total = jnp.zeros((rows, examples), jnp.float32)
        for term in split_terms(solved_ref[...]):
            total = total + jnp.dot(first_ref[...], term, preferred_element_type=jnp.float32)
        terms = jnp.concatenate(split_terms(total.T)[:2], axis=0)
        for index in range(owners):
            product = jnp.dot(terms, cols[index][...], preferred_element_type=jnp.float32)
            outs[index // 2][index % 2] = (product[:examples] + product[examples:]).astype(jnp.bfloat16)

    def owner(index, ref):
        return 2 * lax.rem(ref[0] // 2 + index // 2, pairs) + index % 2

    return pl.pallas_call(
        kernel,
        grid_spec=pltpu.PrefetchScalarGridSpec(
            num_scalar_prefetch=1,
            grid=(1,),
            in_specs=[
                pl.BlockSpec((rows, width), lambda i, ref: (0, 0)),
                pl.BlockSpec((width, examples), lambda i, ref: (0, 0)),
            ]
            + [
                pl.BlockSpec((rows, group), lambda i, ref, index=index: (0, 2 * owner(index, ref) + ref[1]))
                for index in range(owners)
            ]
            + [ANYWHERE] * len(after),
            out_specs=[pl.BlockSpec((2, examples, group), lambda i, ref: (0, 0, 0))] * pairs,
        ),
        out_shape=[jax.ShapeDtypeStruct((2, examples, group), jnp.bfloat16)] * pairs,
        compiler_params=pltpu.CompilerParams(vmem_limit_bytes=VMEM_BYTES),
        cost_estimate=LIGHT,
        name="spread_back",
    )(place, stored, solved, *([stored] * owners), *after)


def sum_pieces(place, came, after=()):
    _, examples, group = came[0].shape

    def kernel(place_ref, *refs):
        mine_ref, away_ref = refs[-2:]
        side = lax.rem(place_ref[0], 2)
        totals = [sum(ref[half].astype(jnp.float32) for ref in refs[: len(came)]) for half in (0, 1)]
        mine_ref[...] = jnp.where(side == 0, totals[0], totals[1])
        away_ref[...] = jnp.where(side == 0, totals[1], totals[0]).astype(jnp.bfloat16)

    return pl.pallas_call(
        kernel,
        in_specs=[pl.BlockSpec(memory_space=pltpu.SMEM)] + [FAST] * len(came) + [ANYWHERE] * len(after),
        out_specs=[FAST, FAST],
        out_shape=[
            jax.ShapeDtypeStruct((examples, group), jnp.float32),
            jax.ShapeDtypeStruct((examples, group), jnp.bfloat16),
        ],
        compiler_params=pltpu.CompilerParams(vmem_limit_bytes=SMALL_BYTES),
        cost_estimate=LIGHT,
        name="sum_pieces",
    )(place, *came, *after)


def pair_products(place, pairs, own_cols, first_pairs, mine, other, solved, after=()):
    examples, group = own_cols.shape
    size = examples // pairs

    def kernel(place_ref, own_ref, first_ref, mine_ref, other_ref, solved_ref, *refs):
        outs, whole = refs[len(after) : -1], refs[-1]
        g = 2 * place_ref[0] + place_ref[1]
        own = own_ref[...]
        damped = solved_ref[pl.ds(pl.multiple_of(place_ref[1] * group, group), group), :].T
        rest = own - lax.dot_general(
            first_ref[...], own, (((0,), (0,)), ((), ())), precision=EXACT, preferred_element_type=jnp.float32
        )
        rest = rest - mine_ref[...] - other_ref[...].astype(jnp.float32) - jnp.where(g < 2, damping * damped, 0.0)
        products = lax.dot_general(
            rest, rest, (((1,), (1,)), ((), ())), precision=EXACT, preferred_element_type=jnp.float32
        )
        whole[...] = products + jnp.where(g == 0, first_ref[...], 0.0)
        for index in range(pairs):
            start = lax.rem(place_ref[0] // 2 + index, pairs) * size
            outs[index][...] = whole[pl.ds(pl.multiple_of(start, size), size), :]

    vmem = pl.BlockSpec(memory_space=pltpu.VMEM)
    return pl.pallas_call(
        kernel,
        in_specs=[pl.BlockSpec(memory_space=pltpu.SMEM)] + [vmem] * 5 + [ANYWHERE] * len(after),
        out_specs=[vmem] * pairs,
        out_shape=[jax.ShapeDtypeStruct((size, examples), jnp.float32)] * pairs,
        scratch_shapes=[pltpu.VMEM((examples, examples), jnp.float32)],
        compiler_params=pltpu.CompilerParams(vmem_limit_bytes=SMALL_BYTES),
        cost_estimate=LIGHT,
        name="pair_products",
    )(place, own_cols, first_pairs, mine, other, solved, *after)


def assembly_tables(ring, slots, d, t):
    start = [0] * ring.count
    arrived = [0] * ring.count
    for offset, _, first in pairs_of(slots):
        start[offset % ring.count] = first
    place = len(slots)
    for offset in ring.offsets:
        start[-offset % ring.count] = place
        arrived[-offset % ring.count] = 1
        place += 2
    here = ring.position_of(d)
    early = here < ring.half

    def look_up(values, offset):
        found = jnp.zeros_like(offset)
        for index, value in enumerate(values):
            if value:
                found = jnp.where(offset == index, value, found)
        return found

    def offsets_of(chips):
        return lax.rem(ring.position_of(chips) - here + 2 * ring.count, ring.count)

    def fetch(offset, j):
        own = (j == t) == early
        quarter = jnp.where(own, start[ring.half], place)
        return jnp.where(offset == ring.half, quarter, look_up(start, offset) + j)

    chips = jnp.arange(ring.half, dtype=jnp.int32)
    j = jnp.arange(2, dtype=jnp.int32)[None, :]
    send = fetch(offsets_of((1 - t) * ring.half + chips)[:, None], j)
    offset = offsets_of(t * ring.half + chips)[:, None, None]
    r = jnp.arange(2, dtype=jnp.int32)[None, :, None]
    u = jnp.arange(2, dtype=jnp.int32)[None, None, :]
    by_columns = jnp.where(offset == ring.half, early.astype(jnp.int32), look_up(arrived, offset)) == 1
    j = jnp.where(by_columns, r, u)
    local = fetch(offset, j)
    other = 2 * chips[:, None, None] + j
    mine = (jnp.where(by_columns, u, r) == t).astype(jnp.int32)
    final = jnp.stack([local, other, mine]).reshape(-1)
    return send.reshape(-1).astype(jnp.int32), final.astype(jnp.int32)


def for_sibling(table, blocks, group):
    total = table.shape[0]
    wide = min(4, total)

    def kernel(table_ref, *refs):
        for k in range(wide):
            refs[-1][k] = refs[k][0]

    return pl.pallas_call(
        kernel,
        grid_spec=pltpu.PrefetchScalarGridSpec(
            num_scalar_prefetch=1,
            grid=(total // wide,),
            in_specs=[
                pl.BlockSpec((1, group, group), lambda c, ref, k=k: (ref[wide * c + k], 0, 0)) for k in range(wide)
            ],
            out_specs=pl.BlockSpec((wide, group, group), lambda c, ref: (c, 0, 0)),
        ),
        out_shape=jax.ShapeDtypeStruct((total, group, group), jnp.bfloat16),
        compiler_params=pltpu.CompilerParams(vmem_limit_bytes=SMALL_BYTES),
        cost_estimate=LIGHT,
        name="for_sibling",
    )(table, *([blocks] * wide))


def finish(place, table, blocks, other, half, group):
    wide = half // 2
    total = 4 * half

    def at(kind, r, c, k, u, ref):
        return ref[kind * total + 4 * (wide * c + k) + 2 * r + u]

    def spec(kind, k, u):
        return pl.BlockSpec((1, group, group), lambda r, c, ref, place: (at(kind, r, c, k, u, ref), 0, 0))

    order = [(k, u) for k in range(wide) for u in (0, 1)]

    def kernel(table_ref, place_ref, *refs):
        r, c = pl.program_id(0), pl.program_id(1)
        out_ref = refs[-1]
        shape = (group, group)
        gap = lax.broadcasted_iota(jnp.int32, shape, 1) - lax.broadcasted_iota(jnp.int32, shape, 0)
        for index, (k, u) in enumerate(order):
            cols = slice(index * group, (index + 1) * group)
            chip = place_ref[1] * half + wide * c + k
            apart = (2 * place_ref[0] + r - 2 * chip - u) * group
            added = jnp.where(gap == apart, jnp.float32(damping), jnp.float32(0.0))
            mine = at(2, r, c, k, u, table_ref) == 1

            @pl.when(mine)
            def _():
                out_ref[:, cols] = added + refs[index][0].astype(jnp.float32)

            @pl.when(jnp.logical_not(mine))
            def _():
                out_ref[:, cols] = added + refs[len(order) + index][0].astype(jnp.float32)

    return pl.pallas_call(
        kernel,
        grid_spec=pltpu.PrefetchScalarGridSpec(
            num_scalar_prefetch=2,
            grid=(2, 2),
            in_specs=[spec(0, k, u) for k, u in order] + [spec(1, k, u) for k, u in order],
            out_specs=pl.BlockSpec((group, 2 * wide * group), lambda r, c, ref, place: (r, c)),
        ),
        out_shape=jax.ShapeDtypeStruct((2 * group, 2 * half * group), jnp.float32),
        compiler_params=pltpu.CompilerParams(vmem_limit_bytes=SMALL_BYTES),
        cost_estimate=LIGHT,
        name="finish",
    )(table, place, *([blocks] * len(order)), *([other] * len(order)))


def in_order(index, mine, other, axis):
    return jnp.where(
        index == 0,
        jnp.concatenate([mine, other], axis=axis),
        jnp.concatenate([other, mine], axis=axis),
    )


def pair_swap(value, count):
    return lax.ppermute(value, "dp", [(index, index ^ 1) for index in range(count)])


def far_shift(value, step, count):
    return lax.ppermute(value, "dp", [(index, (index + 2 * step) % count) for index in range(count)])


def exchange_pairs(slice_of, pair, count):
    pairs = count // 2
    came = [slice_of(pair)]
    for step in range(1, pairs):
        came.append(far_shift(slice_of(lax.rem(pair + step, pairs)), step, count))
    return came


def natural(came, pair):
    pairs = len(came)
    pieces = []
    for index in range(pairs):
        behind = lax.rem(pair - index + pairs, pairs)
        piece = came[0]
        for step in range(1, pairs):
            piece = jnp.where(behind == step, came[step], piece)
        pieces.append(piece)
    return pieces


def scatter_pairs(value, pair, count):
    size = value.shape[0] // (count // 2)

    def slice_of(index):
        return lax.dynamic_slice_in_dim(value, index * size, size, 0)

    return sum(piece.astype(jnp.float32) for piece in exchange_pairs(slice_of, pair, count))


def local(ring, activations, out_grads, proj_in, proj_out, stored, counts, query_ids):
    owners = ring.count
    full = stored.shape[1]
    width = full // owners
    group = width // 2
    half = ring.half
    t = lax.axis_index("tensor")
    d = lax.axis_index("dp")
    pair, side = d // 2, lax.rem(d, 2)
    g = 2 * d + t
    place = jnp.stack([d, t]).astype(jnp.int32)

    pairs_count = owners // 2
    first_stored = stored[:, :width]
    corner_rows = lead_dot(lax.dynamic_slice_in_dim(first_stored, t * group, group, 1), first_stored)
    corner_payload = scatter_pairs(corner_rows, pair, owners)

    sides = jnp.concatenate(
        [
            jnp.dot(activations, proj_in, preferred_element_type=jnp.float32),
            jnp.dot(out_grads, proj_out, preferred_element_type=jnp.float32),
        ],
        axis=1,
    )
    sides = sides + lax.ppermute(sides, "tensor", SWAP)

    examples = counts.shape[0]
    all_examples = examples * owners
    rank = proj_in.shape[1]
    position = jnp.arange(SEQ, dtype=jnp.int32)[None, :]
    weights = jnp.where(
        position < counts[:, None], 1.0 / counts.astype(jnp.float32)[:, None], jnp.float32(0.0)
    )
    outer = jnp.einsum(
        "es,esi,esj->eij",
        weights,
        sides[:, :rank].reshape(examples, SEQ, rank),
        sides[:, rank:].reshape(examples, SEQ, rank),
        precision=EXACT,
    )
    vectors = outer.reshape(examples, full).astype(jnp.bfloat16)

    def columns_for(index):
        groups = [lax.dynamic_slice_in_dim(vectors, (4 * index + 2 * s + t) * group, group, 1) for s in (0, 1)]
        return jnp.concatenate([vectors[:, :width]] + groups, axis=1)

    payloads = [columns_for(lax.rem(pair + step, pairs_count)) for step in range(pairs_count)]

    split = (len(ring.offsets) + 1) // 2
    far_slots = [(half, None)]
    for offset in ring.offsets[:split]:
        far_slots += [(offset, 0), (offset, 1)]
    near_slots = []
    for offset in ring.offsets[split:] + [0]:
        near_slots += [(offset, 0), (offset, 1)]

    slots = far_slots + near_slots
    far_count, near_count = len(far_slots), len(near_slots)
    ahead, back = ring.shift(1), ring.shift(-1)

    def terms_of(steps, parts, after=()):
        return window_terms(ring, place, stored, vectors, group, steps, parts, after)

    came = [payloads[0]] + [far_shift(payloads[step], step, owners) for step in range(1, pairs_count)]
    came = jnp.concatenate(natural(came, pair), axis=0)
    second_group = jnp.concatenate([came[:, :width], came[:, width + group :]], axis=1)
    first_group = came[:, : width + group]
    kept = jnp.where(side == 0, first_group, second_group)
    away = jnp.where(side == 0, second_group, first_group)
    received = pair_swap(away, owners)
    corner_rows = corner_payload + pair_swap(corner_payload, owners)
    corner_rows = [corner_rows] + [far_shift(corner_rows, step, owners) for step in range(1, pairs_count)]
    corner_rows = jnp.concatenate(natural(corner_rows, pair), axis=0)
    corner_other = lax.ppermute(corner_rows, "tensor", SWAP)
    far, near = terms_of([half], [far_slots, near_slots], [received, corner_rows])
    far, near = far[0], near[0]
    second = terms_of([half - 1, 1 - half], [slots], [far])[0]
    shape = (pairs_count, 1, examples, group)
    own_cols = in_order(side, kept[:, width:].reshape(shape), received[:, width:].reshape(shape), 1)
    own_cols = own_cols.reshape(all_examples, group).astype(jnp.float32)
    far_ahead = lax.ppermute(far, "dp", ahead)
    near_back = lax.ppermute(near, "dp", back)
    last = [far_count, near_count] if half == 2 else [far_count + near_count]
    going = add_terms(second, 0, [(far_ahead, 0)], last, group)
    coming = add_terms(second, 1, [(near_back, far_count)], last, group)

    third = terms_of([half - 2, 2 - half], [slots], [going[0], coming[0]])[0]
    solved, first_pairs = solve(place, pairs_count, corner_rows, corner_other, kept, received, [third])
    later_steps = [s for step in range(half - 3, 0, -1) for s in (step, -step)] + [0]
    for step in range(half - 2, 0, -1):
        last = [far_count, near_count] if step == 1 else [far_count + near_count]
        going = [lax.ppermute(value, "dp", ahead) for value in going]
        coming = [lax.ppermute(value, "dp", back) for value in coming]
        if step == half - 2:
            own, index, token = third, 0, [solved]
        else:
            own, index, token = later, later_steps.index(step), [terms_other]
        going = add_terms(own, index, [(going[0], 0)], last, group, token)
        coming = add_terms(own, index + 1, [(coming[0], 0)], last, group, token)
        if step == half - 2:
            pieces = spread_back(place, stored, solved, owners, group, [going[0], coming[0]])
            later = terms_of(later_steps, [slots], list(pieces))[0]
            came = [pieces[0]] + [far_shift(pieces[step], step, owners) for step in range(1, pairs_count)]
            terms, away = sum_pieces(place, came, [later])
            terms_other = pair_swap(away, owners)
    sent = [going[0], coming[0]]
    going = [lax.ppermute(value, "dp", ahead) for value in going]
    coming = [lax.ppermute(value, "dp", back) for value in coming]
    pairs = pair_products(place, pairs_count, own_cols, first_pairs, terms, terms_other, solved, sent)

    far = close_window(later, 0, going[0], coming[0], far_slots, group, [pairs[0]])
    near = close_window(later, far_count, going[1], coming[1], near_slots, group)
    turned = {}
    for (found, slots) in ((far, far_slots), (near, near_slots)):
        chips = [chip for chip in pairs_of(slots) if chip[0] != 0]
        for (offset, _, _), block in zip(chips, found[1:]):
            turned[offset] = block
    shifted = {
        offset: lax.ppermute(turned[offset], "dp", ring.shift(offset))
        for offset in [half] + ring.offsets
    }
    came = [shifted[offset] for offset in ring.offsets + [half]]
    pairs = pairs[0] + sum(far_shift(pairs[step], step, owners) for step in range(1, pairs_count))
    away = lax.dynamic_slice_in_dim(pairs, (1 - side) * examples, examples, 0)
    pairs = lax.dynamic_slice_in_dim(pairs, side * examples, examples, 0) + pair_swap(away, owners)
    pairs = pairs + lax.ppermute(pairs, "tensor", SWAP)
    chosen = (query_ids[:, None] == jnp.arange(all_examples, dtype=jnp.int32)[None, :]).astype(jnp.float32)
    scores = lax.dot_general(chosen, pairs, (((1,), (1,)), ((), ())), precision=EXACT, preferred_element_type=jnp.float32) / R
    blocks = jnp.concatenate([far[0], near[0]] + came, axis=0)
    send_table, final_table = assembly_tables(ring, far_slots + near_slots, d, t)
    other = lax.ppermute(for_sibling(send_table, blocks, group), "tensor", SWAP)
    return finish(place, final_table, blocks, other, half, group), scores


def solution(mesh):
    placed = (
        P(("groups", "dp"), "tensor"),
        P(("groups", "dp"), "tensor"),
        P("tensor", None),
        P("tensor", None),
        P(("groups", "dp"), None),
        P(("groups", "dp")),
        P("groups"),
    )
    ring = Ring(mesh)

    def program(*args):
        return local(ring, *args)

    return jax.shard_map(
        program,
        mesh=mesh,
        in_specs=placed,
        out_specs=(P(("groups", "dp"), "tensor"), P("groups", "dp")),
        check_vma=False,
    )
```

```python
import jax
import jax.numpy as jnp
from jax import lax
from jax.experimental import pallas as pl
from jax.experimental.pallas import tpu as pltpu
from jax.sharding import PartitionSpec as P

R = 64
SEQ = 16
damping = 1.0
EXACT = lax.Precision.HIGHEST
SWAP = [(0, 1), (1, 0)]
VMEM_BYTES = 56 * 1024 * 1024
SMALL_BYTES = 12 * 1024 * 1024
LIGHT = pl.CostEstimate(flops=10**6, bytes_accessed=10**5, transcendentals=0)
ANYWHERE = pl.BlockSpec(memory_space=pl.ANY)
MAIN = pl.BlockSpec(memory_space=pltpu.HBM)
FAST = pl.BlockSpec(memory_space=pltpu.VMEM)


class Ring:
    def __init__(self, mesh):
        self.count = mesh.shape["dp"]
        self.half = self.count // 2
        coords = [getattr(device, "coords", None) for device in mesh.devices[0, :, 0]]
        self.folded = False
        if None not in coords:
            moving = [axis for axis in range(3) if len({place[axis] for place in coords}) > 1]
            fast = [axis for axis in moving if coords[0][axis] != coords[1][axis]]
            self.folded = len(moving) == 2 and len(fast) == 1 and len({place[fast[0]] for place in coords}) == 2
        reach = [0, 0]
        self.offsets = []
        for distance in range(self.half - 1, 0, -1):
            side = 0 if reach[0] <= reach[1] else 1
            reach[side] += distance
            self.offsets.append(distance if side == 0 else -distance)

    def index_at(self, position):
        if isinstance(position, int):
            position = position % self.count
            if not self.folded:
                return position
            return 2 * position if position < self.half else 2 * (self.count - 1 - position) + 1
        position = lax.rem(position + 2 * self.count, self.count)
        if not self.folded:
            return position
        return jnp.where(position < self.half, 2 * position, 2 * (self.count - 1 - position) + 1)

    def position_of(self, index):
        if not self.folded:
            return index
        return jnp.where(lax.rem(index, 2) == 0, index // 2, self.count - 1 - index // 2)

    def shift(self, step):
        return [(self.index_at(p), self.index_at(p + step)) for p in range(self.count)]


def lead_dot(left, right, precision=None):
    return lax.dot_general(
        left, right, (((0,), (0,)), ((), ())), precision=precision, preferred_element_type=jnp.float32
    )


def exact_dot(left, right):
    return jnp.dot(left, right, precision=EXACT, preferred_element_type=jnp.float32)


def pairs_of(slots):
    found = []
    for index, (offset, core) in enumerate(slots):
        if core is None:
            found.append((offset, 1, index))
        elif core == 0:
            found.append((offset, 2, index))
    return found


def window_terms(ring, place, stored, vectors, group, steps, parts, after=()):
    rows, full = stored.shape
    new_rows = vectors.shape[0]
    taps = jnp.array(steps, jnp.int32)
    blocks_in_all = sum(len(slots) for slots in parts)
    chunk = rows // 4

    def kernel(place_ref, step_ref, stored_ref, vectors_ref, *refs):
        outs, (held, total, arrived) = refs[len(after) : -3], refs[-3:]
        i = pl.program_id(0)
        owner = lax.rem(ring.position_of(place_ref[0]) + step_ref[i] + ring.count, ring.count)
        core = place_ref[1]

        def load(index):
            rows_of = pl.ds(index * chunk, chunk)
            return pltpu.make_async_copy(stored_ref.at[rows_of], held.at[rows_of], arrived.at[index])

        @pl.when(i == 0)
        def _():
            for index in range(4):
                load(index).start()

        left = pl.ds(pl.multiple_of((2 * ring.index_at(owner) + core) * group, group), group)
        chips, base = [], 0
        for part, slots in enumerate(parts):
            for offset, blocks, first in pairs_of(slots):
                column = 2 * ring.index_at(owner + offset)
                if blocks == 1:
                    column = column + jnp.where(owner < ring.half, core, 1 - core)
                right = pl.ds(pl.multiple_of(column * group, blocks * group), blocks * group)
                here = slice((base + first) * group, (base + first + blocks) * group)
                chips.append((part, right, here, slice(first * group, (first + blocks) * group)))
            base += len(slots)
        turned_new = vectors_ref[:, left].T

        @pl.when(i == 0)
        def _():
            for _, right, here, _ in chips:
                total[:, here] = jnp.dot(turned_new, vectors_ref[:, right], preferred_element_type=jnp.float32)
            for index in range(4):
                load(index).wait()
                rows_of = slice(index * chunk, (index + 1) * chunk)
                turned = held[rows_of, left].T
                for part, right, here, there in chips:
                    added = total[:, here] + jnp.dot(turned, held[rows_of, right], preferred_element_type=jnp.float32)
                    if index < 3:
                        total[:, here] = added
                    else:
                        outs[part][0, :, there] = added.astype(jnp.bfloat16)

        if len(steps) > 1:

            @pl.when(i > 0)
            def _():
                turned = held[:, left].T
                for part, right, _, there in chips:
                    added = jnp.dot(turned, held[:, right], preferred_element_type=jnp.float32)
                    added = added + jnp.dot(turned_new, vectors_ref[:, right], preferred_element_type=jnp.float32)
                    outs[part][0, :, there] = added.astype(jnp.bfloat16)

    def out(slots):
        return pl.BlockSpec((1, group, len(slots) * group), lambda i, a, b: (i, 0, 0))

    def shape(slots):
        return jax.ShapeDtypeStruct((len(steps), group, len(slots) * group), jnp.bfloat16)

    return pl.pallas_call(
        kernel,
        grid_spec=pltpu.PrefetchScalarGridSpec(
            num_scalar_prefetch=2,
            grid=(len(steps),),
            in_specs=[MAIN, pl.BlockSpec((new_rows, full), lambda i, a, b: (0, 0))] + [ANYWHERE] * len(after),
            out_specs=[out(slots) for slots in parts],
            scratch_shapes=[
                pltpu.VMEM((rows, full), jnp.bfloat16),
                pltpu.VMEM((group, blocks_in_all * group), jnp.float32),
                pltpu.SemaphoreType.DMA((4,)),
            ],
        ),
        out_shape=[shape(slots) for slots in parts],
        compiler_params=pltpu.CompilerParams(vmem_limit_bytes=VMEM_BYTES),
        cost_estimate=LIGHT,
        name="window_terms",
    )(place, taps, stored, vectors, *after)


def add_terms(terms, index, arrived, base, count, group, after=()):
    def kernel(terms_ref, *refs):
        out_ref, own, done = refs[-3:]
        fetch = pltpu.make_async_copy(terms_ref.at[index, :, pl.ds(base * group, count * group)], own, done)
        fetch.start()
        fetch.wait()
        for k in range(count):
            cols = slice(k * group, (k + 1) * group)
            total = own[:, cols].astype(jnp.float32)
            for ref, (array, first) in zip(refs, arrived):
                place = base + k - first
                if 0 <= place < array.shape[1] // group:
                    total = total + ref[:, place * group : (place + 1) * group].astype(jnp.float32)
            out_ref[:, cols] = total.astype(jnp.bfloat16)

    return pl.pallas_call(
        kernel,
        in_specs=[MAIN] + [FAST] * len(arrived) + [ANYWHERE] * len(after),
        out_specs=FAST,
        out_shape=jax.ShapeDtypeStruct((group, count * group), jnp.bfloat16),
        scratch_shapes=[pltpu.VMEM((group, count * group), jnp.bfloat16), pltpu.SemaphoreType.DMA],
        compiler_params=pltpu.CompilerParams(vmem_limit_bytes=SMALL_BYTES),
        cost_estimate=LIGHT,
        name="add_terms",
    )(terms, *[array for array, _ in arrived], *after)


def gate(values, after):
    def kernel(*refs):
        pass

    return pl.pallas_call(
        kernel,
        in_specs=[MAIN] * len(values) + [ANYWHERE] * len(after),
        out_specs=[MAIN] * len(values),
        out_shape=[jax.ShapeDtypeStruct(value.shape, value.dtype) for value in values],
        input_output_aliases={index: index for index in range(len(values))},
        compiler_params=pltpu.CompilerParams(vmem_limit_bytes=SMALL_BYTES),
        cost_estimate=LIGHT,
        name="gate",
    )(*values, *after)


def close_window(terms, base, ahead, back, slots, group, after=()):
    count = len(slots)
    chips = [chip for chip in pairs_of(slots) if chip[0] != 0]
    index = terms.shape[0] - 1

    def kernel(terms_ref, ahead_ref, back_ref, *refs):
        blocks_ref, turned_refs, (own, done) = refs[len(after)], refs[len(after) + 1 : -2], refs[-2:]
        fetch = pltpu.make_async_copy(terms_ref.at[index], own, done)
        fetch.start()
        fetch.wait()
        for k in range(count):
            cols = slice(k * group, (k + 1) * group)
            total = own[:, (base + k) * group : (base + k + 1) * group].astype(jnp.float32)
            total = total + ahead_ref[:, cols].astype(jnp.float32) + back_ref[:, cols].astype(jnp.float32)
            total = total.astype(jnp.bfloat16)
            blocks_ref[k] = total
            for (_, blocks, first), turned_ref in zip(chips, turned_refs):
                if first <= k < first + blocks:
                    turned_ref[k - first] = total.T

    sizes = [count] + [blocks for _, blocks, _ in chips]
    return pl.pallas_call(
        kernel,
        in_specs=[MAIN, FAST, FAST] + [ANYWHERE] * len(after),
        out_specs=[FAST] * len(sizes),
        out_shape=[jax.ShapeDtypeStruct((size, group, group), jnp.bfloat16) for size in sizes],
        scratch_shapes=[pltpu.VMEM(terms.shape[1:], jnp.bfloat16), pltpu.SemaphoreType.DMA],
        compiler_params=pltpu.CompilerParams(vmem_limit_bytes=SMALL_BYTES),
        cost_estimate=LIGHT,
        name="close_window",
    )(terms, ahead, back, *after)


def rough_dot(left, right):
    return jnp.dot(left.astype(jnp.bfloat16), right.astype(jnp.bfloat16), preferred_element_type=jnp.float32)


def split_terms(value):
    high = value.astype(jnp.bfloat16)
    value = value - high.astype(jnp.float32)
    middle = value.astype(jnp.bfloat16)
    value = value - middle.astype(jnp.float32)
    return high, middle, value.astype(jnp.bfloat16)


def identity(size):
    rows = lax.broadcasted_iota(jnp.int32, (size, size), 0)
    cols = lax.broadcasted_iota(jnp.int32, (size, size), 1)
    return (rows == cols).astype(jnp.float32)


def eliminate(matrix_ref, right_ref, out_ref, work, block):
    size = matrix_ref.shape[0]
    work[...] = matrix_ref[...]
    out_ref[...] = right_ref[...]
    eye = identity(block)
    for start in range(0, size, block):
        here = slice(start, start + block)
        rest = slice(start + block, size)
        corner = work[here, here]
        norm = jnp.max(jnp.sum(jnp.abs(corner), axis=0))

        def unfinished(state):
            return jnp.logical_and(state[0] < 40, state[1] > 5e-5)

        def improve(state):
            step, _, inverse = state
            better = inverse + exact_dot(inverse, eye - exact_dot(work[here, here], inverse))
            left_over = eye - exact_dot(work[here, here], better)
            return step + 1, jnp.max(jnp.abs(left_over)), better

        found = lax.while_loop(unfinished, improve, (jnp.int32(0), jnp.float32(1.0), eye / norm))[2]
        found = found + exact_dot(found, eye - exact_dot(work[here, here], found))
        solved = exact_dot(found, out_ref[here, :])
        out_ref[here, :] = solved
        if start + block < size:
            across = exact_dot(found, work[here, rest])
            down = work[rest, here]
            work[rest, rest] = work[rest, rest] - exact_dot(down, across)
            out_ref[rest, :] = out_ref[rest, :] - exact_dot(down, solved)
            work[here, rest] = across
    for start in range(size - 2 * block, -1, -block):
        here = slice(start, start + block)
        rest = slice(start + block, size)
        out_ref[here, :] = out_ref[here, :] - exact_dot(work[here, rest], out_ref[rest, :])


def solve(place, pairs_count, mine, other, kept, came, after=()):
    group, width = mine.shape
    examples = 2 * kept.shape[0]
    size = kept.shape[0] // pairs_count

    def kernel(place_ref, mine_ref, other_ref, kept_ref, came_ref, *refs):
        out_ref, pairs_ref, matrix, right, power, inverse, first_ref = refs[len(after) :]
        for start in range(0, kept_ref.shape[0], size):
            near, far = kept_ref[start : start + size, :width], came_ref[start : start + size, :width]
            even = lax.rem(place_ref[0], 2) == 0
            first_ref[2 * start : 2 * start + size, :] = jnp.where(even, near, far)
            first_ref[2 * start + size : 2 * start + 2 * size, :] = jnp.where(even, far, near)
        eye = identity(width)
        t = place_ref[1]
        matrix[pl.ds(pl.multiple_of(t * group, group), group), :] = mine_ref[...]
        matrix[pl.ds(pl.multiple_of((1 - t) * group, group), group), :] = other_ref[...]
        turned = first_ref[...].T
        full = matrix[...] + jnp.dot(turned, first_ref[...], preferred_element_type=jnp.float32) + damping * eye
        diagonal = full * eye
        rows_scale = lax.rsqrt(jnp.sum(diagonal, axis=1, keepdims=True))
        cols_scale = lax.rsqrt(jnp.sum(diagonal, axis=0, keepdims=True))
        full = full * rows_scale * cols_scale
        matrix[...] = full
        right[...] = turned.astype(jnp.float32) * rows_scale

        sums = jnp.max(jnp.sum(jnp.abs(full), axis=0))
        squared = rough_dot(full, full)
        norm = jnp.sqrt(jnp.max(jnp.sum(jnp.abs(squared), axis=0)) + sums * sums / 128)
        start = eye - full / norm
        inverse[...] = eye + start
        power[...] = start.astype(jnp.bfloat16)
        for _ in range(7):
            raised = jnp.dot(power[...], power[...], preferred_element_type=jnp.float32).astype(jnp.bfloat16)
            power[...] = raised
            held = inverse[...]
            inverse[...] = held + jnp.dot(held.astype(jnp.bfloat16), raised, preferred_element_type=jnp.float32)
        power[...] = (inverse[...] / norm).astype(jnp.bfloat16)

        largest = jnp.max(jnp.abs(right[...]))
        out_ref[...] = jnp.dot(power[...], right[...].astype(jnp.bfloat16), preferred_element_type=jnp.float32)

        def unfinished(state):
            return jnp.logical_and(state[0] < 12, jnp.logical_not(state[1] <= 5e-5 * largest))

        def refine(state):
            left_over = right[...] - exact_dot(matrix[...], out_ref[...])
            change = jnp.dot(power[...], left_over.astype(jnp.bfloat16), preferred_element_type=jnp.float32)
            out_ref[...] = out_ref[...] + change
            return state[0] + 1, jnp.max(jnp.abs(left_over))

        worst = lax.while_loop(unfinished, refine, (jnp.int32(0), 1.0 + largest))[1]

        @pl.when(jnp.logical_not(worst <= 5e-5 * largest))
        def _():
            eliminate(matrix, right, out_ref, inverse, 128)

        solved = out_ref[...] * rows_scale
        out_ref[...] = solved
        pairs = jnp.zeros((examples, examples), jnp.float32)
        for term in split_terms(solved):
            pairs = pairs + jnp.dot(first_ref[...], term, preferred_element_type=jnp.float32)
        pairs_ref[...] = pairs

    whole = pl.BlockSpec(memory_space=pltpu.VMEM)
    return pl.pallas_call(
        kernel,
        in_specs=[pl.BlockSpec(memory_space=pltpu.SMEM)] + [whole] * 4 + [ANYWHERE] * len(after),
        out_shape=[
            jax.ShapeDtypeStruct((width, examples), jnp.float32),
            jax.ShapeDtypeStruct((examples, examples), jnp.float32),
        ],
        scratch_shapes=[
            pltpu.VMEM((width, width), jnp.float32),
            pltpu.VMEM((width, examples), jnp.float32),
            pltpu.VMEM((width, width), jnp.bfloat16),
            pltpu.VMEM((width, width), jnp.float32),
            pltpu.VMEM((examples, width), jnp.bfloat16),
        ],
        compiler_params=pltpu.CompilerParams(vmem_limit_bytes=VMEM_BYTES),
        cost_estimate=LIGHT,
        name="solve",
    )(place, mine, other, kept, came, *after)


def spread_back(place, stored, solved, owners, group, after=()):
    rows = stored.shape[0]
    width, examples = solved.shape
    pairs = owners // 2

    def kernel(place_ref, first_ref, solved_ref, *refs):
        cols, outs = refs[:owners], refs[owners + len(after) :]
        total = jnp.zeros((rows, examples), jnp.float32)
        for term in split_terms(solved_ref[...]):
            total = total + jnp.dot(first_ref[...], term, preferred_element_type=jnp.float32)
        terms = jnp.concatenate(split_terms(total.T)[:2], axis=0)
        for index in range(owners):
            product = jnp.dot(terms, cols[index][...], preferred_element_type=jnp.float32)
            outs[index // 2][index % 2] = (product[:examples] + product[examples:]).astype(jnp.bfloat16)

    def owner(index, ref):
        return 2 * lax.rem(ref[0] // 2 + index // 2, pairs) + index % 2

    return pl.pallas_call(
        kernel,
        grid_spec=pltpu.PrefetchScalarGridSpec(
            num_scalar_prefetch=1,
            grid=(1,),
            in_specs=[
                pl.BlockSpec((rows, width), lambda i, ref: (0, 0)),
                pl.BlockSpec((width, examples), lambda i, ref: (0, 0)),
            ]
            + [
                pl.BlockSpec((rows, group), lambda i, ref, index=index: (0, 2 * owner(index, ref) + ref[1]))
                for index in range(owners)
            ]
            + [ANYWHERE] * len(after),
            out_specs=[pl.BlockSpec((2, examples, group), lambda i, ref: (0, 0, 0))] * pairs,
        ),
        out_shape=[jax.ShapeDtypeStruct((2, examples, group), jnp.bfloat16)] * pairs,
        compiler_params=pltpu.CompilerParams(vmem_limit_bytes=VMEM_BYTES),
        cost_estimate=LIGHT,
        name="spread_back",
    )(place, stored, solved, *([stored] * owners), *after)


def sum_pieces(place, came, after=()):
    _, examples, group = came[0].shape

    def kernel(place_ref, *refs):
        mine_ref, away_ref = refs[-2:]
        side = lax.rem(place_ref[0], 2)
        totals = [sum(ref[half].astype(jnp.float32) for ref in refs[: len(came)]) for half in (0, 1)]
        mine_ref[...] = jnp.where(side == 0, totals[0], totals[1])
        away_ref[...] = jnp.where(side == 0, totals[1], totals[0]).astype(jnp.bfloat16)

    return pl.pallas_call(
        kernel,
        in_specs=[pl.BlockSpec(memory_space=pltpu.SMEM)] + [FAST] * len(came) + [ANYWHERE] * len(after),
        out_specs=[FAST, FAST],
        out_shape=[
            jax.ShapeDtypeStruct((examples, group), jnp.float32),
            jax.ShapeDtypeStruct((examples, group), jnp.bfloat16),
        ],
        compiler_params=pltpu.CompilerParams(vmem_limit_bytes=SMALL_BYTES),
        cost_estimate=LIGHT,
        name="sum_pieces",
    )(place, *came, *after)


def pair_products(place, own_cols, first_pairs, mine, other, solved, after=()):
    examples, group = own_cols.shape

    def kernel(place_ref, own_ref, first_ref, mine_ref, other_ref, solved_ref, *refs):
        g = 2 * place_ref[0] + place_ref[1]
        own = own_ref[...]
        damped = solved_ref[pl.ds(pl.multiple_of(place_ref[1] * group, group), group), :].T
        rest = own - lax.dot_general(
            first_ref[...], own, (((0,), (0,)), ((), ())), precision=EXACT, preferred_element_type=jnp.float32
        )
        rest = rest - mine_ref[...] - other_ref[...].astype(jnp.float32) - jnp.where(g < 2, damping * damped, 0.0)
        products = lax.dot_general(
            rest, rest, (((1,), (1,)), ((), ())), precision=EXACT, preferred_element_type=jnp.float32
        )
        refs[-1][...] = products + jnp.where(g == 0, first_ref[...], 0.0)

    return pl.pallas_call(
        kernel,
        in_specs=[pl.BlockSpec(memory_space=pltpu.SMEM)] + [FAST] * 5 + [ANYWHERE] * len(after),
        out_specs=FAST,
        out_shape=jax.ShapeDtypeStruct((examples, examples), jnp.float32),
        compiler_params=pltpu.CompilerParams(vmem_limit_bytes=SMALL_BYTES),
        cost_estimate=LIGHT,
        name="pair_products",
    )(place, own_cols, first_pairs, mine, other, solved, *after)


def assembly_tables(ring, slots, d, t):
    start = [0] * ring.count
    arrived = [0] * ring.count
    for offset, _, first in pairs_of(slots):
        start[offset % ring.count] = first
    place = len(slots)
    for offset in ring.offsets:
        start[-offset % ring.count] = place
        arrived[-offset % ring.count] = 1
        place += 2
    here = ring.position_of(d)
    early = here < ring.half

    def look_up(values, offset):
        found = jnp.zeros_like(offset)
        for index, value in enumerate(values):
            if value:
                found = jnp.where(offset == index, value, found)
        return found

    def offsets_of(chips):
        return lax.rem(ring.position_of(chips) - here + 2 * ring.count, ring.count)

    def fetch(offset, j):
        own = (j == t) == early
        quarter = jnp.where(own, start[ring.half], place)
        return jnp.where(offset == ring.half, quarter, look_up(start, offset) + j)

    chips = jnp.arange(ring.half, dtype=jnp.int32)
    j = jnp.arange(2, dtype=jnp.int32)[None, :]
    send = fetch(offsets_of((1 - t) * ring.half + chips)[:, None], j)
    offset = offsets_of(t * ring.half + chips)[:, None, None]
    r = jnp.arange(2, dtype=jnp.int32)[None, :, None]
    u = jnp.arange(2, dtype=jnp.int32)[None, None, :]
    by_columns = jnp.where(offset == ring.half, early.astype(jnp.int32), look_up(arrived, offset)) == 1
    j = jnp.where(by_columns, r, u)
    local = fetch(offset, j)
    other = 2 * chips[:, None, None] + j
    mine = (jnp.where(by_columns, u, r) == t).astype(jnp.int32)
    final = jnp.stack([local, other, mine]).reshape(-1)
    return send.reshape(-1).astype(jnp.int32), final.astype(jnp.int32)


def for_sibling(table, blocks, group):
    total = table.shape[0]
    wide = min(4, total)

    def kernel(table_ref, *refs):
        for k in range(wide):
            refs[-1][k] = refs[k][0]

    return pl.pallas_call(
        kernel,
        grid_spec=pltpu.PrefetchScalarGridSpec(
            num_scalar_prefetch=1,
            grid=(total // wide,),
            in_specs=[
                pl.BlockSpec((1, group, group), lambda c, ref, k=k: (ref[wide * c + k], 0, 0)) for k in range(wide)
            ],
            out_specs=pl.BlockSpec((wide, group, group), lambda c, ref: (c, 0, 0)),
        ),
        out_shape=jax.ShapeDtypeStruct((total, group, group), jnp.bfloat16),
        compiler_params=pltpu.CompilerParams(vmem_limit_bytes=SMALL_BYTES),
        cost_estimate=LIGHT,
        name="for_sibling",
    )(table, *([blocks] * wide))


def finish(place, table, blocks, other, half, group):
    wide = half // 2
    total = 4 * half

    def at(kind, r, c, k, u, ref):
        return ref[kind * total + 4 * (wide * c + k) + 2 * r + u]

    def spec(kind, k, u):
        return pl.BlockSpec((1, group, group), lambda r, c, ref, place: (at(kind, r, c, k, u, ref), 0, 0))

    order = [(k, u) for k in range(wide) for u in (0, 1)]

    def kernel(table_ref, place_ref, *refs):
        r, c = pl.program_id(0), pl.program_id(1)
        out_ref = refs[-1]
        shape = (group, group)
        gap = lax.broadcasted_iota(jnp.int32, shape, 1) - lax.broadcasted_iota(jnp.int32, shape, 0)
        for index, (k, u) in enumerate(order):
            cols = slice(index * group, (index + 1) * group)
            chip = place_ref[1] * half + wide * c + k
            apart = (2 * place_ref[0] + r - 2 * chip - u) * group
            added = jnp.where(gap == apart, jnp.float32(damping), jnp.float32(0.0))
            mine = at(2, r, c, k, u, table_ref) == 1

            @pl.when(mine)
            def _():
                out_ref[:, cols] = added + refs[index][0].astype(jnp.float32)

            @pl.when(jnp.logical_not(mine))
            def _():
                out_ref[:, cols] = added + refs[len(order) + index][0].astype(jnp.float32)

    return pl.pallas_call(
        kernel,
        grid_spec=pltpu.PrefetchScalarGridSpec(
            num_scalar_prefetch=2,
            grid=(2, 2),
            in_specs=[spec(0, k, u) for k, u in order] + [spec(1, k, u) for k, u in order],
            out_specs=pl.BlockSpec((group, 2 * wide * group), lambda r, c, ref, place: (r, c)),
        ),
        out_shape=jax.ShapeDtypeStruct((2 * group, 2 * half * group), jnp.float32),
        compiler_params=pltpu.CompilerParams(vmem_limit_bytes=SMALL_BYTES),
        cost_estimate=LIGHT,
        name="finish",
    )(table, place, *([blocks] * len(order)), *([other] * len(order)))


def in_order(index, mine, other, axis):
    return jnp.where(
        index == 0,
        jnp.concatenate([mine, other], axis=axis),
        jnp.concatenate([other, mine], axis=axis),
    )


def pair_swap(value, count):
    return lax.ppermute(value, "dp", [(index, index ^ 1) for index in range(count)])


def far_shift(value, step, count):
    return lax.ppermute(value, "dp", [(index, (index + 2 * step) % count) for index in range(count)])


def exchange_pairs(slice_of, pair, count):
    pairs = count // 2
    came = [slice_of(pair)]
    for step in range(1, pairs):
        came.append(far_shift(slice_of(lax.rem(pair + step, pairs)), step, count))
    return came


def natural(came, pair):
    pairs = len(came)
    pieces = []
    for index in range(pairs):
        behind = lax.rem(pair - index + pairs, pairs)
        piece = came[0]
        for step in range(1, pairs):
            piece = jnp.where(behind == step, came[step], piece)
        pieces.append(piece)
    return pieces


def scatter_pairs(value, pair, count):
    size = value.shape[0] // (count // 2)

    def slice_of(index):
        return lax.dynamic_slice_in_dim(value, index * size, size, 0)

    return sum(piece.astype(jnp.float32) for piece in exchange_pairs(slice_of, pair, count))


def local(ring, activations, out_grads, proj_in, proj_out, stored, counts, query_ids):
    owners = ring.count
    full = stored.shape[1]
    width = full // owners
    group = width // 2
    half = ring.half
    t = lax.axis_index("tensor")
    d = lax.axis_index("dp")
    pair, side = d // 2, lax.rem(d, 2)
    g = 2 * d + t
    place = jnp.stack([d, t]).astype(jnp.int32)

    pairs_count = owners // 2
    first_stored = stored[:, :width]
    corner_rows = lead_dot(lax.dynamic_slice_in_dim(first_stored, t * group, group, 1), first_stored)
    corner_payload = scatter_pairs(corner_rows, pair, owners)

    sides = jnp.concatenate(
        [
            jnp.dot(activations, proj_in, preferred_element_type=jnp.float32),
            jnp.dot(out_grads, proj_out, preferred_element_type=jnp.float32),
        ],
        axis=1,
    )
    sides = sides + lax.ppermute(sides, "tensor", SWAP)

    examples = counts.shape[0]
    all_examples = examples * owners
    rank = proj_in.shape[1]
    position = jnp.arange(SEQ, dtype=jnp.int32)[None, :]
    weights = jnp.where(
        position < counts[:, None], 1.0 / counts.astype(jnp.float32)[:, None], jnp.float32(0.0)
    )
    outer = jnp.einsum(
        "es,esi,esj->eij",
        weights,
        sides[:, :rank].reshape(examples, SEQ, rank),
        sides[:, rank:].reshape(examples, SEQ, rank),
        precision=EXACT,
    )
    vectors = outer.reshape(examples, full).astype(jnp.bfloat16)

    def columns_for(index):
        groups = [lax.dynamic_slice_in_dim(vectors, (4 * index + 2 * s + t) * group, group, 1) for s in (0, 1)]
        return jnp.concatenate([vectors[:, :width]] + groups, axis=1)

    payloads = [columns_for(lax.rem(pair + step, pairs_count)) for step in range(pairs_count)]

    split = (len(ring.offsets) + 1) // 2
    far_slots = [(half, None)]
    for offset in ring.offsets[:split]:
        far_slots += [(offset, 0), (offset, 1)]
    near_slots = []
    for offset in ring.offsets[split:] + [0]:
        near_slots += [(offset, 0), (offset, 1)]

    slots = far_slots + near_slots
    far_count, near_count = len(far_slots), len(near_slots)
    ahead, back = ring.shift(1), ring.shift(-1)

    def terms_of(steps, parts, after=()):
        return window_terms(ring, place, stored, vectors, group, steps, parts, after)

    came = [payloads[0]] + [far_shift(payloads[step], step, owners) for step in range(1, pairs_count)]
    came = jnp.concatenate(natural(came, pair), axis=0)
    second_group = jnp.concatenate([came[:, :width], came[:, width + group :]], axis=1)
    first_group = came[:, : width + group]
    kept = jnp.where(side == 0, first_group, second_group)
    away = jnp.where(side == 0, second_group, first_group)
    received = pair_swap(away, owners)
    corner_second = corner_payload + pair_swap(corner_payload, owners)
    corner_rows = [corner_second] + [far_shift(corner_second, step, owners) for step in range(1, pairs_count)]
    corner_rows = jnp.concatenate(natural(corner_rows, pair), axis=0)
    corner_other = lax.ppermute(corner_rows, "tensor", SWAP)
    far, near = terms_of([half], [far_slots, near_slots], [away, corner_second])
    far, near = far[0], near[0]
    second_steps = [half - 1, 1 - half, half - 2, 2 - half]
    far, near = gate([far, near], [corner_rows, received])
    second = terms_of(second_steps, [slots], [far])[0]
    shape = (pairs_count, 1, examples, group)
    own_cols = in_order(side, kept[:, width:].reshape(shape), received[:, width:].reshape(shape), 1)
    own_cols = own_cols.reshape(all_examples, group).astype(jnp.float32)
    far_ahead = lax.ppermute(far, "dp", ahead)
    near_back = lax.ppermute(near, "dp", back)
    total = far_count + near_count
    going = add_terms(second, 0, [(far_ahead, 0)], 0, total, group)
    coming = add_terms(second, 1, [(near_back, far_count)], 0, total, group)

    solved, first_pairs = solve(place, pairs_count, corner_rows, corner_other, kept, received, [going, coming])
    pieces = spread_back(place, stored, solved, owners, group)
    later_steps = [s for step in range(half - 3, 0, -1) for s in (step, -step)] + [0]
    for step in range(half - 2, 0, -1):
        came_ahead = lax.ppermute(going, "dp", ahead)
        came_back = lax.ppermute(coming, "dp", back)
        own, index, token = (second, 2, [pieces[0]]) if step == half - 2 else (later, later_steps.index(step), [])
        if step == 1:
            far_going = add_terms(own, index, [(came_ahead, 0)], 0, far_count, group, token)
            far_coming = add_terms(own, index + 1, [(came_back, 0)], 0, far_count, group, token)
            token = [far_going, far_coming]
            near_going = add_terms(own, index, [(came_ahead, 0)], far_count, near_count, group, token)
            near_coming = add_terms(own, index + 1, [(came_back, 0)], far_count, near_count, group, token)
            token = [near_going, near_coming]
        else:
            going = add_terms(own, index, [(came_ahead, 0)], 0, total, group, token)
            coming = add_terms(own, index + 1, [(came_back, 0)], 0, total, group, token)
            token = [going, coming]
        if step == half - 2:
            came = [pieces[0]] + [far_shift(pieces[index], index, owners) for index in range(1, pairs_count)]
            terms, away = sum_pieces(place, came)
            terms_other = pair_swap(away, owners)
            going, coming = gate([going, coming], [away])
            later = terms_of(later_steps, [slots], [going])[0]
    far_sums = [lax.ppermute(far_going, "dp", ahead), lax.ppermute(far_coming, "dp", back)]
    near_sums = [lax.ppermute(near_going, "dp", ahead), lax.ppermute(near_coming, "dp", back)]

    far = close_window(later, 0, *far_sums, far_slots, group)
    near = close_window(later, far_count, *near_sums, near_slots, group, [far[0]])
    turned = {}
    for (found, slots) in ((far, far_slots), (near, near_slots)):
        chips = [chip for chip in pairs_of(slots) if chip[0] != 0]
        for (offset, _, _), block in zip(chips, found[1:]):
            turned[offset] = block
    shifted = {
        offset: lax.ppermute(turned[offset], "dp", ring.shift(offset))
        for offset in [half] + ring.offsets
    }
    came = [shifted[offset] for offset in ring.offsets + [half]]
    early = [shifted[offset] for offset in [half] + ring.offsets[:split]]
    pairs = pair_products(place, own_cols, first_pairs, terms, terms_other, solved, early)
    bit = owners // 2
    while bit >= 1:
        kept_rows = jnp.where((d & bit) == 0, pairs[: pairs.shape[0] // 2], pairs[pairs.shape[0] // 2 :])
        sent_rows = jnp.where((d & bit) == 0, pairs[pairs.shape[0] // 2 :], pairs[: pairs.shape[0] // 2])
        pairs = kept_rows + lax.ppermute(sent_rows, "dp", [(index, index ^ bit) for index in range(owners)])
        bit //= 2
    pairs = pairs + lax.ppermute(pairs, "tensor", SWAP)
    chosen = (query_ids[:, None] == jnp.arange(all_examples, dtype=jnp.int32)[None, :]).astype(jnp.float32)
    scores = lax.dot_general(chosen, pairs, (((1,), (1,)), ((), ())), precision=EXACT, preferred_element_type=jnp.float32) / R
    blocks = jnp.concatenate([far[0], near[0]] + came, axis=0)
    send_table, final_table = assembly_tables(ring, far_slots + near_slots, d, t)
    other = lax.ppermute(for_sibling(send_table, blocks, group), "tensor", SWAP)
    return finish(place, final_table, blocks, other, half, group), scores


def solution(mesh):
    placed = (
        P(("groups", "dp"), "tensor"),
        P(("groups", "dp"), "tensor"),
        P("tensor", None),
        P("tensor", None),
        P(("groups", "dp"), None),
        P(("groups", "dp")),
        P("groups"),
    )
    ring = Ring(mesh)

    def program(*args):
        return local(ring, *args)

    return jax.shard_map(
        program,
        mesh=mesh,
        in_specs=placed,
        out_specs=(P(("groups", "dp"), "tensor"), P("groups", "dp")),
        check_vma=False,
    )
```

```python
import jax
import jax.numpy as jnp
from jax import lax
from jax.experimental import pallas as pl
from jax.experimental.pallas import tpu as pltpu
from jax.sharding import PartitionSpec as P

R = 64
SEQ = 16
damping = 1.0
EXACT = lax.Precision.HIGHEST
SWAP = [(0, 1), (1, 0)]
VMEM_BYTES = 56 * 1024 * 1024
SMALL_BYTES = 12 * 1024 * 1024
LIGHT = pl.CostEstimate(flops=10**6, bytes_accessed=10**5, transcendentals=0)
ANYWHERE = pl.BlockSpec(memory_space=pl.ANY)
MAIN = pl.BlockSpec(memory_space=pltpu.HBM)
FAST = pl.BlockSpec(memory_space=pltpu.VMEM)


class Ring:
    def __init__(self, mesh):
        self.count = mesh.shape["dp"]
        self.half = self.count // 2
        coords = [getattr(device, "coords", None) for device in mesh.devices[0, :, 0]]
        self.folded = False
        if None not in coords:
            moving = [axis for axis in range(3) if len({place[axis] for place in coords}) > 1]
            fast = [axis for axis in moving if coords[0][axis] != coords[1][axis]]
            self.folded = len(moving) == 2 and len(fast) == 1 and len({place[fast[0]] for place in coords}) == 2
        reach = [0, 0]
        self.offsets = []
        for distance in range(self.half - 1, 0, -1):
            side = 0 if reach[0] <= reach[1] else 1
            reach[side] += distance
            self.offsets.append(distance if side == 0 else -distance)

    def index_at(self, position):
        if isinstance(position, int):
            position = position % self.count
            if not self.folded:
                return position
            return 2 * position if position < self.half else 2 * (self.count - 1 - position) + 1
        position = lax.rem(position + 2 * self.count, self.count)
        if not self.folded:
            return position
        return jnp.where(position < self.half, 2 * position, 2 * (self.count - 1 - position) + 1)

    def position_of(self, index):
        if not self.folded:
            return index
        return jnp.where(lax.rem(index, 2) == 0, index // 2, self.count - 1 - index // 2)

    def shift(self, step):
        return [(self.index_at(p), self.index_at(p + step)) for p in range(self.count)]


def lead_dot(left, right, precision=None):
    return lax.dot_general(
        left, right, (((0,), (0,)), ((), ())), precision=precision, preferred_element_type=jnp.float32
    )


def exact_dot(left, right):
    return jnp.dot(left, right, precision=EXACT, preferred_element_type=jnp.float32)


def pairs_of(slots):
    found = []
    for index, (offset, core) in enumerate(slots):
        if core is None:
            found.append((offset, 1, index))
        elif core == 0:
            found.append((offset, 2, index))
    return found


def window_terms(ring, place, stored, vectors, group, steps, parts, after=()):
    rows, full = stored.shape
    new_rows = vectors.shape[0]
    taps = jnp.array(steps, jnp.int32)
    blocks_in_all = sum(len(slots) for slots in parts)
    chunk = rows // 4

    def kernel(place_ref, step_ref, stored_ref, vectors_ref, *refs):
        outs, (held, total, arrived) = refs[len(after) : -3], refs[-3:]
        i = pl.program_id(0)
        owner = lax.rem(ring.position_of(place_ref[0]) + step_ref[i] + ring.count, ring.count)
        core = place_ref[1]

        def load(index):
            rows_of = pl.ds(index * chunk, chunk)
            return pltpu.make_async_copy(stored_ref.at[rows_of], held.at[rows_of], arrived.at[index])

        @pl.when(i == 0)
        def _():
            for index in range(4):
                load(index).start()

        left = pl.ds(pl.multiple_of((2 * ring.index_at(owner) + core) * group, group), group)
        chips, base = [], 0
        for part, slots in enumerate(parts):
            for offset, blocks, first in pairs_of(slots):
                column = 2 * ring.index_at(owner + offset)
                if blocks == 1:
                    column = column + jnp.where(owner < ring.half, core, 1 - core)
                right = pl.ds(pl.multiple_of(column * group, blocks * group), blocks * group)
                here = slice((base + first) * group, (base + first + blocks) * group)
                chips.append((part, right, here, slice(first * group, (first + blocks) * group)))
            base += len(slots)
        turned_new = vectors_ref[:, left].T

        @pl.when(i == 0)
        def _():
            for _, right, here, _ in chips:
                total[:, here] = jnp.dot(turned_new, vectors_ref[:, right], preferred_element_type=jnp.float32)
            for index in range(4):
                load(index).wait()
                rows_of = slice(index * chunk, (index + 1) * chunk)
                turned = held[rows_of, left].T
                for part, right, here, there in chips:
                    added = total[:, here] + jnp.dot(turned, held[rows_of, right], preferred_element_type=jnp.float32)
                    if index < 3:
                        total[:, here] = added
                    else:
                        outs[part][0, :, there] = added.astype(jnp.bfloat16)

        if len(steps) > 1:

            @pl.when(i > 0)
            def _():
                turned = held[:, left].T
                for part, right, _, there in chips:
                    added = jnp.dot(turned, held[:, right], preferred_element_type=jnp.float32)
                    added = added + jnp.dot(turned_new, vectors_ref[:, right], preferred_element_type=jnp.float32)
                    outs[part][0, :, there] = added.astype(jnp.bfloat16)

    def out(slots):
        return pl.BlockSpec((1, group, len(slots) * group), lambda i, a, b: (i, 0, 0))

    def shape(slots):
        return jax.ShapeDtypeStruct((len(steps), group, len(slots) * group), jnp.bfloat16)

    return pl.pallas_call(
        kernel,
        grid_spec=pltpu.PrefetchScalarGridSpec(
            num_scalar_prefetch=2,
            grid=(len(steps),),
            in_specs=[MAIN, pl.BlockSpec((new_rows, full), lambda i, a, b: (0, 0))] + [ANYWHERE] * len(after),
            out_specs=[out(slots) for slots in parts],
            scratch_shapes=[
                pltpu.VMEM((rows, full), jnp.bfloat16),
                pltpu.VMEM((group, blocks_in_all * group), jnp.float32),
                pltpu.SemaphoreType.DMA((4,)),
            ],
        ),
        out_shape=[shape(slots) for slots in parts],
        compiler_params=pltpu.CompilerParams(vmem_limit_bytes=VMEM_BYTES),
        cost_estimate=LIGHT,
        name="window_terms",
    )(place, taps, stored, vectors, *after)


def add_terms(terms, index, arrived, base, count, group, after=()):
    def kernel(terms_ref, *refs):
        out_ref, own, done = refs[-3:]
        fetch = pltpu.make_async_copy(terms_ref.at[index, :, pl.ds(base * group, count * group)], own, done)
        fetch.start()
        fetch.wait()
        for k in range(count):
            cols = slice(k * group, (k + 1) * group)
            total = own[:, cols].astype(jnp.float32)
            for ref, (array, first) in zip(refs, arrived):
                place = base + k - first
                if 0 <= place < array.shape[1] // group:
                    total = total + ref[:, place * group : (place + 1) * group].astype(jnp.float32)
            out_ref[:, cols] = total.astype(jnp.bfloat16)

    return pl.pallas_call(
        kernel,
        in_specs=[ANYWHERE] + [FAST] * len(arrived) + [ANYWHERE] * len(after),
        out_specs=FAST,
        out_shape=jax.ShapeDtypeStruct((group, count * group), jnp.bfloat16),
        scratch_shapes=[pltpu.VMEM((group, count * group), jnp.bfloat16), pltpu.SemaphoreType.DMA],
        compiler_params=pltpu.CompilerParams(vmem_limit_bytes=SMALL_BYTES),
        cost_estimate=LIGHT,
        name="add_terms",
    )(terms, *[array for array, _ in arrived], *after)


def gate(values, after):
    def kernel(*refs):
        pass

    return pl.pallas_call(
        kernel,
        in_specs=[MAIN] * len(values) + [ANYWHERE] * len(after),
        out_specs=[MAIN] * len(values),
        out_shape=[jax.ShapeDtypeStruct(value.shape, value.dtype) for value in values],
        input_output_aliases={index: index for index in range(len(values))},
        compiler_params=pltpu.CompilerParams(vmem_limit_bytes=SMALL_BYTES),
        cost_estimate=LIGHT,
        name="gate",
    )(*values, *after)


def close_window(terms, base, ahead, back, slots, group, after=()):
    count = len(slots)
    chips = [chip for chip in pairs_of(slots) if chip[0] != 0]
    index = terms.shape[0] - 1

    def kernel(terms_ref, ahead_ref, back_ref, *refs):
        blocks_ref, turned_refs, (own, done) = refs[len(after)], refs[len(after) + 1 : -2], refs[-2:]
        fetch = pltpu.make_async_copy(terms_ref.at[index], own, done)
        fetch.start()
        fetch.wait()
        for k in range(count):
            cols = slice(k * group, (k + 1) * group)
            total = own[:, (base + k) * group : (base + k + 1) * group].astype(jnp.float32)
            total = total + ahead_ref[:, cols].astype(jnp.float32) + back_ref[:, cols].astype(jnp.float32)
            total = total.astype(jnp.bfloat16)
            blocks_ref[k] = total
            for (_, blocks, first), turned_ref in zip(chips, turned_refs):
                if first <= k < first + blocks:
                    turned_ref[k - first] = total.T

    sizes = [count] + [blocks for _, blocks, _ in chips]
    return pl.pallas_call(
        kernel,
        in_specs=[ANYWHERE, FAST, FAST] + [ANYWHERE] * len(after),
        out_specs=[FAST] * len(sizes),
        out_shape=[jax.ShapeDtypeStruct((size, group, group), jnp.bfloat16) for size in sizes],
        scratch_shapes=[pltpu.VMEM(terms.shape[1:], jnp.bfloat16), pltpu.SemaphoreType.DMA],
        compiler_params=pltpu.CompilerParams(vmem_limit_bytes=SMALL_BYTES),
        cost_estimate=LIGHT,
        name="close_window",
    )(terms, ahead, back, *after)


def rough_dot(left, right):
    return jnp.dot(left.astype(jnp.bfloat16), right.astype(jnp.bfloat16), preferred_element_type=jnp.float32)


def split_terms(value):
    high = value.astype(jnp.bfloat16)
    value = value - high.astype(jnp.float32)
    middle = value.astype(jnp.bfloat16)
    value = value - middle.astype(jnp.float32)
    return high, middle, value.astype(jnp.bfloat16)


def identity(size):
    rows = lax.broadcasted_iota(jnp.int32, (size, size), 0)
    cols = lax.broadcasted_iota(jnp.int32, (size, size), 1)
    return (rows == cols).astype(jnp.float32)


def eliminate(matrix_ref, right_ref, out_ref, work, block):
    size = matrix_ref.shape[0]
    work[...] = matrix_ref[...]
    out_ref[...] = right_ref[...]
    eye = identity(block)
    for start in range(0, size, block):
        here = slice(start, start + block)
        rest = slice(start + block, size)
        corner = work[here, here]
        norm = jnp.max(jnp.sum(jnp.abs(corner), axis=0))

        def unfinished(state):
            return jnp.logical_and(state[0] < 40, state[1] > 5e-5)

        def improve(state):
            step, _, inverse = state
            better = inverse + exact_dot(inverse, eye - exact_dot(work[here, here], inverse))
            left_over = eye - exact_dot(work[here, here], better)
            return step + 1, jnp.max(jnp.abs(left_over)), better

        found = lax.while_loop(unfinished, improve, (jnp.int32(0), jnp.float32(1.0), eye / norm))[2]
        found = found + exact_dot(found, eye - exact_dot(work[here, here], found))
        solved = exact_dot(found, out_ref[here, :])
        out_ref[here, :] = solved
        if start + block < size:
            across = exact_dot(found, work[here, rest])
            down = work[rest, here]
            work[rest, rest] = work[rest, rest] - exact_dot(down, across)
            out_ref[rest, :] = out_ref[rest, :] - exact_dot(down, solved)
            work[here, rest] = across
    for start in range(size - 2 * block, -1, -block):
        here = slice(start, start + block)
        rest = slice(start + block, size)
        out_ref[here, :] = out_ref[here, :] - exact_dot(work[here, rest], out_ref[rest, :])


def solve(place, pairs_count, mine, other, kept, came, after=()):
    group, width = mine.shape
    examples = 2 * kept.shape[0]
    size = kept.shape[0] // pairs_count

    def kernel(place_ref, mine_ref, other_ref, kept_ref, came_ref, *refs):
        out_ref, pairs_ref, matrix, right, power, inverse, first_ref = refs[len(after) :]
        for start in range(0, kept_ref.shape[0], size):
            near, far = kept_ref[start : start + size, :width], came_ref[start : start + size, :width]
            even = lax.rem(place_ref[0], 2) == 0
            first_ref[2 * start : 2 * start + size, :] = jnp.where(even, near, far)
            first_ref[2 * start + size : 2 * start + 2 * size, :] = jnp.where(even, far, near)
        eye = identity(width)
        t = place_ref[1]
        matrix[pl.ds(pl.multiple_of(t * group, group), group), :] = mine_ref[...]
        matrix[pl.ds(pl.multiple_of((1 - t) * group, group), group), :] = other_ref[...]
        turned = first_ref[...].T
        full = matrix[...] + jnp.dot(turned, first_ref[...], preferred_element_type=jnp.float32) + damping * eye
        diagonal = full * eye
        rows_scale = lax.rsqrt(jnp.sum(diagonal, axis=1, keepdims=True))
        cols_scale = lax.rsqrt(jnp.sum(diagonal, axis=0, keepdims=True))
        full = full * rows_scale * cols_scale
        matrix[...] = full
        right[...] = turned.astype(jnp.float32) * rows_scale

        sums = jnp.max(jnp.sum(jnp.abs(full), axis=0))
        squared = rough_dot(full, full)
        norm = jnp.sqrt(jnp.max(jnp.sum(jnp.abs(squared), axis=0)) + sums * sums / 128)
        start = eye - full / norm
        inverse[...] = eye + start
        power[...] = start.astype(jnp.bfloat16)
        for _ in range(7):
            raised = jnp.dot(power[...], power[...], preferred_element_type=jnp.float32).astype(jnp.bfloat16)
            power[...] = raised
            held = inverse[...]
            inverse[...] = held + jnp.dot(held.astype(jnp.bfloat16), raised, preferred_element_type=jnp.float32)
        power[...] = (inverse[...] / norm).astype(jnp.bfloat16)

        largest = jnp.max(jnp.abs(right[...]))
        out_ref[...] = jnp.dot(power[...], right[...].astype(jnp.bfloat16), preferred_element_type=jnp.float32)

        def unfinished(state):
            return jnp.logical_and(state[0] < 12, jnp.logical_not(state[1] <= 5e-5 * largest))

        def refine(state):
            left_over = right[...] - exact_dot(matrix[...], out_ref[...])
            change = jnp.dot(power[...], left_over.astype(jnp.bfloat16), preferred_element_type=jnp.float32)
            out_ref[...] = out_ref[...] + change
            return state[0] + 1, jnp.max(jnp.abs(left_over))

        worst = lax.while_loop(unfinished, refine, (jnp.int32(0), 1.0 + largest))[1]

        @pl.when(jnp.logical_not(worst <= 5e-5 * largest))
        def _():
            eliminate(matrix, right, out_ref, inverse, 128)

        solved = out_ref[...] * rows_scale
        out_ref[...] = solved
        pairs = jnp.zeros((examples, examples), jnp.float32)
        for term in split_terms(solved):
            pairs = pairs + jnp.dot(first_ref[...], term, preferred_element_type=jnp.float32)
        pairs_ref[...] = pairs

    whole = pl.BlockSpec(memory_space=pltpu.VMEM)
    return pl.pallas_call(
        kernel,
        in_specs=[pl.BlockSpec(memory_space=pltpu.SMEM)] + [whole] * 4 + [ANYWHERE] * len(after),
        out_shape=[
            jax.ShapeDtypeStruct((width, examples), jnp.float32),
            jax.ShapeDtypeStruct((examples, examples), jnp.float32),
        ],
        scratch_shapes=[
            pltpu.VMEM((width, width), jnp.float32),
            pltpu.VMEM((width, examples), jnp.float32),
            pltpu.VMEM((width, width), jnp.bfloat16),
            pltpu.VMEM((width, width), jnp.float32),
            pltpu.VMEM((examples, width), jnp.bfloat16),
        ],
        compiler_params=pltpu.CompilerParams(vmem_limit_bytes=VMEM_BYTES),
        cost_estimate=LIGHT,
        name="solve",
    )(place, mine, other, kept, came, *after)


def spread_back(place, stored, solved, owners, group, after=()):
    rows = stored.shape[0]
    width, examples = solved.shape
    pairs = owners // 2

    def kernel(place_ref, first_ref, solved_ref, *refs):
        cols, outs = refs[:owners], refs[owners + len(after) :]
        total = jnp.zeros((rows, examples), jnp.float32)
        for term in split_terms(solved_ref[...]):
            total = total + jnp.dot(first_ref[...], term, preferred_element_type=jnp.float32)
        terms = jnp.concatenate(split_terms(total.T)[:2], axis=0)
        for index in range(owners):
            product = jnp.dot(terms, cols[index][...], preferred_element_type=jnp.float32)
            outs[index // 2][index % 2] = (product[:examples] + product[examples:]).astype(jnp.bfloat16)

    def owner(index, ref):
        return 2 * lax.rem(ref[0] // 2 + index // 2, pairs) + index % 2

    return pl.pallas_call(
        kernel,
        grid_spec=pltpu.PrefetchScalarGridSpec(
            num_scalar_prefetch=1,
            grid=(1,),
            in_specs=[
                pl.BlockSpec((rows, width), lambda i, ref: (0, 0)),
                pl.BlockSpec((width, examples), lambda i, ref: (0, 0)),
            ]
            + [
                pl.BlockSpec((rows, group), lambda i, ref, index=index: (0, 2 * owner(index, ref) + ref[1]))
                for index in range(owners)
            ]
            + [ANYWHERE] * len(after),
            out_specs=[pl.BlockSpec((2, examples, group), lambda i, ref: (0, 0, 0))] * pairs,
        ),
        out_shape=[jax.ShapeDtypeStruct((2, examples, group), jnp.bfloat16)] * pairs,
        compiler_params=pltpu.CompilerParams(vmem_limit_bytes=VMEM_BYTES),
        cost_estimate=LIGHT,
        name="spread_back",
    )(place, stored, solved, *([stored] * owners), *after)


def sum_pieces(place, came, after=()):
    _, examples, group = came[0].shape

    def kernel(place_ref, *refs):
        mine_ref, away_ref = refs[-2:]
        side = lax.rem(place_ref[0], 2)
        totals = [sum(ref[half].astype(jnp.float32) for ref in refs[: len(came)]) for half in (0, 1)]
        mine_ref[...] = jnp.where(side == 0, totals[0], totals[1])
        away_ref[...] = jnp.where(side == 0, totals[1], totals[0]).astype(jnp.bfloat16)

    return pl.pallas_call(
        kernel,
        in_specs=[pl.BlockSpec(memory_space=pltpu.SMEM)] + [FAST] * len(came) + [ANYWHERE] * len(after),
        out_specs=[FAST, FAST],
        out_shape=[
            jax.ShapeDtypeStruct((examples, group), jnp.float32),
            jax.ShapeDtypeStruct((examples, group), jnp.bfloat16),
        ],
        compiler_params=pltpu.CompilerParams(vmem_limit_bytes=SMALL_BYTES),
        cost_estimate=LIGHT,
        name="sum_pieces",
    )(place, *came, *after)


def pair_products(place, own_cols, first_pairs, mine, other, solved, after=()):
    examples, group = own_cols.shape

    def kernel(place_ref, own_ref, first_ref, mine_ref, other_ref, solved_ref, *refs):
        g = 2 * place_ref[0] + place_ref[1]
        own = own_ref[...]
        damped = solved_ref[pl.ds(pl.multiple_of(place_ref[1] * group, group), group), :].T
        rest = own - lax.dot_general(
            first_ref[...], own, (((0,), (0,)), ((), ())), precision=EXACT, preferred_element_type=jnp.float32
        )
        rest = rest - mine_ref[...] - other_ref[...].astype(jnp.float32) - jnp.where(g < 2, damping * damped, 0.0)
        products = lax.dot_general(
            rest, rest, (((1,), (1,)), ((), ())), precision=EXACT, preferred_element_type=jnp.float32
        )
        refs[-1][...] = products + jnp.where(g == 0, first_ref[...], 0.0)

    return pl.pallas_call(
        kernel,
        in_specs=[pl.BlockSpec(memory_space=pltpu.SMEM)] + [FAST] * 5 + [ANYWHERE] * len(after),
        out_specs=FAST,
        out_shape=jax.ShapeDtypeStruct((examples, examples), jnp.float32),
        compiler_params=pltpu.CompilerParams(vmem_limit_bytes=SMALL_BYTES),
        cost_estimate=LIGHT,
        name="pair_products",
    )(place, own_cols, first_pairs, mine, other, solved, *after)


def assembly_tables(ring, slots, d, t):
    start = [0] * ring.count
    arrived = [0] * ring.count
    for offset, _, first in pairs_of(slots):
        start[offset % ring.count] = first
    place = len(slots)
    for offset in ring.offsets:
        start[-offset % ring.count] = place
        arrived[-offset % ring.count] = 1
        place += 2
    here = ring.position_of(d)
    early = here < ring.half

    def look_up(values, offset):
        found = jnp.zeros_like(offset)
        for index, value in enumerate(values):
            if value:
                found = jnp.where(offset == index, value, found)
        return found

    def offsets_of(chips):
        return lax.rem(ring.position_of(chips) - here + 2 * ring.count, ring.count)

    def fetch(offset, j):
        own = (j == t) == early
        quarter = jnp.where(own, start[ring.half], place)
        return jnp.where(offset == ring.half, quarter, look_up(start, offset) + j)

    chips = jnp.arange(ring.half, dtype=jnp.int32)
    j = jnp.arange(2, dtype=jnp.int32)[None, :]
    send = fetch(offsets_of((1 - t) * ring.half + chips)[:, None], j)
    offset = offsets_of(t * ring.half + chips)[:, None, None]
    r = jnp.arange(2, dtype=jnp.int32)[None, :, None]
    u = jnp.arange(2, dtype=jnp.int32)[None, None, :]
    by_columns = jnp.where(offset == ring.half, early.astype(jnp.int32), look_up(arrived, offset)) == 1
    j = jnp.where(by_columns, r, u)
    local = fetch(offset, j)
    other = 2 * chips[:, None, None] + j
    mine = (jnp.where(by_columns, u, r) == t).astype(jnp.int32)
    final = jnp.stack([local, other, mine]).reshape(-1)
    return send.reshape(-1).astype(jnp.int32), final.astype(jnp.int32)


def for_sibling(table, blocks, group):
    total = table.shape[0]
    wide = min(4, total)

    def kernel(table_ref, *refs):
        for k in range(wide):
            refs[-1][k] = refs[k][0]

    return pl.pallas_call(
        kernel,
        grid_spec=pltpu.PrefetchScalarGridSpec(
            num_scalar_prefetch=1,
            grid=(total // wide,),
            in_specs=[
                pl.BlockSpec((1, group, group), lambda c, ref, k=k: (ref[wide * c + k], 0, 0)) for k in range(wide)
            ],
            out_specs=pl.BlockSpec((wide, group, group), lambda c, ref: (c, 0, 0)),
        ),
        out_shape=jax.ShapeDtypeStruct((total, group, group), jnp.bfloat16),
        compiler_params=pltpu.CompilerParams(vmem_limit_bytes=SMALL_BYTES),
        cost_estimate=LIGHT,
        name="for_sibling",
    )(table, *([blocks] * wide))


def finish(place, table, blocks, other, half, group):
    wide = half // 2
    total = 4 * half

    def at(kind, r, c, k, u, ref):
        return ref[kind * total + 4 * (wide * c + k) + 2 * r + u]

    def spec(kind, k, u):
        return pl.BlockSpec((1, group, group), lambda r, c, ref, place: (at(kind, r, c, k, u, ref), 0, 0))

    order = [(k, u) for k in range(wide) for u in (0, 1)]

    def kernel(table_ref, place_ref, *refs):
        r, c = pl.program_id(0), pl.program_id(1)
        out_ref = refs[-1]
        shape = (group, group)
        gap = lax.broadcasted_iota(jnp.int32, shape, 1) - lax.broadcasted_iota(jnp.int32, shape, 0)
        for index, (k, u) in enumerate(order):
            cols = slice(index * group, (index + 1) * group)
            chip = place_ref[1] * half + wide * c + k
            apart = (2 * place_ref[0] + r - 2 * chip - u) * group
            added = jnp.where(gap == apart, jnp.float32(damping), jnp.float32(0.0))
            mine = at(2, r, c, k, u, table_ref) == 1

            @pl.when(mine)
            def _():
                out_ref[:, cols] = added + refs[index][0].astype(jnp.float32)

            @pl.when(jnp.logical_not(mine))
            def _():
                out_ref[:, cols] = added + refs[len(order) + index][0].astype(jnp.float32)

    return pl.pallas_call(
        kernel,
        grid_spec=pltpu.PrefetchScalarGridSpec(
            num_scalar_prefetch=2,
            grid=(2, 2),
            in_specs=[spec(0, k, u) for k, u in order] + [spec(1, k, u) for k, u in order],
            out_specs=pl.BlockSpec((group, 2 * wide * group), lambda r, c, ref, place: (r, c)),
        ),
        out_shape=jax.ShapeDtypeStruct((2 * group, 2 * half * group), jnp.float32),
        compiler_params=pltpu.CompilerParams(vmem_limit_bytes=SMALL_BYTES),
        cost_estimate=LIGHT,
        name="finish",
    )(table, place, *([blocks] * len(order)), *([other] * len(order)))


def in_order(index, mine, other, axis):
    return jnp.where(
        index == 0,
        jnp.concatenate([mine, other], axis=axis),
        jnp.concatenate([other, mine], axis=axis),
    )


def pair_swap(value, count):
    return lax.ppermute(value, "dp", [(index, index ^ 1) for index in range(count)])


def far_shift(value, step, count):
    return lax.ppermute(value, "dp", [(index, (index + 2 * step) % count) for index in range(count)])


def exchange_pairs(slice_of, pair, count):
    pairs = count // 2
    came = [slice_of(pair)]
    for step in range(1, pairs):
        came.append(far_shift(slice_of(lax.rem(pair + step, pairs)), step, count))
    return came


def natural(came, pair):
    pairs = len(came)
    pieces = []
    for index in range(pairs):
        behind = lax.rem(pair - index + pairs, pairs)
        piece = came[0]
        for step in range(1, pairs):
            piece = jnp.where(behind == step, came[step], piece)
        pieces.append(piece)
    return pieces


def scatter_pairs(value, pair, count):
    size = value.shape[0] // (count // 2)

    def slice_of(index):
        return lax.dynamic_slice_in_dim(value, index * size, size, 0)

    return sum(piece.astype(jnp.float32) for piece in exchange_pairs(slice_of, pair, count))


def local(ring, activations, out_grads, proj_in, proj_out, stored, counts, query_ids):
    owners = ring.count
    full = stored.shape[1]
    width = full // owners
    group = width // 2
    half = ring.half
    t = lax.axis_index("tensor")
    d = lax.axis_index("dp")
    pair, side = d // 2, lax.rem(d, 2)
    g = 2 * d + t
    place = jnp.stack([d, t]).astype(jnp.int32)

    pairs_count = owners // 2
    first_stored = stored[:, :width]
    corner_rows = lead_dot(lax.dynamic_slice_in_dim(first_stored, t * group, group, 1), first_stored)
    activations, out_grads, corner_rows = lax.optimization_barrier((activations, out_grads, corner_rows))
    corner_payload = scatter_pairs(corner_rows, pair, owners)

    sides = jnp.concatenate(
        [
            jnp.dot(activations, proj_in, preferred_element_type=jnp.float32),
            jnp.dot(out_grads, proj_out, preferred_element_type=jnp.float32),
        ],
        axis=1,
    )
    sides = sides + lax.ppermute(sides, "tensor", SWAP)

    examples = counts.shape[0]
    all_examples = examples * owners
    rank = proj_in.shape[1]
    position = jnp.arange(SEQ, dtype=jnp.int32)[None, :]
    weights = jnp.where(
        position < counts[:, None], 1.0 / counts.astype(jnp.float32)[:, None], jnp.float32(0.0)
    )
    outer = jnp.einsum(
        "es,esi,esj->eij",
        weights,
        sides[:, :rank].reshape(examples, SEQ, rank),
        sides[:, rank:].reshape(examples, SEQ, rank),
        precision=EXACT,
    )
    vectors = outer.reshape(examples, full).astype(jnp.bfloat16)

    def columns_for(index):
        groups = [lax.dynamic_slice_in_dim(vectors, (4 * index + 2 * s + t) * group, group, 1) for s in (0, 1)]
        return jnp.concatenate([vectors[:, :width]] + groups, axis=1)

    payloads = [columns_for(lax.rem(pair + step, pairs_count)) for step in range(pairs_count)]

    split = (len(ring.offsets) + 1) // 2
    far_slots = [(half, None)]
    for offset in ring.offsets[:split]:
        far_slots += [(offset, 0), (offset, 1)]
    near_slots = []
    for offset in ring.offsets[split:] + [0]:
        near_slots += [(offset, 0), (offset, 1)]

    slots = far_slots + near_slots
    far_count, near_count = len(far_slots), len(near_slots)
    ahead, back = ring.shift(1), ring.shift(-1)

    def terms_of(steps, parts, after=()):
        return window_terms(ring, place, stored, vectors, group, steps, parts, after)

    came = [payloads[0]] + [far_shift(payloads[step], step, owners) for step in range(1, pairs_count)]
    came = jnp.concatenate(natural(came, pair), axis=0)
    second_group = jnp.concatenate([came[:, :width], came[:, width + group :]], axis=1)
    first_group = came[:, : width + group]
    kept = jnp.where(side == 0, first_group, second_group)
    away = jnp.where(side == 0, second_group, first_group)
    received = pair_swap(away, owners)
    corner_second = corner_payload + pair_swap(corner_payload, owners)
    corner_rows = [corner_second] + [far_shift(corner_second, step, owners) for step in range(1, pairs_count)]
    corner_rows = jnp.concatenate(natural(corner_rows, pair), axis=0)
    corner_other = lax.ppermute(corner_rows, "tensor", SWAP)
    far, near = terms_of([half], [far_slots, near_slots], [away, corner_second])
    far, near = far[0], near[0]
    second_steps = [half - 1, 1 - half, half - 2, 2 - half]
    far, near = gate([far, near], [corner_rows, received])
    second = terms_of(second_steps, [slots], [far])[0]
    shape = (pairs_count, 1, examples, group)
    own_cols = in_order(side, kept[:, width:].reshape(shape), received[:, width:].reshape(shape), 1)
    own_cols = own_cols.reshape(all_examples, group).astype(jnp.float32)
    far_ahead = lax.ppermute(far, "dp", ahead)
    near_back = lax.ppermute(near, "dp", back)
    total = far_count + near_count
    going = add_terms(second, 0, [(far_ahead, 0)], 0, total, group)
    coming = add_terms(second, 1, [(near_back, far_count)], 0, total, group)

    solved, first_pairs = solve(place, pairs_count, corner_rows, corner_other, kept, received, [going, coming])
    pieces = spread_back(place, stored, solved, owners, group)
    later_steps = [s for step in range(half - 3, 0, -1) for s in (step, -step)] + [0]
    for step in range(half - 2, 0, -1):
        came_ahead = lax.ppermute(going, "dp", ahead)
        came_back = lax.ppermute(coming, "dp", back)
        own, index, token = (second, 2, [pieces[0]]) if step == half - 2 else (later, later_steps.index(step), [away])
        if step == 1:
            far_going = add_terms(own, index, [(came_ahead, 0)], 0, far_count, group, token)
            far_coming = add_terms(own, index + 1, [(came_back, 0)], 0, far_count, group, token)
            token = [far_going, far_coming]
            near_going = add_terms(own, index, [(came_ahead, 0)], far_count, near_count, group, token)
            near_coming = add_terms(own, index + 1, [(came_back, 0)], far_count, near_count, group, token)
            token = [near_going, near_coming]
        else:
            going = add_terms(own, index, [(came_ahead, 0)], 0, total, group, token)
            coming = add_terms(own, index + 1, [(came_back, 0)], 0, total, group, token)
            token = [going, coming]
        if step == half - 2:
            later = terms_of(later_steps, [slots], token)[0]
            came = [pieces[0]] + [far_shift(pieces[index], index, owners) for index in range(1, pairs_count)]
            terms, away = sum_pieces(place, came, [later])
            terms_other = pair_swap(away, owners)
    far_sums = [lax.ppermute(far_going, "dp", ahead), lax.ppermute(far_coming, "dp", back)]
    near_sums = [lax.ppermute(near_going, "dp", ahead), lax.ppermute(near_coming, "dp", back)]

    far = close_window(later, 0, *far_sums, far_slots, group)
    near = close_window(later, far_count, *near_sums, near_slots, group, [far[0]])
    turned = {}
    for (found, slots) in ((far, far_slots), (near, near_slots)):
        chips = [chip for chip in pairs_of(slots) if chip[0] != 0]
        for (offset, _, _), block in zip(chips, found[1:]):
            turned[offset] = block
    shifted = {
        offset: lax.ppermute(turned[offset], "dp", ring.shift(offset))
        for offset in [half] + ring.offsets
    }
    came = [shifted[offset] for offset in ring.offsets + [half]]
    blocks = jnp.concatenate([far[0], near[0]] + came, axis=0)
    send_table, final_table = assembly_tables(ring, far_slots + near_slots, d, t)
    send = for_sibling(send_table, blocks, group)
    other = lax.ppermute(send, "tensor", SWAP)

    pairs = pair_products(place, own_cols, first_pairs, terms, terms_other, solved, [send])
    bit = owners // 2
    while bit >= 1:
        kept_rows = jnp.where((d & bit) == 0, pairs[: pairs.shape[0] // 2], pairs[pairs.shape[0] // 2 :])
        sent_rows = jnp.where((d & bit) == 0, pairs[pairs.shape[0] // 2 :], pairs[: pairs.shape[0] // 2])
        pairs = kept_rows + lax.ppermute(sent_rows, "dp", [(index, index ^ bit) for index in range(owners)])
        bit //= 2
    pairs = pairs + lax.ppermute(pairs, "tensor", SWAP)
    chosen = (query_ids[:, None] == jnp.arange(all_examples, dtype=jnp.int32)[None, :]).astype(jnp.float32)
    scores = lax.dot_general(chosen, pairs, (((1,), (1,)), ((), ())), precision=EXACT, preferred_element_type=jnp.float32) / R
    return finish(place, final_table, blocks, other, half, group), scores


def solution(mesh):
    placed = (
        P(("groups", "dp"), "tensor"),
        P(("groups", "dp"), "tensor"),
        P("tensor", None),
        P("tensor", None),
        P(("groups", "dp"), None),
        P(("groups", "dp")),
        P("groups"),
    )
    ring = Ring(mesh)

    def program(*args):
        return local(ring, *args)

    return jax.shard_map(
        program,
        mesh=mesh,
        in_specs=placed,
        out_specs=(P(("groups", "dp"), "tensor"), P("groups", "dp")),
        check_vma=False,
    )
```

```python
import jax
import jax.numpy as jnp
from jax import lax
from jax.experimental import pallas as pl
from jax.experimental.pallas import tpu as pltpu
from jax.sharding import PartitionSpec as P

R = 64
SEQ = 16
damping = 1.0
EXACT = lax.Precision.HIGHEST
SWAP = [(0, 1), (1, 0)]
VMEM_BYTES = 56 * 1024 * 1024
SMALL_BYTES = 12 * 1024 * 1024
LIGHT = pl.CostEstimate(flops=10**6, bytes_accessed=10**5, transcendentals=0)
ANYWHERE = pl.BlockSpec(memory_space=pl.ANY)
MAIN = pl.BlockSpec(memory_space=pltpu.HBM)
FAST = pl.BlockSpec(memory_space=pltpu.VMEM)


class Ring:
    def __init__(self, mesh):
        self.count = mesh.shape["dp"]
        self.half = self.count // 2
        coords = [getattr(device, "coords", None) for device in mesh.devices[0, :, 0]]
        self.folded = False
        if None not in coords:
            moving = [axis for axis in range(3) if len({place[axis] for place in coords}) > 1]
            fast = [axis for axis in moving if coords[0][axis] != coords[1][axis]]
            self.folded = len(moving) == 2 and len(fast) == 1 and len({place[fast[0]] for place in coords}) == 2
        reach = [0, 0]
        self.offsets = []
        for distance in range(self.half - 1, 0, -1):
            side = 0 if reach[0] <= reach[1] else 1
            reach[side] += distance
            self.offsets.append(distance if side == 0 else -distance)

    def index_at(self, position):
        if isinstance(position, int):
            position = position % self.count
            if not self.folded:
                return position
            return 2 * position if position < self.half else 2 * (self.count - 1 - position) + 1
        position = lax.rem(position + 2 * self.count, self.count)
        if not self.folded:
            return position
        return jnp.where(position < self.half, 2 * position, 2 * (self.count - 1 - position) + 1)

    def position_of(self, index):
        if not self.folded:
            return index
        return jnp.where(lax.rem(index, 2) == 0, index // 2, self.count - 1 - index // 2)

    def shift(self, step):
        return [(self.index_at(p), self.index_at(p + step)) for p in range(self.count)]


def lead_dot(left, right, precision=None):
    return lax.dot_general(
        left, right, (((0,), (0,)), ((), ())), precision=precision, preferred_element_type=jnp.float32
    )


def exact_dot(left, right):
    return jnp.dot(left, right, precision=EXACT, preferred_element_type=jnp.float32)


def pairs_of(slots):
    found = []
    for index, (offset, core) in enumerate(slots):
        if core is None:
            found.append((offset, 1, index))
        elif core == 0:
            found.append((offset, 2, index))
    return found


def window_terms(ring, place, stored, vectors, group, steps, parts, after=()):
    rows, full = stored.shape
    new_rows = vectors.shape[0]
    taps = jnp.array(steps, jnp.int32)
    blocks_in_all = sum(len(slots) for slots in parts)
    chunk = rows // 4

    width = blocks_in_all * group
    widths = [len(slots) * group for slots in parts]

    def kernel(place_ref, step_ref, stored_ref, vectors_ref, *refs):
        outs, (held, total, made, arrived, left_for) = refs[len(after) : -5], refs[-5:]
        i = pl.program_id(0)
        slot = lax.rem(i, 2)
        owner = lax.rem(ring.position_of(place_ref[0]) + step_ref[i] + ring.count, ring.count)
        core = place_ref[1]

        def load(index):
            rows_of = pl.ds(index * chunk, chunk)
            return pltpu.make_async_copy(stored_ref.at[rows_of], held.at[rows_of], arrived.at[index])

        def leave(step):
            copies, base = [], 0
            for part, columns in enumerate(widths):
                out_ref = outs[step * len(parts) + part]
                source = made.at[step % 2, :, pl.ds(base, columns)]
                copies.append(pltpu.make_async_copy(source, out_ref, left_for.at[step % 2, part]))
                base += columns
            return copies

        @pl.when(i == 0)
        def _():
            for index in range(4):
                load(index).start()

        for step in range(2, len(steps)):

            @pl.when(i == step)
            def _():
                for copy in leave(step - 2):
                    copy.wait()

        left = pl.ds(pl.multiple_of((2 * ring.index_at(owner) + core) * group, group), group)
        chips, base = [], 0
        for slots in parts:
            for offset, blocks, first in pairs_of(slots):
                column = 2 * ring.index_at(owner + offset)
                if blocks == 1:
                    column = column + jnp.where(owner < ring.half, core, 1 - core)
                right = pl.ds(pl.multiple_of(column * group, blocks * group), blocks * group)
                chips.append((right, slice((base + first) * group, (base + first + blocks) * group)))
            base += len(slots)
        turned_new = vectors_ref[:, left].T

        @pl.when(i == 0)
        def _():
            for right, here in chips:
                total[:, here] = jnp.dot(turned_new, vectors_ref[:, right], preferred_element_type=jnp.float32)
            for index in range(4):
                load(index).wait()
                rows_of = slice(index * chunk, (index + 1) * chunk)
                turned = held[rows_of, left].T
                for right, here in chips:
                    added = total[:, here] + jnp.dot(turned, held[rows_of, right], preferred_element_type=jnp.float32)
                    if index < 3:
                        total[:, here] = added
                    else:
                        made[0, :, here] = added.astype(jnp.bfloat16)

        if len(steps) > 1:

            @pl.when(i > 0)
            def _():
                turned = held[:, left].T
                for right, here in chips:
                    added = jnp.dot(turned, held[:, right], preferred_element_type=jnp.float32)
                    added = added + jnp.dot(turned_new, vectors_ref[:, right], preferred_element_type=jnp.float32)
                    made[slot, :, here] = added.astype(jnp.bfloat16)

        for step in range(len(steps)):

            @pl.when(i == step)
            def _():
                for copy in leave(step):
                    copy.start()

        @pl.when(i == len(steps) - 1)
        def _():
            for step in range(max(len(steps) - 2, 0), len(steps)):
                for copy in leave(step):
                    copy.wait()

    found = pl.pallas_call(
        kernel,
        grid_spec=pltpu.PrefetchScalarGridSpec(
            num_scalar_prefetch=2,
            grid=(len(steps),),
            in_specs=[MAIN, pl.BlockSpec((new_rows, full), lambda i, a, b: (0, 0))] + [ANYWHERE] * len(after),
            out_specs=[ANYWHERE] * (len(steps) * len(parts)),
            scratch_shapes=[
                pltpu.VMEM((rows, full), jnp.bfloat16),
                pltpu.VMEM((group, width), jnp.float32),
                pltpu.VMEM((2, group, width), jnp.bfloat16),
                pltpu.SemaphoreType.DMA((4,)),
                pltpu.SemaphoreType.DMA((2, len(parts))),
            ],
        ),
        out_shape=[jax.ShapeDtypeStruct((group, columns), jnp.bfloat16) for _ in steps for columns in widths],
        compiler_params=pltpu.CompilerParams(vmem_limit_bytes=VMEM_BYTES),
        cost_estimate=LIGHT,
        name="window_terms",
    )(place, taps, stored, vectors, *after)
    return [found[step * len(parts) : (step + 1) * len(parts)] for step in range(len(steps))]


def add_terms(terms, arrived, base, count, group, after=()):
    def kernel(terms_ref, *refs):
        out_ref, own, done = refs[-3:]
        fetch = pltpu.make_async_copy(terms_ref.at[:, pl.ds(base * group, count * group)], own, done)
        fetch.start()
        fetch.wait()
        for k in range(count):
            cols = slice(k * group, (k + 1) * group)
            total = own[:, cols].astype(jnp.float32)
            for ref, (array, first) in zip(refs, arrived):
                place = base + k - first
                if 0 <= place < array.shape[1] // group:
                    total = total + ref[:, place * group : (place + 1) * group].astype(jnp.float32)
            out_ref[:, cols] = total.astype(jnp.bfloat16)

    return pl.pallas_call(
        kernel,
        in_specs=[ANYWHERE] + [FAST] * len(arrived) + [ANYWHERE] * len(after),
        out_specs=FAST,
        out_shape=jax.ShapeDtypeStruct((group, count * group), jnp.bfloat16),
        scratch_shapes=[pltpu.VMEM((group, count * group), jnp.bfloat16), pltpu.SemaphoreType.DMA],
        compiler_params=pltpu.CompilerParams(vmem_limit_bytes=SMALL_BYTES),
        cost_estimate=LIGHT,
        name="add_terms",
    )(terms, *[array for array, _ in arrived], *after)


def gate(values, after):
    def kernel(*refs):
        pass

    return pl.pallas_call(
        kernel,
        in_specs=[MAIN] * len(values) + [ANYWHERE] * len(after),
        out_specs=[MAIN] * len(values),
        out_shape=[jax.ShapeDtypeStruct(value.shape, value.dtype) for value in values],
        input_output_aliases={index: index for index in range(len(values))},
        compiler_params=pltpu.CompilerParams(vmem_limit_bytes=SMALL_BYTES),
        cost_estimate=LIGHT,
        name="gate",
    )(*values, *after)


def close_window(terms, base, ahead, back, slots, group, after=()):
    count = len(slots)
    chips = [chip for chip in pairs_of(slots) if chip[0] != 0]
    def kernel(terms_ref, ahead_ref, back_ref, *refs):
        blocks_ref, turned_refs, (own, done) = refs[len(after)], refs[len(after) + 1 : -2], refs[-2:]
        fetch = pltpu.make_async_copy(terms_ref.at[:, pl.ds(base * group, count * group)], own, done)
        fetch.start()
        fetch.wait()
        for k in range(count):
            cols = slice(k * group, (k + 1) * group)
            total = own[:, cols].astype(jnp.float32)
            total = total + ahead_ref[:, cols].astype(jnp.float32) + back_ref[:, cols].astype(jnp.float32)
            total = total.astype(jnp.bfloat16)
            blocks_ref[k] = total
            for (_, blocks, first), turned_ref in zip(chips, turned_refs):
                if first <= k < first + blocks:
                    turned_ref[k - first] = total.T

    sizes = [count] + [blocks for _, blocks, _ in chips]
    return pl.pallas_call(
        kernel,
        in_specs=[ANYWHERE, FAST, FAST] + [ANYWHERE] * len(after),
        out_specs=[FAST] * len(sizes),
        out_shape=[jax.ShapeDtypeStruct((size, group, group), jnp.bfloat16) for size in sizes],
        scratch_shapes=[pltpu.VMEM((group, count * group), jnp.bfloat16), pltpu.SemaphoreType.DMA],
        compiler_params=pltpu.CompilerParams(vmem_limit_bytes=SMALL_BYTES),
        cost_estimate=LIGHT,
        name="close_window",
    )(terms, ahead, back, *after)


def rough_dot(left, right):
    return jnp.dot(left.astype(jnp.bfloat16), right.astype(jnp.bfloat16), preferred_element_type=jnp.float32)


def split_terms(value):
    high = value.astype(jnp.bfloat16)
    value = value - high.astype(jnp.float32)
    middle = value.astype(jnp.bfloat16)
    value = value - middle.astype(jnp.float32)
    return high, middle, value.astype(jnp.bfloat16)


def identity(size):
    rows = lax.broadcasted_iota(jnp.int32, (size, size), 0)
    cols = lax.broadcasted_iota(jnp.int32, (size, size), 1)
    return (rows == cols).astype(jnp.float32)


def eliminate(matrix_ref, right_ref, out_ref, work, block):
    size = matrix_ref.shape[0]
    work[...] = matrix_ref[...]
    out_ref[...] = right_ref[...]
    eye = identity(block)
    for start in range(0, size, block):
        here = slice(start, start + block)
        rest = slice(start + block, size)
        corner = work[here, here]
        norm = jnp.max(jnp.sum(jnp.abs(corner), axis=0))

        def unfinished(state):
            return jnp.logical_and(state[0] < 40, state[1] > 5e-5)

        def improve(state):
            step, _, inverse = state
            better = inverse + exact_dot(inverse, eye - exact_dot(work[here, here], inverse))
            left_over = eye - exact_dot(work[here, here], better)
            return step + 1, jnp.max(jnp.abs(left_over)), better

        found = lax.while_loop(unfinished, improve, (jnp.int32(0), jnp.float32(1.0), eye / norm))[2]
        found = found + exact_dot(found, eye - exact_dot(work[here, here], found))
        solved = exact_dot(found, out_ref[here, :])
        out_ref[here, :] = solved
        if start + block < size:
            across = exact_dot(found, work[here, rest])
            down = work[rest, here]
            work[rest, rest] = work[rest, rest] - exact_dot(down, across)
            out_ref[rest, :] = out_ref[rest, :] - exact_dot(down, solved)
            work[here, rest] = across
    for start in range(size - 2 * block, -1, -block):
        here = slice(start, start + block)
        rest = slice(start + block, size)
        out_ref[here, :] = out_ref[here, :] - exact_dot(work[here, rest], out_ref[rest, :])


def solve(place, pairs_count, mine, other, kept, came, after=()):
    group, width = mine.shape
    examples = 2 * kept.shape[0]
    size = kept.shape[0] // pairs_count

    def kernel(place_ref, mine_ref, other_ref, kept_ref, came_ref, *refs):
        out_ref, pairs_ref, matrix, right, power, inverse, first_ref = refs[len(after) :]
        for start in range(0, kept_ref.shape[0], size):
            near, far = kept_ref[start : start + size, :width], came_ref[start : start + size, :width]
            even = lax.rem(place_ref[0], 2) == 0
            first_ref[2 * start : 2 * start + size, :] = jnp.where(even, near, far)
            first_ref[2 * start + size : 2 * start + 2 * size, :] = jnp.where(even, far, near)
        eye = identity(width)
        t = place_ref[1]
        matrix[pl.ds(pl.multiple_of(t * group, group), group), :] = mine_ref[...]
        matrix[pl.ds(pl.multiple_of((1 - t) * group, group), group), :] = other_ref[...]
        turned = first_ref[...].T
        full = matrix[...] + jnp.dot(turned, first_ref[...], preferred_element_type=jnp.float32) + damping * eye
        diagonal = full * eye
        rows_scale = lax.rsqrt(jnp.sum(diagonal, axis=1, keepdims=True))
        cols_scale = lax.rsqrt(jnp.sum(diagonal, axis=0, keepdims=True))
        full = full * rows_scale * cols_scale
        matrix[...] = full
        right[...] = turned.astype(jnp.float32) * rows_scale

        sums = jnp.max(jnp.sum(jnp.abs(full), axis=0))
        squared = rough_dot(full, full)
        norm = jnp.sqrt(jnp.max(jnp.sum(jnp.abs(squared), axis=0)) + sums * sums / 128)
        start = eye - full / norm
        inverse[...] = eye + start
        power[...] = start.astype(jnp.bfloat16)
        for _ in range(7):
            raised = jnp.dot(power[...], power[...], preferred_element_type=jnp.float32).astype(jnp.bfloat16)
            power[...] = raised
            held = inverse[...]
            inverse[...] = held + jnp.dot(held.astype(jnp.bfloat16), raised, preferred_element_type=jnp.float32)
        power[...] = (inverse[...] / norm).astype(jnp.bfloat16)

        largest = jnp.max(jnp.abs(right[...]))
        out_ref[...] = jnp.dot(power[...], right[...].astype(jnp.bfloat16), preferred_element_type=jnp.float32)

        def unfinished(state):
            return jnp.logical_and(state[0] < 12, jnp.logical_not(state[1] <= 5e-5 * largest))

        def refine(state):
            left_over = right[...] - exact_dot(matrix[...], out_ref[...])
            change = jnp.dot(power[...], left_over.astype(jnp.bfloat16), preferred_element_type=jnp.float32)
            out_ref[...] = out_ref[...] + change
            return state[0] + 1, jnp.max(jnp.abs(left_over))

        worst = lax.while_loop(unfinished, refine, (jnp.int32(0), 1.0 + largest))[1]

        @pl.when(jnp.logical_not(worst <= 5e-5 * largest))
        def _():
            eliminate(matrix, right, out_ref, inverse, 128)

        solved = out_ref[...] * rows_scale
        out_ref[...] = solved
        pairs = jnp.zeros((examples, examples), jnp.float32)
        for term in split_terms(solved):
            pairs = pairs + jnp.dot(first_ref[...], term, preferred_element_type=jnp.float32)
        pairs_ref[...] = pairs

    whole = pl.BlockSpec(memory_space=pltpu.VMEM)
    return pl.pallas_call(
        kernel,
        in_specs=[pl.BlockSpec(memory_space=pltpu.SMEM)] + [whole] * 4 + [ANYWHERE] * len(after),
        out_shape=[
            jax.ShapeDtypeStruct((width, examples), jnp.float32),
            jax.ShapeDtypeStruct((examples, examples), jnp.float32),
        ],
        scratch_shapes=[
            pltpu.VMEM((width, width), jnp.float32),
            pltpu.VMEM((width, examples), jnp.float32),
            pltpu.VMEM((width, width), jnp.bfloat16),
            pltpu.VMEM((width, width), jnp.float32),
            pltpu.VMEM((examples, width), jnp.bfloat16),
        ],
        compiler_params=pltpu.CompilerParams(vmem_limit_bytes=VMEM_BYTES),
        cost_estimate=LIGHT,
        name="solve",
    )(place, mine, other, kept, came, *after)


def spread_back(place, stored, solved, owners, group, after=()):
    rows = stored.shape[0]
    width, examples = solved.shape
    pairs = owners // 2

    def kernel(place_ref, first_ref, solved_ref, *refs):
        cols, outs = refs[:owners], refs[owners + len(after) :]
        total = jnp.zeros((rows, examples), jnp.float32)
        for term in split_terms(solved_ref[...]):
            total = total + jnp.dot(first_ref[...], term, preferred_element_type=jnp.float32)
        terms = jnp.concatenate(split_terms(total.T)[:2], axis=0)
        for index in range(owners):
            product = jnp.dot(terms, cols[index][...], preferred_element_type=jnp.float32)
            outs[index // 2][index % 2] = (product[:examples] + product[examples:]).astype(jnp.bfloat16)

    def owner(index, ref):
        return 2 * lax.rem(ref[0] // 2 + index // 2, pairs) + index % 2

    return pl.pallas_call(
        kernel,
        grid_spec=pltpu.PrefetchScalarGridSpec(
            num_scalar_prefetch=1,
            grid=(1,),
            in_specs=[
                pl.BlockSpec((rows, width), lambda i, ref: (0, 0)),
                pl.BlockSpec((width, examples), lambda i, ref: (0, 0)),
            ]
            + [
                pl.BlockSpec((rows, group), lambda i, ref, index=index: (0, 2 * owner(index, ref) + ref[1]))
                for index in range(owners)
            ]
            + [ANYWHERE] * len(after),
            out_specs=[pl.BlockSpec((2, examples, group), lambda i, ref: (0, 0, 0))] * pairs,
        ),
        out_shape=[jax.ShapeDtypeStruct((2, examples, group), jnp.bfloat16)] * pairs,
        compiler_params=pltpu.CompilerParams(vmem_limit_bytes=VMEM_BYTES),
        cost_estimate=LIGHT,
        name="spread_back",
    )(place, stored, solved, *([stored] * owners), *after)


def sum_pieces(place, came, after=()):
    _, examples, group = came[0].shape

    def kernel(place_ref, *refs):
        mine_ref, away_ref = refs[-2:]
        side = lax.rem(place_ref[0], 2)
        totals = [sum(ref[half].astype(jnp.float32) for ref in refs[: len(came)]) for half in (0, 1)]
        mine_ref[...] = jnp.where(side == 0, totals[0], totals[1])
        away_ref[...] = jnp.where(side == 0, totals[1], totals[0]).astype(jnp.bfloat16)

    return pl.pallas_call(
        kernel,
        in_specs=[pl.BlockSpec(memory_space=pltpu.SMEM)] + [FAST] * len(came) + [ANYWHERE] * len(after),
        out_specs=[FAST, FAST],
        out_shape=[
            jax.ShapeDtypeStruct((examples, group), jnp.float32),
            jax.ShapeDtypeStruct((examples, group), jnp.bfloat16),
        ],
        compiler_params=pltpu.CompilerParams(vmem_limit_bytes=SMALL_BYTES),
        cost_estimate=LIGHT,
        name="sum_pieces",
    )(place, *came, *after)


def pair_products(place, own_cols, first_pairs, mine, other, solved, after=()):
    examples, group = own_cols.shape

    def kernel(place_ref, own_ref, first_ref, mine_ref, other_ref, solved_ref, *refs):
        g = 2 * place_ref[0] + place_ref[1]
        own = own_ref[...]
        damped = solved_ref[pl.ds(pl.multiple_of(place_ref[1] * group, group), group), :].T
        rest = own - lax.dot_general(
            first_ref[...], own, (((0,), (0,)), ((), ())), precision=EXACT, preferred_element_type=jnp.float32
        )
        rest = rest - mine_ref[...] - other_ref[...].astype(jnp.float32) - jnp.where(g < 2, damping * damped, 0.0)
        products = lax.dot_general(
            rest, rest, (((1,), (1,)), ((), ())), precision=EXACT, preferred_element_type=jnp.float32
        )
        refs[-1][...] = products + jnp.where(g == 0, first_ref[...], 0.0)

    return pl.pallas_call(
        kernel,
        in_specs=[pl.BlockSpec(memory_space=pltpu.SMEM)] + [FAST] * 5 + [ANYWHERE] * len(after),
        out_specs=FAST,
        out_shape=jax.ShapeDtypeStruct((examples, examples), jnp.float32),
        compiler_params=pltpu.CompilerParams(vmem_limit_bytes=SMALL_BYTES),
        cost_estimate=LIGHT,
        name="pair_products",
    )(place, own_cols, first_pairs, mine, other, solved, *after)


def assembly_tables(ring, slots, d, t):
    start = [0] * ring.count
    arrived = [0] * ring.count
    for offset, _, first in pairs_of(slots):
        start[offset % ring.count] = first
    place = len(slots)
    for offset in ring.offsets:
        start[-offset % ring.count] = place
        arrived[-offset % ring.count] = 1
        place += 2
    here = ring.position_of(d)
    early = here < ring.half

    def look_up(values, offset):
        found = jnp.zeros_like(offset)
        for index, value in enumerate(values):
            if value:
                found = jnp.where(offset == index, value, found)
        return found

    def offsets_of(chips):
        return lax.rem(ring.position_of(chips) - here + 2 * ring.count, ring.count)

    def fetch(offset, j):
        own = (j == t) == early
        quarter = jnp.where(own, start[ring.half], place)
        return jnp.where(offset == ring.half, quarter, look_up(start, offset) + j)

    chips = jnp.arange(ring.half, dtype=jnp.int32)
    j = jnp.arange(2, dtype=jnp.int32)[None, :]
    send = fetch(offsets_of((1 - t) * ring.half + chips)[:, None], j)
    offset = offsets_of(t * ring.half + chips)[:, None, None]
    r = jnp.arange(2, dtype=jnp.int32)[None, :, None]
    u = jnp.arange(2, dtype=jnp.int32)[None, None, :]
    by_columns = jnp.where(offset == ring.half, early.astype(jnp.int32), look_up(arrived, offset)) == 1
    j = jnp.where(by_columns, r, u)
    local = fetch(offset, j)
    other = 2 * chips[:, None, None] + j
    mine = (jnp.where(by_columns, u, r) == t).astype(jnp.int32)
    final = jnp.stack([local, other, mine]).reshape(-1)
    return send.reshape(-1).astype(jnp.int32), final.astype(jnp.int32)


def for_sibling(table, blocks, group):
    total = table.shape[0]
    wide = min(4, total)

    def kernel(table_ref, *refs):
        for k in range(wide):
            refs[-1][k] = refs[k][0]

    return pl.pallas_call(
        kernel,
        grid_spec=pltpu.PrefetchScalarGridSpec(
            num_scalar_prefetch=1,
            grid=(total // wide,),
            in_specs=[
                pl.BlockSpec((1, group, group), lambda c, ref, k=k: (ref[wide * c + k], 0, 0)) for k in range(wide)
            ],
            out_specs=pl.BlockSpec((wide, group, group), lambda c, ref: (c, 0, 0)),
        ),
        out_shape=jax.ShapeDtypeStruct((total, group, group), jnp.bfloat16),
        compiler_params=pltpu.CompilerParams(vmem_limit_bytes=SMALL_BYTES),
        cost_estimate=LIGHT,
        name="for_sibling",
    )(table, *([blocks] * wide))


def finish(place, table, blocks, other, half, group):
    wide = half // 2
    total = 4 * half

    def at(kind, r, c, k, u, ref):
        return ref[kind * total + 4 * (wide * c + k) + 2 * r + u]

    def spec(kind, k, u):
        return pl.BlockSpec((1, group, group), lambda r, c, ref, place: (at(kind, r, c, k, u, ref), 0, 0))

    order = [(k, u) for k in range(wide) for u in (0, 1)]

    def kernel(table_ref, place_ref, *refs):
        r, c = pl.program_id(0), pl.program_id(1)
        out_ref = refs[-1]
        shape = (group, group)
        gap = lax.broadcasted_iota(jnp.int32, shape, 1) - lax.broadcasted_iota(jnp.int32, shape, 0)
        for index, (k, u) in enumerate(order):
            cols = slice(index * group, (index + 1) * group)
            chip = place_ref[1] * half + wide * c + k
            apart = (2 * place_ref[0] + r - 2 * chip - u) * group
            added = jnp.where(gap == apart, jnp.float32(damping), jnp.float32(0.0))
            mine = at(2, r, c, k, u, table_ref) == 1

            @pl.when(mine)
            def _():
                out_ref[:, cols] = added + refs[index][0].astype(jnp.float32)

            @pl.when(jnp.logical_not(mine))
            def _():
                out_ref[:, cols] = added + refs[len(order) + index][0].astype(jnp.float32)

    return pl.pallas_call(
        kernel,
        grid_spec=pltpu.PrefetchScalarGridSpec(
            num_scalar_prefetch=2,
            grid=(2, 2),
            in_specs=[spec(0, k, u) for k, u in order] + [spec(1, k, u) for k, u in order],
            out_specs=pl.BlockSpec((group, 2 * wide * group), lambda r, c, ref, place: (r, c)),
        ),
        out_shape=jax.ShapeDtypeStruct((2 * group, 2 * half * group), jnp.float32),
        compiler_params=pltpu.CompilerParams(vmem_limit_bytes=SMALL_BYTES),
        cost_estimate=LIGHT,
        name="finish",
    )(table, place, *([blocks] * len(order)), *([other] * len(order)))


def in_order(index, mine, other, axis):
    return jnp.where(
        index == 0,
        jnp.concatenate([mine, other], axis=axis),
        jnp.concatenate([other, mine], axis=axis),
    )


def pair_swap(value, count):
    return lax.ppermute(value, "dp", [(index, index ^ 1) for index in range(count)])


def far_shift(value, step, count):
    return lax.ppermute(value, "dp", [(index, (index + 2 * step) % count) for index in range(count)])


def exchange_pairs(slice_of, pair, count):
    pairs = count // 2
    came = [slice_of(pair)]
    for step in range(1, pairs):
        came.append(far_shift(slice_of(lax.rem(pair + step, pairs)), step, count))
    return came


def natural(came, pair):
    pairs = len(came)
    pieces = []
    for index in range(pairs):
        behind = lax.rem(pair - index + pairs, pairs)
        piece = came[0]
        for step in range(1, pairs):
            piece = jnp.where(behind == step, came[step], piece)
        pieces.append(piece)
    return pieces


def scatter_pairs(value, pair, count):
    size = value.shape[0] // (count // 2)

    def slice_of(index):
        return lax.dynamic_slice_in_dim(value, index * size, size, 0)

    return sum(piece.astype(jnp.float32) for piece in exchange_pairs(slice_of, pair, count))


def local(ring, activations, out_grads, proj_in, proj_out, stored, counts, query_ids):
    owners = ring.count
    full = stored.shape[1]
    width = full // owners
    group = width // 2
    half = ring.half
    t = lax.axis_index("tensor")
    d = lax.axis_index("dp")
    pair, side = d // 2, lax.rem(d, 2)
    g = 2 * d + t
    place = jnp.stack([d, t]).astype(jnp.int32)

    pairs_count = owners // 2
    first_stored = stored[:, :width]
    corner_rows = lead_dot(lax.dynamic_slice_in_dim(first_stored, t * group, group, 1), first_stored)
    activations, out_grads, corner_rows = lax.optimization_barrier((activations, out_grads, corner_rows))
    corner_payload = scatter_pairs(corner_rows, pair, owners)

    sides = jnp.concatenate(
        [
            jnp.dot(activations, proj_in, preferred_element_type=jnp.float32),
            jnp.dot(out_grads, proj_out, preferred_element_type=jnp.float32),
        ],
        axis=1,
    )
    sides = sides + lax.ppermute(sides, "tensor", SWAP)

    examples = counts.shape[0]
    all_examples = examples * owners
    rank = proj_in.shape[1]
    position = jnp.arange(SEQ, dtype=jnp.int32)[None, :]
    weights = jnp.where(
        position < counts[:, None], 1.0 / counts.astype(jnp.float32)[:, None], jnp.float32(0.0)
    )
    outer = jnp.einsum(
        "es,esi,esj->eij",
        weights,
        sides[:, :rank].reshape(examples, SEQ, rank),
        sides[:, rank:].reshape(examples, SEQ, rank),
        precision=EXACT,
    )
    vectors = outer.reshape(examples, full).astype(jnp.bfloat16)

    def columns_for(index):
        groups = [lax.dynamic_slice_in_dim(vectors, (4 * index + 2 * s + t) * group, group, 1) for s in (0, 1)]
        return jnp.concatenate([vectors[:, :width]] + groups, axis=1)

    payloads = [columns_for(lax.rem(pair + step, pairs_count)) for step in range(pairs_count)]

    split = (len(ring.offsets) + 1) // 2
    far_slots = [(half, None)]
    for offset in ring.offsets[:split]:
        far_slots += [(offset, 0), (offset, 1)]
    near_slots = []
    for offset in ring.offsets[split:] + [0]:
        near_slots += [(offset, 0), (offset, 1)]

    slots = far_slots + near_slots
    far_count, near_count = len(far_slots), len(near_slots)
    ahead, back = ring.shift(1), ring.shift(-1)

    def terms_of(steps, parts, after=()):
        return window_terms(ring, place, stored, vectors, group, steps, parts, after)

    came = [payloads[0]] + [far_shift(payloads[step], step, owners) for step in range(1, pairs_count)]
    came = jnp.concatenate(natural(came, pair), axis=0)
    second_group = jnp.concatenate([came[:, :width], came[:, width + group :]], axis=1)
    first_group = came[:, : width + group]
    kept = jnp.where(side == 0, first_group, second_group)
    away = jnp.where(side == 0, second_group, first_group)
    received = pair_swap(away, owners)
    corner_second = corner_payload + pair_swap(corner_payload, owners)
    corner_rows = [corner_second] + [far_shift(corner_second, step, owners) for step in range(1, pairs_count)]
    corner_rows = jnp.concatenate(natural(corner_rows, pair), axis=0)
    corner_other = lax.ppermute(corner_rows, "tensor", SWAP)
    far, near = terms_of([half], [far_slots, near_slots], [away, corner_second])[0]
    second_steps = [half - 1, 1 - half, half - 2, 2 - half]
    far, near = gate([far, near], [corner_rows, received])
    second = terms_of(second_steps, [slots], [far])
    shape = (pairs_count, 1, examples, group)
    own_cols = in_order(side, kept[:, width:].reshape(shape), received[:, width:].reshape(shape), 1)
    own_cols = own_cols.reshape(all_examples, group).astype(jnp.float32)
    far_ahead = lax.ppermute(far, "dp", ahead)
    near_back = lax.ppermute(near, "dp", back)
    total = far_count + near_count
    going = add_terms(second[0][0], [(far_ahead, 0)], 0, total, group)
    coming = add_terms(second[1][0], [(near_back, far_count)], 0, total, group)

    solved, first_pairs = solve(place, pairs_count, corner_rows, corner_other, kept, received, [going, coming])
    pieces = spread_back(place, stored, solved, owners, group)
    later_steps = [s for step in range(half - 3, 0, -1) for s in (step, -step)] + [0]
    for step in range(half - 2, 0, -1):
        came_ahead = lax.ppermute(going, "dp", ahead)
        came_back = lax.ppermute(coming, "dp", back)
        if step == half - 2:
            (own_ahead,), (own_back,) = second[2:]
            token = [pieces[0]]
        else:
            index = later_steps.index(step)
            (own_ahead,), (own_back,) = later[index : index + 2]
            token = came[1:]
        if step == 1:
            far_going = add_terms(own_ahead, [(came_ahead, 0)], 0, far_count, group, token)
            far_coming = add_terms(own_back, [(came_back, 0)], 0, far_count, group, token)
            terms, away = sum_pieces(place, came, [far_going, far_coming])
            terms_other = pair_swap(away, owners)
            near_going = add_terms(own_ahead, [(came_ahead, 0)], far_count, near_count, group, [away])
            near_coming = add_terms(own_back, [(came_back, 0)], far_count, near_count, group, [away])
        else:
            going = add_terms(own_ahead, [(came_ahead, 0)], 0, total, group, token)
            coming = add_terms(own_back, [(came_back, 0)], 0, total, group, token)
        if step == half - 2:
            later = terms_of(later_steps, [slots], [going, coming])
            came = [pieces[0]] + [far_shift(pieces[index], index, owners) for index in range(1, pairs_count)]
    far_sums = [lax.ppermute(far_going, "dp", ahead), lax.ppermute(far_coming, "dp", back)]
    near_sums = [lax.ppermute(near_going, "dp", ahead), lax.ppermute(near_coming, "dp", back)]

    far = close_window(later[-1][0], 0, *far_sums, far_slots, group)
    near = close_window(later[-1][0], far_count, *near_sums, near_slots, group, [far[0]])
    turned = {}
    for (found, slots) in ((far, far_slots), (near, near_slots)):
        chips = [chip for chip in pairs_of(slots) if chip[0] != 0]
        for (offset, _, _), block in zip(chips, found[1:]):
            turned[offset] = block
    shifted = {
        offset: lax.ppermute(turned[offset], "dp", ring.shift(offset))
        for offset in [half] + ring.offsets
    }
    came = [shifted[offset] for offset in ring.offsets + [half]]
    blocks = jnp.concatenate([far[0], near[0]] + came, axis=0)
    send_table, final_table = assembly_tables(ring, far_slots + near_slots, d, t)
    send = for_sibling(send_table, blocks, group)
    other = lax.ppermute(send, "tensor", SWAP)

    pairs = pair_products(place, own_cols, first_pairs, terms, terms_other, solved, [shifted[ring.offsets[0]]])
    bit = owners // 2
    while bit >= 1:
        kept_rows = jnp.where((d & bit) == 0, pairs[: pairs.shape[0] // 2], pairs[pairs.shape[0] // 2 :])
        sent_rows = jnp.where((d & bit) == 0, pairs[pairs.shape[0] // 2 :], pairs[: pairs.shape[0] // 2])
        pairs = kept_rows + lax.ppermute(sent_rows, "dp", [(index, index ^ bit) for index in range(owners)])
        bit //= 2
    pairs = pairs + lax.ppermute(pairs, "tensor", SWAP)
    chosen = (query_ids[:, None] == jnp.arange(all_examples, dtype=jnp.int32)[None, :]).astype(jnp.float32)
    scores = lax.dot_general(chosen, pairs, (((1,), (1,)), ((), ())), precision=EXACT, preferred_element_type=jnp.float32) / R
    return finish(place, final_table, blocks, other, half, group), scores


def solution(mesh):
    placed = (
        P(("groups", "dp"), "tensor"),
        P(("groups", "dp"), "tensor"),
        P("tensor", None),
        P("tensor", None),
        P(("groups", "dp"), None),
        P(("groups", "dp")),
        P("groups"),
    )
    ring = Ring(mesh)

    def program(*args):
        return local(ring, *args)

    return jax.shard_map(
        program,
        mesh=mesh,
        in_specs=placed,
        out_specs=(P(("groups", "dp"), "tensor"), P("groups", "dp")),
        check_vma=False,
    )
```

```python
import jax
import jax.numpy as jnp
from jax import lax
from jax.experimental import pallas as pl
from jax.experimental.pallas import tpu as pltpu
from jax.sharding import PartitionSpec as P

R = 64
SEQ = 16
damping = 1.0
EXACT = lax.Precision.HIGHEST
SWAP = [(0, 1), (1, 0)]
VMEM_BYTES = 56 * 1024 * 1024
SMALL_BYTES = 12 * 1024 * 1024
LIGHT = pl.CostEstimate(flops=10**6, bytes_accessed=10**5, transcendentals=0)
ANYWHERE = pl.BlockSpec(memory_space=pl.ANY)
MAIN = pl.BlockSpec(memory_space=pltpu.HBM)
FAST = pl.BlockSpec(memory_space=pltpu.VMEM)


class Ring:
    def __init__(self, mesh):
        self.count = mesh.shape["dp"]
        self.half = self.count // 2
        coords = [getattr(device, "coords", None) for device in mesh.devices[0, :, 0]]
        self.folded = False
        if None not in coords:
            moving = [axis for axis in range(3) if len({place[axis] for place in coords}) > 1]
            fast = [axis for axis in moving if coords[0][axis] != coords[1][axis]]
            self.folded = len(moving) == 2 and len(fast) == 1 and len({place[fast[0]] for place in coords}) == 2
        reach = [0, 0]
        self.offsets = []
        for distance in range(self.half - 1, 0, -1):
            side = 0 if reach[0] <= reach[1] else 1
            reach[side] += distance
            self.offsets.append(distance if side == 0 else -distance)

    def index_at(self, position):
        if isinstance(position, int):
            position = position % self.count
            if not self.folded:
                return position
            return 2 * position if position < self.half else 2 * (self.count - 1 - position) + 1
        position = lax.rem(position + 2 * self.count, self.count)
        if not self.folded:
            return position
        return jnp.where(position < self.half, 2 * position, 2 * (self.count - 1 - position) + 1)

    def position_of(self, index):
        if not self.folded:
            return index
        return jnp.where(lax.rem(index, 2) == 0, index // 2, self.count - 1 - index // 2)

    def shift(self, step):
        return [(self.index_at(p), self.index_at(p + step)) for p in range(self.count)]


def lead_dot(left, right, precision=None):
    return lax.dot_general(
        left, right, (((0,), (0,)), ((), ())), precision=precision, preferred_element_type=jnp.float32
    )


def exact_dot(left, right):
    return jnp.dot(left, right, precision=EXACT, preferred_element_type=jnp.float32)


def pairs_of(slots):
    found = []
    for index, (offset, core) in enumerate(slots):
        if core is None:
            found.append((offset, 1, index))
        elif core == 0:
            found.append((offset, 2, index))
    return found


def window_terms(ring, place, stored, vectors, group, steps, parts, after=()):
    rows, full = stored.shape
    new_rows = vectors.shape[0]
    taps = jnp.array(steps, jnp.int32)
    blocks_in_all = sum(len(slots) for slots in parts)
    chunk = rows // 4

    width = blocks_in_all * group
    widths = [len(slots) * group for slots in parts]

    def kernel(place_ref, step_ref, stored_ref, vectors_ref, *refs):
        outs, (held, total, made, arrived, left_for) = refs[len(after) : -5], refs[-5:]
        i = pl.program_id(0)
        slot = lax.rem(i, 2)
        owner = lax.rem(ring.position_of(place_ref[0]) + step_ref[i] + ring.count, ring.count)
        core = place_ref[1]

        def load(index):
            rows_of = pl.ds(index * chunk, chunk)
            return pltpu.make_async_copy(stored_ref.at[rows_of], held.at[rows_of], arrived.at[index])

        def leave(step):
            copies, base = [], 0
            for part, columns in enumerate(widths):
                out_ref = outs[step * len(parts) + part]
                source = made.at[step % 2, :, pl.ds(base, columns)]
                copies.append(pltpu.make_async_copy(source, out_ref, left_for.at[step % 2, part]))
                base += columns
            return copies

        @pl.when(i == 0)
        def _():
            for index in range(4):
                load(index).start()

        for step in range(2, len(steps)):

            @pl.when(i == step)
            def _():
                for copy in leave(step - 2):
                    copy.wait()

        left = pl.ds(pl.multiple_of((2 * ring.index_at(owner) + core) * group, group), group)
        chips, base = [], 0
        for slots in parts:
            for offset, blocks, first in pairs_of(slots):
                column = 2 * ring.index_at(owner + offset)
                if blocks == 1:
                    column = column + jnp.where(owner < ring.half, core, 1 - core)
                right = pl.ds(pl.multiple_of(column * group, blocks * group), blocks * group)
                chips.append((right, slice((base + first) * group, (base + first + blocks) * group)))
            base += len(slots)
        turned_new = vectors_ref[:, left].T

        @pl.when(i == 0)
        def _():
            for right, here in chips:
                total[:, here] = jnp.dot(turned_new, vectors_ref[:, right], preferred_element_type=jnp.float32)
            for index in range(4):
                load(index).wait()
                rows_of = slice(index * chunk, (index + 1) * chunk)
                turned = held[rows_of, left].T
                for right, here in chips:
                    added = total[:, here] + jnp.dot(turned, held[rows_of, right], preferred_element_type=jnp.float32)
                    if index < 3:
                        total[:, here] = added
                    else:
                        made[0, :, here] = added.astype(jnp.bfloat16)

        if len(steps) > 1:

            @pl.when(i > 0)
            def _():
                turned = held[:, left].T
                for right, here in chips:
                    added = jnp.dot(turned, held[:, right], preferred_element_type=jnp.float32)
                    added = added + jnp.dot(turned_new, vectors_ref[:, right], preferred_element_type=jnp.float32)
                    made[slot, :, here] = added.astype(jnp.bfloat16)

        for step in range(len(steps)):

            @pl.when(i == step)
            def _():
                for copy in leave(step):
                    copy.start()

        @pl.when(i == len(steps) - 1)
        def _():
            for step in range(max(len(steps) - 2, 0), len(steps)):
                for copy in leave(step):
                    copy.wait()

    found = pl.pallas_call(
        kernel,
        grid_spec=pltpu.PrefetchScalarGridSpec(
            num_scalar_prefetch=2,
            grid=(len(steps),),
            in_specs=[MAIN, pl.BlockSpec((new_rows, full), lambda i, a, b: (0, 0))] + [ANYWHERE] * len(after),
            out_specs=[MAIN] * (len(steps) * len(parts)),
            scratch_shapes=[
                pltpu.VMEM((rows, full), jnp.bfloat16),
                pltpu.VMEM((group, width), jnp.float32),
                pltpu.VMEM((2, group, width), jnp.bfloat16),
                pltpu.SemaphoreType.DMA((4,)),
                pltpu.SemaphoreType.DMA((2, len(parts))),
            ],
        ),
        out_shape=[jax.ShapeDtypeStruct((group, columns), jnp.bfloat16) for _ in steps for columns in widths],
        compiler_params=pltpu.CompilerParams(vmem_limit_bytes=VMEM_BYTES),
        cost_estimate=LIGHT,
        name="window_terms",
    )(place, taps, stored, vectors, *after)
    return [found[step * len(parts) : (step + 1) * len(parts)] for step in range(len(steps))]


def add_terms(terms, arrived, base, count, group, after=()):
    def kernel(terms_ref, *refs):
        out_ref, own, done = refs[-3:]
        fetch = pltpu.make_async_copy(terms_ref.at[:, pl.ds(base * group, count * group)], own, done)
        fetch.start()
        fetch.wait()
        for k in range(count):
            cols = slice(k * group, (k + 1) * group)
            total = own[:, cols].astype(jnp.float32)
            for ref, (array, first) in zip(refs, arrived):
                place = base + k - first
                if 0 <= place < array.shape[1] // group:
                    total = total + ref[:, place * group : (place + 1) * group].astype(jnp.float32)
            out_ref[:, cols] = total.astype(jnp.bfloat16)

    return pl.pallas_call(
        kernel,
        in_specs=[MAIN] + [FAST] * len(arrived) + [ANYWHERE] * len(after),
        out_specs=FAST,
        out_shape=jax.ShapeDtypeStruct((group, count * group), jnp.bfloat16),
        scratch_shapes=[pltpu.VMEM((group, count * group), jnp.bfloat16), pltpu.SemaphoreType.DMA],
        compiler_params=pltpu.CompilerParams(vmem_limit_bytes=SMALL_BYTES),
        cost_estimate=LIGHT,
        name="add_terms",
    )(terms, *[array for array, _ in arrived], *after)


def gate(values, after):
    def kernel(*refs):
        pass

    return pl.pallas_call(
        kernel,
        in_specs=[MAIN] * len(values) + [ANYWHERE] * len(after),
        out_specs=[MAIN] * len(values),
        out_shape=[jax.ShapeDtypeStruct(value.shape, value.dtype) for value in values],
        input_output_aliases={index: index for index in range(len(values))},
        compiler_params=pltpu.CompilerParams(vmem_limit_bytes=SMALL_BYTES),
        cost_estimate=LIGHT,
        name="gate",
    )(*values, *after)


def close_window(terms, base, ahead, back, slots, group, after=()):
    count = len(slots)
    chips = [chip for chip in pairs_of(slots) if chip[0] != 0]
    def kernel(terms_ref, ahead_ref, back_ref, *refs):
        blocks_ref, turned_refs, (own, done) = refs[len(after)], refs[len(after) + 1 : -2], refs[-2:]
        fetch = pltpu.make_async_copy(terms_ref.at[:, pl.ds(base * group, count * group)], own, done)
        fetch.start()
        fetch.wait()
        for k in range(count):
            cols = slice(k * group, (k + 1) * group)
            total = own[:, cols].astype(jnp.float32)
            total = total + ahead_ref[:, cols].astype(jnp.float32) + back_ref[:, cols].astype(jnp.float32)
            total = total.astype(jnp.bfloat16)
            blocks_ref[k] = total
            for (_, blocks, first), turned_ref in zip(chips, turned_refs):
                if first <= k < first + blocks:
                    turned_ref[k - first] = total.T

    sizes = [count] + [blocks for _, blocks, _ in chips]
    return pl.pallas_call(
        kernel,
        in_specs=[MAIN, FAST, FAST] + [ANYWHERE] * len(after),
        out_specs=[FAST] * len(sizes),
        out_shape=[jax.ShapeDtypeStruct((size, group, group), jnp.bfloat16) for size in sizes],
        scratch_shapes=[pltpu.VMEM((group, count * group), jnp.bfloat16), pltpu.SemaphoreType.DMA],
        compiler_params=pltpu.CompilerParams(vmem_limit_bytes=SMALL_BYTES),
        cost_estimate=LIGHT,
        name="close_window",
    )(terms, ahead, back, *after)


def rough_dot(left, right):
    return jnp.dot(left.astype(jnp.bfloat16), right.astype(jnp.bfloat16), preferred_element_type=jnp.float32)


def split_terms(value):
    high = value.astype(jnp.bfloat16)
    value = value - high.astype(jnp.float32)
    middle = value.astype(jnp.bfloat16)
    value = value - middle.astype(jnp.float32)
    return high, middle, value.astype(jnp.bfloat16)


def identity(size):
    rows = lax.broadcasted_iota(jnp.int32, (size, size), 0)
    cols = lax.broadcasted_iota(jnp.int32, (size, size), 1)
    return (rows == cols).astype(jnp.float32)


def eliminate(matrix_ref, right_ref, out_ref, work, block):
    size = matrix_ref.shape[0]
    work[...] = matrix_ref[...]
    out_ref[...] = right_ref[...]
    eye = identity(block)
    for start in range(0, size, block):
        here = slice(start, start + block)
        rest = slice(start + block, size)
        corner = work[here, here]
        norm = jnp.max(jnp.sum(jnp.abs(corner), axis=0))

        def unfinished(state):
            return jnp.logical_and(state[0] < 40, state[1] > 5e-5)

        def improve(state):
            step, _, inverse = state
            better = inverse + exact_dot(inverse, eye - exact_dot(work[here, here], inverse))
            left_over = eye - exact_dot(work[here, here], better)
            return step + 1, jnp.max(jnp.abs(left_over)), better

        found = lax.while_loop(unfinished, improve, (jnp.int32(0), jnp.float32(1.0), eye / norm))[2]
        found = found + exact_dot(found, eye - exact_dot(work[here, here], found))
        solved = exact_dot(found, out_ref[here, :])
        out_ref[here, :] = solved
        if start + block < size:
            across = exact_dot(found, work[here, rest])
            down = work[rest, here]
            work[rest, rest] = work[rest, rest] - exact_dot(down, across)
            out_ref[rest, :] = out_ref[rest, :] - exact_dot(down, solved)
            work[here, rest] = across
    for start in range(size - 2 * block, -1, -block):
        here = slice(start, start + block)
        rest = slice(start + block, size)
        out_ref[here, :] = out_ref[here, :] - exact_dot(work[here, rest], out_ref[rest, :])


def solve(place, pairs_count, mine, other, kept, came, after=()):
    group, width = mine.shape
    examples = 2 * kept.shape[0]
    size = kept.shape[0] // pairs_count

    def kernel(place_ref, mine_ref, other_ref, kept_ref, came_ref, *refs):
        out_ref, pairs_ref, matrix, right, power, inverse, first_ref = refs[len(after) :]
        for start in range(0, kept_ref.shape[0], size):
            near, far = kept_ref[start : start + size, :width], came_ref[start : start + size, :width]
            even = lax.rem(place_ref[0], 2) == 0
            first_ref[2 * start : 2 * start + size, :] = jnp.where(even, near, far)
            first_ref[2 * start + size : 2 * start + 2 * size, :] = jnp.where(even, far, near)
        eye = identity(width)
        t = place_ref[1]
        matrix[pl.ds(pl.multiple_of(t * group, group), group), :] = mine_ref[...]
        matrix[pl.ds(pl.multiple_of((1 - t) * group, group), group), :] = other_ref[...]
        turned = first_ref[...].T
        full = matrix[...] + jnp.dot(turned, first_ref[...], preferred_element_type=jnp.float32) + damping * eye
        diagonal = full * eye
        rows_scale = lax.rsqrt(jnp.sum(diagonal, axis=1, keepdims=True))
        cols_scale = lax.rsqrt(jnp.sum(diagonal, axis=0, keepdims=True))
        full = full * rows_scale * cols_scale
        matrix[...] = full
        right[...] = turned.astype(jnp.float32) * rows_scale

        sums = jnp.max(jnp.sum(jnp.abs(full), axis=0))
        squared = rough_dot(full, full)
        norm = jnp.sqrt(jnp.max(jnp.sum(jnp.abs(squared), axis=0)) + sums * sums / 128)
        start = eye - full / norm
        inverse[...] = eye + start
        power[...] = start.astype(jnp.bfloat16)
        for _ in range(7):
            raised = jnp.dot(power[...], power[...], preferred_element_type=jnp.float32).astype(jnp.bfloat16)
            power[...] = raised
            held = inverse[...]
            inverse[...] = held + jnp.dot(held.astype(jnp.bfloat16), raised, preferred_element_type=jnp.float32)
        power[...] = (inverse[...] / norm).astype(jnp.bfloat16)

        largest = jnp.max(jnp.abs(right[...]))
        out_ref[...] = jnp.dot(power[...], right[...].astype(jnp.bfloat16), preferred_element_type=jnp.float32)

        def unfinished(state):
            return jnp.logical_and(state[0] < 12, jnp.logical_not(state[1] <= 5e-5 * largest))

        def refine(state):
            left_over = right[...] - exact_dot(matrix[...], out_ref[...])
            change = jnp.dot(power[...], left_over.astype(jnp.bfloat16), preferred_element_type=jnp.float32)
            out_ref[...] = out_ref[...] + change
            return state[0] + 1, jnp.max(jnp.abs(left_over))

        worst = lax.while_loop(unfinished, refine, (jnp.int32(0), 1.0 + largest))[1]

        @pl.when(jnp.logical_not(worst <= 5e-5 * largest))
        def _():
            eliminate(matrix, right, out_ref, inverse, 128)

        solved = out_ref[...] * rows_scale
        out_ref[...] = solved
        pairs = jnp.zeros((examples, examples), jnp.float32)
        for term in split_terms(solved):
            pairs = pairs + jnp.dot(first_ref[...], term, preferred_element_type=jnp.float32)
        pairs_ref[...] = pairs

    whole = pl.BlockSpec(memory_space=pltpu.VMEM)
    return pl.pallas_call(
        kernel,
        in_specs=[pl.BlockSpec(memory_space=pltpu.SMEM)] + [whole] * 4 + [ANYWHERE] * len(after),
        out_shape=[
            jax.ShapeDtypeStruct((width, examples), jnp.float32),
            jax.ShapeDtypeStruct((examples, examples), jnp.float32),
        ],
        scratch_shapes=[
            pltpu.VMEM((width, width), jnp.float32),
            pltpu.VMEM((width, examples), jnp.float32),
            pltpu.VMEM((width, width), jnp.bfloat16),
            pltpu.VMEM((width, width), jnp.float32),
            pltpu.VMEM((examples, width), jnp.bfloat16),
        ],
        compiler_params=pltpu.CompilerParams(vmem_limit_bytes=VMEM_BYTES),
        cost_estimate=LIGHT,
        name="solve",
    )(place, mine, other, kept, came, *after)


def spread_back(place, stored, solved, owners, group, after=()):
    rows = stored.shape[0]
    width, examples = solved.shape
    pairs = owners // 2

    def kernel(place_ref, first_ref, solved_ref, *refs):
        cols, outs = refs[:owners], refs[owners + len(after) : -1]
        refs[-1][...] = jnp.zeros_like(refs[-1])
        total = jnp.zeros((rows, examples), jnp.float32)
        for term in split_terms(solved_ref[...]):
            total = total + jnp.dot(first_ref[...], term, preferred_element_type=jnp.float32)
        terms = jnp.concatenate(split_terms(total.T)[:2], axis=0)
        for index in range(owners):
            product = jnp.dot(terms, cols[index][...], preferred_element_type=jnp.float32)
            outs[index // 2][index % 2] = (product[:examples] + product[examples:]).astype(jnp.bfloat16)

    def owner(index, ref):
        return 2 * lax.rem(ref[0] // 2 + index // 2, pairs) + index % 2

    return pl.pallas_call(
        kernel,
        grid_spec=pltpu.PrefetchScalarGridSpec(
            num_scalar_prefetch=1,
            grid=(1,),
            in_specs=[
                pl.BlockSpec((rows, width), lambda i, ref: (0, 0)),
                pl.BlockSpec((width, examples), lambda i, ref: (0, 0)),
            ]
            + [
                pl.BlockSpec((rows, group), lambda i, ref, index=index: (0, 2 * owner(index, ref) + ref[1]))
                for index in range(owners)
            ]
            + [ANYWHERE] * len(after),
            out_specs=[pl.BlockSpec((2, examples, group), lambda i, ref: (0, 0, 0))] * pairs
            + [pl.BlockSpec((8, 128), lambda i, ref: (0, 0))],
        ),
        out_shape=[jax.ShapeDtypeStruct((2, examples, group), jnp.bfloat16)] * pairs
        + [jax.ShapeDtypeStruct((8, 128), jnp.float32)],
        compiler_params=pltpu.CompilerParams(vmem_limit_bytes=VMEM_BYTES),
        cost_estimate=LIGHT,
        name="spread_back",
    )(place, stored, solved, *([stored] * owners), *after)


def sum_pieces(place, came, after=()):
    _, examples, group = came[0].shape

    def kernel(place_ref, *refs):
        mine_ref, away_ref = refs[-2:]
        side = lax.rem(place_ref[0], 2)
        totals = [sum(ref[half].astype(jnp.float32) for ref in refs[: len(came)]) for half in (0, 1)]
        mine_ref[...] = jnp.where(side == 0, totals[0], totals[1])
        away_ref[...] = jnp.where(side == 0, totals[1], totals[0]).astype(jnp.bfloat16)

    return pl.pallas_call(
        kernel,
        in_specs=[pl.BlockSpec(memory_space=pltpu.SMEM)] + [FAST] * len(came) + [ANYWHERE] * len(after),
        out_specs=[FAST, FAST],
        out_shape=[
            jax.ShapeDtypeStruct((examples, group), jnp.float32),
            jax.ShapeDtypeStruct((examples, group), jnp.bfloat16),
        ],
        compiler_params=pltpu.CompilerParams(vmem_limit_bytes=SMALL_BYTES),
        cost_estimate=LIGHT,
        name="sum_pieces",
    )(place, *came, *after)


def pair_products(place, own_cols, first_pairs, mine, other, solved, after=()):
    examples, group = own_cols.shape

    def kernel(place_ref, own_ref, first_ref, mine_ref, other_ref, solved_ref, *refs):
        g = 2 * place_ref[0] + place_ref[1]
        own = own_ref[...]
        damped = solved_ref[pl.ds(pl.multiple_of(place_ref[1] * group, group), group), :].T
        rest = own - lax.dot_general(
            first_ref[...], own, (((0,), (0,)), ((), ())), precision=EXACT, preferred_element_type=jnp.float32
        )
        rest = rest - mine_ref[...] - other_ref[...].astype(jnp.float32) - jnp.where(g < 2, damping * damped, 0.0)
        products = lax.dot_general(
            rest, rest, (((1,), (1,)), ((), ())), precision=EXACT, preferred_element_type=jnp.float32
        )
        refs[-1][...] = products + jnp.where(g == 0, first_ref[...], 0.0)

    return pl.pallas_call(
        kernel,
        in_specs=[pl.BlockSpec(memory_space=pltpu.SMEM)] + [FAST] * 5 + [ANYWHERE] * len(after),
        out_specs=FAST,
        out_shape=jax.ShapeDtypeStruct((examples, examples), jnp.float32),
        compiler_params=pltpu.CompilerParams(vmem_limit_bytes=SMALL_BYTES),
        cost_estimate=LIGHT,
        name="pair_products",
    )(place, own_cols, first_pairs, mine, other, solved, *after)


def assembly_tables(ring, slots, d, t):
    start = [0] * ring.count
    arrived = [0] * ring.count
    for offset, _, first in pairs_of(slots):
        start[offset % ring.count] = first
    place = len(slots)
    for offset in ring.offsets:
        start[-offset % ring.count] = place
        arrived[-offset % ring.count] = 1
        place += 2
    here = ring.position_of(d)
    early = here < ring.half

    def look_up(values, offset):
        found = jnp.zeros_like(offset)
        for index, value in enumerate(values):
            if value:
                found = jnp.where(offset == index, value, found)
        return found

    def offsets_of(chips):
        return lax.rem(ring.position_of(chips) - here + 2 * ring.count, ring.count)

    def fetch(offset, j):
        own = (j == t) == early
        quarter = jnp.where(own, start[ring.half], place)
        return jnp.where(offset == ring.half, quarter, look_up(start, offset) + j)

    chips = jnp.arange(ring.half, dtype=jnp.int32)
    j = jnp.arange(2, dtype=jnp.int32)[None, :]
    send = fetch(offsets_of((1 - t) * ring.half + chips)[:, None], j)
    offset = offsets_of(t * ring.half + chips)[:, None, None]
    r = jnp.arange(2, dtype=jnp.int32)[None, :, None]
    u = jnp.arange(2, dtype=jnp.int32)[None, None, :]
    by_columns = jnp.where(offset == ring.half, early.astype(jnp.int32), look_up(arrived, offset)) == 1
    j = jnp.where(by_columns, r, u)
    local = fetch(offset, j)
    other = 2 * chips[:, None, None] + j
    mine = (jnp.where(by_columns, u, r) == t).astype(jnp.int32)
    final = jnp.stack([local, other, mine]).reshape(-1)
    return send.reshape(-1).astype(jnp.int32), final.astype(jnp.int32)


def for_sibling(table, blocks, group):
    total = table.shape[0]
    wide = min(4, total)

    def kernel(table_ref, *refs):
        for k in range(wide):
            refs[-1][k] = refs[k][0]

    return pl.pallas_call(
        kernel,
        grid_spec=pltpu.PrefetchScalarGridSpec(
            num_scalar_prefetch=1,
            grid=(total // wide,),
            in_specs=[
                pl.BlockSpec((1, group, group), lambda c, ref, k=k: (ref[wide * c + k], 0, 0)) for k in range(wide)
            ],
            out_specs=pl.BlockSpec((wide, group, group), lambda c, ref: (c, 0, 0)),
        ),
        out_shape=jax.ShapeDtypeStruct((total, group, group), jnp.bfloat16),
        compiler_params=pltpu.CompilerParams(vmem_limit_bytes=SMALL_BYTES),
        cost_estimate=LIGHT,
        name="for_sibling",
    )(table, *([blocks] * wide))


def finish(place, table, blocks, other, half, group):
    wide = half // 2
    total = 4 * half

    def at(kind, r, c, k, u, ref):
        return ref[kind * total + 4 * (wide * c + k) + 2 * r + u]

    def spec(kind, k, u):
        return pl.BlockSpec((1, group, group), lambda r, c, ref, place: (at(kind, r, c, k, u, ref), 0, 0))

    order = [(k, u) for k in range(wide) for u in (0, 1)]

    def kernel(table_ref, place_ref, *refs):
        r, c = pl.program_id(0), pl.program_id(1)
        out_ref = refs[-1]
        shape = (group, group)
        gap = lax.broadcasted_iota(jnp.int32, shape, 1) - lax.broadcasted_iota(jnp.int32, shape, 0)
        for index, (k, u) in enumerate(order):
            cols = slice(index * group, (index + 1) * group)
            chip = place_ref[1] * half + wide * c + k
            apart = (2 * place_ref[0] + r - 2 * chip - u) * group
            added = jnp.where(gap == apart, jnp.float32(damping), jnp.float32(0.0))
            mine = at(2, r, c, k, u, table_ref) == 1

            @pl.when(mine)
            def _():
                out_ref[:, cols] = added + refs[index][0].astype(jnp.float32)

            @pl.when(jnp.logical_not(mine))
            def _():
                out_ref[:, cols] = added + refs[len(order) + index][0].astype(jnp.float32)

    return pl.pallas_call(
        kernel,
        grid_spec=pltpu.PrefetchScalarGridSpec(
            num_scalar_prefetch=2,
            grid=(2, 2),
            in_specs=[spec(0, k, u) for k, u in order] + [spec(1, k, u) for k, u in order],
            out_specs=pl.BlockSpec((group, 2 * wide * group), lambda r, c, ref, place: (r, c)),
        ),
        out_shape=jax.ShapeDtypeStruct((2 * group, 2 * half * group), jnp.float32),
        compiler_params=pltpu.CompilerParams(vmem_limit_bytes=SMALL_BYTES),
        cost_estimate=LIGHT,
        name="finish",
    )(table, place, *([blocks] * len(order)), *([other] * len(order)))


def in_order(index, mine, other, axis):
    return jnp.where(
        index == 0,
        jnp.concatenate([mine, other], axis=axis),
        jnp.concatenate([other, mine], axis=axis),
    )


def pair_swap(value, count):
    return lax.ppermute(value, "dp", [(index, index ^ 1) for index in range(count)])


def far_shift(value, step, count):
    return lax.ppermute(value, "dp", [(index, (index + 2 * step) % count) for index in range(count)])


def exchange_pairs(slice_of, pair, count):
    pairs = count // 2
    came = [slice_of(pair)]
    for step in range(1, pairs):
        came.append(far_shift(slice_of(lax.rem(pair + step, pairs)), step, count))
    return came


def natural(came, pair):
    pairs = len(came)
    pieces = []
    for index in range(pairs):
        behind = lax.rem(pair - index + pairs, pairs)
        piece = came[0]
        for step in range(1, pairs):
            piece = jnp.where(behind == step, came[step], piece)
        pieces.append(piece)
    return pieces


def scatter_pairs(value, pair, count):
    size = value.shape[0] // (count // 2)

    def slice_of(index):
        return lax.dynamic_slice_in_dim(value, index * size, size, 0)

    return sum(piece.astype(jnp.float32) for piece in exchange_pairs(slice_of, pair, count))


def local(ring, activations, out_grads, proj_in, proj_out, stored, counts, query_ids):
    owners = ring.count
    full = stored.shape[1]
    width = full // owners
    group = width // 2
    half = ring.half
    t = lax.axis_index("tensor")
    d = lax.axis_index("dp")
    pair, side = d // 2, lax.rem(d, 2)
    g = 2 * d + t
    place = jnp.stack([d, t]).astype(jnp.int32)

    pairs_count = owners // 2
    first_stored = stored[:, :width]
    corner_rows = lead_dot(lax.dynamic_slice_in_dim(first_stored, t * group, group, 1), first_stored)
    activations, out_grads, corner_rows = lax.optimization_barrier((activations, out_grads, corner_rows))
    corner_payload = scatter_pairs(corner_rows, pair, owners)

    sides = jnp.concatenate(
        [
            jnp.dot(activations, proj_in, preferred_element_type=jnp.float32),
            jnp.dot(out_grads, proj_out, preferred_element_type=jnp.float32),
        ],
        axis=1,
    )
    sides = sides + lax.ppermute(sides, "tensor", SWAP)

    examples = counts.shape[0]
    all_examples = examples * owners
    rank = proj_in.shape[1]
    position = jnp.arange(SEQ, dtype=jnp.int32)[None, :]
    weights = jnp.where(
        position < counts[:, None], 1.0 / counts.astype(jnp.float32)[:, None], jnp.float32(0.0)
    )
    outer = jnp.einsum(
        "es,esi,esj->eij",
        weights,
        sides[:, :rank].reshape(examples, SEQ, rank),
        sides[:, rank:].reshape(examples, SEQ, rank),
        precision=EXACT,
    )
    vectors = outer.reshape(examples, full).astype(jnp.bfloat16)

    def columns_for(index):
        groups = [lax.dynamic_slice_in_dim(vectors, (4 * index + 2 * s + t) * group, group, 1) for s in (0, 1)]
        return jnp.concatenate([vectors[:, :width]] + groups, axis=1)

    payloads = [columns_for(lax.rem(pair + step, pairs_count)) for step in range(pairs_count)]

    split = (len(ring.offsets) + 1) // 2
    far_slots = [(half, None)]
    for offset in ring.offsets[:split]:
        far_slots += [(offset, 0), (offset, 1)]
    near_slots = []
    for offset in ring.offsets[split:] + [0]:
        near_slots += [(offset, 0), (offset, 1)]

    slots = far_slots + near_slots
    far_count, near_count = len(far_slots), len(near_slots)
    ahead, back = ring.shift(1), ring.shift(-1)

    def terms_of(steps, parts, after=()):
        return window_terms(ring, place, stored, vectors, group, steps, parts, after)

    came = [payloads[0]] + [far_shift(payloads[step], step, owners) for step in range(1, pairs_count)]
    came = jnp.concatenate(natural(came, pair), axis=0)
    second_group = jnp.concatenate([came[:, :width], came[:, width + group :]], axis=1)
    first_group = came[:, : width + group]
    kept = jnp.where(side == 0, first_group, second_group)
    away = jnp.where(side == 0, second_group, first_group)
    received = pair_swap(away, owners)
    corner_second = corner_payload + pair_swap(corner_payload, owners)
    corner_rows = [corner_second] + [far_shift(corner_second, step, owners) for step in range(1, pairs_count)]
    corner_rows = jnp.concatenate(natural(corner_rows, pair), axis=0)
    corner_other = lax.ppermute(corner_rows, "tensor", SWAP)
    far, near = terms_of([half], [far_slots, near_slots], [away, corner_second])[0]
    second_steps = [half - 1, 1 - half, half - 2, 2 - half]
    far, near = gate([far, near], [corner_rows, received])
    second = terms_of(second_steps, [slots], [far])
    shape = (pairs_count, 1, examples, group)
    own_cols = in_order(side, kept[:, width:].reshape(shape), received[:, width:].reshape(shape), 1)
    own_cols = own_cols.reshape(all_examples, group).astype(jnp.float32)
    far_ahead = lax.ppermute(far, "dp", ahead)
    near_back = lax.ppermute(near, "dp", back)
    total = far_count + near_count
    going = add_terms(second[0][0], [(far_ahead, 0)], 0, total, group)
    coming = add_terms(second[1][0], [(near_back, far_count)], 0, total, group)

    solved, first_pairs = solve(place, pairs_count, corner_rows, corner_other, kept, received, [going, coming])
    *pieces, spread_done = spread_back(place, stored, solved, owners, group)
    later_steps = [s for step in range(half - 3, 0, -1) for s in (step, -step)] + [0]
    for step in range(half - 2, 0, -1):
        came_ahead = lax.ppermute(going, "dp", ahead)
        came_back = lax.ppermute(coming, "dp", back)
        if step == half - 2:
            (own_ahead,), (own_back,) = second[2:]
            token = [spread_done]
        else:
            index = later_steps.index(step)
            (own_ahead,), (own_back,) = later[index : index + 2]
            token = came[1:]
        if step == 1:
            far_going = add_terms(own_ahead, [(came_ahead, 0)], 0, far_count, group, token)
            far_coming = add_terms(own_back, [(came_back, 0)], 0, far_count, group, token)
            terms, away = sum_pieces(place, came, [far_going, far_coming])
            near_going = add_terms(own_ahead, [(came_ahead, 0)], far_count, near_count, group, [away])
            near_coming = add_terms(own_back, [(came_back, 0)], far_count, near_count, group, [away])
        else:
            going = add_terms(own_ahead, [(came_ahead, 0)], 0, total, group, token)
            coming = add_terms(own_back, [(came_back, 0)], 0, total, group, token)
        if step == half - 2:
            later = terms_of(later_steps, [slots], [going, coming])
            came = [pieces[0]] + [far_shift(pieces[index], index, owners) for index in range(1, pairs_count)]
    far_sums = [lax.ppermute(far_going, "dp", ahead), lax.ppermute(far_coming, "dp", back)]
    near_sums = [lax.ppermute(near_going, "dp", ahead), lax.ppermute(near_coming, "dp", back)]

    far = close_window(later[-1][0], 0, *far_sums, far_slots, group)
    near = close_window(later[-1][0], far_count, *near_sums, near_slots, group, [far[0]])
    turned = {}
    for (found, slots) in ((far, far_slots), (near, near_slots)):
        chips = [chip for chip in pairs_of(slots) if chip[0] != 0]
        for (offset, _, _), block in zip(chips, found[1:]):
            turned[offset] = block
    shifted = {
        offset: lax.ppermute(turned[offset], "dp", ring.shift(offset))
        for offset in [half] + ring.offsets
    }
    came = [shifted[offset] for offset in ring.offsets + [half]]
    blocks = jnp.concatenate([far[0], near[0]] + came, axis=0)
    send_table, final_table = assembly_tables(ring, far_slots + near_slots, d, t)
    send = for_sibling(send_table, blocks, group)
    other = lax.ppermute(send, "tensor", SWAP)

    terms_other = pair_swap(away, owners)
    pairs = pair_products(place, own_cols, first_pairs, terms, terms_other, solved, [shifted[ring.offsets[0]]])
    bit = owners // 2
    while bit >= 1:
        kept_rows = jnp.where((d & bit) == 0, pairs[: pairs.shape[0] // 2], pairs[pairs.shape[0] // 2 :])
        sent_rows = jnp.where((d & bit) == 0, pairs[pairs.shape[0] // 2 :], pairs[: pairs.shape[0] // 2])
        came_rows = lax.ppermute(sent_rows, "dp", [(index, index ^ bit) for index in range(owners)])
        if bit == owners // 2:
            (came_rows,) = gate([came_rows], [send])
        pairs = kept_rows + came_rows
        bit //= 2
    pairs = pairs + lax.ppermute(pairs, "tensor", SWAP)
    chosen = (query_ids[:, None] == jnp.arange(all_examples, dtype=jnp.int32)[None, :]).astype(jnp.float32)
    scores = lax.dot_general(chosen, pairs, (((1,), (1,)), ((), ())), precision=EXACT, preferred_element_type=jnp.float32) / R
    return finish(place, final_table, blocks, other, half, group), scores


def solution(mesh):
    placed = (
        P(("groups", "dp"), "tensor"),
        P(("groups", "dp"), "tensor"),
        P("tensor", None),
        P("tensor", None),
        P(("groups", "dp"), None),
        P(("groups", "dp")),
        P("groups"),
    )
    ring = Ring(mesh)

    def program(*args):
        return local(ring, *args)

    return jax.shard_map(
        program,
        mesh=mesh,
        in_specs=placed,
        out_specs=(P(("groups", "dp"), "tensor"), P("groups", "dp")),
        check_vma=False,
    )
```

```python
import jax
import jax.numpy as jnp
from jax import lax
from jax.experimental import pallas as pl
from jax.experimental.pallas import tpu as pltpu
from jax.sharding import PartitionSpec as P

R = 64
SEQ = 16
damping = 1.0
EXACT = lax.Precision.HIGHEST
SWAP = [(0, 1), (1, 0)]
VMEM_BYTES = 56 * 1024 * 1024
SMALL_BYTES = 12 * 1024 * 1024
LIGHT = pl.CostEstimate(flops=10**6, bytes_accessed=10**5, transcendentals=0)
ANYWHERE = pl.BlockSpec(memory_space=pl.ANY)
MAIN = pl.BlockSpec(memory_space=pltpu.HBM)
FAST = pl.BlockSpec(memory_space=pltpu.VMEM)


class Ring:
    def __init__(self, mesh):
        self.count = mesh.shape["dp"]
        self.half = self.count // 2
        coords = [getattr(device, "coords", None) for device in mesh.devices[0, :, 0]]
        self.folded = False
        if None not in coords:
            moving = [axis for axis in range(3) if len({place[axis] for place in coords}) > 1]
            fast = [axis for axis in moving if coords[0][axis] != coords[1][axis]]
            self.folded = len(moving) == 2 and len(fast) == 1 and len({place[fast[0]] for place in coords}) == 2
        reach = [0, 0]
        self.offsets = []
        for distance in range(self.half - 1, 0, -1):
            side = 0 if reach[0] <= reach[1] else 1
            reach[side] += distance
            self.offsets.append(distance if side == 0 else -distance)

    def index_at(self, position):
        if isinstance(position, int):
            position = position % self.count
            if not self.folded:
                return position
            return 2 * position if position < self.half else 2 * (self.count - 1 - position) + 1
        position = lax.rem(position + 2 * self.count, self.count)
        if not self.folded:
            return position
        return jnp.where(position < self.half, 2 * position, 2 * (self.count - 1 - position) + 1)

    def position_of(self, index):
        if not self.folded:
            return index
        return jnp.where(lax.rem(index, 2) == 0, index // 2, self.count - 1 - index // 2)

    def shift(self, step):
        return [(self.index_at(p), self.index_at(p + step)) for p in range(self.count)]


def lead_dot(left, right, precision=None):
    return lax.dot_general(
        left, right, (((0,), (0,)), ((), ())), precision=precision, preferred_element_type=jnp.float32
    )


def exact_dot(left, right):
    return jnp.dot(left, right, precision=EXACT, preferred_element_type=jnp.float32)


def pairs_of(slots):
    found = []
    for index, (offset, core) in enumerate(slots):
        if core is None:
            found.append((offset, 1, index))
        elif core == 0:
            found.append((offset, 2, index))
    return found


def window_terms(ring, place, stored, vectors, group, steps, parts, after=()):
    rows, full = stored.shape
    new_rows = vectors.shape[0]
    taps = jnp.array(steps, jnp.int32)
    blocks_in_all = sum(len(slots) for slots in parts)
    chunk = rows // 4

    width = blocks_in_all * group
    widths = [len(slots) * group for slots in parts]

    def kernel(place_ref, step_ref, stored_ref, vectors_ref, *refs):
        outs, (held, total, made, arrived, left_for) = refs[len(after) : -5], refs[-5:]
        i = pl.program_id(0)
        slot = lax.rem(i, 2)
        owner = lax.rem(ring.position_of(place_ref[0]) + step_ref[i] + ring.count, ring.count)
        core = place_ref[1]

        def load(index):
            rows_of = pl.ds(index * chunk, chunk)
            return pltpu.make_async_copy(stored_ref.at[rows_of], held.at[rows_of], arrived.at[index])

        def leave(step):
            copies, base = [], 0
            for part, columns in enumerate(widths):
                out_ref = outs[step * len(parts) + part]
                source = made.at[step % 2, :, pl.ds(base, columns)]
                copies.append(pltpu.make_async_copy(source, out_ref, left_for.at[step % 2, part]))
                base += columns
            return copies

        @pl.when(i == 0)
        def _():
            for index in range(4):
                load(index).start()

        for step in range(2, len(steps)):

            @pl.when(i == step)
            def _():
                for copy in leave(step - 2):
                    copy.wait()

        left = pl.ds(pl.multiple_of((2 * ring.index_at(owner) + core) * group, group), group)
        chips, base = [], 0
        for slots in parts:
            for offset, blocks, first in pairs_of(slots):
                column = 2 * ring.index_at(owner + offset)
                if blocks == 1:
                    column = column + jnp.where(owner < ring.half, core, 1 - core)
                right = pl.ds(pl.multiple_of(column * group, blocks * group), blocks * group)
                chips.append((right, slice((base + first) * group, (base + first + blocks) * group)))
            base += len(slots)
        turned_new = vectors_ref[:, left].T

        @pl.when(i == 0)
        def _():
            for right, here in chips:
                total[:, here] = jnp.dot(turned_new, vectors_ref[:, right], preferred_element_type=jnp.float32)
            for index in range(4):
                load(index).wait()
                rows_of = slice(index * chunk, (index + 1) * chunk)
                turned = held[rows_of, left].T
                for right, here in chips:
                    added = total[:, here] + jnp.dot(turned, held[rows_of, right], preferred_element_type=jnp.float32)
                    if index < 3:
                        total[:, here] = added
                    else:
                        made[0, :, here] = added.astype(jnp.bfloat16)

        if len(steps) > 1:

            @pl.when(i > 0)
            def _():
                turned = held[:, left].T
                for right, here in chips:
                    added = jnp.dot(turned, held[:, right], preferred_element_type=jnp.float32)
                    added = added + jnp.dot(turned_new, vectors_ref[:, right], preferred_element_type=jnp.float32)
                    made[slot, :, here] = added.astype(jnp.bfloat16)

        for step in range(len(steps)):

            @pl.when(i == step)
            def _():
                for copy in leave(step):
                    copy.start()

        @pl.when(i == len(steps) - 1)
        def _():
            for step in range(max(len(steps) - 2, 0), len(steps)):
                for copy in leave(step):
                    copy.wait()

    found = pl.pallas_call(
        kernel,
        grid_spec=pltpu.PrefetchScalarGridSpec(
            num_scalar_prefetch=2,
            grid=(len(steps),),
            in_specs=[MAIN, pl.BlockSpec((new_rows, full), lambda i, a, b: (0, 0))] + [ANYWHERE] * len(after),
            out_specs=[MAIN] * (len(steps) * len(parts)),
            scratch_shapes=[
                pltpu.VMEM((rows, full), jnp.bfloat16),
                pltpu.VMEM((group, width), jnp.float32),
                pltpu.VMEM((2, group, width), jnp.bfloat16),
                pltpu.SemaphoreType.DMA((4,)),
                pltpu.SemaphoreType.DMA((2, len(parts))),
            ],
        ),
        out_shape=[jax.ShapeDtypeStruct((group, columns), jnp.bfloat16) for _ in steps for columns in widths],
        compiler_params=pltpu.CompilerParams(vmem_limit_bytes=VMEM_BYTES),
        cost_estimate=LIGHT,
        name="window_terms",
    )(place, taps, stored, vectors, *after)
    return [found[step * len(parts) : (step + 1) * len(parts)] for step in range(len(steps))]


def add_terms(terms, arrived, base, count, group, after=()):
    def kernel(terms_ref, *refs):
        out_ref, own, done = refs[-3:]
        fetch = pltpu.make_async_copy(terms_ref.at[:, pl.ds(base * group, count * group)], own, done)
        fetch.start()
        fetch.wait()
        for k in range(count):
            cols = slice(k * group, (k + 1) * group)
            total = own[:, cols].astype(jnp.float32)
            for ref, (array, first) in zip(refs, arrived):
                place = base + k - first
                if 0 <= place < array.shape[1] // group:
                    total = total + ref[:, place * group : (place + 1) * group].astype(jnp.float32)
            out_ref[:, cols] = total.astype(jnp.bfloat16)

    return pl.pallas_call(
        kernel,
        in_specs=[MAIN] + [FAST] * len(arrived) + [ANYWHERE] * len(after),
        out_specs=FAST,
        out_shape=jax.ShapeDtypeStruct((group, count * group), jnp.bfloat16),
        scratch_shapes=[pltpu.VMEM((group, count * group), jnp.bfloat16), pltpu.SemaphoreType.DMA],
        compiler_params=pltpu.CompilerParams(vmem_limit_bytes=SMALL_BYTES),
        cost_estimate=LIGHT,
        name="add_terms",
    )(terms, *[array for array, _ in arrived], *after)


def gate(values, after):
    def kernel(*refs):
        pass

    return pl.pallas_call(
        kernel,
        in_specs=[MAIN] * len(values) + [ANYWHERE] * len(after),
        out_specs=[MAIN] * len(values),
        out_shape=[jax.ShapeDtypeStruct(value.shape, value.dtype) for value in values],
        input_output_aliases={index: index for index in range(len(values))},
        compiler_params=pltpu.CompilerParams(vmem_limit_bytes=SMALL_BYTES),
        cost_estimate=LIGHT,
        name="gate",
    )(*values, *after)


def close_window(terms, base, ahead, back, slots, group, after=()):
    count = len(slots)
    chips = [chip for chip in pairs_of(slots) if chip[0] != 0]
    def kernel(terms_ref, ahead_ref, back_ref, *refs):
        blocks_ref, turned_refs, (own, done) = refs[len(after)], refs[len(after) + 1 : -2], refs[-2:]
        fetch = pltpu.make_async_copy(terms_ref.at[:, pl.ds(base * group, count * group)], own, done)
        fetch.start()
        fetch.wait()
        for k in range(count):
            cols = slice(k * group, (k + 1) * group)
            total = own[:, cols].astype(jnp.float32)
            total = total + ahead_ref[:, cols].astype(jnp.float32) + back_ref[:, cols].astype(jnp.float32)
            total = total.astype(jnp.bfloat16)
            blocks_ref[k] = total
            for (_, blocks, first), turned_ref in zip(chips, turned_refs):
                if first <= k < first + blocks:
                    turned_ref[k - first] = total.T

    sizes = [count] + [blocks for _, blocks, _ in chips]
    return pl.pallas_call(
        kernel,
        in_specs=[MAIN, FAST, FAST] + [ANYWHERE] * len(after),
        out_specs=[FAST] * len(sizes),
        out_shape=[jax.ShapeDtypeStruct((size, group, group), jnp.bfloat16) for size in sizes],
        scratch_shapes=[pltpu.VMEM((group, count * group), jnp.bfloat16), pltpu.SemaphoreType.DMA],
        compiler_params=pltpu.CompilerParams(vmem_limit_bytes=SMALL_BYTES),
        cost_estimate=LIGHT,
        name="close_window",
    )(terms, ahead, back, *after)


def rough_dot(left, right):
    return jnp.dot(left.astype(jnp.bfloat16), right.astype(jnp.bfloat16), preferred_element_type=jnp.float32)


def split_terms(value):
    high = value.astype(jnp.bfloat16)
    value = value - high.astype(jnp.float32)
    middle = value.astype(jnp.bfloat16)
    value = value - middle.astype(jnp.float32)
    return high, middle, value.astype(jnp.bfloat16)


def identity(size):
    rows = lax.broadcasted_iota(jnp.int32, (size, size), 0)
    cols = lax.broadcasted_iota(jnp.int32, (size, size), 1)
    return (rows == cols).astype(jnp.float32)


def eliminate(matrix_ref, right_ref, out_ref, work, block):
    size = matrix_ref.shape[0]
    work[...] = matrix_ref[...]
    out_ref[...] = right_ref[...]
    eye = identity(block)
    for start in range(0, size, block):
        here = slice(start, start + block)
        rest = slice(start + block, size)
        corner = work[here, here]
        norm = jnp.max(jnp.sum(jnp.abs(corner), axis=0))

        def unfinished(state):
            return jnp.logical_and(state[0] < 40, state[1] > 5e-5)

        def improve(state):
            step, _, inverse = state
            better = inverse + exact_dot(inverse, eye - exact_dot(work[here, here], inverse))
            left_over = eye - exact_dot(work[here, here], better)
            return step + 1, jnp.max(jnp.abs(left_over)), better

        found = lax.while_loop(unfinished, improve, (jnp.int32(0), jnp.float32(1.0), eye / norm))[2]
        found = found + exact_dot(found, eye - exact_dot(work[here, here], found))
        solved = exact_dot(found, out_ref[here, :])
        out_ref[here, :] = solved
        if start + block < size:
            across = exact_dot(found, work[here, rest])
            down = work[rest, here]
            work[rest, rest] = work[rest, rest] - exact_dot(down, across)
            out_ref[rest, :] = out_ref[rest, :] - exact_dot(down, solved)
            work[here, rest] = across
    for start in range(size - 2 * block, -1, -block):
        here = slice(start, start + block)
        rest = slice(start + block, size)
        out_ref[here, :] = out_ref[here, :] - exact_dot(work[here, rest], out_ref[rest, :])


def solve(place, pairs_count, mine, other, kept, came, after=()):
    group, width = mine.shape
    examples = 2 * kept.shape[0]
    size = kept.shape[0] // pairs_count

    def kernel(place_ref, mine_ref, other_ref, kept_ref, came_ref, *refs):
        out_ref, pairs_ref, matrix, right, power, inverse, first_ref = refs[len(after) :]
        for start in range(0, kept_ref.shape[0], size):
            near, far = kept_ref[start : start + size, :width], came_ref[start : start + size, :width]
            even = lax.rem(place_ref[0], 2) == 0
            first_ref[2 * start : 2 * start + size, :] = jnp.where(even, near, far)
            first_ref[2 * start + size : 2 * start + 2 * size, :] = jnp.where(even, far, near)
        eye = identity(width)
        t = place_ref[1]
        matrix[pl.ds(pl.multiple_of(t * group, group), group), :] = mine_ref[...]
        matrix[pl.ds(pl.multiple_of((1 - t) * group, group), group), :] = other_ref[...]
        turned = first_ref[...].T
        full = matrix[...] + jnp.dot(turned, first_ref[...], preferred_element_type=jnp.float32) + damping * eye
        diagonal = full * eye
        rows_scale = lax.rsqrt(jnp.sum(diagonal, axis=1, keepdims=True))
        cols_scale = lax.rsqrt(jnp.sum(diagonal, axis=0, keepdims=True))
        full = full * rows_scale * cols_scale
        matrix[...] = full
        right[...] = turned.astype(jnp.float32) * rows_scale

        sums = jnp.max(jnp.sum(jnp.abs(full), axis=0))
        squared = rough_dot(full, full)
        norm = jnp.sqrt(jnp.max(jnp.sum(jnp.abs(squared), axis=0)) + sums * sums / 128)
        start = eye - full / norm
        inverse[...] = eye + start
        power[...] = start.astype(jnp.bfloat16)
        for _ in range(7):
            raised = jnp.dot(power[...], power[...], preferred_element_type=jnp.float32).astype(jnp.bfloat16)
            power[...] = raised
            held = inverse[...]
            inverse[...] = held + jnp.dot(held.astype(jnp.bfloat16), raised, preferred_element_type=jnp.float32)
        power[...] = (inverse[...] / norm).astype(jnp.bfloat16)

        largest = jnp.max(jnp.abs(right[...]))
        out_ref[...] = jnp.dot(power[...], right[...].astype(jnp.bfloat16), preferred_element_type=jnp.float32)

        def unfinished(state):
            return jnp.logical_and(state[0] < 12, jnp.logical_not(state[1] <= 5e-5 * largest))

        def refine(state):
            left_over = right[...] - exact_dot(matrix[...], out_ref[...])
            change = jnp.dot(power[...], left_over.astype(jnp.bfloat16), preferred_element_type=jnp.float32)
            out_ref[...] = out_ref[...] + change
            return state[0] + 1, jnp.max(jnp.abs(left_over))

        worst = lax.while_loop(unfinished, refine, (jnp.int32(0), 1.0 + largest))[1]

        @pl.when(jnp.logical_not(worst <= 5e-5 * largest))
        def _():
            eliminate(matrix, right, out_ref, inverse, 128)

        solved = out_ref[...] * rows_scale
        out_ref[...] = solved
        pairs = jnp.zeros((examples, examples), jnp.float32)
        for term in split_terms(solved):
            pairs = pairs + jnp.dot(first_ref[...], term, preferred_element_type=jnp.float32)
        pairs_ref[...] = pairs

    whole = pl.BlockSpec(memory_space=pltpu.VMEM)
    return pl.pallas_call(
        kernel,
        in_specs=[pl.BlockSpec(memory_space=pltpu.SMEM)] + [whole] * 4 + [ANYWHERE] * len(after),
        out_shape=[
            jax.ShapeDtypeStruct((width, examples), jnp.float32),
            jax.ShapeDtypeStruct((examples, examples), jnp.float32),
        ],
        scratch_shapes=[
            pltpu.VMEM((width, width), jnp.float32),
            pltpu.VMEM((width, examples), jnp.float32),
            pltpu.VMEM((width, width), jnp.bfloat16),
            pltpu.VMEM((width, width), jnp.float32),
            pltpu.VMEM((examples, width), jnp.bfloat16),
        ],
        compiler_params=pltpu.CompilerParams(vmem_limit_bytes=VMEM_BYTES),
        cost_estimate=LIGHT,
        name="solve",
    )(place, mine, other, kept, came, *after)


def spread_back(place, stored, solved, owners, group, after=()):
    rows = stored.shape[0]
    width, examples = solved.shape
    pairs = owners // 2

    def kernel(place_ref, first_ref, solved_ref, *refs):
        cols, outs = refs[:owners], refs[owners + len(after) : -1]
        refs[-1][...] = jnp.zeros_like(refs[-1])
        total = jnp.zeros((rows, examples), jnp.float32)
        for term in split_terms(solved_ref[...]):
            total = total + jnp.dot(first_ref[...], term, preferred_element_type=jnp.float32)
        terms = jnp.concatenate(split_terms(total.T)[:2], axis=0)
        for index in range(owners):
            product = jnp.dot(terms, cols[index][...], preferred_element_type=jnp.float32)
            outs[index // 2][index % 2] = (product[:examples] + product[examples:]).astype(jnp.bfloat16)

    def owner(index, ref):
        return 2 * lax.rem(ref[0] // 2 + index // 2, pairs) + index % 2

    return pl.pallas_call(
        kernel,
        grid_spec=pltpu.PrefetchScalarGridSpec(
            num_scalar_prefetch=1,
            grid=(1,),
            in_specs=[
                pl.BlockSpec((rows, width), lambda i, ref: (0, 0)),
                pl.BlockSpec((width, examples), lambda i, ref: (0, 0)),
            ]
            + [
                pl.BlockSpec((rows, group), lambda i, ref, index=index: (0, 2 * owner(index, ref) + ref[1]))
                for index in range(owners)
            ]
            + [ANYWHERE] * len(after),
            out_specs=[pl.BlockSpec((2, examples, group), lambda i, ref: (0, 0, 0))] * pairs
            + [pl.BlockSpec((8, 128), lambda i, ref: (0, 0))],
        ),
        out_shape=[jax.ShapeDtypeStruct((2, examples, group), jnp.bfloat16)] * pairs
        + [jax.ShapeDtypeStruct((8, 128), jnp.float32)],
        compiler_params=pltpu.CompilerParams(vmem_limit_bytes=VMEM_BYTES),
        cost_estimate=LIGHT,
        name="spread_back",
    )(place, stored, solved, *([stored] * owners), *after)


def sum_pieces(place, came, after=()):
    _, examples, group = came[0].shape

    def kernel(place_ref, *refs):
        mine_ref, away_ref = refs[-2:]
        side = lax.rem(place_ref[0], 2)
        totals = [sum(ref[half].astype(jnp.float32) for ref in refs[: len(came)]) for half in (0, 1)]
        mine_ref[...] = jnp.where(side == 0, totals[0], totals[1])
        away_ref[...] = jnp.where(side == 0, totals[1], totals[0]).astype(jnp.bfloat16)

    return pl.pallas_call(
        kernel,
        in_specs=[pl.BlockSpec(memory_space=pltpu.SMEM)] + [FAST] * len(came) + [ANYWHERE] * len(after),
        out_specs=[FAST, FAST],
        out_shape=[
            jax.ShapeDtypeStruct((examples, group), jnp.float32),
            jax.ShapeDtypeStruct((examples, group), jnp.bfloat16),
        ],
        compiler_params=pltpu.CompilerParams(vmem_limit_bytes=SMALL_BYTES),
        cost_estimate=LIGHT,
        name="sum_pieces",
    )(place, *came, *after)


def pair_products(place, own_cols, first_pairs, mine, other, solved, after=()):
    examples, group = own_cols.shape

    def kernel(place_ref, own_ref, first_ref, mine_ref, other_ref, solved_ref, *refs):
        g = 2 * place_ref[0] + place_ref[1]
        own = own_ref[...]
        damped = solved_ref[pl.ds(pl.multiple_of(place_ref[1] * group, group), group), :].T
        rest = own - lax.dot_general(
            first_ref[...], own, (((0,), (0,)), ((), ())), precision=EXACT, preferred_element_type=jnp.float32
        )
        rest = rest - mine_ref[...] - other_ref[...].astype(jnp.float32) - jnp.where(g < 2, damping * damped, 0.0)
        products = lax.dot_general(
            rest, rest, (((1,), (1,)), ((), ())), precision=EXACT, preferred_element_type=jnp.float32
        )
        refs[-1][...] = products + jnp.where(g == 0, first_ref[...], 0.0)

    return pl.pallas_call(
        kernel,
        in_specs=[pl.BlockSpec(memory_space=pltpu.SMEM)] + [FAST] * 5 + [ANYWHERE] * len(after),
        out_specs=FAST,
        out_shape=jax.ShapeDtypeStruct((examples, examples), jnp.float32),
        compiler_params=pltpu.CompilerParams(vmem_limit_bytes=SMALL_BYTES),
        cost_estimate=LIGHT,
        name="pair_products",
    )(place, own_cols, first_pairs, mine, other, solved, *after)


def assembly_tables(ring, slots, d, t):
    start = [0] * ring.count
    arrived = [0] * ring.count
    for offset, _, first in pairs_of(slots):
        start[offset % ring.count] = first
    place = len(slots)
    for offset in ring.offsets:
        start[-offset % ring.count] = place
        arrived[-offset % ring.count] = 1
        place += 2
    here = ring.position_of(d)
    early = here < ring.half

    def look_up(values, offset):
        found = jnp.zeros_like(offset)
        for index, value in enumerate(values):
            if value:
                found = jnp.where(offset == index, value, found)
        return found

    def offsets_of(chips):
        return lax.rem(ring.position_of(chips) - here + 2 * ring.count, ring.count)

    def fetch(offset, j):
        own = (j == t) == early
        quarter = jnp.where(own, start[ring.half], place)
        return jnp.where(offset == ring.half, quarter, look_up(start, offset) + j)

    chips = jnp.arange(ring.half, dtype=jnp.int32)
    j = jnp.arange(2, dtype=jnp.int32)[None, :]
    send = fetch(offsets_of((1 - t) * ring.half + chips)[:, None], j)
    offset = offsets_of(t * ring.half + chips)[:, None, None]
    r = jnp.arange(2, dtype=jnp.int32)[None, :, None]
    u = jnp.arange(2, dtype=jnp.int32)[None, None, :]
    by_columns = jnp.where(offset == ring.half, early.astype(jnp.int32), look_up(arrived, offset)) == 1
    j = jnp.where(by_columns, r, u)
    local = fetch(offset, j)
    other = 2 * chips[:, None, None] + j
    mine = (jnp.where(by_columns, u, r) == t).astype(jnp.int32)
    final = jnp.stack([local, other, mine]).reshape(-1)
    return send.reshape(-1).astype(jnp.int32), final.astype(jnp.int32)


def for_sibling(table, blocks, group):
    total = table.shape[0]
    wide = min(4, total)

    def kernel(table_ref, *refs):
        for k in range(wide):
            refs[-1][k] = refs[k][0]

    return pl.pallas_call(
        kernel,
        grid_spec=pltpu.PrefetchScalarGridSpec(
            num_scalar_prefetch=1,
            grid=(total // wide,),
            in_specs=[
                pl.BlockSpec((1, group, group), lambda c, ref, k=k: (ref[wide * c + k], 0, 0)) for k in range(wide)
            ],
            out_specs=pl.BlockSpec((wide, group, group), lambda c, ref: (c, 0, 0)),
        ),
        out_shape=jax.ShapeDtypeStruct((total, group, group), jnp.bfloat16),
        compiler_params=pltpu.CompilerParams(vmem_limit_bytes=SMALL_BYTES),
        cost_estimate=LIGHT,
        name="for_sibling",
    )(table, *([blocks] * wide))


def finish(place, table, blocks, other, half, group):
    wide = half // 2
    total = 4 * half

    def at(kind, r, c, k, u, ref):
        return ref[kind * total + 4 * (wide * c + k) + 2 * r + u]

    def spec(kind, k, u):
        return pl.BlockSpec((1, group, group), lambda r, c, ref, place: (at(kind, r, c, k, u, ref), 0, 0))

    order = [(k, u) for k in range(wide) for u in (0, 1)]

    def kernel(table_ref, place_ref, *refs):
        r, c = pl.program_id(0), pl.program_id(1)
        out_ref, done_ref = refs[-2:]
        done_ref[...] = jnp.zeros_like(done_ref)
        shape = (group, group)
        gap = lax.broadcasted_iota(jnp.int32, shape, 1) - lax.broadcasted_iota(jnp.int32, shape, 0)
        for index, (k, u) in enumerate(order):
            cols = slice(index * group, (index + 1) * group)
            chip = place_ref[1] * half + wide * c + k
            apart = (2 * place_ref[0] + r - 2 * chip - u) * group
            added = jnp.where(gap == apart, jnp.float32(damping), jnp.float32(0.0))
            mine = at(2, r, c, k, u, table_ref) == 1

            @pl.when(mine)
            def _():
                out_ref[:, cols] = added + refs[index][0].astype(jnp.float32)

            @pl.when(jnp.logical_not(mine))
            def _():
                out_ref[:, cols] = added + refs[len(order) + index][0].astype(jnp.float32)

    return pl.pallas_call(
        kernel,
        grid_spec=pltpu.PrefetchScalarGridSpec(
            num_scalar_prefetch=2,
            grid=(2, 2),
            in_specs=[spec(0, k, u) for k, u in order] + [spec(1, k, u) for k, u in order],
            out_specs=[
                pl.BlockSpec((group, 2 * wide * group), lambda r, c, ref, place: (r, c)),
                pl.BlockSpec((8, 128), lambda r, c, ref, place: (0, 0)),
            ],
        ),
        out_shape=[
            jax.ShapeDtypeStruct((2 * group, 2 * half * group), jnp.float32),
            jax.ShapeDtypeStruct((8, 128), jnp.float32),
        ],
        compiler_params=pltpu.CompilerParams(vmem_limit_bytes=SMALL_BYTES),
        cost_estimate=LIGHT,
        name="finish",
    )(table, place, *([blocks] * len(order)), *([other] * len(order)))


def in_order(index, mine, other, axis):
    return jnp.where(
        index == 0,
        jnp.concatenate([mine, other], axis=axis),
        jnp.concatenate([other, mine], axis=axis),
    )


def pair_swap(value, count):
    return lax.ppermute(value, "dp", [(index, index ^ 1) for index in range(count)])


def far_shift(value, step, count):
    return lax.ppermute(value, "dp", [(index, (index + 2 * step) % count) for index in range(count)])


def exchange_pairs(slice_of, pair, count):
    pairs = count // 2
    came = [slice_of(pair)]
    for step in range(1, pairs):
        came.append(far_shift(slice_of(lax.rem(pair + step, pairs)), step, count))
    return came


def natural(came, pair):
    pairs = len(came)
    pieces = []
    for index in range(pairs):
        behind = lax.rem(pair - index + pairs, pairs)
        piece = came[0]
        for step in range(1, pairs):
            piece = jnp.where(behind == step, came[step], piece)
        pieces.append(piece)
    return pieces


def scatter_pairs(value, pair, count):
    size = value.shape[0] // (count // 2)

    def slice_of(index):
        return lax.dynamic_slice_in_dim(value, index * size, size, 0)

    return sum(piece.astype(jnp.float32) for piece in exchange_pairs(slice_of, pair, count))


def local(ring, activations, out_grads, proj_in, proj_out, stored, counts, query_ids):
    owners = ring.count
    full = stored.shape[1]
    width = full // owners
    group = width // 2
    half = ring.half
    t = lax.axis_index("tensor")
    d = lax.axis_index("dp")
    pair, side = d // 2, lax.rem(d, 2)
    g = 2 * d + t
    place = jnp.stack([d, t]).astype(jnp.int32)

    pairs_count = owners // 2
    first_stored = stored[:, :width]
    corner_rows = lead_dot(lax.dynamic_slice_in_dim(first_stored, t * group, group, 1), first_stored)
    activations, out_grads, corner_rows = lax.optimization_barrier((activations, out_grads, corner_rows))
    corner_payload = scatter_pairs(corner_rows, pair, owners)

    sides = jnp.concatenate(
        [
            jnp.dot(activations, proj_in, preferred_element_type=jnp.float32),
            jnp.dot(out_grads, proj_out, preferred_element_type=jnp.float32),
        ],
        axis=1,
    )
    sides = sides + lax.ppermute(sides, "tensor", SWAP)

    examples = counts.shape[0]
    all_examples = examples * owners
    rank = proj_in.shape[1]
    position = jnp.arange(SEQ, dtype=jnp.int32)[None, :]
    weights = jnp.where(
        position < counts[:, None], 1.0 / counts.astype(jnp.float32)[:, None], jnp.float32(0.0)
    )
    outer = jnp.einsum(
        "es,esi,esj->eij",
        weights,
        sides[:, :rank].reshape(examples, SEQ, rank),
        sides[:, rank:].reshape(examples, SEQ, rank),
        precision=EXACT,
    )
    vectors = outer.reshape(examples, full).astype(jnp.bfloat16)

    def columns_for(index):
        groups = [lax.dynamic_slice_in_dim(vectors, (4 * index + 2 * s + t) * group, group, 1) for s in (0, 1)]
        return jnp.concatenate([vectors[:, :width]] + groups, axis=1)

    payloads = [columns_for(lax.rem(pair + step, pairs_count)) for step in range(pairs_count)]

    split = (len(ring.offsets) + 1) // 2
    far_slots = [(half, None)]
    for offset in ring.offsets[:split]:
        far_slots += [(offset, 0), (offset, 1)]
    near_slots = []
    for offset in ring.offsets[split:] + [0]:
        near_slots += [(offset, 0), (offset, 1)]

    slots = far_slots + near_slots
    far_count, near_count = len(far_slots), len(near_slots)
    ahead, back = ring.shift(1), ring.shift(-1)

    def terms_of(steps, parts, after=()):
        return window_terms(ring, place, stored, vectors, group, steps, parts, after)

    came = [payloads[0]] + [far_shift(payloads[step], step, owners) for step in range(1, pairs_count)]
    came = jnp.concatenate(natural(came, pair), axis=0)
    second_group = jnp.concatenate([came[:, :width], came[:, width + group :]], axis=1)
    first_group = came[:, : width + group]
    kept = jnp.where(side == 0, first_group, second_group)
    away = jnp.where(side == 0, second_group, first_group)
    received = pair_swap(away, owners)
    corner_second = corner_payload + pair_swap(corner_payload, owners)
    corner_rows = [corner_second] + [far_shift(corner_second, step, owners) for step in range(1, pairs_count)]
    corner_rows = jnp.concatenate(natural(corner_rows, pair), axis=0)
    corner_other = lax.ppermute(corner_rows, "tensor", SWAP)
    far, near = terms_of([half], [far_slots, near_slots], [away, corner_second])[0]
    second_steps = [half - 1, 1 - half, half - 2, 2 - half]
    far, near = gate([far, near], [corner_rows, received])
    second = terms_of(second_steps, [slots], [far])
    shape = (pairs_count, 1, examples, group)
    own_cols = in_order(side, kept[:, width:].reshape(shape), received[:, width:].reshape(shape), 1)
    own_cols = own_cols.reshape(all_examples, group).astype(jnp.float32)
    far_ahead = lax.ppermute(far, "dp", ahead)
    near_back = lax.ppermute(near, "dp", back)
    total = far_count + near_count
    going = add_terms(second[0][0], [(far_ahead, 0)], 0, total, group)
    coming = add_terms(second[1][0], [(near_back, far_count)], 0, total, group)

    solved, first_pairs = solve(place, pairs_count, corner_rows, corner_other, kept, received, [going, coming])
    *pieces, spread_done = spread_back(place, stored, solved, owners, group)
    later_steps = [s for step in range(half - 3, 0, -1) for s in (step, -step)] + [0]
    for step in range(half - 2, 0, -1):
        came_ahead = lax.ppermute(going, "dp", ahead)
        came_back = lax.ppermute(coming, "dp", back)
        if step == half - 2:
            (own_ahead,), (own_back,) = second[2:]
            token = [spread_done]
        else:
            index = later_steps.index(step)
            (own_ahead,), (own_back,) = later[index : index + 2]
            token = came[1:]
        if step == 1:
            far_going = add_terms(own_ahead, [(came_ahead, 0)], 0, far_count, group, token)
            far_coming = add_terms(own_back, [(came_back, 0)], 0, far_count, group, token)
            terms, away = sum_pieces(place, came, [far_going, far_coming])
            near_going = add_terms(own_ahead, [(came_ahead, 0)], far_count, near_count, group, [away])
            near_coming = add_terms(own_back, [(came_back, 0)], far_count, near_count, group, [away])
        else:
            going = add_terms(own_ahead, [(came_ahead, 0)], 0, total, group, token)
            coming = add_terms(own_back, [(came_back, 0)], 0, total, group, token)
        if step == half - 2:
            later = terms_of(later_steps, [slots], [going, coming])
            came = [pieces[0]] + [far_shift(pieces[index], index, owners) for index in range(1, pairs_count)]
    far_sums = [lax.ppermute(far_going, "dp", ahead), lax.ppermute(far_coming, "dp", back)]
    near_sums = [lax.ppermute(near_going, "dp", ahead), lax.ppermute(near_coming, "dp", back)]

    far = close_window(later[-1][0], 0, *far_sums, far_slots, group)
    near = close_window(later[-1][0], far_count, *near_sums, near_slots, group, [far[0]])
    turned = {}
    for (found, slots) in ((far, far_slots), (near, near_slots)):
        chips = [chip for chip in pairs_of(slots) if chip[0] != 0]
        for (offset, _, _), block in zip(chips, found[1:]):
            turned[offset] = block
    shifted = {
        offset: lax.ppermute(turned[offset], "dp", ring.shift(offset))
        for offset in [half] + ring.offsets
    }
    came = [shifted[offset] for offset in ring.offsets + [half]]
    blocks = jnp.concatenate([far[0], near[0]] + came, axis=0)
    send_table, final_table = assembly_tables(ring, far_slots + near_slots, d, t)
    send = for_sibling(send_table, blocks, group)
    other = lax.ppermute(send, "tensor", SWAP)
    gram, gram_done = finish(place, final_table, blocks, other, half, group)

    terms_other = pair_swap(away, owners)
    pairs = pair_products(place, own_cols, first_pairs, terms, terms_other, solved, [shifted[ring.offsets[0]]])
    bit = owners // 2
    while bit >= 1:
        kept_rows = jnp.where((d & bit) == 0, pairs[: pairs.shape[0] // 2], pairs[pairs.shape[0] // 2 :])
        sent_rows = jnp.where((d & bit) == 0, pairs[pairs.shape[0] // 2 :], pairs[: pairs.shape[0] // 2])
        came_rows = lax.ppermute(sent_rows, "dp", [(index, index ^ bit) for index in range(owners)])
        if bit == owners // 2:
            (came_rows,) = gate([came_rows], [send])
        if bit == 1:
            (came_rows,) = gate([came_rows], [gram_done])
        pairs = kept_rows + came_rows
        bit //= 2
    pairs = pairs + lax.ppermute(pairs, "tensor", SWAP)
    chosen = (query_ids[:, None] == jnp.arange(all_examples, dtype=jnp.int32)[None, :]).astype(jnp.float32)
    scores = lax.dot_general(chosen, pairs, (((1,), (1,)), ((), ())), precision=EXACT, preferred_element_type=jnp.float32) / R
    return gram, scores


def solution(mesh):
    placed = (
        P(("groups", "dp"), "tensor"),
        P(("groups", "dp"), "tensor"),
        P("tensor", None),
        P("tensor", None),
        P(("groups", "dp"), None),
        P(("groups", "dp")),
        P("groups"),
    )
    ring = Ring(mesh)

    def program(*args):
        return local(ring, *args)

    return jax.shard_map(
        program,
        mesh=mesh,
        in_specs=placed,
        out_specs=(P(("groups", "dp"), "tensor"), P("groups", "dp")),
        check_vma=False,
    )
```

```python
import jax
import jax.numpy as jnp
from jax import lax
from jax.experimental import pallas as pl
from jax.experimental.pallas import tpu as pltpu
from jax.sharding import PartitionSpec as P

R = 64
SEQ = 16
damping = 1.0
EXACT = lax.Precision.HIGHEST
SWAP = [(0, 1), (1, 0)]
VMEM_BYTES = 56 * 1024 * 1024
SMALL_BYTES = 12 * 1024 * 1024
LIGHT = pl.CostEstimate(flops=10**6, bytes_accessed=10**5, transcendentals=0)
ANYWHERE = pl.BlockSpec(memory_space=pl.ANY)
MAIN = pl.BlockSpec(memory_space=pltpu.HBM)
FAST = pl.BlockSpec(memory_space=pltpu.VMEM)


class Ring:
    def __init__(self, mesh):
        self.count = mesh.shape["dp"]
        self.half = self.count // 2
        coords = [getattr(device, "coords", None) for device in mesh.devices[0, :, 0]]
        self.folded = False
        if None not in coords:
            moving = [axis for axis in range(3) if len({place[axis] for place in coords}) > 1]
            fast = [axis for axis in moving if coords[0][axis] != coords[1][axis]]
            self.folded = len(moving) == 2 and len(fast) == 1 and len({place[fast[0]] for place in coords}) == 2
        reach = [0, 0]
        self.offsets = []
        for distance in range(self.half - 1, 0, -1):
            side = 0 if reach[0] <= reach[1] else 1
            reach[side] += distance
            self.offsets.append(distance if side == 0 else -distance)

    def index_at(self, position):
        if isinstance(position, int):
            position = position % self.count
            if not self.folded:
                return position
            return 2 * position if position < self.half else 2 * (self.count - 1 - position) + 1
        position = lax.rem(position + 2 * self.count, self.count)
        if not self.folded:
            return position
        return jnp.where(position < self.half, 2 * position, 2 * (self.count - 1 - position) + 1)

    def position_of(self, index):
        if not self.folded:
            return index
        return jnp.where(lax.rem(index, 2) == 0, index // 2, self.count - 1 - index // 2)

    def shift(self, step):
        return [(self.index_at(p), self.index_at(p + step)) for p in range(self.count)]


def lead_dot(left, right, precision=None):
    return lax.dot_general(
        left, right, (((0,), (0,)), ((), ())), precision=precision, preferred_element_type=jnp.float32
    )


def exact_dot(left, right):
    return jnp.dot(left, right, precision=EXACT, preferred_element_type=jnp.float32)


def pairs_of(slots):
    found = []
    for index, (offset, core) in enumerate(slots):
        if core is None:
            found.append((offset, 1, index))
        elif core == 0:
            found.append((offset, 2, index))
    return found


def window_terms(ring, place, stored, vectors, group, steps, parts, after=()):
    rows, full = stored.shape
    new_rows = vectors.shape[0]
    taps = jnp.array(steps, jnp.int32)
    blocks_in_all = sum(len(slots) for slots in parts)
    chunk = rows // 4

    width = blocks_in_all * group
    widths = [len(slots) * group for slots in parts]

    def kernel(place_ref, step_ref, stored_ref, vectors_ref, *refs):
        outs, (held, total, made, arrived, left_for) = refs[len(after) : -5], refs[-5:]
        i = pl.program_id(0)
        slot = lax.rem(i, 2)
        owner = lax.rem(ring.position_of(place_ref[0]) + step_ref[i] + ring.count, ring.count)
        core = place_ref[1]

        def load(index):
            rows_of = pl.ds(index * chunk, chunk)
            return pltpu.make_async_copy(stored_ref.at[rows_of], held.at[rows_of], arrived.at[index])

        def leave(step):
            copies, base = [], 0
            for part, columns in enumerate(widths):
                out_ref = outs[step * len(parts) + part]
                source = made.at[step % 2, :, pl.ds(base, columns)]
                copies.append(pltpu.make_async_copy(source, out_ref, left_for.at[step % 2, part]))
                base += columns
            return copies

        @pl.when(i == 0)
        def _():
            for index in range(4):
                load(index).start()

        for step in range(2, len(steps)):

            @pl.when(i == step)
            def _():
                for copy in leave(step - 2):
                    copy.wait()

        left = pl.ds(pl.multiple_of((2 * ring.index_at(owner) + core) * group, group), group)
        chips, base = [], 0
        for slots in parts:
            for offset, blocks, first in pairs_of(slots):
                column = 2 * ring.index_at(owner + offset)
                if blocks == 1:
                    column = column + jnp.where(owner < ring.half, core, 1 - core)
                right = pl.ds(pl.multiple_of(column * group, blocks * group), blocks * group)
                chips.append((right, slice((base + first) * group, (base + first + blocks) * group)))
            base += len(slots)
        turned_new = vectors_ref[:, left].T

        @pl.when(i == 0)
        def _():
            for right, here in chips:
                total[:, here] = jnp.dot(turned_new, vectors_ref[:, right], preferred_element_type=jnp.float32)
            for index in range(4):
                load(index).wait()
                rows_of = slice(index * chunk, (index + 1) * chunk)
                turned = held[rows_of, left].T
                for right, here in chips:
                    added = total[:, here] + jnp.dot(turned, held[rows_of, right], preferred_element_type=jnp.float32)
                    if index < 3:
                        total[:, here] = added
                    else:
                        made[0, :, here] = added.astype(jnp.bfloat16)

        if len(steps) > 1:

            @pl.when(i > 0)
            def _():
                turned = held[:, left].T
                for right, here in chips:
                    added = jnp.dot(turned, held[:, right], preferred_element_type=jnp.float32)
                    added = added + jnp.dot(turned_new, vectors_ref[:, right], preferred_element_type=jnp.float32)
                    made[slot, :, here] = added.astype(jnp.bfloat16)

        for step in range(len(steps)):

            @pl.when(i == step)
            def _():
                for copy in leave(step):
                    copy.start()

        @pl.when(i == len(steps) - 1)
        def _():
            for step in range(max(len(steps) - 2, 0), len(steps)):
                for copy in leave(step):
                    copy.wait()

    found = pl.pallas_call(
        kernel,
        grid_spec=pltpu.PrefetchScalarGridSpec(
            num_scalar_prefetch=2,
            grid=(len(steps),),
            in_specs=[MAIN, pl.BlockSpec((new_rows, full), lambda i, a, b: (0, 0))] + [ANYWHERE] * len(after),
            out_specs=[MAIN] * (len(steps) * len(parts)),
            scratch_shapes=[
                pltpu.VMEM((rows, full), jnp.bfloat16),
                pltpu.VMEM((group, width), jnp.float32),
                pltpu.VMEM((2, group, width), jnp.bfloat16),
                pltpu.SemaphoreType.DMA((4,)),
                pltpu.SemaphoreType.DMA((2, len(parts))),
            ],
        ),
        out_shape=[jax.ShapeDtypeStruct((group, columns), jnp.bfloat16) for _ in steps for columns in widths],
        compiler_params=pltpu.CompilerParams(vmem_limit_bytes=VMEM_BYTES),
        cost_estimate=LIGHT,
        name="window_terms",
    )(place, taps, stored, vectors, *after)
    return [found[step * len(parts) : (step + 1) * len(parts)] for step in range(len(steps))]


def add_terms(terms, arrived, base, count, group, after=()):
    def kernel(terms_ref, *refs):
        out_ref, own, done = refs[-3:]
        fetch = pltpu.make_async_copy(terms_ref.at[:, pl.ds(base * group, count * group)], own, done)
        fetch.start()
        fetch.wait()
        for k in range(count):
            cols = slice(k * group, (k + 1) * group)
            total = own[:, cols].astype(jnp.float32)
            for ref, (array, first) in zip(refs, arrived):
                place = base + k - first
                if 0 <= place < array.shape[1] // group:
                    total = total + ref[:, place * group : (place + 1) * group].astype(jnp.float32)
            out_ref[:, cols] = total.astype(jnp.bfloat16)

    return pl.pallas_call(
        kernel,
        in_specs=[MAIN] + [FAST] * len(arrived) + [ANYWHERE] * len(after),
        out_specs=FAST,
        out_shape=jax.ShapeDtypeStruct((group, count * group), jnp.bfloat16),
        scratch_shapes=[pltpu.VMEM((group, count * group), jnp.bfloat16), pltpu.SemaphoreType.DMA],
        compiler_params=pltpu.CompilerParams(vmem_limit_bytes=SMALL_BYTES),
        cost_estimate=LIGHT,
        name="add_terms",
    )(terms, *[array for array, _ in arrived], *after)


def gate(values, after):
    def kernel(*refs):
        pass

    return pl.pallas_call(
        kernel,
        in_specs=[MAIN] * len(values) + [ANYWHERE] * len(after),
        out_specs=[MAIN] * len(values),
        out_shape=[jax.ShapeDtypeStruct(value.shape, value.dtype) for value in values],
        input_output_aliases={index: index for index in range(len(values))},
        compiler_params=pltpu.CompilerParams(vmem_limit_bytes=SMALL_BYTES),
        cost_estimate=LIGHT,
        name="gate",
    )(*values, *after)


def close_window(terms, base, ahead, back, slots, group, after=()):
    count = len(slots)
    chips = [chip for chip in pairs_of(slots) if chip[0] != 0]
    def kernel(terms_ref, ahead_ref, back_ref, *refs):
        blocks_ref, turned_refs, (own, done) = refs[len(after)], refs[len(after) + 1 : -2], refs[-2:]
        fetch = pltpu.make_async_copy(terms_ref.at[:, pl.ds(base * group, count * group)], own, done)
        fetch.start()
        fetch.wait()
        for k in range(count):
            cols = slice(k * group, (k + 1) * group)
            total = own[:, cols].astype(jnp.float32)
            total = total + ahead_ref[:, cols].astype(jnp.float32) + back_ref[:, cols].astype(jnp.float32)
            total = total.astype(jnp.bfloat16)
            blocks_ref[k] = total
            for (_, blocks, first), turned_ref in zip(chips, turned_refs):
                if first <= k < first + blocks:
                    turned_ref[k - first] = total.T

    sizes = [count] + [blocks for _, blocks, _ in chips]
    return pl.pallas_call(
        kernel,
        in_specs=[MAIN, FAST, FAST] + [ANYWHERE] * len(after),
        out_specs=[FAST] * len(sizes),
        out_shape=[jax.ShapeDtypeStruct((size, group, group), jnp.bfloat16) for size in sizes],
        scratch_shapes=[pltpu.VMEM((group, count * group), jnp.bfloat16), pltpu.SemaphoreType.DMA],
        compiler_params=pltpu.CompilerParams(vmem_limit_bytes=SMALL_BYTES),
        cost_estimate=LIGHT,
        name="close_window",
    )(terms, ahead, back, *after)


def rough_dot(left, right):
    return jnp.dot(left.astype(jnp.bfloat16), right.astype(jnp.bfloat16), preferred_element_type=jnp.float32)


def split_terms(value):
    high = value.astype(jnp.bfloat16)
    value = value - high.astype(jnp.float32)
    middle = value.astype(jnp.bfloat16)
    value = value - middle.astype(jnp.float32)
    return high, middle, value.astype(jnp.bfloat16)


def identity(size):
    rows = lax.broadcasted_iota(jnp.int32, (size, size), 0)
    cols = lax.broadcasted_iota(jnp.int32, (size, size), 1)
    return (rows == cols).astype(jnp.float32)


def eliminate(matrix_ref, right_ref, out_ref, work, block):
    size = matrix_ref.shape[0]
    work[...] = matrix_ref[...]
    out_ref[...] = right_ref[...]
    eye = identity(block)
    for start in range(0, size, block):
        here = slice(start, start + block)
        rest = slice(start + block, size)
        corner = work[here, here]
        norm = jnp.max(jnp.sum(jnp.abs(corner), axis=0))

        def unfinished(state):
            return jnp.logical_and(state[0] < 40, state[1] > 5e-5)

        def improve(state):
            step, _, inverse = state
            better = inverse + exact_dot(inverse, eye - exact_dot(work[here, here], inverse))
            left_over = eye - exact_dot(work[here, here], better)
            return step + 1, jnp.max(jnp.abs(left_over)), better

        found = lax.while_loop(unfinished, improve, (jnp.int32(0), jnp.float32(1.0), eye / norm))[2]
        found = found + exact_dot(found, eye - exact_dot(work[here, here], found))
        solved = exact_dot(found, out_ref[here, :])
        out_ref[here, :] = solved
        if start + block < size:
            across = exact_dot(found, work[here, rest])
            down = work[rest, here]
            work[rest, rest] = work[rest, rest] - exact_dot(down, across)
            out_ref[rest, :] = out_ref[rest, :] - exact_dot(down, solved)
            work[here, rest] = across
    for start in range(size - 2 * block, -1, -block):
        here = slice(start, start + block)
        rest = slice(start + block, size)
        out_ref[here, :] = out_ref[here, :] - exact_dot(work[here, rest], out_ref[rest, :])


def solve(place, pairs_count, mine, other, kept, came, after=()):
    group, width = mine.shape
    examples = 2 * kept.shape[0]
    size = kept.shape[0] // pairs_count

    def kernel(place_ref, mine_ref, other_ref, kept_ref, came_ref, *refs):
        out_ref, pairs_ref, matrix, right, power, inverse, first_ref = refs[len(after) :]
        for start in range(0, kept_ref.shape[0], size):
            near, far = kept_ref[start : start + size, :width], came_ref[start : start + size, :width]
            even = lax.rem(place_ref[0], 2) == 0
            first_ref[2 * start : 2 * start + size, :] = jnp.where(even, near, far)
            first_ref[2 * start + size : 2 * start + 2 * size, :] = jnp.where(even, far, near)
        eye = identity(width)
        t = place_ref[1]
        matrix[pl.ds(pl.multiple_of(t * group, group), group), :] = mine_ref[...]
        matrix[pl.ds(pl.multiple_of((1 - t) * group, group), group), :] = other_ref[...]
        turned = first_ref[...].T
        full = matrix[...] + jnp.dot(turned, first_ref[...], preferred_element_type=jnp.float32) + damping * eye
        diagonal = full * eye
        rows_scale = lax.rsqrt(jnp.sum(diagonal, axis=1, keepdims=True))
        cols_scale = lax.rsqrt(jnp.sum(diagonal, axis=0, keepdims=True))
        full = full * rows_scale * cols_scale
        matrix[...] = full
        right[...] = turned.astype(jnp.float32) * rows_scale

        sums = jnp.max(jnp.sum(jnp.abs(full), axis=0))
        squared = rough_dot(full, full)
        norm = jnp.sqrt(jnp.max(jnp.sum(jnp.abs(squared), axis=0)) + sums * sums / 128)
        start = eye - full / norm
        inverse[...] = eye + start
        power[...] = start.astype(jnp.bfloat16)
        for _ in range(7):
            raised = jnp.dot(power[...], power[...], preferred_element_type=jnp.float32).astype(jnp.bfloat16)
            power[...] = raised
            held = inverse[...]
            inverse[...] = held + jnp.dot(held.astype(jnp.bfloat16), raised, preferred_element_type=jnp.float32)
        power[...] = (inverse[...] / norm).astype(jnp.bfloat16)

        largest = jnp.max(jnp.abs(right[...]))
        out_ref[...] = jnp.dot(power[...], right[...].astype(jnp.bfloat16), preferred_element_type=jnp.float32)

        def unfinished(state):
            return jnp.logical_and(state[0] < 12, jnp.logical_not(state[1] <= 5e-5 * largest))

        def refine(state):
            left_over = right[...] - exact_dot(matrix[...], out_ref[...])
            change = jnp.dot(power[...], left_over.astype(jnp.bfloat16), preferred_element_type=jnp.float32)
            out_ref[...] = out_ref[...] + change
            return state[0] + 1, jnp.max(jnp.abs(left_over))

        worst = lax.while_loop(unfinished, refine, (jnp.int32(0), 1.0 + largest))[1]

        @pl.when(jnp.logical_not(worst <= 5e-5 * largest))
        def _():
            eliminate(matrix, right, out_ref, inverse, 128)

        solved = out_ref[...] * rows_scale
        out_ref[...] = solved
        pairs = jnp.zeros((examples, examples), jnp.float32)
        for term in split_terms(solved):
            pairs = pairs + jnp.dot(first_ref[...], term, preferred_element_type=jnp.float32)
        pairs_ref[...] = pairs

    whole = pl.BlockSpec(memory_space=pltpu.VMEM)
    return pl.pallas_call(
        kernel,
        in_specs=[pl.BlockSpec(memory_space=pltpu.SMEM)] + [whole] * 4 + [ANYWHERE] * len(after),
        out_shape=[
            jax.ShapeDtypeStruct((width, examples), jnp.float32),
            jax.ShapeDtypeStruct((examples, examples), jnp.float32),
        ],
        scratch_shapes=[
            pltpu.VMEM((width, width), jnp.float32),
            pltpu.VMEM((width, examples), jnp.float32),
            pltpu.VMEM((width, width), jnp.bfloat16),
            pltpu.VMEM((width, width), jnp.float32),
            pltpu.VMEM((examples, width), jnp.bfloat16),
        ],
        compiler_params=pltpu.CompilerParams(vmem_limit_bytes=VMEM_BYTES),
        cost_estimate=LIGHT,
        name="solve",
    )(place, mine, other, kept, came, *after)


def spread_back(place, stored, solved, owners, group, after=()):
    rows = stored.shape[0]
    width, examples = solved.shape
    pairs = owners // 2

    def kernel(place_ref, first_ref, solved_ref, *refs):
        cols, outs = refs[:owners], refs[owners + len(after) : -1]
        refs[-1][...] = jnp.zeros_like(refs[-1])
        total = jnp.zeros((rows, examples), jnp.float32)
        for term in split_terms(solved_ref[...]):
            total = total + jnp.dot(first_ref[...], term, preferred_element_type=jnp.float32)
        terms = jnp.concatenate(split_terms(total.T)[:2], axis=0)
        for index in range(owners):
            product = jnp.dot(terms, cols[index][...], preferred_element_type=jnp.float32)
            outs[index // 2][index % 2] = (product[:examples] + product[examples:]).astype(jnp.bfloat16)

    def owner(index, ref):
        return 2 * lax.rem(ref[0] // 2 + index // 2, pairs) + index % 2

    return pl.pallas_call(
        kernel,
        grid_spec=pltpu.PrefetchScalarGridSpec(
            num_scalar_prefetch=1,
            grid=(1,),
            in_specs=[
                pl.BlockSpec((rows, width), lambda i, ref: (0, 0)),
                pl.BlockSpec((width, examples), lambda i, ref: (0, 0)),
            ]
            + [
                pl.BlockSpec((rows, group), lambda i, ref, index=index: (0, 2 * owner(index, ref) + ref[1]))
                for index in range(owners)
            ]
            + [ANYWHERE] * len(after),
            out_specs=[pl.BlockSpec((2, examples, group), lambda i, ref: (0, 0, 0))] * pairs
            + [pl.BlockSpec((8, 128), lambda i, ref: (0, 0))],
        ),
        out_shape=[jax.ShapeDtypeStruct((2, examples, group), jnp.bfloat16)] * pairs
        + [jax.ShapeDtypeStruct((8, 128), jnp.float32)],
        compiler_params=pltpu.CompilerParams(vmem_limit_bytes=VMEM_BYTES),
        cost_estimate=LIGHT,
        name="spread_back",
    )(place, stored, solved, *([stored] * owners), *after)


def sum_pieces(place, came, after=()):
    _, examples, group = came[0].shape

    def kernel(place_ref, *refs):
        mine_ref, away_ref = refs[-2:]
        side = lax.rem(place_ref[0], 2)
        totals = [sum(ref[half].astype(jnp.float32) for ref in refs[: len(came)]) for half in (0, 1)]
        mine_ref[...] = jnp.where(side == 0, totals[0], totals[1])
        away_ref[...] = jnp.where(side == 0, totals[1], totals[0]).astype(jnp.bfloat16)

    return pl.pallas_call(
        kernel,
        in_specs=[pl.BlockSpec(memory_space=pltpu.SMEM)] + [FAST] * len(came) + [ANYWHERE] * len(after),
        out_specs=[FAST, FAST],
        out_shape=[
            jax.ShapeDtypeStruct((examples, group), jnp.float32),
            jax.ShapeDtypeStruct((examples, group), jnp.bfloat16),
        ],
        compiler_params=pltpu.CompilerParams(vmem_limit_bytes=SMALL_BYTES),
        cost_estimate=LIGHT,
        name="sum_pieces",
    )(place, *came, *after)


def pair_products(place, own_cols, first_pairs, mine, other, solved, after=()):
    examples, group = own_cols.shape

    def kernel(place_ref, own_ref, first_ref, mine_ref, other_ref, solved_ref, *refs):
        g = 2 * place_ref[0] + place_ref[1]
        own = own_ref[...]
        damped = solved_ref[pl.ds(pl.multiple_of(place_ref[1] * group, group), group), :].T
        rest = own - lax.dot_general(
            first_ref[...], own, (((0,), (0,)), ((), ())), precision=EXACT, preferred_element_type=jnp.float32
        )
        rest = rest - mine_ref[...] - other_ref[...].astype(jnp.float32) - jnp.where(g < 2, damping * damped, 0.0)
        products = lax.dot_general(
            rest, rest, (((1,), (1,)), ((), ())), precision=EXACT, preferred_element_type=jnp.float32
        )
        refs[-1][...] = products + jnp.where(g == 0, first_ref[...], 0.0)

    return pl.pallas_call(
        kernel,
        in_specs=[pl.BlockSpec(memory_space=pltpu.SMEM)] + [FAST] * 5 + [ANYWHERE] * len(after),
        out_specs=FAST,
        out_shape=jax.ShapeDtypeStruct((examples, examples), jnp.float32),
        compiler_params=pltpu.CompilerParams(vmem_limit_bytes=SMALL_BYTES),
        cost_estimate=LIGHT,
        name="pair_products",
    )(place, own_cols, first_pairs, mine, other, solved, *after)


def assembly_tables(ring, slots, d, t):
    start = [0] * ring.count
    arrived = [0] * ring.count
    for offset, _, first in pairs_of(slots):
        start[offset % ring.count] = first
    place = len(slots)
    for offset in ring.offsets:
        start[-offset % ring.count] = place
        arrived[-offset % ring.count] = 1
        place += 2
    here = ring.position_of(d)
    early = here < ring.half

    def look_up(values, offset):
        found = jnp.zeros_like(offset)
        for index, value in enumerate(values):
            if value:
                found = jnp.where(offset == index, value, found)
        return found

    def offsets_of(chips):
        return lax.rem(ring.position_of(chips) - here + 2 * ring.count, ring.count)

    def fetch(offset, j):
        own = (j == t) == early
        quarter = jnp.where(own, start[ring.half], place)
        return jnp.where(offset == ring.half, quarter, look_up(start, offset) + j)

    chips = jnp.arange(ring.half, dtype=jnp.int32)
    j = jnp.arange(2, dtype=jnp.int32)[None, :]
    send = fetch(offsets_of((1 - t) * ring.half + chips)[:, None], j)
    offset = offsets_of(t * ring.half + chips)[:, None, None]
    r = jnp.arange(2, dtype=jnp.int32)[None, :, None]
    u = jnp.arange(2, dtype=jnp.int32)[None, None, :]
    by_columns = jnp.where(offset == ring.half, early.astype(jnp.int32), look_up(arrived, offset)) == 1
    j = jnp.where(by_columns, r, u)
    local = fetch(offset, j)
    other = 2 * chips[:, None, None] + j
    mine = (jnp.where(by_columns, u, r) == t).astype(jnp.int32)
    final = jnp.stack([local, other, mine]).reshape(-1)
    return send.reshape(-1).astype(jnp.int32), final.astype(jnp.int32)


def for_sibling(table, blocks, group):
    total = table.shape[0]
    wide = min(4, total)

    def kernel(table_ref, *refs):
        for k in range(wide):
            refs[-1][k] = refs[k][0]

    return pl.pallas_call(
        kernel,
        grid_spec=pltpu.PrefetchScalarGridSpec(
            num_scalar_prefetch=1,
            grid=(total // wide,),
            in_specs=[
                pl.BlockSpec((1, group, group), lambda c, ref, k=k: (ref[wide * c + k], 0, 0)) for k in range(wide)
            ],
            out_specs=pl.BlockSpec((wide, group, group), lambda c, ref: (c, 0, 0)),
        ),
        out_shape=jax.ShapeDtypeStruct((total, group, group), jnp.bfloat16),
        compiler_params=pltpu.CompilerParams(vmem_limit_bytes=SMALL_BYTES),
        cost_estimate=LIGHT,
        name="for_sibling",
    )(table, *([blocks] * wide))


def finish(place, table, blocks, other, half, group):
    wide = half // 2
    total = 4 * half

    def at(kind, r, c, k, u, ref):
        return ref[kind * total + 4 * (wide * c + k) + 2 * r + u]

    def spec(kind, k, u):
        return pl.BlockSpec((1, group, group), lambda r, c, ref, place: (at(kind, r, c, k, u, ref), 0, 0))

    order = [(k, u) for k in range(wide) for u in (0, 1)]

    def kernel(table_ref, place_ref, *refs):
        r, c = pl.program_id(0), pl.program_id(1)
        out_ref, done_ref = refs[-2:]
        done_ref[...] = jnp.zeros_like(done_ref)
        shape = (group, group)
        gap = lax.broadcasted_iota(jnp.int32, shape, 1) - lax.broadcasted_iota(jnp.int32, shape, 0)
        for index, (k, u) in enumerate(order):
            cols = slice(index * group, (index + 1) * group)
            chip = place_ref[1] * half + wide * c + k
            apart = (2 * place_ref[0] + r - 2 * chip - u) * group
            added = jnp.where(gap == apart, jnp.float32(damping), jnp.float32(0.0))
            mine = at(2, r, c, k, u, table_ref) == 1

            @pl.when(mine)
            def _():
                out_ref[:, cols] = added + refs[index][0].astype(jnp.float32)

            @pl.when(jnp.logical_not(mine))
            def _():
                out_ref[:, cols] = added + refs[len(order) + index][0].astype(jnp.float32)

    return pl.pallas_call(
        kernel,
        grid_spec=pltpu.PrefetchScalarGridSpec(
            num_scalar_prefetch=2,
            grid=(2, 2),
            in_specs=[spec(0, k, u) for k, u in order] + [spec(1, k, u) for k, u in order],
            out_specs=[
                pl.BlockSpec((group, 2 * wide * group), lambda r, c, ref, place: (r, c)),
                pl.BlockSpec((8, 128), lambda r, c, ref, place: (0, 0)),
            ],
        ),
        out_shape=[
            jax.ShapeDtypeStruct((2 * group, 2 * half * group), jnp.float32),
            jax.ShapeDtypeStruct((8, 128), jnp.float32),
        ],
        compiler_params=pltpu.CompilerParams(vmem_limit_bytes=SMALL_BYTES),
        cost_estimate=LIGHT,
        name="finish",
    )(table, place, *([blocks] * len(order)), *([other] * len(order)))


def in_order(index, mine, other, axis):
    return jnp.where(
        index == 0,
        jnp.concatenate([mine, other], axis=axis),
        jnp.concatenate([other, mine], axis=axis),
    )


def pair_swap(value, count):
    return lax.ppermute(value, "dp", [(index, index ^ 1) for index in range(count)])


def far_shift(value, step, count):
    return lax.ppermute(value, "dp", [(index, (index + 2 * step) % count) for index in range(count)])


def exchange_pairs(slice_of, pair, count):
    pairs = count // 2
    came = [slice_of(pair)]
    for step in range(1, pairs):
        came.append(far_shift(slice_of(lax.rem(pair + step, pairs)), step, count))
    return came


def natural(came, pair):
    pairs = len(came)
    pieces = []
    for index in range(pairs):
        behind = lax.rem(pair - index + pairs, pairs)
        piece = came[0]
        for step in range(1, pairs):
            piece = jnp.where(behind == step, came[step], piece)
        pieces.append(piece)
    return pieces


def scatter_pairs(value, pair, count):
    size = value.shape[0] // (count // 2)

    def slice_of(index):
        return lax.dynamic_slice_in_dim(value, index * size, size, 0)

    return sum(piece.astype(jnp.float32) for piece in exchange_pairs(slice_of, pair, count))


def local(ring, activations, out_grads, proj_in, proj_out, stored, counts, query_ids):
    owners = ring.count
    full = stored.shape[1]
    width = full // owners
    group = width // 2
    half = ring.half
    t = lax.axis_index("tensor")
    d = lax.axis_index("dp")
    pair, side = d // 2, lax.rem(d, 2)
    g = 2 * d + t
    place = jnp.stack([d, t]).astype(jnp.int32)

    pairs_count = owners // 2
    first_stored = stored[:, :width]
    corner_rows = lead_dot(lax.dynamic_slice_in_dim(first_stored, t * group, group, 1), first_stored)
    activations, out_grads, corner_rows = lax.optimization_barrier((activations, out_grads, corner_rows))
    corner_payload = scatter_pairs(corner_rows, pair, owners)

    sides = jnp.concatenate(
        [
            jnp.dot(activations, proj_in, preferred_element_type=jnp.float32),
            jnp.dot(out_grads, proj_out, preferred_element_type=jnp.float32),
        ],
        axis=1,
    )
    sides = sides + lax.ppermute(sides, "tensor", SWAP)

    examples = counts.shape[0]
    all_examples = examples * owners
    rank = proj_in.shape[1]
    position = jnp.arange(SEQ, dtype=jnp.int32)[None, :]
    weights = jnp.where(
        position < counts[:, None], 1.0 / counts.astype(jnp.float32)[:, None], jnp.float32(0.0)
    )
    outer = jnp.einsum(
        "es,esi,esj->eij",
        weights,
        sides[:, :rank].reshape(examples, SEQ, rank),
        sides[:, rank:].reshape(examples, SEQ, rank),
        precision=EXACT,
    )
    vectors = outer.reshape(examples, full).astype(jnp.bfloat16)

    def columns_for(index):
        groups = [lax.dynamic_slice_in_dim(vectors, (4 * index + 2 * s + t) * group, group, 1) for s in (0, 1)]
        return jnp.concatenate([vectors[:, :width]] + groups, axis=1)

    payloads = [columns_for(lax.rem(pair + step, pairs_count)) for step in range(pairs_count)]

    split = (len(ring.offsets) + 1) // 2
    far_slots = [(half, None)]
    for offset in ring.offsets[:split]:
        far_slots += [(offset, 0), (offset, 1)]
    near_slots = []
    for offset in ring.offsets[split:] + [0]:
        near_slots += [(offset, 0), (offset, 1)]

    slots = far_slots + near_slots
    far_count, near_count = len(far_slots), len(near_slots)
    ahead, back = ring.shift(1), ring.shift(-1)

    def terms_of(steps, parts, after=()):
        return window_terms(ring, place, stored, vectors, group, steps, parts, after)

    came = [payloads[0]] + [far_shift(payloads[step], step, owners) for step in range(1, pairs_count)]
    came = jnp.concatenate(natural(came, pair), axis=0)
    second_group = jnp.concatenate([came[:, :width], came[:, width + group :]], axis=1)
    first_group = came[:, : width + group]
    kept = jnp.where(side == 0, first_group, second_group)
    away = jnp.where(side == 0, second_group, first_group)
    received = pair_swap(away, owners)
    corner_second = corner_payload + pair_swap(corner_payload, owners)
    corner_rows = [corner_second] + [far_shift(corner_second, step, owners) for step in range(1, pairs_count)]
    corner_rows = jnp.concatenate(natural(corner_rows, pair), axis=0)
    corner_other = lax.ppermute(corner_rows, "tensor", SWAP)
    far, near = terms_of([half], [far_slots, near_slots], [away, corner_second])[0]
    second_steps = [half - 1, 1 - half, half - 2, 2 - half]
    far, near = gate([far, near], [corner_rows, received])
    second = terms_of(second_steps, [slots], [far])
    shape = (pairs_count, 1, examples, group)
    own_cols = in_order(side, kept[:, width:].reshape(shape), received[:, width:].reshape(shape), 1)
    own_cols = own_cols.reshape(all_examples, group).astype(jnp.float32)
    far_ahead = lax.ppermute(far, "dp", ahead)
    near_back = lax.ppermute(near, "dp", back)
    total = far_count + near_count
    going = add_terms(second[0][0], [(far_ahead, 0)], 0, total, group)
    coming = add_terms(second[1][0], [(near_back, far_count)], 0, total, group)

    solved, first_pairs = solve(place, pairs_count, corner_rows, corner_other, kept, received, [going, coming])
    *pieces, spread_done = spread_back(place, stored, solved, owners, group)
    later_steps = [s for step in range(half - 3, 0, -1) for s in (step, -step)] + [0]
    for step in range(half - 2, 0, -1):
        came_ahead = lax.ppermute(going, "dp", ahead)
        came_back = lax.ppermute(coming, "dp", back)
        if step == half - 2:
            (own_ahead,), (own_back,) = second[2:]
            token = [spread_done]
        else:
            index = later_steps.index(step)
            (own_ahead,), (own_back,) = later[index : index + 2]
            token = came[1:]
        if step == 1:
            far_going = add_terms(own_ahead, [(came_ahead, 0)], 0, far_count, group, token)
            far_coming = add_terms(own_back, [(came_back, 0)], 0, far_count, group, token[:1])
            terms, away = sum_pieces(place, came, [far_going, far_coming])
            near_going = add_terms(own_ahead, [(came_ahead, 0)], far_count, near_count, group, [away])
            near_coming = add_terms(own_back, [(came_back, 0)], far_count, near_count, group, [away])
        else:
            going = add_terms(own_ahead, [(came_ahead, 0)], 0, total, group, token)
            coming = add_terms(own_back, [(came_back, 0)], 0, total, group, token)
        if step == half - 2:
            later = terms_of(later_steps, [slots], [going, coming])
            came = [pieces[0]] + [far_shift(pieces[index], index, owners) for index in range(1, pairs_count)]
    far_sums = [lax.ppermute(far_going, "dp", ahead), lax.ppermute(far_coming, "dp", back)]
    near_sums = [lax.ppermute(near_going, "dp", ahead), lax.ppermute(near_coming, "dp", back)]

    far = close_window(later[-1][0], 0, *far_sums, far_slots, group)
    near = close_window(later[-1][0], far_count, *near_sums, near_slots, group, [far[0]])
    turned = {}
    for (found, slots) in ((far, far_slots), (near, near_slots)):
        chips = [chip for chip in pairs_of(slots) if chip[0] != 0]
        for (offset, _, _), block in zip(chips, found[1:]):
            turned[offset] = block
    shifted = {
        offset: lax.ppermute(turned[offset], "dp", ring.shift(offset))
        for offset in [half] + ring.offsets
    }
    came = [shifted[offset] for offset in ring.offsets + [half]]
    blocks = jnp.concatenate([far[0], near[0]] + came, axis=0)
    send_table, final_table = assembly_tables(ring, far_slots + near_slots, d, t)
    send = for_sibling(send_table, blocks, group)
    other = lax.ppermute(send, "tensor", SWAP)
    gram, gram_done = finish(place, final_table, blocks, other, half, group)

    terms_other = pair_swap(away, owners)
    pairs = pair_products(place, own_cols, first_pairs, terms, terms_other, solved, [shifted[ring.offsets[0]]])
    bit = owners // 2
    while bit >= 1:
        kept_rows = jnp.where((d & bit) == 0, pairs[: pairs.shape[0] // 2], pairs[pairs.shape[0] // 2 :])
        sent_rows = jnp.where((d & bit) == 0, pairs[pairs.shape[0] // 2 :], pairs[: pairs.shape[0] // 2])
        came_rows = lax.ppermute(sent_rows, "dp", [(index, index ^ bit) for index in range(owners)])
        if bit == owners // 2:
            (came_rows,) = gate([came_rows], [send])
        if bit == 1:
            (came_rows,) = gate([came_rows], [gram_done])
        pairs = kept_rows + came_rows
        bit //= 2
    pairs = pairs + lax.ppermute(pairs, "tensor", SWAP)
    chosen = (query_ids[:, None] == jnp.arange(all_examples, dtype=jnp.int32)[None, :]).astype(jnp.float32)
    scores = lax.dot_general(chosen, pairs, (((1,), (1,)), ((), ())), precision=EXACT, preferred_element_type=jnp.float32) / R
    return gram, scores


def solution(mesh):
    placed = (
        P(("groups", "dp"), "tensor"),
        P(("groups", "dp"), "tensor"),
        P("tensor", None),
        P("tensor", None),
        P(("groups", "dp"), None),
        P(("groups", "dp")),
        P("groups"),
    )
    ring = Ring(mesh)

    def program(*args):
        return local(ring, *args)

    return jax.shard_map(
        program,
        mesh=mesh,
        in_specs=placed,
        out_specs=(P(("groups", "dp"), "tensor"), P("groups", "dp")),
        check_vma=False,
    )
```

```python
import jax
import jax.numpy as jnp
from jax import lax
from jax.experimental import pallas as pl
from jax.experimental.pallas import tpu as pltpu
from jax.sharding import PartitionSpec as P

R = 64
SEQ = 16
damping = 1.0
EXACT = lax.Precision.HIGHEST
SWAP = [(0, 1), (1, 0)]
VMEM_BYTES = 56 * 1024 * 1024
SMALL_BYTES = 12 * 1024 * 1024
LIGHT = pl.CostEstimate(flops=10**6, bytes_accessed=10**5, transcendentals=0)
ANYWHERE = pl.BlockSpec(memory_space=pl.ANY)
MAIN = pl.BlockSpec(memory_space=pltpu.HBM)
FAST = pl.BlockSpec(memory_space=pltpu.VMEM)


class Ring:
    def __init__(self, mesh):
        self.count = mesh.shape["dp"]
        self.half = self.count // 2
        coords = [getattr(device, "coords", None) for device in mesh.devices[0, :, 0]]
        self.folded = False
        if None not in coords:
            moving = [axis for axis in range(3) if len({place[axis] for place in coords}) > 1]
            fast = [axis for axis in moving if coords[0][axis] != coords[1][axis]]
            self.folded = len(moving) == 2 and len(fast) == 1 and len({place[fast[0]] for place in coords}) == 2
        reach = [0, 0]
        self.offsets = []
        for distance in range(self.half - 1, 0, -1):
            side = 0 if reach[0] <= reach[1] else 1
            reach[side] += distance
            self.offsets.append(distance if side == 0 else -distance)

    def index_at(self, position):
        if isinstance(position, int):
            position = position % self.count
            if not self.folded:
                return position
            return 2 * position if position < self.half else 2 * (self.count - 1 - position) + 1
        position = lax.rem(position + 2 * self.count, self.count)
        if not self.folded:
            return position
        return jnp.where(position < self.half, 2 * position, 2 * (self.count - 1 - position) + 1)

    def position_of(self, index):
        if not self.folded:
            return index
        return jnp.where(lax.rem(index, 2) == 0, index // 2, self.count - 1 - index // 2)

    def shift(self, step):
        return [(self.index_at(p), self.index_at(p + step)) for p in range(self.count)]


def lead_dot(left, right, precision=None):
    return lax.dot_general(
        left, right, (((0,), (0,)), ((), ())), precision=precision, preferred_element_type=jnp.float32
    )


def exact_dot(left, right):
    return jnp.dot(left, right, precision=EXACT, preferred_element_type=jnp.float32)


def pairs_of(slots):
    found = []
    for index, (offset, core) in enumerate(slots):
        if core is None:
            found.append((offset, 1, index))
        elif core == 0:
            found.append((offset, 2, index))
    return found


def window_terms(ring, place, stored, vectors, group, steps, parts, after=()):
    rows, full = stored.shape
    new_rows = vectors.shape[0]
    taps = jnp.array(steps, jnp.int32)
    blocks_in_all = sum(len(slots) for slots in parts)
    chunk = rows // 4

    width = blocks_in_all * group
    widths = [len(slots) * group for slots in parts]

    def kernel(place_ref, step_ref, stored_ref, vectors_ref, *refs):
        outs, (held, total, made, arrived, left_for) = refs[len(after) : -5], refs[-5:]
        i = pl.program_id(0)
        slot = lax.rem(i, 2)
        owner = lax.rem(ring.position_of(place_ref[0]) + step_ref[i] + ring.count, ring.count)
        core = place_ref[1]

        def load(index):
            rows_of = pl.ds(index * chunk, chunk)
            return pltpu.make_async_copy(stored_ref.at[rows_of], held.at[rows_of], arrived.at[index])

        def leave(step):
            copies, base = [], 0
            for part, columns in enumerate(widths):
                out_ref = outs[step * len(parts) + part]
                source = made.at[step % 2, :, pl.ds(base, columns)]
                copies.append(pltpu.make_async_copy(source, out_ref, left_for.at[step % 2, part]))
                base += columns
            return copies

        @pl.when(i == 0)
        def _():
            for index in range(4):
                load(index).start()

        for step in range(2, len(steps)):

            @pl.when(i == step)
            def _():
                for copy in leave(step - 2):
                    copy.wait()

        left = pl.ds(pl.multiple_of((2 * ring.index_at(owner) + core) * group, group), group)
        chips, base = [], 0
        for slots in parts:
            for offset, blocks, first in pairs_of(slots):
                column = 2 * ring.index_at(owner + offset)
                if blocks == 1:
                    column = column + jnp.where(owner < ring.half, core, 1 - core)
                right = pl.ds(pl.multiple_of(column * group, blocks * group), blocks * group)
                chips.append((right, slice((base + first) * group, (base + first + blocks) * group)))
            base += len(slots)
        turned_new = vectors_ref[:, left].T

        @pl.when(i == 0)
        def _():
            for right, here in chips:
                total[:, here] = jnp.dot(turned_new, vectors_ref[:, right], preferred_element_type=jnp.float32)
            for index in range(4):
                load(index).wait()
                rows_of = slice(index * chunk, (index + 1) * chunk)
                turned = held[rows_of, left].T
                for right, here in chips:
                    added = total[:, here] + jnp.dot(turned, held[rows_of, right], preferred_element_type=jnp.float32)
                    if index < 3:
                        total[:, here] = added
                    else:
                        made[0, :, here] = added.astype(jnp.bfloat16)

        if len(steps) > 1:

            @pl.when(i > 0)
            def _():
                turned = held[:, left].T
                for right, here in chips:
                    added = jnp.dot(turned, held[:, right], preferred_element_type=jnp.float32)
                    added = added + jnp.dot(turned_new, vectors_ref[:, right], preferred_element_type=jnp.float32)
                    made[slot, :, here] = added.astype(jnp.bfloat16)

        for step in range(len(steps)):

            @pl.when(i == step)
            def _():
                for copy in leave(step):
                    copy.start()

        @pl.when(i == len(steps) - 1)
        def _():
            for step in range(max(len(steps) - 2, 0), len(steps)):
                for copy in leave(step):
                    copy.wait()

    found = pl.pallas_call(
        kernel,
        grid_spec=pltpu.PrefetchScalarGridSpec(
            num_scalar_prefetch=2,
            grid=(len(steps),),
            in_specs=[MAIN, pl.BlockSpec((new_rows, full), lambda i, a, b: (0, 0))] + [ANYWHERE] * len(after),
            out_specs=[MAIN] * (len(steps) * len(parts)),
            scratch_shapes=[
                pltpu.VMEM((rows, full), jnp.bfloat16),
                pltpu.VMEM((group, width), jnp.float32),
                pltpu.VMEM((2, group, width), jnp.bfloat16),
                pltpu.SemaphoreType.DMA((4,)),
                pltpu.SemaphoreType.DMA((2, len(parts))),
            ],
        ),
        out_shape=[jax.ShapeDtypeStruct((group, columns), jnp.bfloat16) for _ in steps for columns in widths],
        compiler_params=pltpu.CompilerParams(vmem_limit_bytes=VMEM_BYTES),
        cost_estimate=LIGHT,
        name="window_terms",
    )(place, taps, stored, vectors, *after)
    return [found[step * len(parts) : (step + 1) * len(parts)] for step in range(len(steps))]


def add_terms(terms, arrived, base, count, group, after=()):
    def kernel(terms_ref, *refs):
        out_ref, own, done = refs[-3:]
        fetch = pltpu.make_async_copy(terms_ref.at[:, pl.ds(base * group, count * group)], own, done)
        fetch.start()
        fetch.wait()
        for k in range(count):
            cols = slice(k * group, (k + 1) * group)
            total = own[:, cols].astype(jnp.float32)
            for ref, (array, first) in zip(refs, arrived):
                place = base + k - first
                if 0 <= place < array.shape[1] // group:
                    total = total + ref[:, place * group : (place + 1) * group].astype(jnp.float32)
            out_ref[:, cols] = total.astype(jnp.bfloat16)

    return pl.pallas_call(
        kernel,
        in_specs=[MAIN] + [FAST] * len(arrived) + [ANYWHERE] * len(after),
        out_specs=FAST,
        out_shape=jax.ShapeDtypeStruct((group, count * group), jnp.bfloat16),
        scratch_shapes=[pltpu.VMEM((group, count * group), jnp.bfloat16), pltpu.SemaphoreType.DMA],
        compiler_params=pltpu.CompilerParams(vmem_limit_bytes=SMALL_BYTES),
        cost_estimate=LIGHT,
        name="add_terms",
    )(terms, *[array for array, _ in arrived], *after)


def gate(values, after):
    def kernel(*refs):
        pass

    return pl.pallas_call(
        kernel,
        in_specs=[MAIN] * len(values) + [ANYWHERE] * len(after),
        out_specs=[MAIN] * len(values),
        out_shape=[jax.ShapeDtypeStruct(value.shape, value.dtype) for value in values],
        input_output_aliases={index: index for index in range(len(values))},
        compiler_params=pltpu.CompilerParams(vmem_limit_bytes=SMALL_BYTES),
        cost_estimate=LIGHT,
        name="gate",
    )(*values, *after)


def close_window(terms, base, ahead, back, slots, group, after=()):
    count = len(slots)
    chips = [chip for chip in pairs_of(slots) if chip[0] != 0]
    def kernel(terms_ref, ahead_ref, back_ref, *refs):
        blocks_ref, turned_refs, (own, done) = refs[len(after)], refs[len(after) + 1 : -2], refs[-2:]
        fetch = pltpu.make_async_copy(terms_ref.at[:, pl.ds(base * group, count * group)], own, done)
        fetch.start()
        fetch.wait()
        for k in range(count):
            cols = slice(k * group, (k + 1) * group)
            total = own[:, cols].astype(jnp.float32)
            total = total + ahead_ref[:, cols].astype(jnp.float32) + back_ref[:, cols].astype(jnp.float32)
            total = total.astype(jnp.bfloat16)
            blocks_ref[k] = total
            for (_, blocks, first), turned_ref in zip(chips, turned_refs):
                if first <= k < first + blocks:
                    turned_ref[k - first] = total.T

    sizes = [count] + [blocks for _, blocks, _ in chips]
    return pl.pallas_call(
        kernel,
        in_specs=[MAIN, FAST, FAST] + [ANYWHERE] * len(after),
        out_specs=[FAST] * len(sizes),
        out_shape=[jax.ShapeDtypeStruct((size, group, group), jnp.bfloat16) for size in sizes],
        scratch_shapes=[pltpu.VMEM((group, count * group), jnp.bfloat16), pltpu.SemaphoreType.DMA],
        compiler_params=pltpu.CompilerParams(vmem_limit_bytes=SMALL_BYTES),
        cost_estimate=LIGHT,
        name="close_window",
    )(terms, ahead, back, *after)


def rough_dot(left, right):
    return jnp.dot(left.astype(jnp.bfloat16), right.astype(jnp.bfloat16), preferred_element_type=jnp.float32)


def split_terms(value):
    high = value.astype(jnp.bfloat16)
    value = value - high.astype(jnp.float32)
    middle = value.astype(jnp.bfloat16)
    value = value - middle.astype(jnp.float32)
    return high, middle, value.astype(jnp.bfloat16)


def identity(size):
    rows = lax.broadcasted_iota(jnp.int32, (size, size), 0)
    cols = lax.broadcasted_iota(jnp.int32, (size, size), 1)
    return (rows == cols).astype(jnp.float32)


def eliminate(matrix_ref, right_ref, out_ref, work, block):
    size = matrix_ref.shape[0]
    work[...] = matrix_ref[...]
    out_ref[...] = right_ref[...]
    eye = identity(block)
    for start in range(0, size, block):
        here = slice(start, start + block)
        rest = slice(start + block, size)
        corner = work[here, here]
        norm = jnp.max(jnp.sum(jnp.abs(corner), axis=0))

        def unfinished(state):
            return jnp.logical_and(state[0] < 40, state[1] > 5e-5)

        def improve(state):
            step, _, inverse = state
            better = inverse + exact_dot(inverse, eye - exact_dot(work[here, here], inverse))
            left_over = eye - exact_dot(work[here, here], better)
            return step + 1, jnp.max(jnp.abs(left_over)), better

        found = lax.while_loop(unfinished, improve, (jnp.int32(0), jnp.float32(1.0), eye / norm))[2]
        found = found + exact_dot(found, eye - exact_dot(work[here, here], found))
        solved = exact_dot(found, out_ref[here, :])
        out_ref[here, :] = solved
        if start + block < size:
            across = exact_dot(found, work[here, rest])
            down = work[rest, here]
            work[rest, rest] = work[rest, rest] - exact_dot(down, across)
            out_ref[rest, :] = out_ref[rest, :] - exact_dot(down, solved)
            work[here, rest] = across
    for start in range(size - 2 * block, -1, -block):
        here = slice(start, start + block)
        rest = slice(start + block, size)
        out_ref[here, :] = out_ref[here, :] - exact_dot(work[here, rest], out_ref[rest, :])


def solve(place, pairs_count, mine, other, kept, came, after=()):
    group, width = mine.shape
    examples = 2 * kept.shape[0]
    size = kept.shape[0] // pairs_count

    def kernel(place_ref, mine_ref, other_ref, kept_ref, came_ref, *refs):
        out_ref, pairs_ref, matrix, right, power, inverse, first_ref = refs[len(after) :]
        for start in range(0, kept_ref.shape[0], size):
            near, far = kept_ref[start : start + size, :width], came_ref[start : start + size, :width]
            even = lax.rem(place_ref[0], 2) == 0
            first_ref[2 * start : 2 * start + size, :] = jnp.where(even, near, far)
            first_ref[2 * start + size : 2 * start + 2 * size, :] = jnp.where(even, far, near)
        eye = identity(width)
        t = place_ref[1]
        matrix[pl.ds(pl.multiple_of(t * group, group), group), :] = mine_ref[...]
        matrix[pl.ds(pl.multiple_of((1 - t) * group, group), group), :] = other_ref[...]
        turned = first_ref[...].T
        full = matrix[...] + jnp.dot(turned, first_ref[...], preferred_element_type=jnp.float32) + damping * eye
        diagonal = full * eye
        rows_scale = lax.rsqrt(jnp.sum(diagonal, axis=1, keepdims=True))
        cols_scale = lax.rsqrt(jnp.sum(diagonal, axis=0, keepdims=True))
        full = full * rows_scale * cols_scale
        matrix[...] = full
        right[...] = turned.astype(jnp.float32) * rows_scale

        sums = jnp.max(jnp.sum(jnp.abs(full), axis=0))
        squared = rough_dot(full, full)
        norm = jnp.sqrt(jnp.max(jnp.sum(jnp.abs(squared), axis=0)) + sums * sums / 128)
        start = eye - full / norm
        inverse[...] = eye + start
        power[...] = start.astype(jnp.bfloat16)
        for _ in range(7):
            raised = jnp.dot(power[...], power[...], preferred_element_type=jnp.float32).astype(jnp.bfloat16)
            power[...] = raised
            held = inverse[...]
            inverse[...] = held + jnp.dot(held.astype(jnp.bfloat16), raised, preferred_element_type=jnp.float32)
        power[...] = (inverse[...] / norm).astype(jnp.bfloat16)

        largest = jnp.max(jnp.abs(right[...]))
        out_ref[...] = jnp.dot(power[...], right[...].astype(jnp.bfloat16), preferred_element_type=jnp.float32)

        def unfinished(state):
            return jnp.logical_and(state[0] < 12, jnp.logical_not(state[1] <= 5e-5 * largest))

        def refine(state):
            left_over = right[...] - exact_dot(matrix[...], out_ref[...])
            change = jnp.dot(power[...], left_over.astype(jnp.bfloat16), preferred_element_type=jnp.float32)
            out_ref[...] = out_ref[...] + change
            return state[0] + 1, jnp.max(jnp.abs(left_over))

        worst = lax.while_loop(unfinished, refine, (jnp.int32(0), 1.0 + largest))[1]

        @pl.when(jnp.logical_not(worst <= 5e-5 * largest))
        def _():
            eliminate(matrix, right, out_ref, inverse, 128)

        solved = out_ref[...] * rows_scale
        out_ref[...] = solved
        pairs = jnp.zeros((examples, examples), jnp.float32)
        for term in split_terms(solved):
            pairs = pairs + jnp.dot(first_ref[...], term, preferred_element_type=jnp.float32)
        pairs_ref[...] = pairs

    whole = pl.BlockSpec(memory_space=pltpu.VMEM)
    return pl.pallas_call(
        kernel,
        in_specs=[pl.BlockSpec(memory_space=pltpu.SMEM)] + [whole] * 4 + [ANYWHERE] * len(after),
        out_shape=[
            jax.ShapeDtypeStruct((width, examples), jnp.float32),
            jax.ShapeDtypeStruct((examples, examples), jnp.float32),
        ],
        scratch_shapes=[
            pltpu.VMEM((width, width), jnp.float32),
            pltpu.VMEM((width, examples), jnp.float32),
            pltpu.VMEM((width, width), jnp.bfloat16),
            pltpu.VMEM((width, width), jnp.float32),
            pltpu.VMEM((examples, width), jnp.bfloat16),
        ],
        compiler_params=pltpu.CompilerParams(vmem_limit_bytes=VMEM_BYTES),
        cost_estimate=LIGHT,
        name="solve",
    )(place, mine, other, kept, came, *after)


def spread_back(place, stored, solved, owners, group, after=()):
    rows = stored.shape[0]
    width, examples = solved.shape
    pairs = owners // 2

    def kernel(place_ref, first_ref, solved_ref, *refs):
        cols, outs = refs[:owners], refs[owners + len(after) : -1]
        refs[-1][...] = jnp.zeros_like(refs[-1])
        total = jnp.zeros((rows, examples), jnp.float32)
        for term in split_terms(solved_ref[...]):
            total = total + jnp.dot(first_ref[...], term, preferred_element_type=jnp.float32)
        terms = jnp.concatenate(split_terms(total.T)[:2], axis=0)
        for index in range(owners):
            product = jnp.dot(terms, cols[index][...], preferred_element_type=jnp.float32)
            outs[index // 2][index % 2] = (product[:examples] + product[examples:]).astype(jnp.bfloat16)

    def owner(index, ref):
        return 2 * lax.rem(ref[0] // 2 + index // 2, pairs) + index % 2

    return pl.pallas_call(
        kernel,
        grid_spec=pltpu.PrefetchScalarGridSpec(
            num_scalar_prefetch=1,
            grid=(1,),
            in_specs=[
                pl.BlockSpec((rows, width), lambda i, ref: (0, 0)),
                pl.BlockSpec((width, examples), lambda i, ref: (0, 0)),
            ]
            + [
                pl.BlockSpec((rows, group), lambda i, ref, index=index: (0, 2 * owner(index, ref) + ref[1]))
                for index in range(owners)
            ]
            + [ANYWHERE] * len(after),
            out_specs=[pl.BlockSpec((2, examples, group), lambda i, ref: (0, 0, 0))] * pairs
            + [pl.BlockSpec((8, 128), lambda i, ref: (0, 0))],
        ),
        out_shape=[jax.ShapeDtypeStruct((2, examples, group), jnp.bfloat16)] * pairs
        + [jax.ShapeDtypeStruct((8, 128), jnp.float32)],
        compiler_params=pltpu.CompilerParams(vmem_limit_bytes=VMEM_BYTES),
        cost_estimate=LIGHT,
        name="spread_back",
    )(place, stored, solved, *([stored] * owners), *after)


def sum_pieces(place, came, after=()):
    _, examples, group = came[0].shape

    def kernel(place_ref, *refs):
        mine_ref, away_ref = refs[-2:]
        side = lax.rem(place_ref[0], 2)
        totals = [sum(ref[half].astype(jnp.float32) for ref in refs[: len(came)]) for half in (0, 1)]
        mine_ref[...] = jnp.where(side == 0, totals[0], totals[1])
        away_ref[...] = jnp.where(side == 0, totals[1], totals[0]).astype(jnp.bfloat16)

    return pl.pallas_call(
        kernel,
        in_specs=[pl.BlockSpec(memory_space=pltpu.SMEM)] + [FAST] * len(came) + [ANYWHERE] * len(after),
        out_specs=[FAST, FAST],
        out_shape=[
            jax.ShapeDtypeStruct((examples, group), jnp.float32),
            jax.ShapeDtypeStruct((examples, group), jnp.bfloat16),
        ],
        compiler_params=pltpu.CompilerParams(vmem_limit_bytes=SMALL_BYTES),
        cost_estimate=LIGHT,
        name="sum_pieces",
    )(place, *came, *after)


def pair_products(place, own_cols, first_pairs, mine, other, solved, after=()):
    examples, group = own_cols.shape

    def kernel(place_ref, own_ref, first_ref, mine_ref, other_ref, solved_ref, *refs):
        g = 2 * place_ref[0] + place_ref[1]
        own = own_ref[...]
        damped = solved_ref[pl.ds(pl.multiple_of(place_ref[1] * group, group), group), :].T
        rest = own - lax.dot_general(
            first_ref[...], own, (((0,), (0,)), ((), ())), precision=EXACT, preferred_element_type=jnp.float32
        )
        rest = rest - mine_ref[...] - other_ref[...].astype(jnp.float32) - jnp.where(g < 2, damping * damped, 0.0)
        products = lax.dot_general(
            rest, rest, (((1,), (1,)), ((), ())), precision=EXACT, preferred_element_type=jnp.float32
        )
        refs[-1][...] = products + jnp.where(g == 0, first_ref[...], 0.0)

    return pl.pallas_call(
        kernel,
        in_specs=[pl.BlockSpec(memory_space=pltpu.SMEM)] + [FAST] * 5 + [ANYWHERE] * len(after),
        out_specs=FAST,
        out_shape=jax.ShapeDtypeStruct((examples, examples), jnp.float32),
        compiler_params=pltpu.CompilerParams(vmem_limit_bytes=SMALL_BYTES),
        cost_estimate=LIGHT,
        name="pair_products",
    )(place, own_cols, first_pairs, mine, other, solved, *after)


def assembly_tables(ring, slots, d, t):
    start = [0] * ring.count
    arrived = [0] * ring.count
    for offset, _, first in pairs_of(slots):
        start[offset % ring.count] = first
    place = len(slots)
    for offset in ring.offsets:
        start[-offset % ring.count] = place
        arrived[-offset % ring.count] = 1
        place += 2
    here = ring.position_of(d)
    early = here < ring.half

    def look_up(values, offset):
        found = jnp.zeros_like(offset)
        for index, value in enumerate(values):
            if value:
                found = jnp.where(offset == index, value, found)
        return found

    def offsets_of(chips):
        return lax.rem(ring.position_of(chips) - here + 2 * ring.count, ring.count)

    def fetch(offset, j):
        own = (j == t) == early
        quarter = jnp.where(own, start[ring.half], place)
        return jnp.where(offset == ring.half, quarter, look_up(start, offset) + j)

    chips = jnp.arange(ring.half, dtype=jnp.int32)
    j = jnp.arange(2, dtype=jnp.int32)[None, :]
    send = fetch(offsets_of((1 - t) * ring.half + chips)[:, None], j)
    offset = offsets_of(t * ring.half + chips)[:, None, None]
    r = jnp.arange(2, dtype=jnp.int32)[None, :, None]
    u = jnp.arange(2, dtype=jnp.int32)[None, None, :]
    by_columns = jnp.where(offset == ring.half, early.astype(jnp.int32), look_up(arrived, offset)) == 1
    j = jnp.where(by_columns, r, u)
    local = fetch(offset, j)
    other = 2 * chips[:, None, None] + j
    mine = (jnp.where(by_columns, u, r) == t).astype(jnp.int32)
    final = jnp.stack([local, other, mine]).reshape(-1)
    return send.reshape(-1).astype(jnp.int32), final.astype(jnp.int32)


def for_sibling(table, blocks, group):
    total = table.shape[0]
    wide = min(4, total)

    def kernel(table_ref, *refs):
        for k in range(wide):
            refs[-1][k] = refs[k][0]

    return pl.pallas_call(
        kernel,
        grid_spec=pltpu.PrefetchScalarGridSpec(
            num_scalar_prefetch=1,
            grid=(total // wide,),
            in_specs=[
                pl.BlockSpec((1, group, group), lambda c, ref, k=k: (ref[wide * c + k], 0, 0)) for k in range(wide)
            ],
            out_specs=pl.BlockSpec((wide, group, group), lambda c, ref: (c, 0, 0)),
        ),
        out_shape=jax.ShapeDtypeStruct((total, group, group), jnp.bfloat16),
        compiler_params=pltpu.CompilerParams(vmem_limit_bytes=SMALL_BYTES),
        cost_estimate=LIGHT,
        name="for_sibling",
    )(table, *([blocks] * wide))


def finish(place, table, blocks, other, half, group):
    wide = half // 2
    total = 4 * half

    def at(kind, r, c, k, u, ref):
        return ref[kind * total + 4 * (wide * c + k) + 2 * r + u]

    def spec(kind, k, u):
        return pl.BlockSpec((1, group, group), lambda r, c, ref, place: (at(kind, r, c, k, u, ref), 0, 0))

    order = [(k, u) for k in range(wide) for u in (0, 1)]

    def kernel(table_ref, place_ref, *refs):
        r, c = pl.program_id(0), pl.program_id(1)
        out_ref, done_ref = refs[-2:]
        done_ref[...] = jnp.zeros_like(done_ref)
        shape = (group, group)
        gap = lax.broadcasted_iota(jnp.int32, shape, 1) - lax.broadcasted_iota(jnp.int32, shape, 0)
        for index, (k, u) in enumerate(order):
            cols = slice(index * group, (index + 1) * group)
            chip = place_ref[1] * half + wide * c + k
            apart = (2 * place_ref[0] + r - 2 * chip - u) * group
            added = jnp.where(gap == apart, jnp.float32(damping), jnp.float32(0.0))
            mine = at(2, r, c, k, u, table_ref) == 1

            @pl.when(mine)
            def _():
                out_ref[:, cols] = added + refs[index][0].astype(jnp.float32)

            @pl.when(jnp.logical_not(mine))
            def _():
                out_ref[:, cols] = added + refs[len(order) + index][0].astype(jnp.float32)

    return pl.pallas_call(
        kernel,
        grid_spec=pltpu.PrefetchScalarGridSpec(
            num_scalar_prefetch=2,
            grid=(2, 2),
            in_specs=[spec(0, k, u) for k, u in order] + [spec(1, k, u) for k, u in order],
            out_specs=[
                pl.BlockSpec((group, 2 * wide * group), lambda r, c, ref, place: (r, c)),
                pl.BlockSpec((8, 128), lambda r, c, ref, place: (0, 0)),
            ],
        ),
        out_shape=[
            jax.ShapeDtypeStruct((2 * group, 2 * half * group), jnp.float32),
            jax.ShapeDtypeStruct((8, 128), jnp.float32),
        ],
        compiler_params=pltpu.CompilerParams(vmem_limit_bytes=SMALL_BYTES),
        cost_estimate=LIGHT,
        name="finish",
    )(table, place, *([blocks] * len(order)), *([other] * len(order)))


def in_order(index, mine, other, axis):
    return jnp.where(
        index == 0,
        jnp.concatenate([mine, other], axis=axis),
        jnp.concatenate([other, mine], axis=axis),
    )


def pair_swap(value, count):
    return lax.ppermute(value, "dp", [(index, index ^ 1) for index in range(count)])


def far_shift(value, step, count):
    return lax.ppermute(value, "dp", [(index, (index + 2 * step) % count) for index in range(count)])


def exchange_pairs(slice_of, pair, count):
    pairs = count // 2
    came = [slice_of(pair)]
    for step in range(1, pairs):
        came.append(far_shift(slice_of(lax.rem(pair + step, pairs)), step, count))
    return came


def natural(came, pair):
    pairs = len(came)
    pieces = []
    for index in range(pairs):
        behind = lax.rem(pair - index + pairs, pairs)
        piece = came[0]
        for step in range(1, pairs):
            piece = jnp.where(behind == step, came[step], piece)
        pieces.append(piece)
    return pieces


def scatter_pairs(value, pair, count):
    size = value.shape[0] // (count // 2)

    def slice_of(index):
        return lax.dynamic_slice_in_dim(value, index * size, size, 0)

    return sum(piece.astype(jnp.float32) for piece in exchange_pairs(slice_of, pair, count))


def local(ring, activations, out_grads, proj_in, proj_out, stored, counts, query_ids):
    owners = ring.count
    full = stored.shape[1]
    width = full // owners
    group = width // 2
    half = ring.half
    t = lax.axis_index("tensor")
    d = lax.axis_index("dp")
    pair, side = d // 2, lax.rem(d, 2)
    g = 2 * d + t
    place = jnp.stack([d, t]).astype(jnp.int32)

    pairs_count = owners // 2
    first_stored = stored[:, :width]
    corner_rows = lead_dot(lax.dynamic_slice_in_dim(first_stored, t * group, group, 1), first_stored)
    activations, out_grads, corner_rows = lax.optimization_barrier((activations, out_grads, corner_rows))
    corner_payload = scatter_pairs(corner_rows, pair, owners)

    sides = jnp.concatenate(
        [
            jnp.dot(activations, proj_in, preferred_element_type=jnp.float32),
            jnp.dot(out_grads, proj_out, preferred_element_type=jnp.float32),
        ],
        axis=1,
    )
    sides = sides + lax.ppermute(sides, "tensor", SWAP)

    examples = counts.shape[0]
    all_examples = examples * owners
    rank = proj_in.shape[1]
    position = jnp.arange(SEQ, dtype=jnp.int32)[None, :]
    weights = jnp.where(
        position < counts[:, None], 1.0 / counts.astype(jnp.float32)[:, None], jnp.float32(0.0)
    )
    outer = jnp.einsum(
        "es,esi,esj->eij",
        weights,
        sides[:, :rank].reshape(examples, SEQ, rank),
        sides[:, rank:].reshape(examples, SEQ, rank),
        precision=EXACT,
    )
    vectors = outer.reshape(examples, full).astype(jnp.bfloat16)

    def columns_for(index):
        groups = [lax.dynamic_slice_in_dim(vectors, (4 * index + 2 * s + t) * group, group, 1) for s in (0, 1)]
        return jnp.concatenate([vectors[:, :width]] + groups, axis=1)

    payloads = [columns_for(lax.rem(pair + step, pairs_count)) for step in range(pairs_count)]

    split = (len(ring.offsets) + 1) // 2
    far_slots = [(half, None)]
    for offset in ring.offsets[:split]:
        far_slots += [(offset, 0), (offset, 1)]
    near_slots = []
    for offset in ring.offsets[split:] + [0]:
        near_slots += [(offset, 0), (offset, 1)]

    slots = far_slots + near_slots
    far_count, near_count = len(far_slots), len(near_slots)
    ahead, back = ring.shift(1), ring.shift(-1)

    def terms_of(steps, parts, after=()):
        return window_terms(ring, place, stored, vectors, group, steps, parts, after)

    came = [payloads[0]] + [far_shift(payloads[step], step, owners) for step in range(1, pairs_count)]
    came = jnp.concatenate(natural(came, pair), axis=0)
    second_group = jnp.concatenate([came[:, :width], came[:, width + group :]], axis=1)
    first_group = came[:, : width + group]
    kept = jnp.where(side == 0, first_group, second_group)
    away = jnp.where(side == 0, second_group, first_group)
    received = pair_swap(away, owners)
    corner_second = corner_payload + pair_swap(corner_payload, owners)
    corner_rows = [corner_second] + [far_shift(corner_second, step, owners) for step in range(1, pairs_count)]
    corner_rows = jnp.concatenate(natural(corner_rows, pair), axis=0)
    corner_other = lax.ppermute(corner_rows, "tensor", SWAP)
    far, near = terms_of([half], [far_slots, near_slots], [away, corner_second])[0]
    second_steps = [half - 1, 1 - half, half - 2, 2 - half]
    far, near = gate([far, near], [corner_rows, received])
    second = terms_of(second_steps, [slots], [far])
    shape = (pairs_count, 1, examples, group)
    own_cols = in_order(side, kept[:, width:].reshape(shape), received[:, width:].reshape(shape), 1)
    own_cols = own_cols.reshape(all_examples, group).astype(jnp.float32)
    far_ahead = lax.ppermute(far, "dp", ahead)
    near_back = lax.ppermute(near, "dp", back)
    total = far_count + near_count
    going = add_terms(second[0][0], [(far_ahead, 0)], 0, total, group)
    coming = add_terms(second[1][0], [(near_back, far_count)], 0, total, group)

    solved, first_pairs = solve(place, pairs_count, corner_rows, corner_other, kept, received, [going, coming])
    *pieces, spread_done = spread_back(place, stored, solved, owners, group)
    later_steps = [s for step in range(half - 3, 0, -1) for s in (step, -step)] + [0]
    for step in range(half - 2, 0, -1):
        came_ahead = lax.ppermute(going, "dp", ahead)
        came_back = lax.ppermute(coming, "dp", back)
        if step == half - 2:
            (own_ahead,), (own_back,) = second[2:]
            token = [spread_done]
        else:
            index = later_steps.index(step)
            (own_ahead,), (own_back,) = later[index : index + 2]
            token = came[1:]
        if step == 1:
            far_going = add_terms(own_ahead, [(came_ahead, 0)], 0, far_count, group, token)
            far_coming = add_terms(own_back, [(came_back, 0)], 0, far_count, group)
            terms, away = sum_pieces(place, came, [far_going, far_coming])
            near_going = add_terms(own_ahead, [(came_ahead, 0)], far_count, near_count, group, [away])
            near_coming = add_terms(own_back, [(came_back, 0)], far_count, near_count, group, [away])
        else:
            going = add_terms(own_ahead, [(came_ahead, 0)], 0, total, group, token)
            coming = add_terms(own_back, [(came_back, 0)], 0, total, group, token)
        if step == half - 2:
            later = terms_of(later_steps, [slots], [going, coming])
            came = [pieces[0]] + [far_shift(pieces[index], index, owners) for index in range(1, pairs_count)]
    far_sums = [lax.ppermute(far_going, "dp", ahead), lax.ppermute(far_coming, "dp", back)]
    near_sums = [lax.ppermute(near_going, "dp", ahead), lax.ppermute(near_coming, "dp", back)]

    far = close_window(later[-1][0], 0, *far_sums, far_slots, group)
    near = close_window(later[-1][0], far_count, *near_sums, near_slots, group, [far[0]])
    turned = {}
    for (found, slots) in ((far, far_slots), (near, near_slots)):
        chips = [chip for chip in pairs_of(slots) if chip[0] != 0]
        for (offset, _, _), block in zip(chips, found[1:]):
            turned[offset] = block
    shifted = {
        offset: lax.ppermute(turned[offset], "dp", ring.shift(offset))
        for offset in [half] + ring.offsets
    }
    came = [shifted[offset] for offset in ring.offsets + [half]]
    blocks = jnp.concatenate([far[0], near[0]] + came, axis=0)
    send_table, final_table = assembly_tables(ring, far_slots + near_slots, d, t)
    send = for_sibling(send_table, blocks, group)
    other = lax.ppermute(send, "tensor", SWAP)
    gram, gram_done = finish(place, final_table, blocks, other, half, group)

    terms_other = pair_swap(away, owners)
    pairs = pair_products(place, own_cols, first_pairs, terms, terms_other, solved, [shifted[ring.offsets[0]]])
    bit = owners // 2
    while bit >= 1:
        kept_rows = jnp.where((d & bit) == 0, pairs[: pairs.shape[0] // 2], pairs[pairs.shape[0] // 2 :])
        sent_rows = jnp.where((d & bit) == 0, pairs[pairs.shape[0] // 2 :], pairs[: pairs.shape[0] // 2])
        came_rows = lax.ppermute(sent_rows, "dp", [(index, index ^ bit) for index in range(owners)])
        if bit == owners // 2:
            (came_rows,) = gate([came_rows], [send])
        if bit == 1:
            (came_rows,) = gate([came_rows], [gram_done])
        pairs = kept_rows + came_rows
        bit //= 2
    pairs = pairs + lax.ppermute(pairs, "tensor", SWAP)
    chosen = (query_ids[:, None] == jnp.arange(all_examples, dtype=jnp.int32)[None, :]).astype(jnp.float32)
    scores = lax.dot_general(chosen, pairs, (((1,), (1,)), ((), ())), precision=EXACT, preferred_element_type=jnp.float32) / R
    return gram, scores


def solution(mesh):
    placed = (
        P(("groups", "dp"), "tensor"),
        P(("groups", "dp"), "tensor"),
        P("tensor", None),
        P("tensor", None),
        P(("groups", "dp"), None),
        P(("groups", "dp")),
        P("groups"),
    )
    ring = Ring(mesh)

    def program(*args):
        return local(ring, *args)

    return jax.shard_map(
        program,
        mesh=mesh,
        in_specs=placed,
        out_specs=(P(("groups", "dp"), "tensor"), P("groups", "dp")),
        check_vma=False,
    )
```
